32 devices in a mesh: dp: 8 (over z, y), blk: 4 (over x, core).
Axes of the slice: x: 2, y: 2, z: 4, core: 2. Of those that a mesh axis runs over, the one named last changes fastest.
Arguments:
- tokens: bfloat16 [8, 1024, 768], P('dp', 'blk'), may hold values from -6 to 6
- lengths: int32 [8, 5], P('dp'), may hold values from 40 to 197, as said below
- w_qkv: bfloat16 [768, 2304], replicated, may hold values from -0.3125 to 0.3125
- w_out: bfloat16 [768, 768], replicated, may hold values from -0.4375 to 0.4375
- w_up: bfloat16 [768, 3072], replicated, may hold values from -0.21875 to 0.21875
- w_down: bfloat16 [3072, 768], replicated, may hold values from -0.15625 to 0.15625
- vectors: float32 [10752], replicated, may hold values from -0.3 to 2.5
- cotangent: bfloat16 [8, 1024, 768], P('dp', 'blk'), may hold values from -6 to 6
Outputs:
- out: bfloat16 [8, 1024, 768], P('dp', 'blk')
- grad_tokens: bfloat16 [8, 1024, 768], P('dp', 'blk')
- grad_w_qkv: float32 [768, 2304], P('blk', 'dp')
- grad_w_out: float32 [768, 768], P('blk', 'dp')
- grad_w_up: float32 [768, 3072], P('blk', 'dp')
- grad_w_down: float32 [3072, 768], P('blk', 'dp')
- grad_vectors: float32 [10752], P(('dp', 'blk'))
The draws below stay inside these ranges and needn't reach their ends.
Inputs may be any that keep to these rules, and one draw needn't show every extreme that they name: `lengths`: images fill a set's packing places in order from place 0 and padding fills the rest; in every set one image has exactly 197 visible patches and each other image 40 to 197.
All inputs are finite; a program needn't handle non-finite values.
Results may differ from the reference program's by a relative error of at most 0.022.
Values may be sent and summed in bfloat16 or wider, within the bound.
No kernel may reach another device: no remote copies, remote signals or barrier semaphores. Data moves between devices by JAX's collectives and lax.ppermute only.
A program may use at most 128 MiB of HBM per device.

```python
import math
import jax
import jax.numpy as jnp
import numpy as np
from jax import lax

D = 768
H = 12
HD = 64
FF = 3072
ROWS = 256
IMG_MOST = 197
IMG_LEAST = 40
SET_LEN = 1024
ITEMS = 5
SETS = 8


def draw_lengths(key, part):
    key = jax.random.fold_in(key, 5)
    first, second = jax.random.split(key)
    drawn = jax.random.randint(first, (SETS, ITEMS), IMG_LEAST, IMG_MOST + 1)
    placed = jax.random.randint(second, (SETS, 1), 0, ITEMS)
    column = lax.iota(jnp.int32, ITEMS)[None, :]
    return jnp.where(column == placed, IMG_MOST, drawn).astype(jnp.int32)


def draw_vectors(key, part):
    key = jax.random.fold_in(key, 7)
    first, second = jax.random.split(key)
    total = 10 * D + FF
    noise = jnp.clip(jax.random.normal(first, (total,), jnp.float32), -3.0, 3.0)
    layer_scale = jnp.exp(jax.random.uniform(second, (total,), jnp.float32, math.log(0.5), math.log(1.5)))
    slot = jnp.minimum(lax.iota(jnp.int32, total) // D, 10)
    bias_table = jnp.array(np.array([0.0, 0.1, 0.1, 0.02, 0.1, 0.0, 0.0, 0.1, 0.1, 0.0, 0.1], np.float32))
    bias_scale = jnp.take(bias_table, slot)
    is_gain = (slot == 0) | (slot == 6)
    is_scale = (slot == 5) | (slot == 9)
    gains = jnp.exp(0.3 * noise)
    return jnp.where(is_gain, gains, jnp.where(is_scale, layer_scale, bias_scale * noise)).astype(jnp.float32)


def block_levels(rng, extent, cuts, least, top_value):
    level, own = 1.0, jax.random.fold_in(rng, 6)
    for axis_at, parts in cuts:
        steps = jnp.exp(jax.random.uniform(jax.random.fold_in(own, axis_at), (parts,), jnp.float32, least / len(cuts), top_value / len(cuts)))
        level = level * jnp.repeat(steps, extent[axis_at] // parts).reshape([-1 if axis == axis_at else 1 for axis in range(len(extent))])
    return level


def gaussian(stream_key, dims, scale, most, cuts=(), kind=jnp.bfloat16):
    factor_of = block_levels(stream_key, dims, cuts, -0.22, 0.18) if cuts else 1.0
    values = jax.random.normal(stream_key, dims, jnp.float32) * scale * factor_of
    return jnp.minimum(jnp.maximum(values, -most), most).astype(kind)


def setup_inputs(seed: int = 0) -> dict:
    key_of = jax.random.split(jax.random.key(seed), 9)
    return {
        "tokens": gaussian(key_of[0], (SETS, SET_LEN, D), 1.0, 6.0, ((0, 8), (1, 4))),
        "lengths": draw_lengths(jax.random.fold_in(key_of[8], 71), 0),
        "w_qkv": gaussian(key_of[2], (D, 3 * D), (D // 2) ** -0.5, 0.3125),
        "w_out": gaussian(key_of[3], (D, D), (D // 4) ** -0.5, 0.4375),
        "w_up": gaussian(key_of[4], (D, FF), D ** -0.5, 0.21875),
        "w_down": gaussian(key_of[5], (FF, D), (FF // 2) ** -0.5, 0.15625),
        "vectors": draw_vectors(jax.random.fold_in(key_of[8], 71), 0),
        "cotangent": gaussian(key_of[7], (SETS, SET_LEN, D), 1.0, 6.0, ((0, 8), (1, 4))),
    }


EPSILON = 1e-06
HIGHEST = lax.Precision.HIGHEST

@jax.custom_vjp
def low(v):
    return lax.optimization_barrier(v.astype(jnp.bfloat16)).astype(jnp.float32)

@jax.custom_vjp
def low_back(v):
    return v

def low_keep(v):
    return (low(v), None)

def low_pass(kept, grad):
    return (grad,)

def back_keep(v):
    return (v, None)

def back_low(kept, grad):
    return (low(grad),)
low.defvjp(low_keep, low_pass)
low_back.defvjp(back_keep, back_low)

def product(left, right):
    return jnp.dot(left, right, precision=HIGHEST, preferred_element_type=jnp.float32)

def norm_rows(values, gain, shift):
    centre = lax.optimization_barrier(jnp.mean(values, axis=-1, keepdims=True))
    centred = values - centre
    spread = lax.optimization_barrier(jnp.mean(centred * centred, axis=-1, keepdims=True))
    return centred * lax.rsqrt(spread + EPSILON) * gain + shift

def attention(query, keys, values, item_of):
    total = query.shape[0]
    block = min(512, total)
    scale = HD ** (-0.5)
    query_blocks = query.reshape(total // block, block, H, HD)
    item_blocks = item_of.reshape(total // block, block)

    def one_block(item):
        query_part, item_part = item
        score = jnp.einsum('qhd,khd->hqk', query_part, keys, precision=HIGHEST) * scale
        score = low_back(score)
        allowed = (item_part[:, None] == item_of[None, :])[None]
        score = jnp.where(allowed, score, -jnp.inf)
        prob = jax.nn.softmax(score, axis=-1)
        return jnp.einsum('hqk,khd->qhd', low(prob), values, precision=HIGHEST)
    result = lax.map(jax.checkpoint(one_block), (query_blocks, item_blocks))
    return result.reshape(total, H * HD)

def layer(inputs, w_qkv, w_out, w_up, w_down, vectors, item_of):
    width = inputs.shape[1]
    pieces = [vectors[index * width:(index + 1) * width] for index in range(10)]
    gain_one, shift_one, bias_q, bias_v, bias_o, scale_one, gain_two, shift_two, bias_d, scale_two = pieces
    bias_up = vectors[10 * width:]
    normed = low(norm_rows(inputs, gain_one, shift_one))
    qkv_bias = jnp.concatenate([bias_q, jnp.zeros_like(bias_q), bias_v])
    projected = low_back(low(product(normed, w_qkv) + qkv_bias))
    query = projected[:, :width].reshape(-1, H, HD)
    keys = projected[:, width:2 * width].reshape(-1, H, HD)
    values = projected[:, 2 * width:].reshape(-1, H, HD)
    attended = low_back(low(attention(query, keys, values, item_of)))
    branch = low_back(product(attended, w_out) + bias_o)
    mid = inputs + scale_one * branch
    normed_two = low(norm_rows(mid, gain_two, shift_two))
    before = low_back(product(normed_two, w_up) + bias_up)
    activated = low(jax.nn.gelu(before, approximate=False))
    feed = low_back(product(activated, w_down) + bias_d)
    result = mid + scale_two * feed
    valid = (item_of < ITEMS).astype(result.dtype)
    return result * valid[:, None]

def reference(tokens, lengths, w_qkv, w_out, w_up, w_down, vectors, cotangent):
    weights = (w_qkv.astype(jnp.float32), w_out.astype(jnp.float32), w_up.astype(jnp.float32), w_down.astype(jnp.float32), vectors)
    zeros = tuple((jnp.zeros_like(weight) for weight in weights))

    def per_set(totals, item):
        set_rows, set_lengths, set_cotangent = item
        ends = jnp.cumsum(set_lengths).astype(jnp.int32)
        rows_index = lax.iota(jnp.int32, set_rows.shape[0])
        place = (rows_index % ROWS * (SET_LEN // ROWS) + rows_index // ROWS).astype(jnp.int32)
        item_of = lax.optimization_barrier(jnp.sum((place[:, None] >= ends[None, :]).astype(jnp.int32), axis=1)).astype(jnp.int32)

        def run(inputs, first, second, third, fourth, fifth):
            return layer(inputs, first, second, third, fourth, fifth, item_of)
        result, pull = jax.vjp(run, set_rows.astype(jnp.float32), *weights)
        grads = pull(set_cotangent.astype(jnp.float32))
        totals = tuple((running + fresh for running, fresh in zip(totals, grads[1:])))
        return (totals, (result.astype(jnp.bfloat16), grads[0].astype(jnp.bfloat16)))
    totals, (out, grad_tokens) = lax.scan(per_set, zeros, (tokens, lengths, cotangent))
    return (out, grad_tokens, totals[0], totals[1], totals[2], totals[3], totals[4])
```

```python
import functools
import math

import jax
import jax.numpy as jnp
from jax import lax
from jax.experimental import pallas as pl
from jax.experimental.pallas import tpu as pltpu
from jax.sharding import PartitionSpec as P

H = 12
HEAD_SIZE = 64
TILE = 64


EPSILON = 1e-06
FLOOR_SCORE = -1e30


def passed_along(array, axis, by):
    length = lax.axis_size(axis)
    return lax.ppermute(array, axis, [(i, (i + by) % length) for i in range(length)])


def norm_rows(values, gain, shift):
    centre = jnp.mean(values, axis=-1, keepdims=True)
    centred = values - centre
    spread = jnp.mean(centred * centred, axis=-1, keepdims=True)
    return centred * lax.rsqrt(spread + EPSILON) * gain + shift


def exact_gelu(values):
    return jax.nn.gelu(values, approximate=False)


def segment_of(rows_index, rows, parts, ends):
    place = rows_index % rows * parts + rows_index // rows
    return jnp.sum((place[:, None] >= ends[None, :]).astype(jnp.int32), axis=1)


def contract_rows(left, right):
    return lax.dot_general(
        left, right, (((0,), (0,)), ((), ())), preferred_element_type=jnp.float32
    )


def contract_cols(left, right):
    return lax.dot_general(
        left, right, (((1,), (1,)), ((), ())), preferred_element_type=jnp.float32
    )


def attend_block(query, query_item, keys, values, key_item, scale, carry):
    best, total, weighted = carry
    count = keys.shape[0]
    heads = query.shape[1]
    key_heads = keys.reshape(count, heads, -1)
    value_heads = values.reshape(count, heads, -1)
    allowed = (query_item[:, None] == key_item[None, :])[None]
    score = jnp.einsum("qhd,khd->hqk", query, key_heads, preferred_element_type=jnp.float32) * scale
    score = jnp.where(allowed, score, FLOOR_SCORE)
    newbest = jnp.maximum(best, jnp.max(score, axis=-1))
    weight = jnp.where(allowed, jnp.exp(score - newbest[..., None]), 0.0)
    factor = jnp.exp(best - newbest)
    total = total * factor + jnp.sum(weight, axis=-1)
    weighted = weighted * factor[..., None] + jnp.einsum(
        "hqk,khd->hqd", weight.astype(jnp.bfloat16), value_heads, preferred_element_type=jnp.float32
    )
    return (newbest, total, weighted)


def grad_block(query, d_out, logsum, delta, query_item, keys, values, key_item, scale):
    count = keys.shape[0]
    heads = query.shape[1]
    key_heads = keys.reshape(count, heads, -1)
    value_heads = values.reshape(count, heads, -1)
    allowed = (query_item[:, None] == key_item[None, :])[None]
    score = jnp.einsum("qhd,khd->hqk", query, key_heads, preferred_element_type=jnp.float32) * scale
    prob = jnp.where(allowed, jnp.exp(score - logsum[..., None]), 0.0)
    d_prob = jnp.einsum("qhd,khd->hqk", d_out, value_heads, preferred_element_type=jnp.float32)
    d_score = (prob * (d_prob - delta[..., None])).astype(jnp.bfloat16)
    d_query = (
        jnp.einsum("hqk,khd->qhd", d_score, key_heads, preferred_element_type=jnp.float32) * scale
    )
    d_keys = jnp.einsum("hqk,qhd->khd", d_score, query, preferred_element_type=jnp.float32) * scale
    d_values = jnp.einsum(
        "hqk,qhd->khd", prob.astype(jnp.bfloat16), d_out, preferred_element_type=jnp.float32
    )
    return (d_query, d_keys.reshape(count, -1), d_values.reshape(count, -1))


def on_device(tokens, lengths, w_qkv, w_out, w_up, w_down, vectors, cotangent):
    inputs = tokens[0].astype(jnp.float32)
    rows, width = inputs.shape
    heads = H
    head_size = width // heads
    scale = head_size ** (-0.5)
    items = lengths.shape[1]
    ends = jnp.cumsum(lengths[0])
    parts = lax.axis_size("blk")
    position = lax.axis_index("blk")
    query_item = segment_of(position * rows + lax.iota(jnp.int32, rows), rows, parts, ends)
    valid = (query_item < items).astype(jnp.float32)[:, None]
    pieces = [vectors[index * width : (index + 1) * width] for index in range(10)]
    (
        gain_one,
        shift_one,
        bias_q,
        bias_v,
        bias_o,
        scale_one,
        gain_two,
        shift_two,
        bias_d,
        scale_two,
    ) = pieces
    bias_up = vectors[10 * width :]
    normed, norm_one_pull = jax.vjp(norm_rows, inputs, gain_one, shift_one)
    normed_low = normed.astype(jnp.bfloat16)
    qkv_bias = jnp.concatenate([bias_q, jnp.zeros_like(bias_q), bias_v])
    projected = (jnp.dot(normed_low, w_qkv, preferred_element_type=jnp.float32) + qkv_bias).astype(
        jnp.bfloat16
    )
    query = projected[:, :width].reshape(rows, heads, head_size)
    keys = projected[:, width : 2 * width]
    values = projected[:, 2 * width :]
    start_state = (
        jnp.full((heads, rows), FLOOR_SCORE, jnp.float32),
        jnp.zeros((heads, rows), jnp.float32),
        jnp.zeros((heads, rows, head_size), jnp.float32),
    )
    carry = start_state
    piece = (
        lax.all_gather(keys, "blk", axis=0, tiled=True),
        lax.all_gather(values, "blk", axis=0, tiled=True),
    )
    count = piece[0].shape[0]
    size = math.gcd(count, 512)
    steps = count // size
    key_blocks = piece[0].reshape(steps, size, width)
    value_blocks = piece[1].reshape(steps, size, width)

    def inner(state, item):
        block_keys, block_values, offset = item
        key_item = segment_of(offset + lax.iota(jnp.int32, size), rows, parts, ends)
        return (
            attend_block(query, query_item, block_keys, block_values, key_item, scale, state),
            None,
        )

    carry, unused = lax.scan(
        inner, carry, (key_blocks, value_blocks, lax.iota(jnp.int32, steps) * size)
    )
    best, total, weighted = carry
    logsum = best + jnp.log(total)
    attended = (weighted / total[..., None]).transpose(1, 0, 2).reshape(rows, width)
    attended_low = attended.astype(jnp.bfloat16)
    branch = jnp.dot(attended_low, w_out, preferred_element_type=jnp.float32) + bias_o
    mid = inputs + scale_one * branch
    normed_two, norm_two_pull = jax.vjp(norm_rows, mid, gain_two, shift_two)
    normed_two_low = normed_two.astype(jnp.bfloat16)
    before = jnp.dot(normed_two_low, w_up, preferred_element_type=jnp.float32) + bias_up
    activated, gelu_pull = jax.vjp(exact_gelu, before)
    activated_low = activated.astype(jnp.bfloat16)
    feed = jnp.dot(activated_low, w_down, preferred_element_type=jnp.float32) + bias_d
    result = mid + scale_two * feed
    out = (result * valid).astype(jnp.bfloat16)
    d_result = cotangent[0].astype(jnp.float32) * valid
    d_feed = (scale_two * d_result).astype(jnp.bfloat16)
    g_scale_two = jnp.sum(d_result * feed, axis=0)
    g_bias_d = jnp.sum(d_feed.astype(jnp.float32), axis=0)
    g_w_down = contract_rows(activated_low, d_feed)
    d_activated = contract_cols(d_feed, w_down)
    d_before = gelu_pull(d_activated)[0].astype(jnp.bfloat16)
    g_bias_up = jnp.sum(d_before.astype(jnp.float32), axis=0)
    g_w_up = contract_rows(normed_two_low, d_before)
    d_normed_two = contract_cols(d_before, w_up)
    d_mid_norm, g_gain_two, g_shift_two = norm_two_pull(d_normed_two)
    d_mid = d_result + d_mid_norm
    d_branch = (scale_one * d_mid).astype(jnp.bfloat16)
    g_scale_one = jnp.sum(d_mid * branch, axis=0)
    g_bias_o = jnp.sum(d_branch.astype(jnp.float32), axis=0)
    g_w_out = contract_rows(attended_low, d_branch)
    d_attended = contract_cols(d_branch, w_out).astype(jnp.bfloat16)
    d_heads = d_attended.reshape(rows, heads, head_size)
    delta = jnp.sum(
        (d_attended.astype(jnp.float32) * attended).reshape(rows, heads, head_size), axis=-1
    ).T
    zero_query = jnp.zeros((rows, heads, head_size), jnp.float32)

    def visit_block(block_keys, block_values, owner):
        key_item = segment_of(owner * rows + lax.iota(jnp.int32, rows), rows, parts, ends)
        return grad_block(
            query, d_heads, logsum, delta, query_item, block_keys, block_values, key_item, scale
        )

    def send_back(d_keys, d_values):
        return (
            passed_along(d_keys.astype(jnp.bfloat16), "blk", 1).astype(d_keys.dtype),
            passed_along(d_values.astype(jnp.bfloat16), "blk", 1).astype(d_values.dtype),
        )

    def accumulate(state, owner):
        d_query, block_keys, block_values, d_keys, d_values = state
        dq_part, dk_part, dv_part = visit_block(block_keys, block_values, owner)
        d_keys, d_values = send_back(d_keys + dk_part, d_values + dv_part)
        return (d_query + dq_part, d_keys, d_values)

    def turn(step, state):
        owner = (position - step) % parts
        d_query, d_keys, d_values = accumulate(state, owner)
        block_keys, block_values = passed_along((state[1], state[2]), "blk", 1)
        return (d_query, block_keys, block_values, d_keys, d_values)

    zero_rows = jnp.zeros((rows, width), jnp.float32)
    state = lax.fori_loop(0, parts - 1, turn, (zero_query, keys, values, zero_rows, zero_rows))
    d_query, d_keys, d_values = accumulate(state, (position + 1) % parts)
    d_projected = jnp.concatenate([d_query.reshape(rows, width), d_keys, d_values], axis=1).astype(
        jnp.bfloat16
    )
    g_bias_q = jnp.sum(d_projected[:, :width].astype(jnp.float32), axis=0)
    g_bias_v = jnp.sum(d_projected[:, 2 * width :].astype(jnp.float32), axis=0)
    g_w_qkv = contract_rows(normed_low, d_projected)
    d_normed = contract_cols(d_projected, w_qkv)
    d_input_norm, g_gain_one, g_shift_one = norm_one_pull(d_normed)
    d_inputs = d_mid + d_input_norm
    g_vectors = jnp.concatenate(
        [
            g_gain_one,
            g_shift_one,
            g_bias_q,
            g_bias_v,
            g_bias_o,
            g_scale_one,
            g_gain_two,
            g_shift_two,
            g_bias_d,
            g_scale_two,
            g_bias_up,
        ]
    )
    column_sums = (
        lax.psum_scatter(
            g_w_qkv.astype(jnp.bfloat16), "dp", scatter_dimension=1, tiled=True
        ).astype(jnp.float32),
        lax.psum_scatter(
            g_w_out.astype(jnp.bfloat16), "dp", scatter_dimension=1, tiled=True
        ).astype(jnp.float32),
        lax.psum_scatter(g_w_up.astype(jnp.bfloat16), "dp", scatter_dimension=1, tiled=True).astype(
            jnp.float32
        ),
        lax.psum_scatter(
            g_w_down.astype(jnp.bfloat16), "dp", scatter_dimension=1, tiled=True
        ).astype(jnp.float32),
        lax.psum_scatter(
            g_vectors.astype(jnp.bfloat16), "dp", scatter_dimension=0, tiled=True
        ).astype(jnp.float32),
    )
    g_w_qkv, g_w_out, g_w_up, g_w_down, g_vectors = (
        lax.psum_scatter(
            column_sums[0].astype(jnp.bfloat16), "blk", scatter_dimension=0, tiled=True
        ).astype(jnp.float32),
        lax.psum_scatter(
            column_sums[1].astype(jnp.bfloat16), "blk", scatter_dimension=0, tiled=True
        ).astype(jnp.float32),
        lax.psum_scatter(
            column_sums[2].astype(jnp.bfloat16), "blk", scatter_dimension=0, tiled=True
        ).astype(jnp.float32),
        lax.psum_scatter(
            column_sums[3].astype(jnp.bfloat16), "blk", scatter_dimension=0, tiled=True
        ).astype(jnp.float32),
        lax.psum_scatter(
            column_sums[4].astype(jnp.bfloat16), "blk", scatter_dimension=0, tiled=True
        ).astype(jnp.float32),
    )
    return (
        out[None],
        d_inputs.astype(jnp.bfloat16)[None],
        g_w_qkv,
        g_w_out,
        g_w_up,
        g_w_down,
        g_vectors,
    )


BF = jnp.bfloat16
F32 = jnp.float32
MASKED = -1e30
VMEM_BYTES = 48 * 1024 * 1024


def dot_nn(left, right):
    return lax.dot_general(left, right, (((1,), (0,)), ((), ())), preferred_element_type=F32)


def dot_nt(left, right):
    return lax.dot_general(left, right, (((1,), (1,)), ((), ())), preferred_element_type=F32)


def dot_tn(left, right):
    return lax.dot_general(left, right, (((0,), (0,)), ((), ())), preferred_element_type=F32)


def standardise(values):
    centred = values - jnp.mean(values, axis=-1, keepdims=True)
    inverse = lax.rsqrt(jnp.mean(centred * centred, axis=-1, keepdims=True) + EPSILON)
    return centred * inverse, inverse


def standardise_grad(grad, xhat, inverse):
    first = jnp.mean(grad, axis=-1, keepdims=True)
    second = jnp.mean(grad * xhat, axis=-1, keepdims=True)
    return (grad - first - xhat * second) * inverse


def column_sum(values):
    return jnp.sum(values, axis=0, keepdims=True)


def item_at(place, where_ref, items):
    found = jnp.zeros_like(place)
    for index in range(items):
        found = found + (place >= where_ref[4 + index]).astype(jnp.int32)
    return found


def own_block(where_ref, rel_x, rel_c):
    return 2 * (where_ref[0] ^ rel_x) + (where_ref[1] ^ rel_c)


def valid_rows(where_ref, rel_c, rows, parts, items):
    row = lax.broadcasted_iota(jnp.int32, (rows, 1), 0)
    item = item_at(row * parts + own_block(where_ref, 0, rel_c), where_ref, items)
    return (item < items).astype(F32)


def chip_call(body, grid, in_specs, out_specs, out_shape, scratch=(), flops=0, moved=0):
    return pl.pallas_call(
        body,
        grid_spec=pltpu.PrefetchScalarGridSpec(
            num_scalar_prefetch=1,
            grid=grid,
            in_specs=in_specs,
            out_specs=out_specs,
            scratch_shapes=list(scratch),
        ),
        out_shape=out_shape,
        compiler_params=pltpu.CompilerParams(
            vmem_limit_bytes=VMEM_BYTES, dimension_semantics=("arbitrary",) * len(grid)
        ),
        cost_estimate=pl.CostEstimate(flops=flops, bytes_accessed=moved, transcendentals=0),
    )


def whole(*shape):
    return pl.BlockSpec(shape, lambda *at: (0,) * len(shape))


def shaped(shape, dtype):
    return jax.ShapeDtypeStruct(shape, dtype)


def local_qkv_kernel(
    where_ref, own_ref, sib_ref, vec_ref, bias_ref, weight_ref, normed_ref, query_ref, key_ref, value_ref
):
    rows = own_ref.shape[0]
    for rel_c, ref in enumerate((own_ref, sib_ref)):
        xhat, unused = standardise(ref[...].astype(F32))
        normed_ref[rel_c * rows : (rel_c + 1) * rows] = (xhat * vec_ref[0:1] + vec_ref[1:2]).astype(BF)
    projected = dot_nn(normed_ref[...], weight_ref[...])
    half = projected.shape[1] // 3
    scale = HEAD_SIZE ** (-0.5)
    query = ((projected[:, :half] + bias_ref[0:1]).astype(BF).astype(F32) * scale).astype(BF)
    key_ref[...] = projected[:, half : 2 * half].astype(BF)
    value_ref[...] = (projected[:, 2 * half :] + bias_ref[1:2]).astype(BF)
    for tile in range(rows // TILE):
        for rel_c in range(2):
            query_ref[(2 * tile + rel_c) * TILE : (2 * tile + rel_c + 1) * TILE] = query[
                rel_c * rows + tile * TILE : rel_c * rows + (tile + 1) * TILE
            ]


def feed_grad_kernel(parts, items, where_ref, own_ref, sib_ref, vec_ref, down_ref, dact_ref, turned_ref, sum_ref, held):
    rows = own_ref.shape[0]

    @pl.when(pl.program_id(0) == 0)
    def first():
        for rel_c, ref in enumerate((own_ref, sib_ref)):
            valid = valid_rows(where_ref, rel_c, rows, parts, items)
            part = (vec_ref[9:10] * (ref[...].astype(F32) * valid)).astype(BF)
            held[rel_c * rows : (rel_c + 1) * rows] = part
        turned_ref[...] = held[...].T
        sum_ref[...] = column_sum(held[:rows].astype(F32))

    dact_ref[...] = dot_nt(held[...], down_ref[...]).astype(BF)


def lanes_below(shape, count):
    return lax.broadcasted_iota(jnp.int32, shape, 1) < count


def stack_heads(pair):
    low = lanes_below(pair.shape, HEAD_SIZE)
    zero = jnp.zeros_like(pair)
    return jnp.concatenate([jnp.where(low, pair, zero), jnp.where(low, zero, pair)], axis=0)


def join_heads(stacked_turned):
    stacked = stacked_turned.T
    count = stacked.shape[0] // 2
    return jnp.where(
        lanes_below((count, stacked.shape[1]), HEAD_SIZE), stacked[:count], stacked[count:]
    )


def query_items(where_ref, tile, parts, items):
    lane = lax.broadcasted_iota(jnp.int32, (1, 4 * TILE), 1)
    rel_c = (lane // TILE) % 2
    block = 2 * where_ref[0] + (where_ref[1] ^ rel_c)
    return item_at((tile * TILE + lane % TILE) * parts + block, where_ref, items)


def key_items(where_ref, first, count, parts, items):
    row = lax.broadcasted_iota(jnp.int32, (count * parts * TILE, 1), 0)
    tile = first + row // (parts * TILE)
    slot = (row // TILE) % parts
    block = 2 * (where_ref[0] ^ (slot // 2)) + (where_ref[1] ^ (slot % 2))
    return item_at((tile * TILE + row % TILE) * parts + block, where_ref, items)


def item_of_place(where_ref, place, items):
    found = jnp.int32(0)
    for index in range(items):
        found = found + (place >= where_ref[4 + index]).astype(jnp.int32)
    return found


def tiles_meet(where_ref, one, other, parts, items):
    span = TILE * parts
    low, high = min(one, other), max(one, other)
    return item_of_place(where_ref, low * span + span - 1, items) >= item_of_place(
        where_ref, high * span, items
    )


def near_tiles(tile, tiles):
    return max(0, tile - 1), min(tiles, tile + 2)


def attend_kernel(
    parts, items, where_ref, far_a_ref, far_b_ref, vec_ref, bias_ref, weight_ref, query_ref, key_ref, value_ref,
    normed_ref, keys_ref, values_ref, attended_ref, logsum_ref, best_ref, total_ref, mixed_ref,
):
    rows = far_a_ref.shape[0]
    tiles = rows // TILE
    span = parts * TILE
    width = query_ref.shape[1]
    for rel_c, ref in enumerate((far_a_ref, far_b_ref)):
        xhat, unused = standardise(ref[...].astype(F32))
        normed_ref[rel_c * rows : (rel_c + 1) * rows] = (xhat * vec_ref[0:1] + vec_ref[1:2]).astype(BF)
    projected = dot_nn(normed_ref[...], weight_ref[:, width:])
    far_keys = projected[:, :width].astype(BF)
    far_values = (projected[:, width:] + bias_ref[1:2]).astype(BF)
    for tile in range(tiles):
        for slot in range(2):
            to = slice(tile * span + slot * TILE, tile * span + (slot + 1) * TILE)
            at = slice(slot * rows + tile * TILE, slot * rows + (tile + 1) * TILE)
            keys_ref[to] = key_ref[at]
            values_ref[to] = value_ref[at]
            to = slice(tile * span + (slot + 2) * TILE, tile * span + (slot + 3) * TILE)
            keys_ref[to] = far_keys[at]
            values_ref[to] = far_values[at]

    def pair(index, carry):
        lanes = pl.ds(pl.multiple_of(index * 2 * HEAD_SIZE, 2 * HEAD_SIZE), 2 * HEAD_SIZE)
        for tile in range(tiles):
            query = stack_heads(query_ref[2 * TILE * tile : 2 * TILE * (tile + 1), lanes])
            query_item = query_items(where_ref, tile, parts, items)

            def visit(first, last):
                key_item = key_items(where_ref, first, last - first, parts, items)
                score = dot_nt(keys_ref[first * span : last * span, lanes], query)
                return jnp.where(key_item == query_item, score, MASKED)

            def mix(weight, first, last):
                return dot_tn(values_ref[first * span : last * span, lanes], weight.astype(BF))

            first, last = near_tiles(tile, tiles)
            score = visit(first, last)
            best = jnp.max(score, axis=0, keepdims=True)
            weight = jnp.exp(score - best)
            best_ref[...] = best
            total_ref[...] = column_sum(weight)
            mixed_ref[...] = mix(weight, first, last)
            for other in range(tiles):
                if first <= other < last:
                    continue

                @pl.when(tiles_meet(where_ref, tile, other, parts, items))
                def far(other=other):
                    score = visit(other, other + 1)
                    best = jnp.maximum(best_ref[...], jnp.max(score, axis=0, keepdims=True))
                    factor = jnp.exp(best_ref[...] - best)
                    weight = jnp.exp(score - best)
                    total_ref[...] = total_ref[...] * factor + column_sum(weight)
                    mixed_ref[...] = mixed_ref[...] * factor + mix(weight, other, other + 1)
                    best_ref[...] = best

            total = total_ref[...]
            logsum_ref[pl.ds(index * tiles + tile, 1)] = best_ref[...] + jnp.log(total)
            attended = join_heads(mixed_ref[...] / total).astype(BF)
            for rel_c in range(2):
                attended_ref[rel_c * rows + tile * TILE : rel_c * rows + (tile + 1) * TILE, lanes] = attended[
                    rel_c * TILE : (rel_c + 1) * TILE
                ]
        return carry

    lax.fori_loop(0, width // (2 * HEAD_SIZE), pair, 0)


def forward_kernel(
    parts, items, where_ref, att_own_ref, att_sib_ref, own_ref, sib_ref, vec_ref, bias_ref, out_own_ref, out_sib_ref,
    up_ref, dact_ref, turned_ref,
    act_ref, dbefore_ref, down_ref, mid_ref, branch_ref, normed_ref, bias_sum_ref,
):
    rows = own_ref.shape[0]

    @pl.when(pl.program_id(0) == 0)
    def first():
        for rel_c, ref in enumerate((own_ref, sib_ref)):
            here = slice(rel_c * rows, (rel_c + 1) * rows)
            there = slice((1 - rel_c) * rows, (2 - rel_c) * rows)
            branch = (
                dot_nn(att_own_ref[here], out_own_ref[...])
                + dot_nn(att_sib_ref[there], out_sib_ref[...])
                + vec_ref[4:5]
            )
            if rel_c == 0:
                branch_ref[...] = branch
            mid = ref[...].astype(F32) + vec_ref[5:6] * branch
            mid_ref[here] = mid
            xhat, unused = standardise(mid)
            normed_ref[here] = (xhat * vec_ref[6:7] + vec_ref[7:8]).astype(BF)

    before = dot_nn(normed_ref[...], up_ref[...]) + bias_ref[...]
    normal = 0.5 + 0.5 * lax.erf(before * (0.5**0.5))
    act = (before * normal).astype(BF)
    act_ref[...] = act
    slope = normal + before * (jnp.exp(-0.5 * before * before) * ((2.0 * math.pi) ** -0.5))
    dbefore = (dact_ref[...].astype(F32) * slope).astype(BF)
    dbefore_ref[...] = dbefore
    bias_sum_ref[...] = column_sum(dbefore.astype(F32))
    down_ref[0] = dot_nn(turned_ref[...], act).astype(BF)


def up_grad_kernel(rows_block, where_ref, normed_ref, dbefore_ref, keep_ref, send_ref, turned):
    @pl.when(pl.program_id(0) == 0)
    def first():
        turned[...] = normed_ref[...].T

    dbefore = dbefore_ref[...]
    core = where_ref[1]
    for at_x in range(2):
        for ref, block in ((keep_ref, 2 * at_x + core), (send_ref, 2 * at_x + 1 - core)):
            left = turned[pl.ds(pl.multiple_of(block * rows_block, rows_block), rows_block)]
            ref[at_x, 0, 0] = dot_nn(left, dbefore).astype(BF)


def back_up_kernel(where_ref, dbefore_ref, up_ref, keep_ref, send_ref, total):
    step = pl.program_id(0)

    @pl.when(step == 0)
    def first():
        total[...] = jnp.zeros_like(total)

    total[...] += dot_nt(dbefore_ref[...], up_ref[...])

    @pl.when(step == pl.num_programs(0) - 1)
    def last():
        keep_ref[...] = total[...]
        send_ref[...] = total[...].astype(BF)


def feed_kernel(where_ref, act_ref, down_ref, keep_ref, send_ref, total):
    step = pl.program_id(0)
    rows = keep_ref.shape[0]

    @pl.when(step == 0)
    def first():
        total[...] = jnp.zeros_like(total)

    total[...] += dot_nn(act_ref[...], down_ref[...])

    @pl.when(step == pl.num_programs(0) - 1)
    def last():
        keep_ref[...] = total[:rows]
        send_ref[...] = total[rows:].astype(BF)


def result_kernel(parts, items, where_ref, keep_ref, got_ref, mid_ref, cot_ref, vec_ref, out_ref, sum_ref):
    rows = keep_ref.shape[0]
    valid = valid_rows(where_ref, 0, rows, parts, items)
    feed = keep_ref[...] + got_ref[...].astype(F32) + vec_ref[8:9]
    out_ref[...] = (valid * (mid_ref[...] + vec_ref[9:10] * feed)).astype(BF)
    sum_ref[...] = column_sum(cot_ref[...].astype(F32) * valid * feed)


def middle_kernel(
    parts, items, where_ref, keep_ref, got_ref, mid_ref, own_ref, sib_ref, vec_ref, att_ref, out_ref, branch_ref,
    dmid_ref, datt_ref, gout_ref, sum_ref, held,
):
    rows = own_ref.shape[0]
    for rel_c, ref in enumerate((own_ref, sib_ref)):
        here = slice(rel_c * rows, (rel_c + 1) * rows)
        there = slice((1 - rel_c) * rows, (2 - rel_c) * rows)
        valid = valid_rows(where_ref, rel_c, rows, parts, items)
        dnormed = keep_ref[here] + got_ref[there].astype(F32)
        xhat, inverse = standardise(mid_ref[here])
        dmid = ref[...].astype(F32) * valid + standardise_grad(vec_ref[6:7] * dnormed, xhat, inverse)
        dbranch = (vec_ref[5:6] * dmid).astype(BF)
        held[here] = dbranch
        if rel_c == 0:
            dmid_ref[...] = dmid
            sum_ref[0:1] = column_sum(dbranch.astype(F32))
            sum_ref[1:2] = column_sum(dmid * branch_ref[...])
            sum_ref[2:3] = column_sum(dnormed * xhat)
            sum_ref[3:4] = column_sum(dnormed)
    datt_ref[...] = dot_nt(held[...], out_ref[...]).astype(BF)
    grad = dot_tn(held[...], att_ref[...])
    count = gout_ref.shape[1]
    size = grad.shape[0] // count
    for index in range(count):
        for side, packed in enumerate(pack_unit(grad[index * size : (index + 1) * size])):
            gout_ref[side, index] = packed.astype(BF)


def pack_unit(unit):
    half = unit.shape[0] // 2
    width = unit.shape[1]
    top, bottom = unit[:half], unit[half:]
    low = lanes_below((half, width), width // 2)
    left = jnp.where(low, top, pltpu.roll(bottom, width // 2, 1))
    right = jnp.where(low, pltpu.roll(top, width // 2, 1), bottom)
    return left, right


def attend_grad_kernel(
    parts, items, where_ref, query_ref, keys_ref, values_ref, attended_ref, datt_ref, logsum_ref,
    dquery_ref, dkeys_ref, dvalues_ref, dk, dv, dq,
):
    width = query_ref.shape[1]
    rows = query_ref.shape[0] // 2
    tiles = rows // TILE
    span = parts * TILE
    scale = HEAD_SIZE ** (-0.5)

    def pair(index, carry):
        lanes = pl.ds(pl.multiple_of(index * 2 * HEAD_SIZE, 2 * HEAD_SIZE), 2 * HEAD_SIZE)
        dk[...] = jnp.zeros_like(dk)
        dv[...] = jnp.zeros_like(dv)
        for tile in range(tiles):
            query = stack_heads(query_ref[2 * TILE * tile : 2 * TILE * (tile + 1), lanes])
            query_item = query_items(where_ref, tile, parts, items)
            places = [slice(rel_c * rows + tile * TILE, rel_c * rows + (tile + 1) * TILE) for rel_c in range(2)]
            grad = jnp.concatenate([datt_ref[at, lanes] for at in places], axis=0)
            attended = jnp.concatenate([attended_ref[at, lanes] for at in places], axis=0)
            product = (grad.astype(F32) * attended.astype(F32)).T
            delta = jnp.concatenate(
                [column_sum(product[:HEAD_SIZE]), column_sum(product[HEAD_SIZE:])], axis=1
            )
            grad = stack_heads(grad)
            logsum = logsum_ref[pl.ds(index * tiles + tile, 1)]

            def visit(first, last):
                at = slice(first * span, last * span)
                key_item = key_items(where_ref, first, last - first, parts, items)
                keys = keys_ref[at, lanes]
                score = dot_nt(keys, query)
                prob = jnp.exp(jnp.where(key_item == query_item, score, MASKED) - logsum)
                dprob = dot_nt(values_ref[at, lanes], grad)
                dscore = (prob * (dprob - delta)).astype(BF)
                dv[at] += dot_nn(prob.astype(BF), grad)
                dk[at] += dot_nn(dscore, query)
                return dot_tn(keys, dscore)

            first, last = near_tiles(tile, tiles)
            dq[...] = visit(first, last)
            for other in range(tiles):
                if first <= other < last:
                    continue

                @pl.when(tiles_meet(where_ref, tile, other, parts, items))
                def far(other=other):
                    dq[...] += visit(other, other + 1)

            dquery = (join_heads(dq[...]) * scale).astype(BF)
            for rel_c in range(2):
                dquery_ref[places[rel_c], lanes] = dquery[rel_c * TILE : (rel_c + 1) * TILE]
        for tile in range(tiles):
            for slot in range(parts):
                to = slice(slot * rows + tile * TILE, slot * rows + (tile + 1) * TILE)
                at = slice(tile * span + slot * TILE, tile * span + (slot + 1) * TILE)
                dkeys_ref[to, lanes] = dk[at].astype(BF)
                dvalues_ref[to, lanes] = dv[at].astype(BF)
        return carry

    lax.fori_loop(0, width // (2 * HEAD_SIZE), pair, 0)


def qkv_grad_kernel(where_ref, near_ref, far_ref, dquery_ref, dkeys_ref, dvalues_ref, keep_ref, send_ref, sum_ref):
    rows = near_ref.shape[0]
    width = near_ref.shape[1]
    mine = where_ref[1] == 0
    sum_ref[0:1] = column_sum(dquery_ref[...].astype(F32))
    sum_ref[1:2] = column_sum(dvalues_ref[...].astype(F32))
    for part, ref in enumerate((dquery_ref, dkeys_ref, dvalues_ref)):
        grad = dot_tn(ref[:rows], near_ref[...])
        if part:
            grad = grad + dot_tn(ref[rows:], far_ref[...])
        size = grad.shape[0] // 4
        for unit in range(4):
            for at_x in range(2):
                left, right = pack_unit(
                    grad[unit * size : (unit + 1) * size, at_x * width // 2 : (at_x + 1) * width // 2]
                )
                keep_ref[at_x, 4 * part + unit] = jnp.where(mine, left, right).astype(BF)
                send_ref[at_x, 4 * part + unit] = jnp.where(mine, right, left).astype(BF)


def tokens_grad_kernel(
    where_ref, own_ref, sib_ref, far_a_ref, far_b_ref, dquery_ref, dkeys_ref, dvalues_ref, weight_ref,
    keep_ref, send_ref, sum_ref,
):
    rows = own_ref.shape[0]
    half = dquery_ref.shape[1]
    gain = jnp.zeros((1, own_ref.shape[1]), F32)
    shift = gain
    for slot, ref in enumerate((own_ref, sib_ref, far_a_ref, far_b_ref)):
        at = slice(slot * rows, (slot + 1) * rows)
        part = dot_nt(dkeys_ref[at], weight_ref[:, half : 2 * half]) + dot_nt(
            dvalues_ref[at], weight_ref[:, 2 * half :]
        )
        if slot < 2:
            part = part + dot_nt(dquery_ref[at], weight_ref[:, :half])
        xhat, unused = standardise(ref[...].astype(F32))
        gain = gain + column_sum(part * xhat)
        shift = shift + column_sum(part)
        if slot % 2:
            send_ref[slot // 2] = part.astype(BF)
        else:
            keep_ref[slot // 2] = part
    sum_ref[0:1] = gain
    sum_ref[1:2] = shift


def first_norm_grad_kernel(where_ref, keep_ref, got_ref, own_ref, dmid_ref, vec_ref, out_ref):
    dnormed = keep_ref[...] + got_ref[...].astype(F32)
    xhat, inverse = standardise(own_ref[...].astype(F32))
    out_ref[...] = (dmid_ref[...] + standardise_grad(vec_ref[0:1] * dnormed, xhat, inverse)).astype(BF)


def to_core(array):
    length = lax.axis_size("blk")
    return lax.ppermute(array, "blk", [(i, i ^ 1) for i in range(length)])


def to_x(array):
    length = lax.axis_size("blk")
    return lax.ppermute(array, "blk", [(i, i ^ 2) for i in range(length)])


def to_y(array):
    length = lax.axis_size("dp")
    return lax.ppermute(array, "dp", [(i, i ^ 1) for i in range(length)])


def along_z(array, by):
    length = lax.axis_size("dp")
    return lax.ppermute(array, "dp", [(i, (i + 2 * by) % length) for i in range(length)])


def picked(array, index, axis):
    return lax.dynamic_index_in_dim(array, index, axis, keepdims=False)


def added(one, other):
    return (one.astype(F32) + other.astype(F32)).astype(BF)


def sum_to_owner(blocks, at, first_rows):
    x, z, y = at
    one, two = blocks[..., :first_rows, :], blocks[..., first_rows:, :]
    one_got = to_x(picked(one, 1 - x, 0))
    two_got = to_y(picked(two, 1 - y, 2))
    one = added(one_got, picked(one, x, 0))
    two = added(two_got, picked(two, y, 2))
    one_got = to_y(picked(one, 1 - y, 1))
    two_got = to_x(picked(two, 1 - x, 0))
    one = added(one_got, picked(one, y, 1))
    two = added(two_got, picked(two, x, 0))
    joined = jnp.concatenate([one, two], axis=1)
    length = joined.shape[0]
    got = [along_z(picked(joined, (z + by) % length, 0), by) for by in range(1, length)]
    total = picked(joined, z, 0).astype(F32)
    for part in got:
        total = total + part.astype(F32)
    return total


def unpacked(units):
    count, half, lanes = units.shape
    return units.reshape(count, half, 2, lanes // 2).transpose(0, 2, 1, 3).reshape(-1, lanes // 2)


def on_device_aligned(tokens, lengths, w_qkv, w_out, w_up, w_down, vectors, cotangent):
    tokens, cotangent = tokens[0], cotangent[0]
    rows, width = tokens.shape
    hidden = w_up.shape[1]
    items = lengths.shape[1]
    parts = lax.axis_size("blk")
    sets = lax.axis_size("dp")
    position, turn = lax.axis_index("blk"), lax.axis_index("dp")
    x, core, z, y = position // 2, position % 2, turn // 2, turn % 2
    where = jnp.concatenate([jnp.stack([x, core, z, y]).astype(jnp.int32), jnp.cumsum(lengths[0]).astype(jnp.int32)])
    half = width // 2
    inner = hidden // 2
    piece = hidden // sets
    steps = inner // piece
    both = 2 * rows
    total_rows = parts * rows
    block = width // parts
    names = (parts, items)

    far_a = to_x(tokens)
    sib = to_core(tokens)
    cot_sib = to_core(cotangent)
    far_b = to_core(far_a)

    vec = vectors[: 10 * width].reshape(10, width)
    bias_up = picked(vectors[10 * width :].reshape(2, 2, -1), core, 1).reshape(1, inner)
    bias_qv = picked(vec[2:4].reshape(2, 2, 2, block), core, 2).reshape(2, half)
    w_qkv_own = picked(w_qkv.reshape(width, 3, 2, 2, block), core, 3).reshape(width, 3 * half)
    w_out_cut = w_out.reshape(2, 2, block, width)
    w_out_own = picked(w_out_cut, core, 1).reshape(half, width)
    w_out_sib = picked(w_out_cut, 1 - core, 1).reshape(half, width)

    def unit_of(step, where_ref):
        return 4 * (step // 2) + 2 * where_ref[1] + step % 2

    up_spec = pl.BlockSpec((width, piece), lambda j, w: (0, unit_of(j, w)))
    down_spec = pl.BlockSpec((piece, width), lambda j, w: (unit_of(j, w), 0))
    wide_spec = pl.BlockSpec((both, piece), lambda j, w: (0, j))
    vec_spec = whole(10, width)

    normed_near, query, key_near, value_near = chip_call(
        local_qkv_kernel,
        (1,),
        [whole(rows, width), whole(rows, width), vec_spec, whole(2, half), whole(width, 3 * half)],
        [whole(both, width), whole(both, half), whole(both, half), whole(both, half)],
        [shaped((both, width), BF)] + [shaped((both, half), BF)] * 3,
        flops=2 * both * width * 3 * half,
        moved=4 * 2**20,
    )(where, tokens, sib, vec, bias_qv, w_qkv_own)

    dact, dfeed_turned, bias_d_sum = chip_call(
        functools.partial(feed_grad_kernel, *names),
        (steps,),
        [whole(rows, width), whole(rows, width), vec_spec, down_spec],
        [wide_spec, whole(width, both), whole(1, width)],
        [shaped((both, inner), BF), shaped((width, both), BF), shaped((1, width), F32)],
        scratch=[pltpu.VMEM((both, width), BF)],
        flops=2 * both * width * inner,
        moved=5 * 2**20,
    )(where, cotangent, cot_sib, vec, w_down)

    tiles = rows // TILE
    pairs = half // (2 * HEAD_SIZE)
    normed_far, keys, values, attended, logsum = chip_call(
        functools.partial(attend_kernel, *names),
        (1,),
        [whole(rows, width), whole(rows, width), vec_spec, whole(2, half), whole(width, 3 * half)]
        + [whole(both, half)] * 3,
        [whole(both, width), whole(total_rows, half), whole(total_rows, half), whole(both, half), whole(pairs * tiles, 4 * TILE)],
        [shaped((both, width), BF), shaped((total_rows, half), BF), shaped((total_rows, half), BF), shaped((both, half), BF), shaped((pairs * tiles, 4 * TILE), F32)],
        scratch=[pltpu.VMEM((1, 4 * TILE), F32), pltpu.VMEM((1, 4 * TILE), F32), pltpu.VMEM((2 * HEAD_SIZE, 4 * TILE), F32)],
        flops=4 * both * width * half + 4 * both * total_rows * half,
        moved=8 * 2**20,
    )(where, far_a, far_b, vec, bias_qv, w_qkv_own, query, key_near, value_near)

    attended_sib = to_core(attended)

    act, dbefore, gdown, mid, branch, normed_two, bias_up_sum = chip_call(
        functools.partial(forward_kernel, *names),
        (steps,),
        [whole(both, half), whole(both, half), whole(rows, width), whole(rows, width), vec_spec,
         pl.BlockSpec((1, piece), lambda j, w: (0, j)), whole(half, width), whole(half, width), up_spec, wide_spec,
         whole(width, both)],
        [wide_spec, wide_spec, pl.BlockSpec((1, width, piece), lambda j, w: (j // 2, 0, j % 2)),
         whole(both, width), whole(rows, width), whole(both, width), pl.BlockSpec((1, piece), lambda j, w: (0, j))],
        [shaped((both, inner), BF), shaped((both, inner), BF), shaped((2, width, inner // 2), BF),
         shaped((both, width), F32), shaped((rows, width), F32), shaped((both, width), BF), shaped((1, inner), F32)],
        flops=2 * both * width * (width + 2 * inner),
        moved=12 * 2**20,
    )(where, attended, attended_sib, tokens, sib, vec, bias_up, w_out_own, w_out_sib, w_up, dact, dfeed_turned)

    at = (x, z, y)
    zs = sets // 2
    down_blocks = gdown.reshape(2, zs, 2, width // sets, inner // 2)
    down_total = sum_to_owner(down_blocks, at, width // sets // 2)
    g_w_down = down_total.T

    swap_spec = pl.BlockSpec((2, 1, 1, block, piece), lambda j, w: (0, j // 2, j % 2, 0, 0))
    up_keep, up_send = chip_call(
        functools.partial(up_grad_kernel, block),
        (steps,),
        [whole(both, width), wide_spec],
        [swap_spec, swap_spec],
        [shaped((2, 2, 2, block, piece), BF)] * 2,
        scratch=[pltpu.VMEM((width, both), BF)],
        flops=2 * both * width * inner,
        moved=5 * 2**20,
    )(where, normed_two, dbefore)
    up_got = to_core(up_send)

    def by_core(kept, got):
        first = core == 0
        return jnp.stack([jnp.where(first, kept, got), jnp.where(first, got, kept)], axis=2)

    up_blocks = by_core(up_keep, up_got).reshape(2, zs, 2, block, piece)
    g_w_up = sum_to_owner(up_blocks, at, block // 2)

    dnormed_keep, dnormed_send = chip_call(
        back_up_kernel,
        (steps,),
        [wide_spec, up_spec],
        [whole(both, width)] * 2,
        [shaped((both, width), F32), shaped((both, width), BF)],
        scratch=[pltpu.VMEM((both, width), F32)],
        flops=2 * both * width * inner,
        moved=6 * 2**20,
    )(where, dbefore, w_up)
    dnormed_got = to_core(dnormed_send)

    feed_keep, feed_send = chip_call(
        feed_kernel,
        (steps,),
        [wide_spec, down_spec],
        [whole(rows, width)] * 2,
        [shaped((rows, width), F32), shaped((rows, width), BF)],
        scratch=[pltpu.VMEM((both, width), F32)],
        flops=2 * both * width * inner,
        moved=5 * 2**20,
    )(where, act, w_down)
    feed_got = to_core(feed_send)
    out, scale_two_sum = chip_call(
        functools.partial(result_kernel, *names),
        (1,),
        [whole(rows, width), whole(rows, width), whole(rows, width), whole(rows, width), vec_spec],
        [whole(rows, width), whole(1, width)],
        [shaped((rows, width), BF), shaped((1, width), F32)],
        moved=3 * 2**20,
    )(where, feed_keep, feed_got, mid, cotangent, vec)

    dmid, dattended, gout, middle_sums = chip_call(
        functools.partial(middle_kernel, *names),
        (1,),
        [whole(both, width)] * 3
        + [whole(rows, width), whole(rows, width), vec_spec, whole(both, half), whole(half, width), whole(rows, width)],
        [whole(rows, width), whole(both, half), whole(2, sets, width // sets // 2, half), whole(4, width)],
        [shaped((rows, width), F32), shaped((both, half), BF), shaped((2, sets, width // sets // 2, half), BF),
         shaped((4, width), F32)],
        scratch=[pltpu.VMEM((both, width), BF)],
        flops=4 * both * width * half,
        moved=8 * 2**20,
    )(where, dnormed_keep, dnormed_got, mid, cotangent, cot_sib, vec, attended, w_out_own, branch)

    dquery, dkeys, dvalues = chip_call(
        functools.partial(attend_grad_kernel, *names),
        (1,),
        [whole(both, half), whole(total_rows, half), whole(total_rows, half), whole(both, half), whole(both, half),
         whole(pairs * tiles, 4 * TILE)],
        [whole(both, half), whole(total_rows, half), whole(total_rows, half)],
        [shaped((both, half), BF), shaped((total_rows, half), BF), shaped((total_rows, half), BF)],
        scratch=[pltpu.VMEM((total_rows, 2 * HEAD_SIZE), F32)] * 2 + [pltpu.VMEM((2 * HEAD_SIZE, 4 * TILE), F32)],
        flops=10 * both * total_rows * half,
        moved=6 * 2**20,
    )(where, query, keys, values, attended, dattended, logsum)

    units = 12
    unit_rows = 3 * half // units // 2
    qkv_keep, qkv_send, bias_qv_sum = chip_call(
        qkv_grad_kernel,
        (1,),
        [whole(both, width), whole(both, width), whole(both, half), whole(total_rows, half), whole(total_rows, half)],
        [whole(2, units, unit_rows, half), whole(2, units, unit_rows, half), whole(2, half)],
        [shaped((2, units, unit_rows, half), BF)] * 2 + [shaped((2, half), F32)],
        flops=2 * (both + 2 * total_rows) * width * half,
        moved=6 * 2**20,
    )(where, normed_near, normed_far, dquery, dkeys, dvalues)
    qkv_got = to_core(qkv_send)

    dtok_keep, dtok_send, first_sums = chip_call(
        tokens_grad_kernel,
        (1,),
        [whole(rows, width)] * 4
        + [whole(both, half), whole(total_rows, half), whole(total_rows, half), whole(width, 3 * half)],
        [whole(2, rows, width), whole(2, rows, width), whole(2, width)],
        [shaped((2, rows, width), F32), shaped((2, rows, width), BF), shaped((2, width), F32)],
        flops=2 * (both + 2 * total_rows) * width * half,
        moved=8 * 2**20,
    )(where, tokens, sib, far_a, far_b, dquery, dkeys, dvalues, w_qkv_own)
    dtok = dtok_keep + to_core(dtok_send).astype(F32)
    grad_tokens = chip_call(
        first_norm_grad_kernel,
        (1,),
        [whole(rows, width)] * 4 + [vec_spec],
        whole(rows, width),
        shaped((rows, width), BF),
        moved=3 * 2**20,
    )(where, dtok[0], to_x(dtok[1].astype(BF)), tokens, dmid, vec)

    def placed(halves, groups):
        cut = halves.reshape(groups, 2, 1, -1)
        mine = lax.broadcasted_iota(jnp.int32, (1, 1, 2, 1), 2) == core
        return jnp.where(mine, cut, 0.0).reshape(-1)

    bias_q_sum, bias_v_sum = placed(bias_qv_sum[0:1], 1), placed(bias_qv_sum[1:2], 1)
    g_vectors = jnp.concatenate(
        [
            first_sums.reshape(-1),
            bias_q_sum,
            bias_v_sum,
            middle_sums.reshape(-1),
            bias_d_sum.reshape(-1),
            scale_two_sum.reshape(-1),
            placed(bias_up_sum, 1),
        ]
    )
    share = vectors.shape[0] // (sets * parts)
    g_vectors = g_vectors.reshape(zs, 2, 2, 2, share)
    g_vectors = picked(g_vectors, core, 3) + to_core(picked(g_vectors, 1 - core, 3))
    g_vectors = g_vectors.transpose(2, 0, 1, 3)[:, :, :, None, :].astype(BF)
    g_vectors = jnp.pad(g_vectors, ((0, 0), (0, 0), (0, 0), (0, 15), (0, half - share)))

    cut = (2, 3, 2, 2, unit_rows, half)
    qkv_blocks = jnp.stack(
        [jnp.where(core == 0, qkv_keep.reshape(cut), qkv_got.reshape(cut)),
         jnp.where(core == 0, qkv_got.reshape(cut), qkv_keep.reshape(cut))], axis=3
    ).reshape(2, zs, 2, 3 * unit_rows, half)
    out_blocks = gout.reshape(2, zs, 2, unit_rows, half)
    last_blocks = jnp.concatenate([qkv_blocks, out_blocks, g_vectors], axis=3)
    last = sum_to_owner(last_blocks, at, last_blocks.shape[3] // 2)
    g_w_qkv = unpacked(last[: 3 * unit_rows].reshape(3, unit_rows, half)).T
    g_w_out = unpacked(last[3 * unit_rows : 4 * unit_rows].reshape(1, unit_rows, half)).T
    g_vec = last[4 * unit_rows, :share]
    return (out[None], grad_tokens[None], g_w_qkv, g_w_out, g_w_up, g_w_down, g_vec)


def is_aligned(mesh, tokens, w_up):
    parts, sets = mesh.shape["blk"], mesh.shape["dp"]
    width, hidden = w_up.shape
    rows = tokens.shape[1] // parts
    return (
        parts == 4
        and sets == 2 * parts
        and rows % TILE == 0
        and (hidden // sets) % 128 == 0
        and (width // 2) % 128 == 0
        and (width // sets) % 32 == 0
        and width == H * HEAD_SIZE
    )


def solution(mesh):
    def run(tokens, lengths, w_qkv, w_out, w_up, w_down, vectors, cotangent):
        body = on_device_aligned if is_aligned(mesh, tokens, w_up) else on_device
        return jax.shard_map(
            body,
            mesh=mesh,
            in_specs=(
                P("dp", "blk", None),
                P("dp", None),
                P(),
                P(),
                P(),
                P(),
                P(),
                P("dp", "blk", None),
            ),
            out_specs=(
                P("dp", "blk", None),
                P("dp", "blk", None),
                P("blk", "dp"),
                P("blk", "dp"),
                P("blk", "dp"),
                P("blk", "dp"),
                P(("dp", "blk")),
            ),
            check_vma=False,
        )(tokens, lengths, w_qkv, w_out, w_up, w_down, vectors, cotangent)

    return run
```

```python
import functools
import math

import jax
import jax.numpy as jnp
import numpy as np
from jax import lax
from jax.experimental import pallas as pl
from jax.experimental.pallas import tpu as pltpu
from jax.sharding import PartitionSpec as P

H = 12
HEAD_SIZE = 64
TILE = 64


EPSILON = 1e-06
FLOOR_SCORE = -1e30


def passed_along(array, axis, by):
    length = lax.axis_size(axis)
    return lax.ppermute(array, axis, [(i, (i + by) % length) for i in range(length)])


def norm_rows(values, gain, shift):
    centre = jnp.mean(values, axis=-1, keepdims=True)
    centred = values - centre
    spread = jnp.mean(centred * centred, axis=-1, keepdims=True)
    return centred * lax.rsqrt(spread + EPSILON) * gain + shift


def exact_gelu(values):
    return jax.nn.gelu(values, approximate=False)


def segment_of(rows_index, rows, parts, ends):
    place = rows_index % rows * parts + rows_index // rows
    return jnp.sum((place[:, None] >= ends[None, :]).astype(jnp.int32), axis=1)


def contract_rows(left, right):
    return lax.dot_general(
        left, right, (((0,), (0,)), ((), ())), preferred_element_type=jnp.float32
    )


def contract_cols(left, right):
    return lax.dot_general(
        left, right, (((1,), (1,)), ((), ())), preferred_element_type=jnp.float32
    )


def attend_block(query, query_item, keys, values, key_item, scale, carry):
    best, total, weighted = carry
    count = keys.shape[0]
    heads = query.shape[1]
    key_heads = keys.reshape(count, heads, -1)
    value_heads = values.reshape(count, heads, -1)
    allowed = (query_item[:, None] == key_item[None, :])[None]
    score = jnp.einsum("qhd,khd->hqk", query, key_heads, preferred_element_type=jnp.float32) * scale
    score = jnp.where(allowed, score, FLOOR_SCORE)
    newbest = jnp.maximum(best, jnp.max(score, axis=-1))
    weight = jnp.where(allowed, jnp.exp(score - newbest[..., None]), 0.0)
    factor = jnp.exp(best - newbest)
    total = total * factor + jnp.sum(weight, axis=-1)
    weighted = weighted * factor[..., None] + jnp.einsum(
        "hqk,khd->hqd", weight.astype(jnp.bfloat16), value_heads, preferred_element_type=jnp.float32
    )
    return (newbest, total, weighted)


def grad_block(query, d_out, logsum, delta, query_item, keys, values, key_item, scale):
    count = keys.shape[0]
    heads = query.shape[1]
    key_heads = keys.reshape(count, heads, -1)
    value_heads = values.reshape(count, heads, -1)
    allowed = (query_item[:, None] == key_item[None, :])[None]
    score = jnp.einsum("qhd,khd->hqk", query, key_heads, preferred_element_type=jnp.float32) * scale
    prob = jnp.where(allowed, jnp.exp(score - logsum[..., None]), 0.0)
    d_prob = jnp.einsum("qhd,khd->hqk", d_out, value_heads, preferred_element_type=jnp.float32)
    d_score = (prob * (d_prob - delta[..., None])).astype(jnp.bfloat16)
    d_query = (
        jnp.einsum("hqk,khd->qhd", d_score, key_heads, preferred_element_type=jnp.float32) * scale
    )
    d_keys = jnp.einsum("hqk,qhd->khd", d_score, query, preferred_element_type=jnp.float32) * scale
    d_values = jnp.einsum(
        "hqk,qhd->khd", prob.astype(jnp.bfloat16), d_out, preferred_element_type=jnp.float32
    )
    return (d_query, d_keys.reshape(count, -1), d_values.reshape(count, -1))


def on_device(tokens, lengths, w_qkv, w_out, w_up, w_down, vectors, cotangent):
    inputs = tokens[0].astype(jnp.float32)
    rows, width = inputs.shape
    heads = H
    head_size = width // heads
    scale = head_size ** (-0.5)
    items = lengths.shape[1]
    ends = jnp.cumsum(lengths[0])
    parts = lax.axis_size("blk")
    position = lax.axis_index("blk")
    query_item = segment_of(position * rows + lax.iota(jnp.int32, rows), rows, parts, ends)
    valid = (query_item < items).astype(jnp.float32)[:, None]
    pieces = [vectors[index * width : (index + 1) * width] for index in range(10)]
    (
        gain_one,
        shift_one,
        bias_q,
        bias_v,
        bias_o,
        scale_one,
        gain_two,
        shift_two,
        bias_d,
        scale_two,
    ) = pieces
    bias_up = vectors[10 * width :]
    normed, norm_one_pull = jax.vjp(norm_rows, inputs, gain_one, shift_one)
    normed_low = normed.astype(jnp.bfloat16)
    qkv_bias = jnp.concatenate([bias_q, jnp.zeros_like(bias_q), bias_v])
    projected = (jnp.dot(normed_low, w_qkv, preferred_element_type=jnp.float32) + qkv_bias).astype(
        jnp.bfloat16
    )
    query = projected[:, :width].reshape(rows, heads, head_size)
    keys = projected[:, width : 2 * width]
    values = projected[:, 2 * width :]
    start_state = (
        jnp.full((heads, rows), FLOOR_SCORE, jnp.float32),
        jnp.zeros((heads, rows), jnp.float32),
        jnp.zeros((heads, rows, head_size), jnp.float32),
    )
    carry = start_state
    piece = (
        lax.all_gather(keys, "blk", axis=0, tiled=True),
        lax.all_gather(values, "blk", axis=0, tiled=True),
    )
    count = piece[0].shape[0]
    size = math.gcd(count, 512)
    steps = count // size
    key_blocks = piece[0].reshape(steps, size, width)
    value_blocks = piece[1].reshape(steps, size, width)

    def inner(state, item):
        block_keys, block_values, offset = item
        key_item = segment_of(offset + lax.iota(jnp.int32, size), rows, parts, ends)
        return (
            attend_block(query, query_item, block_keys, block_values, key_item, scale, state),
            None,
        )

    carry, unused = lax.scan(
        inner, carry, (key_blocks, value_blocks, lax.iota(jnp.int32, steps) * size)
    )
    best, total, weighted = carry
    logsum = best + jnp.log(total)
    attended = (weighted / total[..., None]).transpose(1, 0, 2).reshape(rows, width)
    attended_low = attended.astype(jnp.bfloat16)
    branch = jnp.dot(attended_low, w_out, preferred_element_type=jnp.float32) + bias_o
    mid = inputs + scale_one * branch
    normed_two, norm_two_pull = jax.vjp(norm_rows, mid, gain_two, shift_two)
    normed_two_low = normed_two.astype(jnp.bfloat16)
    before = jnp.dot(normed_two_low, w_up, preferred_element_type=jnp.float32) + bias_up
    activated, gelu_pull = jax.vjp(exact_gelu, before)
    activated_low = activated.astype(jnp.bfloat16)
    feed = jnp.dot(activated_low, w_down, preferred_element_type=jnp.float32) + bias_d
    result = mid + scale_two * feed
    out = (result * valid).astype(jnp.bfloat16)
    d_result = cotangent[0].astype(jnp.float32) * valid
    d_feed = (scale_two * d_result).astype(jnp.bfloat16)
    g_scale_two = jnp.sum(d_result * feed, axis=0)
    g_bias_d = jnp.sum(d_feed.astype(jnp.float32), axis=0)
    g_w_down = contract_rows(activated_low, d_feed)
    d_activated = contract_cols(d_feed, w_down)
    d_before = gelu_pull(d_activated)[0].astype(jnp.bfloat16)
    g_bias_up = jnp.sum(d_before.astype(jnp.float32), axis=0)
    g_w_up = contract_rows(normed_two_low, d_before)
    d_normed_two = contract_cols(d_before, w_up)
    d_mid_norm, g_gain_two, g_shift_two = norm_two_pull(d_normed_two)
    d_mid = d_result + d_mid_norm
    d_branch = (scale_one * d_mid).astype(jnp.bfloat16)
    g_scale_one = jnp.sum(d_mid * branch, axis=0)
    g_bias_o = jnp.sum(d_branch.astype(jnp.float32), axis=0)
    g_w_out = contract_rows(attended_low, d_branch)
    d_attended = contract_cols(d_branch, w_out).astype(jnp.bfloat16)
    d_heads = d_attended.reshape(rows, heads, head_size)
    delta = jnp.sum(
        (d_attended.astype(jnp.float32) * attended).reshape(rows, heads, head_size), axis=-1
    ).T
    zero_query = jnp.zeros((rows, heads, head_size), jnp.float32)

    def visit_block(block_keys, block_values, owner):
        key_item = segment_of(owner * rows + lax.iota(jnp.int32, rows), rows, parts, ends)
        return grad_block(
            query, d_heads, logsum, delta, query_item, block_keys, block_values, key_item, scale
        )

    def send_back(d_keys, d_values):
        return (
            passed_along(d_keys.astype(jnp.bfloat16), "blk", 1).astype(d_keys.dtype),
            passed_along(d_values.astype(jnp.bfloat16), "blk", 1).astype(d_values.dtype),
        )

    def accumulate(state, owner):
        d_query, block_keys, block_values, d_keys, d_values = state
        dq_part, dk_part, dv_part = visit_block(block_keys, block_values, owner)
        d_keys, d_values = send_back(d_keys + dk_part, d_values + dv_part)
        return (d_query + dq_part, d_keys, d_values)

    def turn(step, state):
        owner = (position - step) % parts
        d_query, d_keys, d_values = accumulate(state, owner)
        block_keys, block_values = passed_along((state[1], state[2]), "blk", 1)
        return (d_query, block_keys, block_values, d_keys, d_values)

    zero_rows = jnp.zeros((rows, width), jnp.float32)
    state = lax.fori_loop(0, parts - 1, turn, (zero_query, keys, values, zero_rows, zero_rows))
    d_query, d_keys, d_values = accumulate(state, (position + 1) % parts)
    d_projected = jnp.concatenate([d_query.reshape(rows, width), d_keys, d_values], axis=1).astype(
        jnp.bfloat16
    )
    g_bias_q = jnp.sum(d_projected[:, :width].astype(jnp.float32), axis=0)
    g_bias_v = jnp.sum(d_projected[:, 2 * width :].astype(jnp.float32), axis=0)
    g_w_qkv = contract_rows(normed_low, d_projected)
    d_normed = contract_cols(d_projected, w_qkv)
    d_input_norm, g_gain_one, g_shift_one = norm_one_pull(d_normed)
    d_inputs = d_mid + d_input_norm
    g_vectors = jnp.concatenate(
        [
            g_gain_one,
            g_shift_one,
            g_bias_q,
            g_bias_v,
            g_bias_o,
            g_scale_one,
            g_gain_two,
            g_shift_two,
            g_bias_d,
            g_scale_two,
            g_bias_up,
        ]
    )
    column_sums = (
        lax.psum_scatter(
            g_w_qkv.astype(jnp.bfloat16), "dp", scatter_dimension=1, tiled=True
        ).astype(jnp.float32),
        lax.psum_scatter(
            g_w_out.astype(jnp.bfloat16), "dp", scatter_dimension=1, tiled=True
        ).astype(jnp.float32),
        lax.psum_scatter(g_w_up.astype(jnp.bfloat16), "dp", scatter_dimension=1, tiled=True).astype(
            jnp.float32
        ),
        lax.psum_scatter(
            g_w_down.astype(jnp.bfloat16), "dp", scatter_dimension=1, tiled=True
        ).astype(jnp.float32),
        lax.psum_scatter(
            g_vectors.astype(jnp.bfloat16), "dp", scatter_dimension=0, tiled=True
        ).astype(jnp.float32),
    )
    g_w_qkv, g_w_out, g_w_up, g_w_down, g_vectors = (
        lax.psum_scatter(
            column_sums[0].astype(jnp.bfloat16), "blk", scatter_dimension=0, tiled=True
        ).astype(jnp.float32),
        lax.psum_scatter(
            column_sums[1].astype(jnp.bfloat16), "blk", scatter_dimension=0, tiled=True
        ).astype(jnp.float32),
        lax.psum_scatter(
            column_sums[2].astype(jnp.bfloat16), "blk", scatter_dimension=0, tiled=True
        ).astype(jnp.float32),
        lax.psum_scatter(
            column_sums[3].astype(jnp.bfloat16), "blk", scatter_dimension=0, tiled=True
        ).astype(jnp.float32),
        lax.psum_scatter(
            column_sums[4].astype(jnp.bfloat16), "blk", scatter_dimension=0, tiled=True
        ).astype(jnp.float32),
    )
    return (
        out[None],
        d_inputs.astype(jnp.bfloat16)[None],
        g_w_qkv,
        g_w_out,
        g_w_up,
        g_w_down,
        g_vectors,
    )


BF = jnp.bfloat16
F32 = jnp.float32
MASKED = -1e30
GRANT = 60 * 1024 * 1024
WIDE_CHUNK = 128


def unit_tables():
    lists, places = np.zeros((2, 2, 2, 6), np.int32), np.zeros((2, 2, 4, 3), np.int32)
    units = {core: [unit for unit in range(24) if unit // 4 % 2 == core] for core in range(2)}
    for y in range(2):
        for low_z in range(2):
            first = {}
            for core in range(2):
                own = [unit for unit in units[core] if unit // 3 % 2 == y]
                first[core] = [unit for unit in own if unit // 6 % 2 == low_z]
                rest = [unit for unit in own if unit // 6 % 2 != low_z]
                lists[core, y, low_z] = [units[core].index(unit) for unit in first[core] + rest]
            for core in range(2):
                held = first[core] + first[1 - core]
                for z in (low_z, low_z + 2):
                    places[core, y, z] = [held.index(3 * (2 * z + y) + index) for index in range(3)]
    return lists.reshape(-1), places


UNIT_TABLE, UNIT_PLACE = unit_tables()
UNIT_LIST = 4
ENDS = UNIT_LIST + UNIT_TABLE.size


def dot_nn(left, right):
    return lax.dot_general(left, right, (((1,), (0,)), ((), ())), preferred_element_type=F32)


def dot_nt(left, right):
    return lax.dot_general(left, right, (((1,), (1,)), ((), ())), preferred_element_type=F32)


def dot_tn(left, right):
    return lax.dot_general(left, right, (((0,), (0,)), ((), ())), preferred_element_type=F32)


def standardise(values):
    centred = values - jnp.mean(values, axis=-1, keepdims=True)
    inverse = lax.rsqrt(jnp.mean(centred * centred, axis=-1, keepdims=True) + EPSILON)
    return centred * inverse, inverse


def standardise_grad(grad, xhat, inverse):
    first = jnp.mean(grad, axis=-1, keepdims=True)
    second = jnp.mean(grad * xhat, axis=-1, keepdims=True)
    return (grad - first - xhat * second) * inverse


def column_sum(values):
    return jnp.sum(values, axis=0, keepdims=True)


def item_at(place, where_ref, items):
    found = jnp.zeros_like(place)
    for index in range(items):
        found = found + (place >= where_ref[ENDS + index]).astype(jnp.int32)
    return found


def own_block(where_ref, rel_x, rel_c):
    return 2 * (where_ref[0] ^ rel_x) + (where_ref[1] ^ rel_c)


def low(*shape):
    return jax.ShapeDtypeStruct(shape, BF)


def full(*shape):
    return jax.ShapeDtypeStruct(shape, F32)


def lanes_at(index, size):
    return pl.ds(pl.multiple_of(index * size, size), size)


class Stage:
    def __init__(self, reads, places, writes):
        self.reads, self.places, self.writes = reads, places, writes
        self.started, self.waited, self.begun = set(), set(), []

    def start(self, *indices):
        for index in indices:
            if index not in self.started:
                self.started.add(index)
                for copy in self.reads[index]:
                    copy.start()

    def __getitem__(self, index):
        self.start(index)
        if index not in self.waited:
            self.waited.add(index)
            for copy in self.reads[index]:
                copy.wait()
        return self.places[index]

    def out(self, index):
        return self.writes[index][0]

    def put(self, *indices):
        for index in indices:
            self.writes[index][1].start()
            self.begun.append(index)

    def finish(self):
        for index in range(len(self.reads)):
            self[index]
        self.put(*(index for index in range(len(self.writes)) if index not in self.begun))
        for place, copy in self.writes:
            copy.wait()


class Place:
    def __init__(self, lengths_ref, table_ref):
        position, turn = lax.axis_index("blk"), lax.axis_index("dp")
        self.four = (position // 2, position % 2, turn // 2, turn % 2)
        self.table_ref = table_ref
        self.ends, end = [], jnp.int32(0)
        for index in range(lengths_ref.shape[1]):
            end = end + lengths_ref[0, index]
            self.ends.append(end)

    def __getitem__(self, index):
        if isinstance(index, int) and index < UNIT_LIST:
            return self.four[index]
        if isinstance(index, int) and index >= ENDS:
            return self.ends[index - ENDS]
        return self.table_ref[index - UNIT_LIST]


def unpack_rows(raw_ref, vec_ref):
    count = vec_ref.shape[1] // 128
    for row in range(vec_ref.shape[0]):
        for part in range(count):
            vec_ref[row : row + 1, part * 128 : (part + 1) * 128] = raw_ref[row * count + part : row * count + part + 1]


def staged_call(body, where, operands, out_shape, cuts=None, scratch=(), late=(), pairs=(), tables=False):
    cuts = cuts or {}
    count, results = len(operands), len(out_shape)
    shapes, parts = [], []
    for index, operand in enumerate(operands):
        shape, pieces = (operand.shape, 1) if index not in cuts else cuts[index][:2]
        shapes.append(pltpu.VMEM(shape, operand.dtype))
        parts.append(pieces)
    held_shapes, held_at = [], {}
    for index, item in enumerate(out_shape):
        if index - 1 in pairs:
            held_at[index] = (len(held_shapes) - 1, 1)
        elif index in pairs:
            held_at[index] = (len(held_shapes), 0)
            held_shapes.append(pltpu.VMEM((2, *item.shape), item.dtype))
        else:
            held_at[index] = (len(held_shapes), None)
            held_shapes.append(pltpu.VMEM(item.shape, item.dtype))

    def kernel(*refs):
        where_ref = Place(refs[0], refs[1] if tables else None)
        refs = refs[2 if tables else 1 :]
        ins, outs = refs[:count], refs[count : count + results]
        places = refs[count + results : 2 * count + results]
        held = refs[2 * count + results : 2 * count + results + len(held_shapes)]
        read_sem, write_sem, *rest = refs[2 * count + results + len(held_shapes) :]
        reads, used = [], 0
        for index in range(count):
            moves = [(ins[index], places[index])] if index not in cuts else cuts[index][2](where_ref, ins[index], places[index])
            reads.append([])
            for source, target in moves:
                reads[-1].append(pltpu.make_async_copy(source, target, read_sem.at[used]))
                used += 1
        writes = []
        for index in range(results):
            place, entry = held_at[index]
            source = held[place] if entry is None else held[place].at[entry]
            writes.append((held[place], pltpu.make_async_copy(source, outs[index], write_sem.at[index])))
        stage = Stage(reads, places, writes)
        stage.start(*(index for index in range(count) if index not in late))
        body(where_ref, stage, *rest)
        stage.finish()

    return pl.pallas_call(
        kernel,
        in_specs=[pl.BlockSpec(memory_space=pltpu.SMEM)] * (2 if tables else 1)
        + [pl.BlockSpec(memory_space=pl.ANY)] * count,
        out_specs=[pl.BlockSpec(memory_space=pl.ANY)] * results,
        out_shape=out_shape,
        scratch_shapes=shapes
        + held_shapes
        + [pltpu.SemaphoreType.DMA((sum(parts),)), pltpu.SemaphoreType.DMA((results,))]
        + list(scratch),
        compiler_params=pltpu.CompilerParams(vmem_limit_bytes=GRANT),
    )(where, *((UNIT_TABLE,) if tables else ()), *operands)


def each(count, body):
    def step(index, carry):
        body(index)
        return carry

    lax.fori_loop(0, count, step, 0)


def hidden_unit(where_ref, rel_x, side):
    return 4 * (where_ref[0] ^ rel_x) + 2 * where_ref[1] + side


def lanes_below(shape, count):
    return lax.broadcasted_iota(jnp.int32, shape, 1) < count


def stack_heads(pair):
    first = lanes_below(pair.shape, HEAD_SIZE)
    zero = jnp.zeros_like(pair)
    return jnp.concatenate([jnp.where(first, pair, zero), jnp.where(first, zero, pair)], axis=0)


def turn(source, target):
    each(source.shape[1] // 128, lambda index: target.__setitem__(lanes_at(index, 128), source[:, lanes_at(index, 128)].T))


def valid_at(where_ref, rel_c, first, count, parts, items):
    row = first + lax.broadcasted_iota(jnp.int32, (count, 1), 0)
    item = item_at(row * parts + own_block(where_ref, 0, rel_c), where_ref, items)
    return (item < items).astype(F32)


def normed_rows(xhat, vec_ref, first):
    return (xhat.astype(F32) * vec_ref[first : first + 1] + vec_ref[first + 1 : first + 2]).astype(BF)


def prepare_kernel(parts, items, where_ref, stage, vec_ref, held, normed_ref, row_ref):
    unpack_rows(stage[2], vec_ref)
    own_ref, sib_ref = stage[0], stage[1]
    stage.start(3, 4, 5, 6)
    xhat_ref, qkv_ref, dact_ref, turned_ref, sum_ref = (stage.out(index) for index in range(5))
    rows, width = own_ref.shape
    half = width // 2
    core = where_ref[1]
    for rel_c, ref in enumerate((own_ref, sib_ref)):

        def norm(index, rel_c=rel_c, ref=ref):
            xhat, unused = standardise(ref[lanes_at(index, WIDE_CHUNK)].astype(F32))
            to = lanes_at(index + rel_c * (rows // WIDE_CHUNK), WIDE_CHUNK)
            xhat_ref[to] = xhat.astype(BF)
            normed_ref[to] = (xhat * vec_ref[0:1] + vec_ref[1:2]).astype(BF)

        each(rows // WIDE_CHUNK, norm)
    stage.put(0)
    sum_ref[...] = jnp.zeros_like(sum_ref)
    for rel_c in range(2):

        def grad(index, rel_c=rel_c, ref=stage[4 + rel_c]):
            valid = valid_at(where_ref, rel_c, index * WIDE_CHUNK, WIDE_CHUNK, parts, items)
            part = (vec_ref[9:10] * (ref[lanes_at(index, WIDE_CHUNK)].astype(F32) * valid)).astype(BF)
            held[lanes_at(index + rel_c * (rows // WIDE_CHUNK), WIDE_CHUNK)] = part
            if rel_c == 0:
                sum_ref[...] += column_sum(part.astype(F32))

        each(rows // WIDE_CHUNK, grad)
    turn(held, turned_ref)
    stage.put(3, 4)
    row_ref[0:1, :half] = vec_ref[2:3, lanes_at(core, half)]
    row_ref[0:1, half : 2 * half] = jnp.zeros((1, half), F32)
    row_ref[0:1, 2 * half :] = vec_ref[3:4, lanes_at(core, half)]
    row_ref[1:2, :half] = jnp.full((1, half), HEAD_SIZE ** (-0.5), F32)
    row_ref[1:2, half:] = jnp.ones((1, 2 * half), F32)
    weight_ref = stage[3]

    def project(index):
        lanes = lanes_at(index, half)
        part = dot_nn(normed_ref[...], weight_ref[:, lanes]) + row_ref[0:1, lanes]
        qkv_ref[:, lanes] = (part.astype(BF).astype(F32) * row_ref[1:2, lanes]).astype(BF)

    each(3, project)
    stage.put(1)
    down_ref = stage[6]
    piece = dact_ref.shape[1] // 4

    def back(index):
        dact_ref[:, lanes_at(index, piece)] = dot_nt(held[...], down_ref[lanes_at(index, piece)]).astype(BF)

    each(4, back)


def item_of_place(where_ref, place, items):
    found = jnp.int32(0)
    for index in range(items):
        found = found + (place >= where_ref[ENDS + index]).astype(jnp.int32)
    return found


def tiles_meet(where_ref, one, other, parts, items):
    span = TILE * parts
    first, last = min(one, other), max(one, other)
    return item_of_place(where_ref, first * span + span - 1, items) >= item_of_place(
        where_ref, last * span, items
    )


def near_tiles(tile, tiles):
    return max(0, tile - 1), min(tiles, tile + 2)


def far_pairs(tiles):
    return [(one, other) for one in range(tiles) for other in range(tiles) if abs(one - other) > 1]


def any_far(where_ref, tiles, parts, items):
    found = jnp.bool_(False)
    for one, other in far_pairs(tiles):
        if one < other:
            found = found | tiles_meet(where_ref, one, other, parts, items)
    return found


def attend_kernel(parts, items, where_ref, stage, vec_ref, wide_ref, normed_ref, asks_ref):
    unpack_rows(stage[2], vec_ref)
    xhat_ref, kv_ref, attended_ref, logsum_ref = (stage.out(index) for index in range(4))
    far_a_ref, far_b_ref = stage[0], stage[1]
    stage.start(3, 4)
    rows, width = far_a_ref.shape
    tiles = rows // TILE
    span = parts * TILE
    both = 2 * HEAD_SIZE
    half = width // 2
    core = where_ref[1]
    for rel_c, ref in enumerate((far_a_ref, far_b_ref)):
        xhat, unused = standardise(ref[...].astype(F32))
        xhat_ref[rel_c * rows : (rel_c + 1) * rows] = xhat.astype(BF)
        normed_ref[rel_c * rows : (rel_c + 1) * rows] = normed_rows(xhat, vec_ref, 0)
    stage.put(0)
    row = lax.broadcasted_iota(jnp.int32, (2 * TILE, 2 * TILE), 0)
    block = 2 * where_ref[0] + (where_ref[1] ^ (row // TILE))
    for tile in range(tiles):
        asks_ref[tile] = item_at((tile * TILE + row % TILE) * parts + block, where_ref, items)
    lane = lax.broadcasted_iota(jnp.int32, (1, span), 1)
    slot = lane // TILE
    block = 2 * (where_ref[0] ^ (slot // 2)) + (where_ref[1] ^ (slot % 2))
    key_item = [item_at((tile * TILE + lane % TILE) * parts + block, where_ref, items) for tile in range(tiles)]
    weight_ref = stage[3]
    row_ref = jnp.concatenate([jnp.zeros((1, half), F32), vec_ref[3:4, lanes_at(core, half)]], axis=1)
    far_kv = (dot_nn(normed_ref[...], weight_ref[...]) + row_ref).astype(BF)
    qkv_ref = stage[4]
    for tile in range(tiles):
        for slot in range(2):
            at = slice(slot * rows + tile * TILE, slot * rows + (tile + 1) * TILE)
            kv_ref[tile * span + slot * TILE : tile * span + (slot + 1) * TILE] = qkv_ref[at, half:]
            kv_ref[tile * span + (slot + 2) * TILE : tile * span + (slot + 3) * TILE] = far_kv[at]
    stage.put(1)
    for index in range(half // both):
        wide_ref[:, 2 * index * both : (2 * index + 1) * both] = kv_ref[:, half + index * both : half + (index + 1) * both]
        wide_ref[:, (2 * index + 1) * both : (2 * index + 2) * both] = jnp.ones((tiles * span, both), BF)

    def attend(index, tile, first, last):
        lanes = lanes_at(index, both)
        at = slice(first * span, last * span)
        places = [pl.ds(pl.multiple_of(rel_c * rows + tile * TILE, TILE), TILE) for rel_c in range(2)]
        query = stack_heads(jnp.concatenate([qkv_ref[place, lanes] for place in places], axis=0))
        score = dot_nt(query, kv_ref[at, lanes])
        asked = asks_ref[tile][:, :1]
        allowed = jnp.concatenate([asked == key_item[other] for other in range(first, last)], axis=1)
        score = jnp.where(jnp.concatenate([allowed, allowed], axis=0), score, MASKED)
        best = jnp.max(score, axis=1, keepdims=True)
        weight = jnp.exp(score - best).astype(BF)
        mixed = dot_nn(weight, wide_ref[at, lanes_at(index, 2 * both)])
        total = mixed[:, both:]
        logsum_ref[index, pl.ds(tile, 1)] = (best + jnp.log(total)).T[:1]
        mixed = mixed[:, :both] / total
        attended = jnp.where(lanes_below((both, both), HEAD_SIZE), mixed[:both], mixed[both:]).astype(BF)
        for rel_c, place in enumerate(places):
            attended_ref[place, lanes] = attended[rel_c * TILE : (rel_c + 1) * TILE]

    def pair(index):
        for tile in range(tiles):
            attend(index, tile, *near_tiles(tile, tiles))

    each(half // both, pair)

    @pl.when(any_far(where_ref, tiles, parts, items))
    def far():
        def again(step):
            tile = step % tiles
            found = jnp.bool_(False)
            for one, other in far_pairs(tiles):
                found = found | ((tile == one) & tiles_meet(where_ref, one, other, parts, items))
            pl.when(found)(lambda: attend(step // tiles, tile, 0, tiles))

        each(half // both * tiles, again)


def gelu_with_slope(values):
    bell = jnp.exp(-0.5 * values * values)
    inverse = 1.0 / (1.0 + (0.3275911 * 0.5**0.5) * jnp.abs(values))
    series = 1.061405429
    for coefficient in (-1.453152027, 1.421413741, -0.284496736, 0.254829592):
        series = series * inverse + coefficient
    tail = 0.5 * (series * inverse) * bell
    normal = jnp.where(values >= 0, 1.0 - tail, tail)
    return values * normal, normal + values * bell * ((2.0 * math.pi) ** -0.5)


def set_block(where_ref, rel_y, low_z, high_z):
    return 2 * (where_ref[2] ^ (low_z + 2 * high_z)) + (where_ref[3] ^ rel_y)


def mlp_kernel(where_ref, stage, vec_ref, bias_ref, mid_ref, joined, normed, grad, turned, act_ref, dbefore_ref):
    py_ref, ux_ref, dz_ref = stage.out(0), stage.out(2), stage.out(4)
    xhat_ref, inverse_ref, mid_own_ref, branch_ref, dn_ref, feed_keep, feed_send, bias_sum_ref = (
        stage.out(index) for index in range(6, 14)
    )
    unpack_rows(stage[4], vec_ref)
    att_own_ref, att_sib_ref, own_ref, sib_ref, raw_ref, out_ref = (stage[index] for index in range(6))
    stage.start(6, 7, 8, 9)
    x, core, z, y = (where_ref[index] for index in range(4))
    rows, width = own_ref.shape
    half = width // 2
    piece = act_ref.shape[1] // 4
    joined[:, :half] = att_own_ref[...]
    joined[:rows, half:] = att_sib_ref[rows:]
    joined[rows:, half:] = att_sib_ref[:rows]

    def project(index):
        lanes = lanes_at(index, 256)
        branch = dot_nn(joined[...], out_ref[:, lanes]) + vec_ref[4:5, lanes]
        branch_ref[:, lanes] = branch[:rows].astype(BF)
        branch = vec_ref[5:6, lanes] * branch
        mid_ref[:rows, lanes] = own_ref[:, lanes].astype(F32) + branch[:rows]
        mid_ref[rows:, lanes] = sib_ref[:, lanes].astype(F32) + branch[rows:]

    each(width // 256, project)

    mid_own_ref[...] = mid_ref[:rows]

    def norm(index):
        at = lanes_at(index, WIDE_CHUNK)
        xhat, inverse = standardise(mid_ref[at])
        normed[at] = (xhat * vec_ref[6:7] + vec_ref[7:8]).astype(BF)
        xhat_ref[at] = xhat.astype(BF)
        inverse_ref[at] = inverse

    each(2 * rows // WIDE_CHUNK, norm)
    stage.put(6, 7, 8, 9)
    count = piece // 128
    for unit in range(8):
        for part in range(count):
            row = 10 * width // 128 + unit * count + part
            bias_ref[unit : unit + 1, part * 128 : (part + 1) * 128] = raw_ref[row : row + 1]
    up_ref, dact_ref, turned_ref = stage[6], stage[7], stage[8]
    size = grad.shape[0] // 8

    def hidden(index):
        rel_x = 1 - index
        for side in range(2):
            at = lanes_at(2 * rel_x + side, piece)
            before = dot_nn(normed[...], up_ref[:, at]) + bias_ref[pl.ds(hidden_unit(where_ref, rel_x, side), 1)]
            act, slope = gelu_with_slope(before)
            act_ref[:, at] = act.astype(BF)
            dbefore = (dact_ref[:, at].astype(F32) * slope).astype(BF)
            dbefore_ref[:, at] = dbefore
            bias_sum_ref[:, at] = column_sum(dbefore.astype(F32))
            grad[:, side * piece : (side + 1) * piece] = dot_nn(turned_ref[...], act_ref[:, at]).astype(BF)

        def lay(block):
            low_z, high_z, rel_y = block // 4, block // 2 % 2, block % 2
            at = lanes_at(set_block(where_ref, rel_y, low_z, high_z), size)
            dz_ref[low_z, high_z, rel_x, rel_y] = grad[at, :piece]
            py_ref[rel_y, rel_x, lanes_at(2 * low_z + high_z, size)] = grad[at, piece:]

        each(8, lay)

    each(2, hidden)
    stage.put(4, 5)
    turn(normed, turned)
    block = ux_ref.shape[3]

    def up(index):
        rel_y, high_z = index // 2, index % 2
        unit = 2 * (x ^ (z // 2) ^ high_z) + (y ^ rel_y)
        grad[:, :piece] = dot_nn(turned[...], dbefore_ref[:, lanes_at(unit, piece)]).astype(BF)
        for rel_x in range(2):
            to = pl.ds(pl.multiple_of(4 * size + high_z * block, 2 * size), block)
            py_ref[rel_y, rel_x, to] = grad[lanes_at(own_block(where_ref, rel_x, 0), block), :piece]
            ux_ref[rel_x, rel_y, high_z] = grad[lanes_at(own_block(where_ref, rel_x, 1), block), :piece]

    each(4, up)
    stage.put(0, 1, 2, 3)

    def back(index):
        lanes = lanes_at(index, 256)
        total = dot_nt(dbefore_ref[...], up_ref[lanes])
        dn_ref[:, lanes] = total.astype(BF)

    each(width // 256, back)
    stage.put(10)
    down_ref = stage[9]

    def feed(index):
        lanes = lanes_at(index, 256)
        total = dot_nn(act_ref[...], down_ref[:, lanes])
        feed_keep[:, lanes] = total[:rows]
        feed_send[:, lanes] = total[rows:].astype(BF)

    each(width // 256, feed)


def middle(parts, items, where_ref, stage, vec_ref, datt_ref, held, chosen, packed):
    dmid_ref, out_ref, sum_ref = stage.out(0), stage.out(5), stage.out(10)
    keep_ref, got_ref, xhat_ref, inverse_ref, own_ref, sib_ref, raw_ref = (stage[index] for index in range(7))
    unpack_rows(raw_ref, vec_ref)
    rows, width = own_ref.shape
    half = width // 2
    core = where_ref[1]
    left_is_own = lanes_below((rows, half), half // 2) == (core == 0)
    for rel_c, ref in enumerate((own_ref, sib_ref)):
        here = slice(rel_c * rows, (rel_c + 1) * rows)
        there = slice((1 - rel_c) * rows, (2 - rel_c) * rows)
        valid = valid_at(where_ref, rel_c, 0, rows, parts, items)
        dnormed = keep_ref[here].astype(F32) + got_ref[there].astype(F32)
        xhat, inverse = xhat_ref[here].astype(F32), inverse_ref[here]
        dmid = ref[...].astype(F32) * valid + standardise_grad(vec_ref[6:7] * dnormed, xhat, inverse)
        dbranch = (vec_ref[5:6] * dmid).astype(BF)
        held[here] = dbranch
        if rel_c == 0:
            dmid_ref[...] = dmid
            sum_ref[0:1] = column_sum(dbranch.astype(F32))
            sum_ref[1:2] = column_sum(dmid * stage[10][...].astype(F32))
            sum_ref[2:3] = column_sum(dnormed * xhat)
            sum_ref[3:4] = column_sum(dnormed)
    stage.put(0)
    datt_ref[...] = dot_nt(held[...], stage[9][...]).astype(BF)
    att_own_ref, att_sib_ref = stage[7], stage[8]
    for rel_c in range(2):
        here = slice(rel_c * rows, (rel_c + 1) * rows)
        there = slice((1 - rel_c) * rows, (2 - rel_c) * rows)
        other = pltpu.roll(att_sib_ref[there].astype(F32), half // 2, 1)
        chosen[here] = jnp.where(left_is_own, att_own_ref[here].astype(F32), other).astype(BF)
    grad = dot_tn(held[...], chosen[...])
    count, unit_rows = packed.shape[1:3]
    for index in range(count):
        left, right = pack_unit(grad[2 * index * unit_rows : 2 * (index + 1) * unit_rows])
        packed[0, index] = left.astype(BF)
        packed[1, index] = right.astype(BF)

    def lay(index):
        low_z, high_z, rel_x, rel_y = index // 8, index // 4 % 2, index // 2 % 2, index % 2
        at = set_block(where_ref, rel_y, low_z, high_z)
        out_ref[low_z, high_z, rel_x, rel_y] = packed[where_ref[0] ^ rel_x, at]

    each(16, lay)
    stage.put(5, 6)


def pack_unit(unit):
    half = unit.shape[0] // 2
    width = unit.shape[1]
    top, bottom = unit[:half], unit[half:]
    first = lanes_below((half, width), width // 2)
    left = jnp.where(first, top, pltpu.roll(bottom, width // 2, 1))
    right = jnp.where(first, pltpu.roll(top, width // 2, 1), bottom)
    return left, right


def join_heads(stacked_turned):
    stacked = stacked_turned.T
    count = stacked.shape[0] // 2
    return jnp.where(
        lanes_below((count, stacked.shape[1]), HEAD_SIZE), stacked[:count], stacked[count:]
    )


def query_items(where_ref, tile, parts, items):
    lane = lax.broadcasted_iota(jnp.int32, (1, 4 * TILE), 1)
    rel_c = (lane // TILE) % 2
    block = 2 * where_ref[0] + (where_ref[1] ^ rel_c)
    return item_at((tile * TILE + lane % TILE) * parts + block, where_ref, items)


def fill_key_items(where_ref, item_ref, tiles, parts, items):
    row = lax.broadcasted_iota(jnp.int32, (TILE, item_ref.shape[1]), 0)
    for tile in range(tiles):
        for slot in range(parts):
            block = own_block(where_ref, slot // 2, slot % 2)
            at = (tile * parts + slot) * TILE
            item_ref[at : at + TILE] = item_at((tile * TILE + row) * parts + block, where_ref, items)


def both_heads(array):
    return jnp.concatenate([array, array], axis=1)


def attend_grad(
    parts, items, where_ref, stage, datt_ref, dquery_ref, dkeys_ref, dvalues_ref, asks_ref, item_ref, turned_ref, dk, dv, dq
):
    attended_ref, qkv_ref, kv_ref, logsum_ref = stage[7], stage[11], stage[12], stage[13]
    half = datt_ref.shape[1]
    rows = datt_ref.shape[0] // 2
    tiles = rows // TILE
    span = parts * TILE
    scale = HEAD_SIZE ** (-0.5)
    turned_ref[...] = kv_ref[:, :half].T
    fill_key_items(where_ref, item_ref, tiles, parts, items)
    for tile in range(tiles):
        asks_ref[tile : tile + 1] = query_items(where_ref, tile, parts, items)
    some_far = any_far(where_ref, tiles, parts, items)

    def pair(index, carry):
        lanes = lanes_at(index, 2 * HEAD_SIZE)
        value_lanes = pl.ds(pl.multiple_of(half + index * 2 * HEAD_SIZE, 2 * HEAD_SIZE), 2 * HEAD_SIZE)
        dk[...] = jnp.zeros_like(dk)
        dv[...] = jnp.zeros_like(dv)

        def places(tile):
            return [pl.ds(pl.multiple_of(rel_c * rows + tile * TILE, TILE), TILE) for rel_c in range(2)]

        def visit(tile, at):
            query = stack_heads(jnp.concatenate([qkv_ref[place, lanes] for place in places(tile)], axis=0))
            grad = jnp.concatenate([datt_ref[place, lanes] for place in places(tile)], axis=0)
            attended = jnp.concatenate([attended_ref[place, lanes] for place in places(tile)], axis=0)
            product = (grad.astype(F32) * attended.astype(F32)).T
            delta = jnp.concatenate([column_sum(product[:HEAD_SIZE]), column_sum(product[HEAD_SIZE:])], axis=1)
            grad = stack_heads(grad)
            score = dot_nt(kv_ref[at, lanes], query)
            allowed = both_heads(item_ref[at]) == asks_ref[pl.ds(tile, 1)]
            prob = jnp.exp(jnp.where(allowed, score, MASKED) - logsum_ref[index, pl.ds(tile, 1)])
            dprob = dot_nt(kv_ref[at, value_lanes], grad)
            dscore = (prob * (dprob - delta)).astype(BF)
            dv[at] += dot_nn(prob.astype(BF), grad)
            dk[at] += dot_nn(dscore, query)
            return dot_nn(turned_ref[lanes, at], dscore)

        for tile in range(tiles):
            first, last = near_tiles(tile, tiles)
            dq[tile] = visit(tile, slice(first * span, last * span))

        @pl.when(some_far)
        def far():
            def add(step):
                tile, other = step // tiles, step % tiles
                found = jnp.bool_(False)
                for one, two in far_pairs(tiles):
                    found = found | ((step == one * tiles + two) & tiles_meet(where_ref, one, two, parts, items))

                @pl.when(found)
                def meet():
                    at = pl.ds(pl.multiple_of(other * span, span), span)
                    dq[tile] += visit(tile, at)

            each(tiles * tiles, add)

        for tile in range(tiles):
            dquery = (join_heads(dq[tile]) * scale).astype(BF)
            for rel_c, place in enumerate(places(tile)):
                dquery_ref[place, lanes] = dquery[rel_c * TILE : (rel_c + 1) * TILE]
            for slot in range(parts):
                to = slice(slot * rows + tile * TILE, slot * rows + (tile + 1) * TILE)
                at = slice(tile * span + slot * TILE, tile * span + (slot + 1) * TILE)
                dkeys_ref[to, lanes] = dk[at].astype(BF)
                dvalues_ref[to, lanes] = dv[at].astype(BF)
        return carry

    lax.fori_loop(0, half // (2 * HEAD_SIZE), pair, 0)


def twice(half_row, where_ref):
    row = both_heads(half_row)
    return jnp.where(lanes_below(row.shape, half_row.shape[1]) == (where_ref[1] == 0), row, 0.0)


def qkv_grad(where_ref, stage, vec_ref, dquery_ref, dkeys_ref, dvalues_ref, normed_ref, packed):
    a_ref, b_ref, sum_ref = stage.out(1), stage.out(3), stage.out(10)
    near_ref, far_ref = stage[14], stage[15]
    rows, width = near_ref.shape
    core, z, y = where_ref[1], where_ref[2], where_ref[3]
    normed_ref[:rows] = normed_rows(near_ref[...], vec_ref, 0)
    normed_ref[rows:] = normed_rows(far_ref[...], vec_ref, 0)
    sum_ref[4:5] = twice(column_sum(dquery_ref[...].astype(F32)), where_ref)
    sum_ref[5:6] = twice(column_sum(dvalues_ref[...].astype(F32)), where_ref)
    for part, ref in enumerate((dquery_ref, dkeys_ref, dvalues_ref)):
        grad = dot_tn(ref[...], normed_ref[: ref.shape[0]])
        size = grad.shape[0] // 4
        for unit in range(4):
            for at_x in range(2):
                left, right = pack_unit(
                    grad[unit * size : (unit + 1) * size, at_x * width // 2 : (at_x + 1) * width // 2]
                )
                packed[2 * at_x, 4 * part + unit] = left.astype(BF)
                packed[2 * at_x + 1, 4 * part + unit] = right.astype(BF)

    def lay(index):
        rel_x, rel_y, at = index // 12, index // 6 % 2, index % 6
        unit = where_ref[UNIT_LIST + 24 * core + 12 * (y ^ rel_y) + 6 * (z % 2) + at]
        a_ref[rel_x, rel_y, at] = packed[own_block(where_ref, rel_x, 0), unit]
        b_ref[rel_y, rel_x, at] = packed[own_block(where_ref, rel_x, 1), unit]

    each(24, lay)
    stage.put(1, 2, 3, 4)


def tokens_grad(where_ref, stage, dquery_ref, dkeys_ref, dvalues_ref):
    own_ref, far_ref, send_ref, sum_ref = (stage.out(index) for index in (7, 8, 9, 10))
    near_ref, beyond_ref, weight_ref = stage[14], stage[15], stage[16]
    rows, width = own_ref.shape
    half = dquery_ref.shape[1]
    gain = jnp.zeros((1, width), F32)
    shift = gain
    for slot in range(4):
        at = slice(slot * rows, (slot + 1) * rows)
        part = dot_nt(dkeys_ref[at], weight_ref[:, half : 2 * half]) + dot_nt(dvalues_ref[at], weight_ref[:, 2 * half :])
        if slot < 2:
            part = part + dot_nt(dquery_ref[at], weight_ref[:, :half])
        xhat = (near_ref if slot < 2 else beyond_ref)[(slot % 2) * rows : (slot % 2 + 1) * rows].astype(F32)
        gain = gain + column_sum(part * xhat)
        shift = shift + column_sum(part)
        if slot % 2:
            send_ref[slot // 2] = part.astype(BF)
        elif slot:
            far_ref[...] = part.astype(BF)
        else:
            own_ref[...] = part.astype(BF)
    sum_ref[6:7] = gain
    sum_ref[7:8] = shift


def backward_kernel(
    parts, items, where_ref, stage, vec_ref, datt_ref, held, chosen, gpacked, dquery_ref, dkeys_ref, dvalues_ref,
    normed_ref, packed, asks_ref, item_ref, turned_ref, dk, dv, dq,
):
    stage[0], stage[1]
    stage.start(*range(2, 17))
    middle(parts, items, where_ref, stage, vec_ref, datt_ref, held, chosen, gpacked)
    attend_grad(
        parts, items, where_ref, stage, datt_ref, dquery_ref, dkeys_ref, dvalues_ref, asks_ref, item_ref, turned_ref,
        dk, dv, dq,
    )
    qkv_grad(where_ref, stage, vec_ref, dquery_ref, dkeys_ref, dvalues_ref, normed_ref, packed)
    tokens_grad(where_ref, stage, dquery_ref, dkeys_ref, dvalues_ref)


def result_kernel(parts, items, where_ref, stage, vec_ref):
    unpack_rows(stage[4], vec_ref)
    out_ref, sum_ref = stage.out(0), stage.out(1)
    keep_ref, got_ref, mid_ref, cot_ref, raw_ref, back_ref, bias_d_ref, bias_up_ref = (stage[index] for index in range(8))
    rows, width = keep_ref.shape
    valid = valid_at(where_ref, 0, 0, rows, parts, items)
    feed = keep_ref[...] + got_ref[...].astype(F32) + vec_ref[8:9]
    out_ref[...] = (valid * (mid_ref[...] + vec_ref[9:10] * feed)).astype(BF)
    stage.put(0)
    sum_ref[0:2] = back_ref[6:8]
    sum_ref[2:4] = back_ref[4:6]
    sum_ref[4:8] = back_ref[0:4]
    sum_ref[8:9] = bias_d_ref[...]
    sum_ref[9:10] = column_sum(cot_ref[...].astype(F32) * valid * feed)
    for at_x in range(2):
        one = bias_up_ref[:, at_x * width : (at_x + 1) * width]
        two = bias_up_ref[:, (1 - at_x) * width : (2 - at_x) * width]
        here = jnp.where(where_ref[0] == 0, one, two)
        for at_c in range(2):
            at = 10 + 2 * at_x + at_c
            sum_ref[at : at + 1] = jnp.where(where_ref[1] == at_c, here, 0.0)
    sum_ref[14:] = jnp.zeros((2, width), F32)


def unpack_unit(unit, target, first):
    half, lanes = unit.shape
    target[first : first + half] = unit[:, : target.shape[1]]
    target[first + half : first + 2 * half] = pltpu.roll(unit, lanes // 2, 1)[:, : target.shape[1]]


def finish_qkv_kernel(where_ref, stage, rows_ref):
    result_ref = stage.out(0)
    total = stage[0][...].astype(F32) + stage[1][...].astype(F32)
    rows_ref[...] = jnp.zeros_like(rows_ref)
    half = total.shape[0] // 3
    for unit in range(3):
        unpack_unit(total[unit * half : (unit + 1) * half], rows_ref, 2 * unit * half)
    result_ref[...] = rows_ref[...].T[: result_ref.shape[0], : result_ref.shape[1]]


def finish_kernel(where_ref, stage, rows_ref, out_rows_ref, flat):
    mlp_keep, mlp_got, mlp_far, dz_keep, dz_far = (stage[index] for index in range(5))
    down_ref, up_ref, out_ref, vec_ref = (stage.out(index) for index in range(4))
    size, block = down_ref.shape[1], up_ref.shape[0]
    lanes = up_ref.shape[1]
    mlp = mlp_keep[0].astype(F32) + mlp_got[: size + block].astype(F32) + mlp_far[...].astype(F32)
    dz = dz_keep[...].astype(F32) + dz_far[...].astype(F32)
    up_ref[...] = mlp[size:]
    rows_ref[...] = jnp.zeros_like(rows_ref)
    rows_ref[:size, :lanes] = dz[:size]
    rows_ref[:size, lanes:] = mlp[:size]
    down_ref[...] = rows_ref[...].T[:, :size]
    out_rows_ref[...] = jnp.zeros_like(out_rows_ref)
    unpack_unit(dz[size : size + size // 2], out_rows_ref, 0)
    out_ref[...] = out_rows_ref[...].T[: out_ref.shape[0], : out_ref.shape[1]]
    sums = dz[size + size // 2 :]
    for row in range(sums.shape[0]):
        flat[:, row * lanes : (row + 1) * lanes] = sums[row : row + 1]
    share = vec_ref.shape[1]
    start = (4 * set_block(where_ref, 0, 0, 0) + own_block(where_ref, 0, 0)) * share
    window = flat[:, pl.ds(pl.multiple_of(start // 128 * 128, 128), 512)]
    window = pltpu.roll(jnp.broadcast_to(window, (8, 512)), (512 - start % 128) % 512, 1)
    vec_ref[...] = window[:1, :share]


def first_norm_grad_kernel(where_ref, stage, vec_ref):
    keep_ref, near_ref, far_ref, own_ref, dmid_ref, raw_ref = (stage[index] for index in range(6))
    unpack_rows(raw_ref, vec_ref)
    dnormed = keep_ref[...].astype(F32) + near_ref[...].astype(F32) + far_ref[...].astype(F32)
    xhat, inverse = standardise(own_ref[...].astype(F32))
    stage.out(0)[...] = (dmid_ref[...] + standardise_grad(vec_ref[0:1] * dnormed, xhat, inverse)).astype(BF)


def swapped(array, axis, bit):
    length = lax.axis_size(axis)
    return lax.ppermute(array, axis, [(i, i ^ bit) for i in range(length)])


def to_core(array):
    return swapped(array, "blk", 1)


def to_x(array):
    return swapped(array, "blk", 2)


def to_y(array):
    return swapped(array, "dp", 1)


def to_z(array):
    return swapped(array, "dp", 2)


def to_zz(array):
    return swapped(array, "dp", 4)


def after(done, *arrays):
    return lax.optimization_barrier((done, *arrays))[1:]


def rows_of(array, lanes):
    return array.reshape(-1, lanes)


def added(*terms):
    total = terms[0].astype(F32)
    for term in terms[1:]:
        total = total + term.astype(F32)
    return total


def first_rows(count):
    def cut(where_ref, source, target):
        return [(source.at[:count], target)]

    return cut


def first_block(where_ref, source, target):
    return [(source.at[0], target)]


def own_columns(first):
    def cut(where_ref, source, target):
        half = source.shape[0] // 2
        return [
            (source.at[:, lanes_at(where_ref[1] + 2 * part, half)], target.at[:, (part - first) * half : (part - first + 1) * half])
            for part in range(first, 3)
        ]

    return cut


def own_hidden(axis):
    def cut(where_ref, source, target):
        pairs = []
        piece = target.shape[axis] // 4
        for rel_x in range(2):
            for side in range(2):
                at = lanes_at(hidden_unit(where_ref, rel_x, side), piece)
                to = slice((2 * rel_x + side) * piece, (2 * rel_x + side + 1) * piece)
                pairs.append((source.at[at], target.at[to]) if axis == 0 else (source.at[:, at], target.at[:, to]))
        return pairs

    return cut


def both_head_rows(where_ref, source, target):
    half = target.shape[0] // 2
    return [
        (source.at[lanes_at(where_ref[1], half), :], target.at[:half]),
        (source.at[lanes_at(1 - where_ref[1], half), :], target.at[half:]),
    ]


def own_head_rows(where_ref, source, target):
    return [(source.at[lanes_at(where_ref[1], target.shape[0]), :], target)]


def on_device_aligned(tokens, lengths, w_qkv, w_out, w_up, w_down, vectors, cotangent):
    tokens, cotangent = tokens[0], cotangent[0]
    rows, width = tokens.shape
    hidden = w_up.shape[1]
    items = lengths.shape[1]
    parts = lax.axis_size("blk")
    sets = lax.axis_size("dp")
    position, turn = lax.axis_index("blk"), lax.axis_index("dp")
    x, core, z, y = position // 2, position % 2, turn // 2, turn % 2
    where = lengths
    half = width // 2
    inner = hidden // 2
    piece = hidden // sets
    both = 2 * rows
    total_rows = parts * rows
    block = width // parts
    share = width // sets
    names = (parts, items)
    zs = sets // 2
    all_columns = ((width, 3 * half), 3, own_columns(0))
    kv_columns = ((width, 2 * half), 2, own_columns(1))
    up_columns = ((width, inner), 4, own_hidden(1))
    down_rows = ((inner, width), 4, own_hidden(0))
    head_rows = ((half, width), 1, own_head_rows)
    out_rows = ((width, width), 2, both_head_rows)

    far_a = to_x(tokens)
    sib = to_core(tokens)
    cot_sib = to_core(cotangent)

    vec = vectors.reshape(-1, 128)
    rows_of_vec = pltpu.VMEM((10, width), F32)

    xhat_near, qkv_near, dact, dfeed_turned, bias_d_sum = staged_call(
        functools.partial(prepare_kernel, *names),
        where,
        (tokens, sib, vec, w_qkv, cotangent, cot_sib, w_down),
        [low(both, width), low(both, 3 * half), low(both, inner), low(width, both), full(1, width)],
        cuts={3: all_columns, 6: down_rows},
        late=(3, 4, 5, 6),
        scratch=[rows_of_vec, pltpu.VMEM((both, width), BF), pltpu.VMEM((both, width), BF), pltpu.VMEM((2, 3 * half), F32)],
    )

    far_a, qkv_near, dact = lax.optimization_barrier((far_a, qkv_near, dact))
    far_b = to_core(far_a)

    xhat_far, kv, attended, logsum = staged_call(
        functools.partial(attend_kernel, *names),
        where,
        (far_a, far_b, vec, w_qkv, qkv_near),
        [low(both, width), low(total_rows, width), low(both, half), full(half // (2 * HEAD_SIZE), rows // TILE, 4 * TILE)],
        cuts={3: kv_columns},
        late=(3, 4),
        scratch=[
            rows_of_vec,
            pltpu.VMEM((total_rows, 2 * half), BF),
            pltpu.VMEM((both, width), BF),
            pltpu.VMEM((rows // TILE, 2 * TILE, 2 * TILE), jnp.int32),
        ],
    )
    attended_sib = to_core(attended)

    unit_rows = share // 2
    py, ux, dz = low(2, 2 * width // 2, piece), low(2, 2, block, piece), low(2, 2, 2, share, piece)
    (py_keep, py_send, ux_keep, ux_send, dz_keep, dz_send, xhat_two, inverse_two, mid, branch, dn, feed_keep, feed_send,
     bias_up_sum) = staged_call(
        mlp_kernel,
        where,
        (attended, attended_sib, tokens, sib, vec, w_out, w_up, dact, dfeed_turned, w_down),
        [py, py, ux, ux, dz, dz, low(both, width), full(both, 1), full(rows, width), low(rows, width), low(both, width),
         full(rows, width), low(rows, width), full(1, inner)],
        cuts={5: out_rows, 6: up_columns, 9: down_rows},
        late=(6, 7, 8, 9),
        pairs=(0, 2, 4),
        scratch=[rows_of_vec, pltpu.VMEM((sets, piece), F32), pltpu.VMEM((both, width), F32),
                 pltpu.VMEM((both, width), BF), pltpu.VMEM((both, width), BF), pltpu.VMEM((width, 2 * piece), BF),
                 pltpu.VMEM((width, both), BF), pltpu.VMEM((both, inner), BF), pltpu.VMEM((both, inner), BF)],
    )
    dn_got = to_core(dn)
    py_got = to_y(py_send)
    ux_got = to_x(ux_send)
    dz_got = to_z(dz_send)
    feed_got = to_core(feed_send)

    dmid, a_keep, a_send, b_keep, b_send, o_keep, o_send, dtok_own, dtok_far, dtok_send, back_sums = staged_call(
        functools.partial(backward_kernel, *names),
        where,
        (dn, dn_got, xhat_two, inverse_two, cotangent, cot_sib, vec, attended, attended_sib, w_out, branch,
         qkv_near, kv, logsum, xhat_near, xhat_far, w_qkv),
        [full(rows, width)] + [low(2, 6, unit_rows, half)] * 4 + [low(2, 2, 2, unit_rows, half)] * 2
        + [low(rows, width), low(rows, width), low(2, rows, width), full(8, width)],
        cuts={9: head_rows, 16: all_columns},
        late=tuple(range(2, 17)),
        pairs=(1, 3, 5),
        tables=True,
        scratch=[rows_of_vec, pltpu.VMEM((both, half), BF), pltpu.VMEM((both, width), BF), pltpu.VMEM((both, half), BF),
                 pltpu.VMEM((2, sets, unit_rows, half), BF), pltpu.VMEM((both, half), BF),
                 pltpu.VMEM((total_rows, half), BF), pltpu.VMEM((total_rows, half), BF),
                 pltpu.VMEM((total_rows, width), BF), pltpu.VMEM((4, 12, unit_rows, half), BF),
                 pltpu.VMEM((rows // TILE, 4 * TILE), jnp.int32), pltpu.VMEM((total_rows, 2 * TILE), jnp.int32),
                 pltpu.VMEM((half, total_rows), BF), pltpu.VMEM((total_rows, 2 * HEAD_SIZE), F32),
                 pltpu.VMEM((total_rows, 2 * HEAD_SIZE), F32),
                 pltpu.VMEM((rows // TILE, 2 * HEAD_SIZE, 4 * TILE), F32)],
    )
    a_got = to_x(a_send)
    b_send = to_core(b_send)
    b_got = to_y(b_send)
    b_keep = to_core(b_keep)
    dtok_got = to_core(dtok_send)

    ux_got, ux_keep = after(back_sums, ux_got, ux_keep)
    ux_step = added(ux_keep[1], ux_got[1]).astype(BF)
    ux_far = to_y(ux_step)

    (feed_got,) = after(ux_step, feed_got)
    out, sums = staged_call(
        functools.partial(result_kernel, *names),
        where,
        (feed_keep, feed_got, mid, cotangent, vec, back_sums, bias_d_sum, bias_up_sum),
        [low(rows, width), full(16, width)],
        scratch=[rows_of_vec],
    )
    sums_got = to_core(sums)

    py_got, py_keep = after(sums, py_got, py_keep)
    py_step = added(py_keep[1], py_got[1]).astype(BF)
    py_far = to_x(py_step)

    def dz_rows(*parts):
        return jnp.concatenate([rows_of(part.astype(BF), half) for part in parts], axis=0)

    sums = rows_of(added(sums, sums_got), half)
    o_got = to_z(dz_rows(o_send, sums))
    sums = added(sums, o_got[4 * share :])
    o_got = o_got[: 4 * share].reshape(o_keep.shape)
    (dz_got,) = after(py_step, dz_got)
    dz_step = dz_rows(added(dz_keep[1], dz_got[1]), added(o_keep[1], o_got[1]), sums)
    dz_far = to_zz(dz_step)

    (a_got,) = after(dz_step, a_got)
    a_step = added(a_keep[1], a_got[1]).astype(BF)
    a_far = to_y(a_step)

    (ux_far,) = after(a_step, ux_far)
    ux_sum = added(ux_keep[0], ux_got[0], ux_far).astype(BF)
    up_sib = to_core(ux_sum)

    (b_got,) = after(ux_sum, b_got)
    b_step = added(b_keep[1], b_got[1]).astype(BF)
    b_far = to_x(b_step)

    (dtok_got,) = after(b_step, dtok_got)
    dtok_step = added(dtok_far, dtok_got[1]).astype(BF)
    dtok_x = to_x(dtok_step)

    (py_far,) = after(dtok_step, py_far)
    py_sum = added(py_keep[0], py_got[0], py_far).astype(BF)
    down = py_sum[: 4 * share].reshape(2, 2, share, piece)
    up_own = py_sum[4 * share :].reshape(2, block, piece)
    same = z % 2 == core
    mlp_send = jnp.concatenate([down[1], jnp.where(same, up_sib, up_own)], axis=1)
    mlp_keep = jnp.concatenate([down[0], jnp.where(same, up_own, up_sib)], axis=1)
    mlp_got = to_z(mlp_send)

    (dz_far,) = after(mlp_send, dz_far)
    four = 4 * share
    dz_low = (
        added(dz_keep[0], dz_got[0], dz_far[:four].reshape(2, 2, share, piece)),
        added(o_keep[0], o_got[0], dz_far[four : four + 2 * share].reshape(2, 2, unit_rows, half)),
    )
    sums = added(sums, dz_far[four + 2 * share :])
    dz_step = dz_rows(dz_low[0][1], dz_low[1][1], sums)
    dz_x = to_x(dz_step)

    a_far, b_far = after(dz_step, a_far, b_far)
    one = added(a_keep[0], a_got[0], a_far).astype(BF)
    two = added(b_keep[0], b_got[0], b_far).astype(BF)
    last_send = jnp.concatenate([one[3:], two[3:]], axis=0)
    last_got = to_z(last_send)

    (mlp_got,) = after(last_send, mlp_got)
    mlp_step = added(mlp_keep[1], mlp_got[1]).astype(BF)
    mlp_far = to_zz(mlp_step)

    (dz_x,) = after(mlp_step, dz_x)
    two_shares = 2 * share
    dz_low = (
        added(dz_low[0][0], dz_x[:two_shares].reshape(2, share, piece)),
        added(dz_low[1][0], dz_x[two_shares : two_shares + share].reshape(2, unit_rows, half)),
    )
    sums = added(sums, dz_x[two_shares + share :])
    dz_step = dz_rows(dz_low[0][1], dz_low[1][1], sums)
    dz_keep = dz_rows(dz_low[0][0], dz_low[1][0], sums)
    dz_y = to_y(dz_step)

    (last_got,) = after(dz_step, last_got)
    last = added(jnp.concatenate([one[:3], two[:3]], axis=0), last_got).astype(BF)

    def chosen(owner_z):
        here = (core * 2 + y) * zs + owner_z
        units = []
        for index in range(3):
            at = jnp.int32(0)
            for code, place in enumerate(UNIT_PLACE[..., index].reshape(-1)):
                at = jnp.where(here == code, int(place), at)
            units.append(lax.dynamic_slice_in_dim(last, at, 1, 0))
        return jnp.concatenate(units, axis=0)

    last_step = chosen(z ^ 2)
    last_keep = chosen(z)
    last_far = to_zz(last_step)

    (dtok_x,) = after(last_step, dtok_x)
    (grad_tokens,) = staged_call(
        first_norm_grad_kernel,
        where,
        (dtok_own, dtok_got, dtok_x, tokens, dmid, vec),
        [low(rows, width)],
        cuts={1: ((rows, width), 1, first_block)},
        scratch=[rows_of_vec],
    )
    mlp_far, dz_y = after(grad_tokens, mlp_far, dz_y)
    g_w_down, g_w_up, g_w_out, g_vec = staged_call(
        finish_kernel,
        where,
        (mlp_keep, mlp_got, mlp_far, dz_keep, dz_y),
        [full(2 * piece, share), full(block, piece), full(block, share), full(1, vectors.shape[0] // (sets * parts))],
        cuts={1: ((share + block, piece), 1, first_block)},
        scratch=[pltpu.VMEM((128, 2 * piece), F32), pltpu.VMEM((128, 256), F32), pltpu.VMEM((1, 16 * width + 512), F32)],
    )
    (last_far,) = after(g_w_down, last_far)
    (g_w_qkv,) = staged_call(
        finish_qkv_kernel,
        where,
        (rows_of(last_keep, half), rows_of(last_far, half)),
        [full(block, 3 * share)],
        scratch=[pltpu.VMEM((384, 256), F32)],
    )
    return (out[None], grad_tokens[None], g_w_qkv, g_w_out, g_w_up, g_w_down, g_vec.reshape(-1))


def is_aligned(mesh, tokens, w_up):
    parts, sets = mesh.shape["blk"], mesh.shape["dp"]
    width, hidden = w_up.shape
    rows = tokens.shape[1] // parts
    return (
        parts == 4
        and sets == 2 * parts
        and rows == 4 * TILE
        and (hidden // sets) % 128 == 0
        and (width // 2) % 128 == 0
        and (width // sets) % 32 == 0
        and width == H * HEAD_SIZE
    )


def solution(mesh):
    def run(tokens, lengths, w_qkv, w_out, w_up, w_down, vectors, cotangent):
        body = on_device_aligned if is_aligned(mesh, tokens, w_up) else on_device
        return jax.shard_map(
            body,
            mesh=mesh,
            in_specs=(
                P("dp", "blk", None),
                P("dp", None),
                P(),
                P(),
                P(),
                P(),
                P(),
                P("dp", "blk", None),
            ),
            out_specs=(
                P("dp", "blk", None),
                P("dp", "blk", None),
                P("blk", "dp"),
                P("blk", "dp"),
                P("blk", "dp"),
                P("blk", "dp"),
                P(("dp", "blk")),
            ),
            check_vma=False,
        )(tokens, lengths, w_qkv, w_out, w_up, w_down, vectors, cotangent)

    return run
```

```python
import functools
import math

import jax
import jax.numpy as jnp
import numpy as np
from jax import lax
from jax.experimental import pallas as pl
from jax.experimental.pallas import tpu as pltpu
from jax.sharding import PartitionSpec as P

H = 12
HEAD_SIZE = 64
TILE = 64


EPSILON = 1e-06
FLOOR_SCORE = -1e30


def passed_along(array, axis, by):
    length = lax.axis_size(axis)
    return lax.ppermute(array, axis, [(i, (i + by) % length) for i in range(length)])


def norm_rows(values, gain, shift):
    centre = jnp.mean(values, axis=-1, keepdims=True)
    centred = values - centre
    spread = jnp.mean(centred * centred, axis=-1, keepdims=True)
    return centred * lax.rsqrt(spread + EPSILON) * gain + shift


def exact_gelu(values):
    return jax.nn.gelu(values, approximate=False)


def segment_of(rows_index, rows, parts, ends):
    place = rows_index % rows * parts + rows_index // rows
    return jnp.sum((place[:, None] >= ends[None, :]).astype(jnp.int32), axis=1)


def contract_rows(left, right):
    return lax.dot_general(
        left, right, (((0,), (0,)), ((), ())), preferred_element_type=jnp.float32
    )


def contract_cols(left, right):
    return lax.dot_general(
        left, right, (((1,), (1,)), ((), ())), preferred_element_type=jnp.float32
    )


def attend_block(query, query_item, keys, values, key_item, scale, carry):
    best, total, weighted = carry
    count = keys.shape[0]
    heads = query.shape[1]
    key_heads = keys.reshape(count, heads, -1)
    value_heads = values.reshape(count, heads, -1)
    allowed = (query_item[:, None] == key_item[None, :])[None]
    score = jnp.einsum("qhd,khd->hqk", query, key_heads, preferred_element_type=jnp.float32) * scale
    score = jnp.where(allowed, score, FLOOR_SCORE)
    newbest = jnp.maximum(best, jnp.max(score, axis=-1))
    weight = jnp.where(allowed, jnp.exp(score - newbest[..., None]), 0.0)
    factor = jnp.exp(best - newbest)
    total = total * factor + jnp.sum(weight, axis=-1)
    weighted = weighted * factor[..., None] + jnp.einsum(
        "hqk,khd->hqd", weight.astype(jnp.bfloat16), value_heads, preferred_element_type=jnp.float32
    )
    return (newbest, total, weighted)


def grad_block(query, d_out, logsum, delta, query_item, keys, values, key_item, scale):
    count = keys.shape[0]
    heads = query.shape[1]
    key_heads = keys.reshape(count, heads, -1)
    value_heads = values.reshape(count, heads, -1)
    allowed = (query_item[:, None] == key_item[None, :])[None]
    score = jnp.einsum("qhd,khd->hqk", query, key_heads, preferred_element_type=jnp.float32) * scale
    prob = jnp.where(allowed, jnp.exp(score - logsum[..., None]), 0.0)
    d_prob = jnp.einsum("qhd,khd->hqk", d_out, value_heads, preferred_element_type=jnp.float32)
    d_score = (prob * (d_prob - delta[..., None])).astype(jnp.bfloat16)
    d_query = (
        jnp.einsum("hqk,khd->qhd", d_score, key_heads, preferred_element_type=jnp.float32) * scale
    )
    d_keys = jnp.einsum("hqk,qhd->khd", d_score, query, preferred_element_type=jnp.float32) * scale
    d_values = jnp.einsum(
        "hqk,qhd->khd", prob.astype(jnp.bfloat16), d_out, preferred_element_type=jnp.float32
    )
    return (d_query, d_keys.reshape(count, -1), d_values.reshape(count, -1))


def on_device(tokens, lengths, w_qkv, w_out, w_up, w_down, vectors, cotangent):
    inputs = tokens[0].astype(jnp.float32)
    rows, width = inputs.shape
    heads = H
    head_size = width // heads
    scale = head_size ** (-0.5)
    items = lengths.shape[1]
    ends = jnp.cumsum(lengths[0])
    parts = lax.axis_size("blk")
    position = lax.axis_index("blk")
    query_item = segment_of(position * rows + lax.iota(jnp.int32, rows), rows, parts, ends)
    valid = (query_item < items).astype(jnp.float32)[:, None]
    pieces = [vectors[index * width : (index + 1) * width] for index in range(10)]
    (
        gain_one,
        shift_one,
        bias_q,
        bias_v,
        bias_o,
        scale_one,
        gain_two,
        shift_two,
        bias_d,
        scale_two,
    ) = pieces
    bias_up = vectors[10 * width :]
    normed, norm_one_pull = jax.vjp(norm_rows, inputs, gain_one, shift_one)
    normed_low = normed.astype(jnp.bfloat16)
    qkv_bias = jnp.concatenate([bias_q, jnp.zeros_like(bias_q), bias_v])
    projected = (jnp.dot(normed_low, w_qkv, preferred_element_type=jnp.float32) + qkv_bias).astype(
        jnp.bfloat16
    )
    query = projected[:, :width].reshape(rows, heads, head_size)
    keys = projected[:, width : 2 * width]
    values = projected[:, 2 * width :]
    start_state = (
        jnp.full((heads, rows), FLOOR_SCORE, jnp.float32),
        jnp.zeros((heads, rows), jnp.float32),
        jnp.zeros((heads, rows, head_size), jnp.float32),
    )
    carry = start_state
    piece = (
        lax.all_gather(keys, "blk", axis=0, tiled=True),
        lax.all_gather(values, "blk", axis=0, tiled=True),
    )
    count = piece[0].shape[0]
    size = math.gcd(count, 512)
    steps = count // size
    key_blocks = piece[0].reshape(steps, size, width)
    value_blocks = piece[1].reshape(steps, size, width)

    def inner(state, item):
        block_keys, block_values, offset = item
        key_item = segment_of(offset + lax.iota(jnp.int32, size), rows, parts, ends)
        return (
            attend_block(query, query_item, block_keys, block_values, key_item, scale, state),
            None,
        )

    carry, unused = lax.scan(
        inner, carry, (key_blocks, value_blocks, lax.iota(jnp.int32, steps) * size)
    )
    best, total, weighted = carry
    logsum = best + jnp.log(total)
    attended = (weighted / total[..., None]).transpose(1, 0, 2).reshape(rows, width)
    attended_low = attended.astype(jnp.bfloat16)
    branch = jnp.dot(attended_low, w_out, preferred_element_type=jnp.float32) + bias_o
    mid = inputs + scale_one * branch
    normed_two, norm_two_pull = jax.vjp(norm_rows, mid, gain_two, shift_two)
    normed_two_low = normed_two.astype(jnp.bfloat16)
    before = jnp.dot(normed_two_low, w_up, preferred_element_type=jnp.float32) + bias_up
    activated, gelu_pull = jax.vjp(exact_gelu, before)
    activated_low = activated.astype(jnp.bfloat16)
    feed = jnp.dot(activated_low, w_down, preferred_element_type=jnp.float32) + bias_d
    result = mid + scale_two * feed
    out = (result * valid).astype(jnp.bfloat16)
    d_result = cotangent[0].astype(jnp.float32) * valid
    d_feed = (scale_two * d_result).astype(jnp.bfloat16)
    g_scale_two = jnp.sum(d_result * feed, axis=0)
    g_bias_d = jnp.sum(d_feed.astype(jnp.float32), axis=0)
    g_w_down = contract_rows(activated_low, d_feed)
    d_activated = contract_cols(d_feed, w_down)
    d_before = gelu_pull(d_activated)[0].astype(jnp.bfloat16)
    g_bias_up = jnp.sum(d_before.astype(jnp.float32), axis=0)
    g_w_up = contract_rows(normed_two_low, d_before)
    d_normed_two = contract_cols(d_before, w_up)
    d_mid_norm, g_gain_two, g_shift_two = norm_two_pull(d_normed_two)
    d_mid = d_result + d_mid_norm
    d_branch = (scale_one * d_mid).astype(jnp.bfloat16)
    g_scale_one = jnp.sum(d_mid * branch, axis=0)
    g_bias_o = jnp.sum(d_branch.astype(jnp.float32), axis=0)
    g_w_out = contract_rows(attended_low, d_branch)
    d_attended = contract_cols(d_branch, w_out).astype(jnp.bfloat16)
    d_heads = d_attended.reshape(rows, heads, head_size)
    delta = jnp.sum(
        (d_attended.astype(jnp.float32) * attended).reshape(rows, heads, head_size), axis=-1
    ).T
    zero_query = jnp.zeros((rows, heads, head_size), jnp.float32)

    def visit_block(block_keys, block_values, owner):
        key_item = segment_of(owner * rows + lax.iota(jnp.int32, rows), rows, parts, ends)
        return grad_block(
            query, d_heads, logsum, delta, query_item, block_keys, block_values, key_item, scale
        )

    def send_back(d_keys, d_values):
        return (
            passed_along(d_keys.astype(jnp.bfloat16), "blk", 1).astype(d_keys.dtype),
            passed_along(d_values.astype(jnp.bfloat16), "blk", 1).astype(d_values.dtype),
        )

    def accumulate(state, owner):
        d_query, block_keys, block_values, d_keys, d_values = state
        dq_part, dk_part, dv_part = visit_block(block_keys, block_values, owner)
        d_keys, d_values = send_back(d_keys + dk_part, d_values + dv_part)
        return (d_query + dq_part, d_keys, d_values)

    def turn(step, state):
        owner = (position - step) % parts
        d_query, d_keys, d_values = accumulate(state, owner)
        block_keys, block_values = passed_along((state[1], state[2]), "blk", 1)
        return (d_query, block_keys, block_values, d_keys, d_values)

    zero_rows = jnp.zeros((rows, width), jnp.float32)
    state = lax.fori_loop(0, parts - 1, turn, (zero_query, keys, values, zero_rows, zero_rows))
    d_query, d_keys, d_values = accumulate(state, (position + 1) % parts)
    d_projected = jnp.concatenate([d_query.reshape(rows, width), d_keys, d_values], axis=1).astype(
        jnp.bfloat16
    )
    g_bias_q = jnp.sum(d_projected[:, :width].astype(jnp.float32), axis=0)
    g_bias_v = jnp.sum(d_projected[:, 2 * width :].astype(jnp.float32), axis=0)
    g_w_qkv = contract_rows(normed_low, d_projected)
    d_normed = contract_cols(d_projected, w_qkv)
    d_input_norm, g_gain_one, g_shift_one = norm_one_pull(d_normed)
    d_inputs = d_mid + d_input_norm
    g_vectors = jnp.concatenate(
        [
            g_gain_one,
            g_shift_one,
            g_bias_q,
            g_bias_v,
            g_bias_o,
            g_scale_one,
            g_gain_two,
            g_shift_two,
            g_bias_d,
            g_scale_two,
            g_bias_up,
        ]
    )
    column_sums = (
        lax.psum_scatter(
            g_w_qkv.astype(jnp.bfloat16), "dp", scatter_dimension=1, tiled=True
        ).astype(jnp.float32),
        lax.psum_scatter(
            g_w_out.astype(jnp.bfloat16), "dp", scatter_dimension=1, tiled=True
        ).astype(jnp.float32),
        lax.psum_scatter(g_w_up.astype(jnp.bfloat16), "dp", scatter_dimension=1, tiled=True).astype(
            jnp.float32
        ),
        lax.psum_scatter(
            g_w_down.astype(jnp.bfloat16), "dp", scatter_dimension=1, tiled=True
        ).astype(jnp.float32),
        lax.psum_scatter(
            g_vectors.astype(jnp.bfloat16), "dp", scatter_dimension=0, tiled=True
        ).astype(jnp.float32),
    )
    g_w_qkv, g_w_out, g_w_up, g_w_down, g_vectors = (
        lax.psum_scatter(
            column_sums[0].astype(jnp.bfloat16), "blk", scatter_dimension=0, tiled=True
        ).astype(jnp.float32),
        lax.psum_scatter(
            column_sums[1].astype(jnp.bfloat16), "blk", scatter_dimension=0, tiled=True
        ).astype(jnp.float32),
        lax.psum_scatter(
            column_sums[2].astype(jnp.bfloat16), "blk", scatter_dimension=0, tiled=True
        ).astype(jnp.float32),
        lax.psum_scatter(
            column_sums[3].astype(jnp.bfloat16), "blk", scatter_dimension=0, tiled=True
        ).astype(jnp.float32),
        lax.psum_scatter(
            column_sums[4].astype(jnp.bfloat16), "blk", scatter_dimension=0, tiled=True
        ).astype(jnp.float32),
    )
    return (
        out[None],
        d_inputs.astype(jnp.bfloat16)[None],
        g_w_qkv,
        g_w_out,
        g_w_up,
        g_w_down,
        g_vectors,
    )


BF = jnp.bfloat16
F32 = jnp.float32
MASKED = -1e30
GRANT = 60 * 1024 * 1024
WIDE_CHUNK = 128


def unit_tables():
    lists, places = np.zeros((2, 2, 2, 6), np.int32), np.zeros((2, 2, 4, 3), np.int32)
    units = {core: [unit for unit in range(24) if unit // 4 % 2 == core] for core in range(2)}
    for y in range(2):
        for low_z in range(2):
            first = {}
            for core in range(2):
                own = [unit for unit in units[core] if unit // 3 % 2 == y]
                first[core] = [unit for unit in own if unit // 6 % 2 == low_z]
                rest = [unit for unit in own if unit // 6 % 2 != low_z]
                lists[core, y, low_z] = [units[core].index(unit) for unit in first[core] + rest]
            for core in range(2):
                held = first[core] + first[1 - core]
                for z in (low_z, low_z + 2):
                    places[core, y, z] = [held.index(3 * (2 * z + y) + index) for index in range(3)]
    return lists.reshape(-1), places


UNIT_TABLE, UNIT_PLACE = unit_tables()
UNIT_LIST = 4
ENDS = UNIT_LIST + UNIT_TABLE.size


def dot_nn(left, right):
    return lax.dot_general(left, right, (((1,), (0,)), ((), ())), preferred_element_type=F32)


def dot_nt(left, right):
    return lax.dot_general(left, right, (((1,), (1,)), ((), ())), preferred_element_type=F32)


def dot_tn(left, right):
    return lax.dot_general(left, right, (((0,), (0,)), ((), ())), preferred_element_type=F32)


def standardise(values):
    centred = values - jnp.mean(values, axis=-1, keepdims=True)
    inverse = lax.rsqrt(jnp.mean(centred * centred, axis=-1, keepdims=True) + EPSILON)
    return centred * inverse, inverse


def standardise_grad(grad, xhat, inverse):
    first = jnp.mean(grad, axis=-1, keepdims=True)
    second = jnp.mean(grad * xhat, axis=-1, keepdims=True)
    return (grad - first - xhat * second) * inverse


def column_sum(values):
    return jnp.sum(values, axis=0, keepdims=True)


def item_at(place, where_ref, items):
    found = jnp.zeros_like(place)
    for index in range(items):
        found = found + (place >= where_ref[ENDS + index]).astype(jnp.int32)
    return found


def own_block(where_ref, rel_x, rel_c):
    return 2 * (where_ref[0] ^ rel_x) + (where_ref[1] ^ rel_c)


def low(*shape):
    return jax.ShapeDtypeStruct(shape, BF)


def full(*shape):
    return jax.ShapeDtypeStruct(shape, F32)


def lanes_at(index, size):
    return pl.ds(pl.multiple_of(index * size, size), size)


class Stage:
    def __init__(self, reads, places, writes):
        self.reads, self.places, self.writes = reads, places, writes
        self.started, self.waited, self.begun = set(), set(), []

    def start(self, *indices):
        for index in indices:
            if index not in self.started:
                self.started.add(index)
                for copy in self.reads[index]:
                    copy.start()

    def __getitem__(self, index):
        self.start(index)
        if index not in self.waited:
            self.waited.add(index)
            for copy in self.reads[index]:
                copy.wait()
        return self.places[index]

    def out(self, index):
        return self.writes[index][0]

    def put(self, *indices):
        for index in indices:
            self.writes[index][1].start()
            self.begun.append(index)

    def finish(self):
        for index in range(len(self.reads)):
            self[index]
        self.put(*(index for index in range(len(self.writes)) if index not in self.begun))
        for place, copy in self.writes:
            copy.wait()


class Place:
    def __init__(self, lengths_ref, table_ref):
        position, turn = lax.axis_index("blk"), lax.axis_index("dp")
        self.four = (position // 2, position % 2, turn // 2, turn % 2)
        self.table_ref = table_ref
        self.ends, end = [], jnp.int32(0)
        for index in range(lengths_ref.shape[1]):
            end = end + lengths_ref[0, index]
            self.ends.append(end)

    def __getitem__(self, index):
        if isinstance(index, int) and index < UNIT_LIST:
            return self.four[index]
        if isinstance(index, int) and index >= ENDS:
            return self.ends[index - ENDS]
        return self.table_ref[index - UNIT_LIST]


def unpack_rows(raw_ref, vec_ref):
    count = vec_ref.shape[1] // 128
    for row in range(vec_ref.shape[0]):
        for part in range(count):
            vec_ref[row : row + 1, part * 128 : (part + 1) * 128] = raw_ref[row * count + part : row * count + part + 1]


def staged_call(body, where, operands, out_shape, cuts=None, scratch=(), late=(), pairs=(), tables=False):
    cuts = cuts or {}
    count, results = len(operands), len(out_shape)
    shapes, parts = [], []
    for index, operand in enumerate(operands):
        shape, pieces = (operand.shape, 1) if index not in cuts else cuts[index][:2]
        shapes.append(pltpu.VMEM(shape, operand.dtype))
        parts.append(pieces)
    held_shapes, held_at = [], {}
    for index, item in enumerate(out_shape):
        if index - 1 in pairs:
            held_at[index] = (len(held_shapes) - 1, 1)
        elif index in pairs:
            held_at[index] = (len(held_shapes), 0)
            held_shapes.append(pltpu.VMEM((2, *item.shape), item.dtype))
        else:
            held_at[index] = (len(held_shapes), None)
            held_shapes.append(pltpu.VMEM(item.shape, item.dtype))

    def kernel(*refs):
        where_ref = Place(refs[0], refs[1] if tables else None)
        refs = refs[2 if tables else 1 :]
        ins, outs = refs[:count], refs[count : count + results]
        places = refs[count + results : 2 * count + results]
        held = refs[2 * count + results : 2 * count + results + len(held_shapes)]
        read_sem, write_sem, *rest = refs[2 * count + results + len(held_shapes) :]
        reads, used = [], 0
        for index in range(count):
            moves = [(ins[index], places[index])] if index not in cuts else cuts[index][2](where_ref, ins[index], places[index])
            reads.append([])
            for source, target in moves:
                reads[-1].append(pltpu.make_async_copy(source, target, read_sem.at[used]))
                used += 1
        writes = []
        for index in range(results):
            place, entry = held_at[index]
            source = held[place] if entry is None else held[place].at[entry]
            writes.append((held[place], pltpu.make_async_copy(source, outs[index], write_sem.at[index])))
        stage = Stage(reads, places, writes)
        stage.start(*(index for index in range(count) if index not in late))
        body(where_ref, stage, *rest)
        stage.finish()

    return pl.pallas_call(
        kernel,
        in_specs=[pl.BlockSpec(memory_space=pltpu.SMEM)] * (2 if tables else 1)
        + [pl.BlockSpec(memory_space=pl.ANY)] * count,
        out_specs=[pl.BlockSpec(memory_space=pl.ANY)] * results,
        out_shape=out_shape,
        scratch_shapes=shapes
        + held_shapes
        + [pltpu.SemaphoreType.DMA((sum(parts),)), pltpu.SemaphoreType.DMA((results,))]
        + list(scratch),
        compiler_params=pltpu.CompilerParams(vmem_limit_bytes=GRANT),
    )(where, *((UNIT_TABLE,) if tables else ()), *operands)


def each(count, body):
    def step(index, carry):
        body(index)
        return carry

    lax.fori_loop(0, count, step, 0)


def hidden_unit(where_ref, rel_x, side):
    return 4 * (where_ref[0] ^ rel_x) + 2 * where_ref[1] + side


def lanes_below(shape, count):
    return lax.broadcasted_iota(jnp.int32, shape, 1) < count


def stack_heads(pair):
    first = lanes_below(pair.shape, HEAD_SIZE)
    zero = jnp.zeros_like(pair)
    return jnp.concatenate([jnp.where(first, pair, zero), jnp.where(first, zero, pair)], axis=0)


def turn(source, target):
    each(source.shape[1] // 128, lambda index: target.__setitem__(lanes_at(index, 128), source[:, lanes_at(index, 128)].T))


def valid_at(where_ref, rel_c, first, count, parts, items):
    row = first + lax.broadcasted_iota(jnp.int32, (count, 1), 0)
    item = item_at(row * parts + own_block(where_ref, 0, rel_c), where_ref, items)
    return (item < items).astype(F32)


def normed_rows(xhat, vec_ref, first):
    return (xhat.astype(F32) * vec_ref[first : first + 1] + vec_ref[first + 1 : first + 2]).astype(BF)


def prepare_kernel(parts, items, where_ref, stage, vec_ref, held, normed_ref, row_ref):
    unpack_rows(stage[2], vec_ref)
    own_ref, sib_ref = stage[0], stage[1]
    stage.start(3, 4, 5, 6)
    xhat_ref, qkv_ref, dact_ref, turned_ref, sum_ref = (stage.out(index) for index in range(5))
    rows, width = own_ref.shape
    half = width // 2
    core = where_ref[1]
    for rel_c, ref in enumerate((own_ref, sib_ref)):

        def norm(index, rel_c=rel_c, ref=ref):
            xhat, unused = standardise(ref[lanes_at(index, WIDE_CHUNK)].astype(F32))
            to = lanes_at(index + rel_c * (rows // WIDE_CHUNK), WIDE_CHUNK)
            xhat_ref[to] = xhat.astype(BF)
            normed_ref[to] = (xhat * vec_ref[0:1] + vec_ref[1:2]).astype(BF)

        each(rows // WIDE_CHUNK, norm)
    stage.put(0)
    sum_ref[...] = jnp.zeros_like(sum_ref)
    for rel_c in range(2):

        def grad(index, rel_c=rel_c, ref=stage[4 + rel_c]):
            valid = valid_at(where_ref, rel_c, index * WIDE_CHUNK, WIDE_CHUNK, parts, items)
            part = (vec_ref[9:10] * (ref[lanes_at(index, WIDE_CHUNK)].astype(F32) * valid)).astype(BF)
            held[lanes_at(index + rel_c * (rows // WIDE_CHUNK), WIDE_CHUNK)] = part
            if rel_c == 0:
                sum_ref[...] += column_sum(part.astype(F32))

        each(rows // WIDE_CHUNK, grad)
    turn(held, turned_ref)
    stage.put(3, 4)
    row_ref[0:1, :half] = vec_ref[2:3, lanes_at(core, half)]
    row_ref[0:1, half : 2 * half] = jnp.zeros((1, half), F32)
    row_ref[0:1, 2 * half :] = vec_ref[3:4, lanes_at(core, half)]
    row_ref[1:2, :half] = jnp.full((1, half), HEAD_SIZE ** (-0.5), F32)
    row_ref[1:2, half:] = jnp.ones((1, 2 * half), F32)
    weight_ref = stage[3]

    def project(index):
        lanes = lanes_at(index, half)
        part = dot_nn(normed_ref[...], weight_ref[:, lanes]) + row_ref[0:1, lanes]
        qkv_ref[:, lanes] = (part.astype(BF).astype(F32) * row_ref[1:2, lanes]).astype(BF)

    each(3, project)
    stage.put(1)
    down_ref = stage[6]
    piece = dact_ref.shape[1] // 4

    def back(index):
        dact_ref[:, lanes_at(index, piece)] = dot_nt(held[...], down_ref[lanes_at(index, piece)]).astype(BF)

    each(4, back)


def item_of_place(where_ref, place, items):
    found = jnp.int32(0)
    for index in range(items):
        found = found + (place >= where_ref[ENDS + index]).astype(jnp.int32)
    return found


def tiles_meet(where_ref, one, other, parts, items):
    span = TILE * parts
    first, last = min(one, other), max(one, other)
    return item_of_place(where_ref, first * span + span - 1, items) >= item_of_place(
        where_ref, last * span, items
    )


def near_tiles(tile, tiles):
    return max(0, tile - 1), min(tiles, tile + 2)


def far_pairs(tiles):
    return [(one, other) for one in range(tiles) for other in range(tiles) if abs(one - other) > 1]


def any_far(where_ref, tiles, parts, items):
    found = jnp.bool_(False)
    for one, other in far_pairs(tiles):
        if one < other:
            found = found | tiles_meet(where_ref, one, other, parts, items)
    return found


def attend_kernel(parts, items, where_ref, stage, vec_ref, wide_ref, normed_ref, asks_ref):
    unpack_rows(stage[2], vec_ref)
    xhat_ref, kv_ref, attended_ref, logsum_ref = (stage.out(index) for index in range(4))
    far_a_ref, far_b_ref = stage[0], stage[1]
    stage.start(3, 4)
    rows, width = far_a_ref.shape
    tiles = rows // TILE
    span = parts * TILE
    both = 2 * HEAD_SIZE
    half = width // 2
    core = where_ref[1]
    for rel_c, ref in enumerate((far_a_ref, far_b_ref)):
        xhat, unused = standardise(ref[...].astype(F32))
        xhat_ref[rel_c * rows : (rel_c + 1) * rows] = xhat.astype(BF)
        normed_ref[rel_c * rows : (rel_c + 1) * rows] = normed_rows(xhat, vec_ref, 0)
    stage.put(0)
    row = lax.broadcasted_iota(jnp.int32, (2 * TILE, 2 * TILE), 0)
    block = 2 * where_ref[0] + (where_ref[1] ^ (row // TILE))
    for tile in range(tiles):
        asks_ref[tile] = item_at((tile * TILE + row % TILE) * parts + block, where_ref, items)
    lane = lax.broadcasted_iota(jnp.int32, (1, span), 1)
    slot = lane // TILE
    block = 2 * (where_ref[0] ^ (slot // 2)) + (where_ref[1] ^ (slot % 2))
    key_item = [item_at((tile * TILE + lane % TILE) * parts + block, where_ref, items) for tile in range(tiles)]
    weight_ref = stage[3]
    row_ref = jnp.concatenate([jnp.zeros((1, half), F32), vec_ref[3:4, lanes_at(core, half)]], axis=1)
    far_kv = (dot_nn(normed_ref[...], weight_ref[...]) + row_ref).astype(BF)
    qkv_ref = stage[4]
    for tile in range(tiles):
        for slot in range(2):
            at = slice(slot * rows + tile * TILE, slot * rows + (tile + 1) * TILE)
            kv_ref[tile * span + slot * TILE : tile * span + (slot + 1) * TILE] = qkv_ref[at, half:]
            kv_ref[tile * span + (slot + 2) * TILE : tile * span + (slot + 3) * TILE] = far_kv[at]
    stage.put(1)
    for index in range(half // both):
        wide_ref[:, 2 * index * both : (2 * index + 1) * both] = kv_ref[:, half + index * both : half + (index + 1) * both]
        wide_ref[:, (2 * index + 1) * both : (2 * index + 2) * both] = jnp.ones((tiles * span, both), BF)

    def attend(index, tile, first, last):
        lanes = lanes_at(index, both)
        at = slice(first * span, last * span)
        places = [pl.ds(pl.multiple_of(rel_c * rows + tile * TILE, TILE), TILE) for rel_c in range(2)]
        query = stack_heads(jnp.concatenate([qkv_ref[place, lanes] for place in places], axis=0))
        score = dot_nt(query, kv_ref[at, lanes])
        asked = asks_ref[tile][:, :1]
        allowed = jnp.concatenate([asked == key_item[other] for other in range(first, last)], axis=1)
        score = jnp.where(jnp.concatenate([allowed, allowed], axis=0), score, MASKED)
        best = jnp.max(score, axis=1, keepdims=True)
        weight = jnp.exp(score - best).astype(BF)
        mixed = dot_nn(weight, wide_ref[at, lanes_at(index, 2 * both)])
        total = mixed[:, both:]
        logsum_ref[index, pl.ds(tile, 1)] = (best + jnp.log(total)).T[:1]
        mixed = mixed[:, :both] / total
        attended = jnp.where(lanes_below((both, both), HEAD_SIZE), mixed[:both], mixed[both:]).astype(BF)
        for rel_c, place in enumerate(places):
            attended_ref[place, lanes] = attended[rel_c * TILE : (rel_c + 1) * TILE]

    def pair(index):
        for tile in range(tiles):
            attend(index, tile, *near_tiles(tile, tiles))

    each(half // both, pair)

    @pl.when(any_far(where_ref, tiles, parts, items))
    def far():
        def again(step):
            tile = step % tiles
            found = jnp.bool_(False)
            for one, other in far_pairs(tiles):
                found = found | ((tile == one) & tiles_meet(where_ref, one, other, parts, items))
            pl.when(found)(lambda: attend(step // tiles, tile, 0, tiles))

        each(half // both * tiles, again)


def gelu_with_slope(values):
    bell = jnp.exp(-0.5 * values * values)
    inverse = 1.0 / (1.0 + (0.3275911 * 0.5**0.5) * jnp.abs(values))
    series = 1.061405429
    for coefficient in (-1.453152027, 1.421413741, -0.284496736, 0.254829592):
        series = series * inverse + coefficient
    tail = 0.5 * (series * inverse) * bell
    normal = jnp.where(values >= 0, 1.0 - tail, tail)
    return values * normal, normal + values * bell * ((2.0 * math.pi) ** -0.5)


def set_block(where_ref, rel_y, low_z, high_z):
    return 2 * (where_ref[2] ^ (low_z + 2 * high_z)) + (where_ref[3] ^ rel_y)


def mlp_kernel(where_ref, stage, vec_ref, bias_ref, mid_ref, joined, normed, grad, turned, act_ref, dbefore_ref):
    py_ref, ux_ref, dz_ref = stage.out(0), stage.out(2), stage.out(4)
    xhat_ref, inverse_ref, mid_own_ref, branch_ref, swap_ref, feed_keep, bias_sum_ref = (
        stage.out(index) for index in range(6, 13)
    )
    unpack_rows(stage[4], vec_ref)
    att_own_ref, att_sib_ref, own_ref, sib_ref, raw_ref, out_ref = (stage[index] for index in range(6))
    stage.start(6, 7, 8)
    x, core, z, y = (where_ref[index] for index in range(4))
    rows, width = own_ref.shape
    half = width // 2
    piece = act_ref.shape[1] // 4
    joined[:, :half] = att_own_ref[...]
    joined[:rows, half:] = att_sib_ref[rows:]
    joined[rows:, half:] = att_sib_ref[:rows]

    def project(index):
        lanes = lanes_at(index, 256)
        branch = dot_nn(joined[...], out_ref[:, lanes]) + vec_ref[4:5, lanes]
        branch_ref[:, lanes] = branch[:rows].astype(BF)
        branch = vec_ref[5:6, lanes] * branch
        mid_ref[:rows, lanes] = own_ref[:, lanes].astype(F32) + branch[:rows]
        mid_ref[rows:, lanes] = sib_ref[:, lanes].astype(F32) + branch[rows:]

    each(width // 256, project)

    mid_own_ref[...] = mid_ref[:rows]

    def norm(index):
        at = lanes_at(index, WIDE_CHUNK)
        xhat, inverse = standardise(mid_ref[at])
        normed[at] = (xhat * vec_ref[6:7] + vec_ref[7:8]).astype(BF)
        xhat_ref[at] = xhat.astype(BF)
        inverse_ref[at] = inverse

    each(2 * rows // WIDE_CHUNK, norm)
    stage.put(6, 7, 8, 9)
    stage.start(9)
    count = piece // 128
    for unit in range(8):
        for part in range(count):
            row = 10 * width // 128 + unit * count + part
            bias_ref[unit : unit + 1, part * 128 : (part + 1) * 128] = raw_ref[row : row + 1]
    up_ref, dact_ref, turned_ref = stage[6], stage[7], stage[8]
    size = grad.shape[0] // 8

    def hidden(index):
        rel_x = 1 - index
        for side in range(2):
            at = lanes_at(2 * rel_x + side, piece)
            before = dot_nn(normed[...], up_ref[:, at]) + bias_ref[pl.ds(hidden_unit(where_ref, rel_x, side), 1)]
            act, slope = gelu_with_slope(before)
            act_ref[:, at] = act.astype(BF)
            dbefore = (dact_ref[:, at].astype(F32) * slope).astype(BF)
            dbefore_ref[:, at] = dbefore
            bias_sum_ref[:, at] = column_sum(dbefore.astype(F32))
            grad[:, side * piece : (side + 1) * piece] = dot_nn(turned_ref[...], act_ref[:, at]).astype(BF)

        def lay(index):
            low_z, high_z, rel_y = index // 4, index // 2 % 2, index % 2
            at = lanes_at(set_block(where_ref, rel_y, low_z, high_z), size)
            dz_ref[low_z, high_z, rel_x, rel_y] = grad[at, :piece]
            to = lanes_at(2 * low_z + high_z, size // 2)
            block = set_block(where_ref, rel_y, low_z, high_z)
            ux_ref[rel_x, rel_y, to] = grad[lanes_at(2 * block, size // 2), piece:]
            py_ref[rel_y, rel_x, to] = grad[lanes_at(2 * block + 1, size // 2), piece:]

        each(8, lay)

    each(2, hidden)
    stage.put(4, 5)
    turn(normed, turned)
    block = 2 * size

    def up(index):
        rel_y, high_z = index // 2, index % 2
        unit = 2 * (x ^ (z // 2) ^ high_z) + (y ^ rel_y)
        grad[:, :piece] = dot_nn(turned[...], dbefore_ref[:, lanes_at(unit, piece)]).astype(BF)
        for rel_x in range(2):
            to = lanes_at(1 + high_z, block)
            py_ref[rel_y, rel_x, to] = grad[lanes_at(own_block(where_ref, rel_x, 0), block), :piece]
            ux_ref[rel_x, rel_y, to] = grad[lanes_at(own_block(where_ref, rel_x, 1), block), :piece]

    each(4, up)
    stage.put(0, 1, 2, 3)

    def back(index):
        lanes = lanes_at(index, 256)
        total = dot_nt(dbefore_ref[...], up_ref[lanes])
        swap_ref[: 2 * rows, lanes] = total.astype(BF)

    each(width // 256, back)
    down_ref = stage[9]

    def feed(index):
        lanes = lanes_at(index, 256)
        total = dot_nn(act_ref[...], down_ref[:, lanes])
        feed_keep[:, lanes] = total[:rows]
        swap_ref[2 * rows :, lanes] = total[rows:].astype(BF)

    each(width // 256, feed)


def middle(parts, items, where_ref, stage, vec_ref, sum_ref, datt_ref, held, chosen, packed):
    dmid_ref, out_ref = stage.out(0), stage.out(4)
    keep_ref, got_ref, xhat_ref, inverse_ref, own_ref, sib_ref, raw_ref = (stage[index] for index in range(7))
    stage.start(10, 9, 7, 8, 11, 12, 13)
    unpack_rows(raw_ref, vec_ref)
    rows, width = own_ref.shape
    half = width // 2
    core = where_ref[1]
    left_is_own = lanes_below((rows, half), half // 2) == (core == 0)
    for rel_c, ref in enumerate((own_ref, sib_ref)):
        here = slice(rel_c * rows, (rel_c + 1) * rows)
        there = slice((1 - rel_c) * rows, (2 - rel_c) * rows)
        valid = valid_at(where_ref, rel_c, 0, rows, parts, items)
        dnormed = keep_ref[here].astype(F32) + got_ref[there].astype(F32)
        xhat, inverse = xhat_ref[here].astype(F32), inverse_ref[here]
        dmid = ref[...].astype(F32) * valid + standardise_grad(vec_ref[6:7] * dnormed, xhat, inverse)
        dbranch = (vec_ref[5:6] * dmid).astype(BF)
        held[here] = dbranch
        if rel_c == 0:
            dmid_ref[...] = dmid
            sum_ref[0:1] = column_sum(dbranch.astype(F32))
            sum_ref[1:2] = column_sum(dmid * stage[10][...].astype(F32))
            sum_ref[2:3] = column_sum(dnormed * xhat)
            sum_ref[3:4] = column_sum(dnormed)
    stage.put(0)
    stage.start(*range(14, 21))
    datt_ref[...] = dot_nt(held[...], stage[9][...]).astype(BF)
    att_own_ref, att_sib_ref = stage[7], stage[8]
    for rel_c in range(2):
        here = slice(rel_c * rows, (rel_c + 1) * rows)
        there = slice((1 - rel_c) * rows, (2 - rel_c) * rows)
        other = pltpu.roll(att_sib_ref[there].astype(F32), half // 2, 1)
        chosen[here] = jnp.where(left_is_own, att_own_ref[here].astype(F32), other).astype(BF)
    grad = dot_tn(held[...], chosen[...])
    count, unit_rows = packed.shape[1:3]
    for index in range(count):
        left, right = pack_unit(grad[2 * index * unit_rows : 2 * (index + 1) * unit_rows])
        packed[0, index] = left.astype(BF)
        packed[1, index] = right.astype(BF)

    def lay(index):
        low_z, high_z, rel_x, rel_y = index // 8, index // 4 % 2, index // 2 % 2, index % 2
        at = set_block(where_ref, rel_y, low_z, high_z)
        out_ref[low_z, high_z, rel_x, rel_y] = packed[where_ref[0] ^ rel_x, at]

    each(16, lay)
    stage.put(4, 5)


def pack_unit(unit):
    half = unit.shape[0] // 2
    width = unit.shape[1]
    top, bottom = unit[:half], unit[half:]
    first = lanes_below((half, width), width // 2)
    left = jnp.where(first, top, pltpu.roll(bottom, width // 2, 1))
    right = jnp.where(first, pltpu.roll(top, width // 2, 1), bottom)
    return left, right


def join_heads(stacked_turned):
    stacked = stacked_turned.T
    count = stacked.shape[0] // 2
    return jnp.where(
        lanes_below((count, stacked.shape[1]), HEAD_SIZE), stacked[:count], stacked[count:]
    )


def query_items(where_ref, tile, parts, items):
    lane = lax.broadcasted_iota(jnp.int32, (1, 4 * TILE), 1)
    rel_c = (lane // TILE) % 2
    block = 2 * where_ref[0] + (where_ref[1] ^ rel_c)
    return item_at((tile * TILE + lane % TILE) * parts + block, where_ref, items)


def fill_key_items(where_ref, item_ref, tiles, parts, items):
    row = lax.broadcasted_iota(jnp.int32, (TILE, item_ref.shape[1]), 0)
    for tile in range(tiles):
        for slot in range(parts):
            block = own_block(where_ref, slot // 2, slot % 2)
            at = (tile * parts + slot) * TILE
            item_ref[at : at + TILE] = item_at((tile * TILE + row) * parts + block, where_ref, items)


def both_heads(array):
    return jnp.concatenate([array, array], axis=1)


def attend_grad(
    parts, items, where_ref, stage, datt_ref, dquery_ref, dkeys_ref, dvalues_ref, asks_ref, item_ref, turned_ref, dk, dv, dq
):
    attended_ref, qkv_ref, kv_ref, logsum_ref = stage[7], stage[11], stage[12], stage[13]
    half = datt_ref.shape[1]
    rows = datt_ref.shape[0] // 2
    tiles = rows // TILE
    span = parts * TILE
    scale = HEAD_SIZE ** (-0.5)
    turned_ref[...] = kv_ref[:, :half].T
    fill_key_items(where_ref, item_ref, tiles, parts, items)
    for tile in range(tiles):
        asks_ref[tile : tile + 1] = query_items(where_ref, tile, parts, items)
    some_far = any_far(where_ref, tiles, parts, items)

    def pair(index, carry):
        lanes = lanes_at(index, 2 * HEAD_SIZE)
        value_lanes = pl.ds(pl.multiple_of(half + index * 2 * HEAD_SIZE, 2 * HEAD_SIZE), 2 * HEAD_SIZE)
        dk[...] = jnp.zeros_like(dk)
        dv[...] = jnp.zeros_like(dv)

        def places(tile):
            return [pl.ds(pl.multiple_of(rel_c * rows + tile * TILE, TILE), TILE) for rel_c in range(2)]

        def visit(tile, at):
            query = stack_heads(jnp.concatenate([qkv_ref[place, lanes] for place in places(tile)], axis=0))
            grad = jnp.concatenate([datt_ref[place, lanes] for place in places(tile)], axis=0)
            attended = jnp.concatenate([attended_ref[place, lanes] for place in places(tile)], axis=0)
            product = (grad.astype(F32) * attended.astype(F32)).T
            delta = jnp.concatenate([column_sum(product[:HEAD_SIZE]), column_sum(product[HEAD_SIZE:])], axis=1)
            grad = stack_heads(grad)
            score = dot_nt(kv_ref[at, lanes], query)
            allowed = both_heads(item_ref[at]) == asks_ref[pl.ds(tile, 1)]
            prob = jnp.exp(jnp.where(allowed, score, MASKED) - logsum_ref[index, pl.ds(tile, 1)])
            dprob = dot_nt(kv_ref[at, value_lanes], grad)
            dscore = (prob * (dprob - delta)).astype(BF)
            dv[at] += dot_nn(prob.astype(BF), grad)
            dk[at] += dot_nn(dscore, query)
            return dot_nn(turned_ref[lanes, at], dscore)

        for tile in range(tiles):
            first, last = near_tiles(tile, tiles)
            dq[tile] = visit(tile, slice(first * span, last * span))

        @pl.when(some_far)
        def far():
            def add(step):
                tile, other = step // tiles, step % tiles
                found = jnp.bool_(False)
                for one, two in far_pairs(tiles):
                    found = found | ((step == one * tiles + two) & tiles_meet(where_ref, one, two, parts, items))

                @pl.when(found)
                def meet():
                    at = pl.ds(pl.multiple_of(other * span, span), span)
                    dq[tile] += visit(tile, at)

            each(tiles * tiles, add)

        for tile in range(tiles):
            dquery = (join_heads(dq[tile]) * scale).astype(BF)
            for rel_c, place in enumerate(places(tile)):
                dquery_ref[place, lanes] = dquery[rel_c * TILE : (rel_c + 1) * TILE]
            for slot in range(parts):
                to = slice(slot * rows + tile * TILE, slot * rows + (tile + 1) * TILE)
                at = slice(tile * span + slot * TILE, tile * span + (slot + 1) * TILE)
                dkeys_ref[to, lanes] = dk[at].astype(BF)
                dvalues_ref[to, lanes] = dv[at].astype(BF)
        return carry

    lax.fori_loop(0, half // (2 * HEAD_SIZE), pair, 0)


def twice(half_row, where_ref):
    row = both_heads(half_row)
    return jnp.where(lanes_below(row.shape, half_row.shape[1]) == (where_ref[1] == 0), row, 0.0)


def qkv_grad(where_ref, stage, vec_ref, sum_ref, dquery_ref, dkeys_ref, dvalues_ref, normed_ref, packed):
    a_ref, b_ref = stage.out(1), stage.out(3)
    near_ref, far_ref = stage[14], stage[15]
    rows, width = near_ref.shape
    core, z, y = where_ref[1], where_ref[2], where_ref[3]
    normed_ref[:rows] = normed_rows(near_ref[...], vec_ref, 0)
    normed_ref[rows:] = normed_rows(far_ref[...], vec_ref, 0)
    sum_ref[4:5] = twice(column_sum(dquery_ref[...].astype(F32)), where_ref)
    sum_ref[5:6] = twice(column_sum(dvalues_ref[...].astype(F32)), where_ref)
    for part, ref in enumerate((dquery_ref, dkeys_ref, dvalues_ref)):
        grad = dot_tn(ref[...], normed_ref[: ref.shape[0]])
        size = grad.shape[0] // 4
        for unit in range(4):
            for at_x in range(2):
                left, right = pack_unit(
                    grad[unit * size : (unit + 1) * size, at_x * width // 2 : (at_x + 1) * width // 2]
                )
                packed[2 * at_x, 4 * part + unit] = left.astype(BF)
                packed[2 * at_x + 1, 4 * part + unit] = right.astype(BF)

    def lay(index):
        rel_x, rel_y, at = index // 12, index // 6 % 2, index % 6
        unit = where_ref[UNIT_LIST + 24 * core + 12 * (y ^ rel_y) + 6 * (z % 2) + at]
        a_ref[rel_x, rel_y, at] = packed[own_block(where_ref, rel_x, 0), unit]
        b_ref[rel_y, rel_x, at] = packed[own_block(where_ref, rel_x, 1), unit]

    each(24, lay)
    stage.put(1, 2, 3)


def tokens_grad(where_ref, stage, sum_ref, dquery_ref, dkeys_ref, dvalues_ref):
    own_ref, far_ref, send_ref = (stage.out(index) for index in (6, 7, 8))
    near_ref, beyond_ref, weight_ref = stage[14], stage[15], stage[16]
    rows, width = own_ref.shape
    half = dquery_ref.shape[1]
    gain = jnp.zeros((1, width), F32)
    shift = gain
    for slot in range(4):
        at = slice(slot * rows, (slot + 1) * rows)
        part = dot_nt(dkeys_ref[at], weight_ref[:, half : 2 * half]) + dot_nt(dvalues_ref[at], weight_ref[:, 2 * half :])
        if slot < 2:
            part = part + dot_nt(dquery_ref[at], weight_ref[:, :half])
        xhat = (near_ref if slot < 2 else beyond_ref)[(slot % 2) * rows : (slot % 2 + 1) * rows].astype(F32)
        gain = gain + column_sum(part * xhat)
        shift = shift + column_sum(part)
        if slot % 2:
            send_ref[slot // 2] = part.astype(BF)
        elif slot:
            far_ref[...] = part.astype(BF)
        else:
            own_ref[...] = part.astype(BF)
    sum_ref[6:7] = gain
    sum_ref[7:8] = shift


def backward_kernel(
    parts, items, where_ref, stage, vec_ref, sum_ref, datt_ref, held, chosen, gpacked, dquery_ref, dkeys_ref, dvalues_ref,
    normed_ref, packed, asks_ref, item_ref, turned_ref, dk, dv, dq,
):
    middle(parts, items, where_ref, stage, vec_ref, sum_ref, datt_ref, held, chosen, gpacked)
    attend_grad(
        parts, items, where_ref, stage, datt_ref, dquery_ref, dkeys_ref, dvalues_ref, asks_ref, item_ref, turned_ref,
        dk, dv, dq,
    )
    qkv_grad(where_ref, stage, vec_ref, sum_ref, dquery_ref, dkeys_ref, dvalues_ref, normed_ref, packed)
    tokens_grad(where_ref, stage, sum_ref, dquery_ref, dkeys_ref, dvalues_ref)
    result(parts, items, where_ref, stage, vec_ref, sum_ref)


def result(parts, items, where_ref, stage, vec_ref, back_ref):
    out_ref, sum_ref = stage.out(9), stage.out(10)
    keep_ref, mid_ref, bias_d_ref, bias_up_ref = (stage[index] for index in range(17, 21))
    rows, width = keep_ref.shape
    got_ref = stage[1]
    valid = valid_at(where_ref, 0, 0, rows, parts, items)
    feed = keep_ref[...] + got_ref[2 * rows :].astype(F32) + vec_ref[8:9]
    out_ref[...] = (valid * (mid_ref[...] + vec_ref[9:10] * feed)).astype(BF)
    stage.put(9)
    sum_ref[0:2] = back_ref[6:8]
    sum_ref[2:4] = back_ref[4:6]
    sum_ref[4:8] = back_ref[0:4]
    sum_ref[8:9] = bias_d_ref[...]
    sum_ref[9:10] = column_sum(stage[4][...].astype(F32) * valid * feed)
    for at_x in range(2):
        one = bias_up_ref[:, at_x * width : (at_x + 1) * width]
        two = bias_up_ref[:, (1 - at_x) * width : (2 - at_x) * width]
        here = jnp.where(where_ref[0] == 0, one, two)
        for at_c in range(2):
            at = 10 + 2 * at_x + at_c
            sum_ref[at : at + 1] = jnp.where(where_ref[1] == at_c, here, 0.0)
    sum_ref[14:] = jnp.zeros((2, width), F32)


def unpack_unit(unit, target, first):
    half, lanes = unit.shape
    target[first : first + half] = unit[:, : target.shape[1]]
    target[first + half : first + 2 * half] = pltpu.roll(unit, lanes // 2, 1)[:, : target.shape[1]]


def finish_kernel(where_ref, stage, rows_ref, out_rows_ref, flat):
    mlp_keep, mlp_got, mlp_far, dz_keep, dz_far, last_keep, last_far = (stage[index] for index in range(7))
    down_ref, up_ref, out_ref, vec_ref, qkv_ref = (stage.out(index) for index in range(5))
    size, block = down_ref.shape[0], up_ref.shape[0]
    lanes = up_ref.shape[1]
    mlp = mlp_keep[...].astype(F32) + mlp_got[...].astype(F32) + mlp_far[...].astype(F32)
    dz = dz_keep[...].astype(F32) + dz_far[...].astype(F32)
    up_ref[...] = mlp[size:]
    down_ref[:, :lanes] = dz[:size]
    down_ref[:, lanes:] = mlp[:size]
    stage.put(0, 1)
    out_rows_ref[...] = jnp.zeros_like(out_rows_ref)
    unpack_unit(dz[size : size + size // 2], out_rows_ref, 0)
    out_ref[...] = out_rows_ref[...].T[: out_ref.shape[0], : out_ref.shape[1]]
    sums = dz[size + size // 2 :]
    for row in range(sums.shape[0]):
        flat[:, row * lanes : (row + 1) * lanes] = sums[row : row + 1]
    share = vec_ref.shape[1]
    start = (4 * set_block(where_ref, 0, 0, 0) + own_block(where_ref, 0, 0)) * share
    window = flat[:, pl.ds(pl.multiple_of(start // 128 * 128, 128), 512)]
    window = pltpu.roll(jnp.broadcast_to(window, (8, 512)), (512 - start % 128) % 512, 1)
    vec_ref[...] = window[:1, :share]
    stage.put(2, 3)
    last = last_keep[...].astype(F32) + last_far[...].astype(F32)
    rows_ref[...] = jnp.zeros_like(rows_ref)
    half = last.shape[0] // 3
    for unit in range(3):
        unpack_unit(last[unit * half : (unit + 1) * half], rows_ref, 2 * unit * half)
    qkv_ref[...] = rows_ref[...].T[: qkv_ref.shape[0], : qkv_ref.shape[1]]


def first_norm_grad_kernel(where_ref, stage, vec_ref):
    keep_ref, near_ref, far_ref, own_ref, dmid_ref, raw_ref = (stage[index] for index in range(6))
    unpack_rows(raw_ref, vec_ref)
    dnormed = keep_ref[...].astype(F32) + near_ref[...].astype(F32) + far_ref[...].astype(F32)
    xhat, inverse = standardise(own_ref[...].astype(F32))
    stage.out(0)[...] = (dmid_ref[...] + standardise_grad(vec_ref[0:1] * dnormed, xhat, inverse)).astype(BF)


def swapped(array, axis, bit):
    length = lax.axis_size(axis)
    return lax.ppermute(array, axis, [(i, i ^ bit) for i in range(length)])


def to_core(array):
    return swapped(array, "blk", 1)


def to_x(array):
    return swapped(array, "blk", 2)


def to_y(array):
    return swapped(array, "dp", 1)


def to_z(array):
    return swapped(array, "dp", 2)


def to_zz(array):
    return swapped(array, "dp", 4)


def after(done, *arrays):
    return lax.optimization_barrier((done, *arrays))[1:]


def rows_of(array, lanes):
    return array.reshape(-1, lanes)


def added(*terms):
    total = terms[0].astype(F32)
    for term in terms[1:]:
        total = total + term.astype(F32)
    return total


def first_rows(count):
    def cut(where_ref, source, target):
        return [(source.at[:count], target)]

    return cut


def first_block(where_ref, source, target):
    return [(source.at[0], target)]


def own_columns(first):
    def cut(where_ref, source, target):
        half = source.shape[0] // 2
        return [
            (source.at[:, lanes_at(where_ref[1] + 2 * part, half)], target.at[:, (part - first) * half : (part - first + 1) * half])
            for part in range(first, 3)
        ]

    return cut


def own_hidden(axis):
    def cut(where_ref, source, target):
        pairs = []
        piece = target.shape[axis] // 4
        for rel_x in range(2):
            for side in range(2):
                at = lanes_at(hidden_unit(where_ref, rel_x, side), piece)
                to = slice((2 * rel_x + side) * piece, (2 * rel_x + side + 1) * piece)
                pairs.append((source.at[at], target.at[to]) if axis == 0 else (source.at[:, at], target.at[:, to]))
        return pairs

    return cut


def both_head_rows(where_ref, source, target):
    half = target.shape[0] // 2
    return [
        (source.at[lanes_at(where_ref[1], half), :], target.at[:half]),
        (source.at[lanes_at(1 - where_ref[1], half), :], target.at[half:]),
    ]


def own_head_rows(where_ref, source, target):
    return [(source.at[lanes_at(where_ref[1], target.shape[0]), :], target)]


def on_device_aligned(tokens, lengths, w_qkv, w_out, w_up, w_down, vectors, cotangent):
    tokens, cotangent = tokens[0], cotangent[0]
    rows, width = tokens.shape
    hidden = w_up.shape[1]
    items = lengths.shape[1]
    parts = lax.axis_size("blk")
    sets = lax.axis_size("dp")
    position, turn = lax.axis_index("blk"), lax.axis_index("dp")
    x, core, z, y = position // 2, position % 2, turn // 2, turn % 2
    where = lengths
    half = width // 2
    inner = hidden // 2
    piece = hidden // sets
    both = 2 * rows
    total_rows = parts * rows
    block = width // parts
    share = width // sets
    names = (parts, items)
    zs = sets // 2
    all_columns = ((width, 3 * half), 3, own_columns(0))
    kv_columns = ((width, 2 * half), 2, own_columns(1))
    up_columns = ((width, inner), 4, own_hidden(1))
    down_rows = ((inner, width), 4, own_hidden(0))
    head_rows = ((half, width), 1, own_head_rows)
    out_rows = ((width, width), 2, both_head_rows)

    far_a = to_x(tokens)
    sib = to_core(tokens)
    cot_sib = to_core(cotangent)

    vec = vectors.reshape(-1, 128)
    rows_of_vec = pltpu.VMEM((10, width), F32)

    xhat_near, qkv_near, dact, dfeed_turned, bias_d_sum = staged_call(
        functools.partial(prepare_kernel, *names),
        where,
        (tokens, sib, vec, w_qkv, cotangent, cot_sib, w_down),
        [low(both, width), low(both, 3 * half), low(both, inner), low(width, both), full(1, width)],
        cuts={3: all_columns, 6: down_rows},
        scratch=[rows_of_vec, pltpu.VMEM((both, width), BF), pltpu.VMEM((both, width), BF), pltpu.VMEM((2, 3 * half), F32)],
    )

    far_a, qkv_near, dact = lax.optimization_barrier((far_a, qkv_near, dact))
    far_b = to_core(far_a)

    xhat_far, kv, attended, logsum = staged_call(
        functools.partial(attend_kernel, *names),
        where,
        (far_a, far_b, vec, w_qkv, qkv_near),
        [low(both, width), low(total_rows, width), low(both, half), full(half // (2 * HEAD_SIZE), rows // TILE, 4 * TILE)],
        cuts={3: kv_columns},
        scratch=[
            rows_of_vec,
            pltpu.VMEM((total_rows, 2 * half), BF),
            pltpu.VMEM((both, width), BF),
            pltpu.VMEM((rows // TILE, 2 * TILE, 2 * TILE), jnp.int32),
        ],
    )
    attended_sib = to_core(attended)

    unit_rows = share // 2
    py, dz = low(2, 2 * share + 2 * block, piece), low(2, 2, 2, share, piece)
    (py_keep, py_send, ux_keep, ux_send, dz_keep, dz_send, xhat_two, inverse_two, mid, branch, swap, feed_keep,
     bias_up_sum) = staged_call(
        mlp_kernel,
        where,
        (attended, attended_sib, tokens, sib, vec, w_out, w_up, dact, dfeed_turned, w_down),
        [py, py, py, py, dz, dz, low(both, width), full(both, 1), full(rows, width), low(rows, width), low(both + rows, width),
         full(rows, width), full(1, inner)],
        cuts={5: out_rows, 6: up_columns, 9: down_rows},
        late=(6, 7, 8, 9),
        pairs=(0, 2, 4),
        scratch=[rows_of_vec, pltpu.VMEM((sets, piece), F32), pltpu.VMEM((both, width), F32),
                 pltpu.VMEM((both, width), BF), pltpu.VMEM((both, width), BF), pltpu.VMEM((width, 2 * piece), BF),
                 pltpu.VMEM((width, both), BF), pltpu.VMEM((both, inner), BF), pltpu.VMEM((both, inner), BF)],
    )
    swap_got = to_core(swap)
    py_got = to_y(py_send)
    ux_got = to_x(ux_send)
    dz_got = to_z(dz_send)

    dmid, a_keep, a_send, b_both, o_keep, o_send, dtok_own, dtok_far, dtok_send, out, sums = staged_call(
        functools.partial(backward_kernel, *names),
        where,
        (swap, swap_got, xhat_two, inverse_two, cotangent, cot_sib, vec, attended, attended_sib, w_out, branch,
         qkv_near, kv, logsum, xhat_near, xhat_far, w_qkv, feed_keep, mid, bias_d_sum, bias_up_sum),
        [full(rows, width)] + [low(2, 6, unit_rows, half)] * 2 + [low(2, 2, 6, unit_rows, half)] + [low(2, 2, 2, unit_rows, half)] * 2
        + [low(rows, width), low(rows, width), low(2, rows, width), low(rows, width), full(16, width)],
        cuts={0: ((both, width), 1, first_rows(both)), 9: head_rows, 16: all_columns},
        late=tuple(range(7, 21)),
        pairs=(1, 4),
        tables=True,
        scratch=[rows_of_vec, pltpu.VMEM((8, width), F32), pltpu.VMEM((both, half), BF), pltpu.VMEM((both, width), BF),
                 pltpu.VMEM((both, half), BF), pltpu.VMEM((2, sets, unit_rows, half), BF), pltpu.VMEM((both, half), BF),
                 pltpu.VMEM((total_rows, half), BF), pltpu.VMEM((total_rows, half), BF),
                 pltpu.VMEM((total_rows, width), BF), pltpu.VMEM((4, 12, unit_rows, half), BF),
                 pltpu.VMEM((rows // TILE, 4 * TILE), jnp.int32), pltpu.VMEM((total_rows, 2 * TILE), jnp.int32),
                 pltpu.VMEM((half, total_rows), BF), pltpu.VMEM((total_rows, 2 * HEAD_SIZE), F32),
                 pltpu.VMEM((total_rows, 2 * HEAD_SIZE), F32),
                 pltpu.VMEM((rows // TILE, 2 * HEAD_SIZE, 4 * TILE), F32)],
    )
    def stacked(*parts):
        return jnp.concatenate([rows_of(part.astype(BF), half) for part in parts], axis=0)

    def stacked(*parts):
        return jnp.concatenate([rows_of(part.astype(BF), half) for part in parts], axis=0)

    b_both = to_core(b_both)
    sums_got = to_core(sums)
    dtok_got = to_core(dtok_send)
    two, four, six = 2 * share, 4 * share, 6 * unit_rows

    dz_got, py_got, ux_got = after(sums, dz_got, py_got, ux_got)
    x_step = stacked(a_send, added(py_keep[1], py_got[1]))
    x_got = to_x(x_step)
    (b_both,) = after(x_step, b_both)
    b_keep = b_both[0]
    y_step = stacked(added(ux_keep[1], ux_got[1]), b_both[1])
    y_got = to_y(y_step)
    (dz_got,) = after(y_step, dz_got)
    dz_step = added(dz_keep[1], dz_got[1]).astype(BF)
    dz_far = to_zz(dz_step)
    (sums_got,) = after(dz_step, sums_got)
    sums = rows_of(added(sums, sums_got), half)
    o_step = stacked(o_send, sums)
    o_got = to_z(o_step)

    x_got, y_got, dz_far, o_got, dtok_got = lax.optimization_barrier((x_got, y_got, dz_far, o_got, dtok_got))
    a_got, py_far = x_got[: 2 * six].reshape(a_keep.shape), x_got[2 * six :]
    count = ux_keep.shape[1]
    ux_far, b_got = y_got[:count], y_got[count:].reshape(b_keep.shape)

    up_step = added(ux_keep[0, two:], ux_got[0, two:], ux_far[two:]).astype(BF)
    up_sib = to_core(up_step)
    b_got, o_got = after(up_step, b_got, o_got)
    b_step = added(b_keep[1], b_got[1]).astype(BF)
    b_far = to_x(b_step)
    (a_got,) = after(b_step, a_got)
    a_step = added(a_keep[1], a_got[1]).astype(BF)
    a_far = to_y(a_step)
    same = z % 2 == core

    def mlp_part(side):
        rest = [
            added(*(term[side * share : (side + 1) * share] for term in terms)).reshape(2, share // 2, piece)
            for terms in ((ux_keep[0], ux_got[0], ux_far), (py_keep[0], py_got[0], py_far))
        ]
        up_own = added(py_keep[0, two:], py_got[0, two:], py_far[two:]).reshape(2, block, piece)
        sib = up_sib.reshape(2, block, piece).astype(F32)
        up = jnp.where(same, sib, up_own) if side else jnp.where(same, up_own, sib)
        return jnp.concatenate([*rest, up], axis=1).astype(BF)

    py_far, up_sib = after(a_step, py_far, up_sib)
    mlp_send = mlp_part(1)
    mlp_got = to_z(mlp_send)
    (o_got,) = after(mlp_send, o_got)
    sums = added(sums, o_got[four:])
    o_sum = added(o_keep, o_got[:four].reshape(o_keep.shape)).astype(BF)
    o_step = stacked(o_sum[1], sums)
    o_far = to_zz(o_step)
    (up_sib,) = after(o_step, up_sib)
    mlp_keep = mlp_part(0)
    a_far, b_far, mlp_got, o_far, mlp_keep = lax.optimization_barrier((a_far, b_far, mlp_got, o_far, mlp_keep))

    mlp_step = added(mlp_keep[1], mlp_got[1]).astype(BF)
    mlp_far = to_zz(mlp_step)
    a_far, b_far = after(mlp_step, a_far, b_far)
    one = added(a_keep[0], a_got[0], a_far).astype(BF)
    other = added(b_keep[0], b_got[0], b_far).astype(BF)
    last_send = stacked(one[3:], other[3:])
    last_got = to_z(last_send)
    (o_far,) = after(last_send, o_far)
    dz_low = added(dz_keep[0], dz_got[0], dz_far).astype(BF)
    o_low = added(o_sum[0], o_far[:two].reshape(2, 2, unit_rows, half)).astype(BF)
    sums = added(sums, o_far[two:])
    dz_step = stacked(dz_low[1], o_low[1], sums)
    dz_x = to_x(dz_step)
    (dtok_got,) = after(dz_step, dtok_got)
    dtok_step = added(dtok_far, dtok_got[1]).astype(BF)
    dtok_x = to_x(dtok_step)
    last_got, dz_x = after(dtok_step, last_got, dz_x)

    last = added(stacked(one[:3], other[:3]), last_got).astype(BF).reshape(6, unit_rows, half)

    def chosen(owner_z):
        here = (core * 2 + y) * zs + owner_z
        units = []
        for index in range(3):
            at = jnp.int32(0)
            for code, place in enumerate(UNIT_PLACE[..., index].reshape(-1)):
                at = jnp.where(here == code, int(place), at)
            units.append(lax.dynamic_slice_in_dim(last, at, 1, 0))
        return jnp.concatenate(units, axis=0)

    last_step = rows_of(chosen(z ^ 2), half)
    last_keep = rows_of(chosen(z), half)
    last_far = to_zz(last_step)

    (dz_x,) = after(last_step, dz_x)
    dz_low = added(dz_low[0], dz_x[:two].reshape(2, share, piece))
    o_low = added(o_low[0], dz_x[two : two + share].reshape(2, unit_rows, half))
    sums = added(sums, dz_x[two + share :])
    dz_step = stacked(dz_low[1], o_low[1], sums)
    dz_kept = stacked(dz_low[0], o_low[0], sums)
    dz_y = to_y(dz_step)

    (dtok_x,) = after(dz_step, dtok_x)
    (grad_tokens,) = staged_call(
        first_norm_grad_kernel,
        where,
        (dtok_own, dtok_got, dtok_x, tokens, dmid, vec),
        [low(rows, width)],
        cuts={1: ((rows, width), 1, first_block)},
        scratch=[rows_of_vec],
    )

    mlp_far, dz_y, last_far = after(grad_tokens, mlp_far, dz_y, last_far)
    g_w_down, g_w_up, g_w_out, g_vec, g_w_qkv = staged_call(
        finish_kernel,
        where,
        (mlp_keep, mlp_got, mlp_far, dz_kept, dz_y, last_keep, last_far),
        [full(share, 2 * piece), full(block, piece), full(block, share), full(1, vectors.shape[0] // (sets * parts)),
         full(block, 3 * share)],
        cuts={index: ((share + block, piece), 1, first_block) for index in range(2)},
        scratch=[pltpu.VMEM((384, 256), F32), pltpu.VMEM((128, 256), F32), pltpu.VMEM((1, 16 * width + 512), F32)],
    )
    return (out[None], grad_tokens[None], g_w_qkv, g_w_out, g_w_up, g_w_down.T, g_vec.reshape(-1))


def is_aligned(mesh, tokens, w_up):
    parts, sets = mesh.shape["blk"], mesh.shape["dp"]
    width, hidden = w_up.shape
    rows = tokens.shape[1] // parts
    return (
        parts == 4
        and sets == 2 * parts
        and rows == 4 * TILE
        and (hidden // sets) % 128 == 0
        and (width // 2) % 128 == 0
        and (width // sets) % 32 == 0
        and width == H * HEAD_SIZE
    )


def solution(mesh):
    def run(tokens, lengths, w_qkv, w_out, w_up, w_down, vectors, cotangent):
        body = on_device_aligned if is_aligned(mesh, tokens, w_up) else on_device
        return jax.shard_map(
            body,
            mesh=mesh,
            in_specs=(
                P("dp", "blk", None),
                P("dp", None),
                P(),
                P(),
                P(),
                P(),
                P(),
                P("dp", "blk", None),
            ),
            out_specs=(
                P("dp", "blk", None),
                P("dp", "blk", None),
                P("blk", "dp"),
                P("blk", "dp"),
                P("blk", "dp"),
                P("blk", "dp"),
                P(("dp", "blk")),
            ),
            check_vma=False,
        )(tokens, lengths, w_qkv, w_out, w_up, w_down, vectors, cotangent)

    return run
```

```python
import functools
import math

import jax
import jax.numpy as jnp
import numpy as np
from jax import lax
from jax.experimental import pallas as pl
from jax.experimental.pallas import tpu as pltpu
from jax.sharding import PartitionSpec as P

H = 12
HEAD_SIZE = 64
TILE = 64


EPSILON = 1e-06
FLOOR_SCORE = -1e30


def passed_along(array, axis, by):
    length = lax.axis_size(axis)
    return lax.ppermute(array, axis, [(i, (i + by) % length) for i in range(length)])


def norm_rows(values, gain, shift):
    centre = jnp.mean(values, axis=-1, keepdims=True)
    centred = values - centre
    spread = jnp.mean(centred * centred, axis=-1, keepdims=True)
    return centred * lax.rsqrt(spread + EPSILON) * gain + shift


def exact_gelu(values):
    return jax.nn.gelu(values, approximate=False)


def segment_of(rows_index, rows, parts, ends):
    place = rows_index % rows * parts + rows_index // rows
    return jnp.sum((place[:, None] >= ends[None, :]).astype(jnp.int32), axis=1)


def contract_rows(left, right):
    return lax.dot_general(
        left, right, (((0,), (0,)), ((), ())), preferred_element_type=jnp.float32
    )


def contract_cols(left, right):
    return lax.dot_general(
        left, right, (((1,), (1,)), ((), ())), preferred_element_type=jnp.float32
    )


def attend_block(query, query_item, keys, values, key_item, scale, carry):
    best, total, weighted = carry
    count = keys.shape[0]
    heads = query.shape[1]
    key_heads = keys.reshape(count, heads, -1)
    value_heads = values.reshape(count, heads, -1)
    allowed = (query_item[:, None] == key_item[None, :])[None]
    score = jnp.einsum("qhd,khd->hqk", query, key_heads, preferred_element_type=jnp.float32) * scale
    score = jnp.where(allowed, score, FLOOR_SCORE)
    newbest = jnp.maximum(best, jnp.max(score, axis=-1))
    weight = jnp.where(allowed, jnp.exp(score - newbest[..., None]), 0.0)
    factor = jnp.exp(best - newbest)
    total = total * factor + jnp.sum(weight, axis=-1)
    weighted = weighted * factor[..., None] + jnp.einsum(
        "hqk,khd->hqd", weight.astype(jnp.bfloat16), value_heads, preferred_element_type=jnp.float32
    )
    return (newbest, total, weighted)


def grad_block(query, d_out, logsum, delta, query_item, keys, values, key_item, scale):
    count = keys.shape[0]
    heads = query.shape[1]
    key_heads = keys.reshape(count, heads, -1)
    value_heads = values.reshape(count, heads, -1)
    allowed = (query_item[:, None] == key_item[None, :])[None]
    score = jnp.einsum("qhd,khd->hqk", query, key_heads, preferred_element_type=jnp.float32) * scale
    prob = jnp.where(allowed, jnp.exp(score - logsum[..., None]), 0.0)
    d_prob = jnp.einsum("qhd,khd->hqk", d_out, value_heads, preferred_element_type=jnp.float32)
    d_score = (prob * (d_prob - delta[..., None])).astype(jnp.bfloat16)
    d_query = (
        jnp.einsum("hqk,khd->qhd", d_score, key_heads, preferred_element_type=jnp.float32) * scale
    )
    d_keys = jnp.einsum("hqk,qhd->khd", d_score, query, preferred_element_type=jnp.float32) * scale
    d_values = jnp.einsum(
        "hqk,qhd->khd", prob.astype(jnp.bfloat16), d_out, preferred_element_type=jnp.float32
    )
    return (d_query, d_keys.reshape(count, -1), d_values.reshape(count, -1))


def on_device(tokens, lengths, w_qkv, w_out, w_up, w_down, vectors, cotangent):
    inputs = tokens[0].astype(jnp.float32)
    rows, width = inputs.shape
    heads = H
    head_size = width // heads
    scale = head_size ** (-0.5)
    items = lengths.shape[1]
    ends = jnp.cumsum(lengths[0])
    parts = lax.axis_size("blk")
    position = lax.axis_index("blk")
    query_item = segment_of(position * rows + lax.iota(jnp.int32, rows), rows, parts, ends)
    valid = (query_item < items).astype(jnp.float32)[:, None]
    pieces = [vectors[index * width : (index + 1) * width] for index in range(10)]
    (
        gain_one,
        shift_one,
        bias_q,
        bias_v,
        bias_o,
        scale_one,
        gain_two,
        shift_two,
        bias_d,
        scale_two,
    ) = pieces
    bias_up = vectors[10 * width :]
    normed, norm_one_pull = jax.vjp(norm_rows, inputs, gain_one, shift_one)
    normed_low = normed.astype(jnp.bfloat16)
    qkv_bias = jnp.concatenate([bias_q, jnp.zeros_like(bias_q), bias_v])
    projected = (jnp.dot(normed_low, w_qkv, preferred_element_type=jnp.float32) + qkv_bias).astype(
        jnp.bfloat16
    )
    query = projected[:, :width].reshape(rows, heads, head_size)
    keys = projected[:, width : 2 * width]
    values = projected[:, 2 * width :]
    start_state = (
        jnp.full((heads, rows), FLOOR_SCORE, jnp.float32),
        jnp.zeros((heads, rows), jnp.float32),
        jnp.zeros((heads, rows, head_size), jnp.float32),
    )
    carry = start_state
    piece = (
        lax.all_gather(keys, "blk", axis=0, tiled=True),
        lax.all_gather(values, "blk", axis=0, tiled=True),
    )
    count = piece[0].shape[0]
    size = math.gcd(count, 512)
    steps = count // size
    key_blocks = piece[0].reshape(steps, size, width)
    value_blocks = piece[1].reshape(steps, size, width)

    def inner(state, item):
        block_keys, block_values, offset = item
        key_item = segment_of(offset + lax.iota(jnp.int32, size), rows, parts, ends)
        return (
            attend_block(query, query_item, block_keys, block_values, key_item, scale, state),
            None,
        )

    carry, unused = lax.scan(
        inner, carry, (key_blocks, value_blocks, lax.iota(jnp.int32, steps) * size)
    )
    best, total, weighted = carry
    logsum = best + jnp.log(total)
    attended = (weighted / total[..., None]).transpose(1, 0, 2).reshape(rows, width)
    attended_low = attended.astype(jnp.bfloat16)
    branch = jnp.dot(attended_low, w_out, preferred_element_type=jnp.float32) + bias_o
    mid = inputs + scale_one * branch
    normed_two, norm_two_pull = jax.vjp(norm_rows, mid, gain_two, shift_two)
    normed_two_low = normed_two.astype(jnp.bfloat16)
    before = jnp.dot(normed_two_low, w_up, preferred_element_type=jnp.float32) + bias_up
    activated, gelu_pull = jax.vjp(exact_gelu, before)
    activated_low = activated.astype(jnp.bfloat16)
    feed = jnp.dot(activated_low, w_down, preferred_element_type=jnp.float32) + bias_d
    result = mid + scale_two * feed
    out = (result * valid).astype(jnp.bfloat16)
    d_result = cotangent[0].astype(jnp.float32) * valid
    d_feed = (scale_two * d_result).astype(jnp.bfloat16)
    g_scale_two = jnp.sum(d_result * feed, axis=0)
    g_bias_d = jnp.sum(d_feed.astype(jnp.float32), axis=0)
    g_w_down = contract_rows(activated_low, d_feed)
    d_activated = contract_cols(d_feed, w_down)
    d_before = gelu_pull(d_activated)[0].astype(jnp.bfloat16)
    g_bias_up = jnp.sum(d_before.astype(jnp.float32), axis=0)
    g_w_up = contract_rows(normed_two_low, d_before)
    d_normed_two = contract_cols(d_before, w_up)
    d_mid_norm, g_gain_two, g_shift_two = norm_two_pull(d_normed_two)
    d_mid = d_result + d_mid_norm
    d_branch = (scale_one * d_mid).astype(jnp.bfloat16)
    g_scale_one = jnp.sum(d_mid * branch, axis=0)
    g_bias_o = jnp.sum(d_branch.astype(jnp.float32), axis=0)
    g_w_out = contract_rows(attended_low, d_branch)
    d_attended = contract_cols(d_branch, w_out).astype(jnp.bfloat16)
    d_heads = d_attended.reshape(rows, heads, head_size)
    delta = jnp.sum(
        (d_attended.astype(jnp.float32) * attended).reshape(rows, heads, head_size), axis=-1
    ).T
    zero_query = jnp.zeros((rows, heads, head_size), jnp.float32)

    def visit_block(block_keys, block_values, owner):
        key_item = segment_of(owner * rows + lax.iota(jnp.int32, rows), rows, parts, ends)
        return grad_block(
            query, d_heads, logsum, delta, query_item, block_keys, block_values, key_item, scale
        )

    def send_back(d_keys, d_values):
        return (
            passed_along(d_keys.astype(jnp.bfloat16), "blk", 1).astype(d_keys.dtype),
            passed_along(d_values.astype(jnp.bfloat16), "blk", 1).astype(d_values.dtype),
        )

    def accumulate(state, owner):
        d_query, block_keys, block_values, d_keys, d_values = state
        dq_part, dk_part, dv_part = visit_block(block_keys, block_values, owner)
        d_keys, d_values = send_back(d_keys + dk_part, d_values + dv_part)
        return (d_query + dq_part, d_keys, d_values)

    def turn(step, state):
        owner = (position - step) % parts
        d_query, d_keys, d_values = accumulate(state, owner)
        block_keys, block_values = passed_along((state[1], state[2]), "blk", 1)
        return (d_query, block_keys, block_values, d_keys, d_values)

    zero_rows = jnp.zeros((rows, width), jnp.float32)
    state = lax.fori_loop(0, parts - 1, turn, (zero_query, keys, values, zero_rows, zero_rows))
    d_query, d_keys, d_values = accumulate(state, (position + 1) % parts)
    d_projected = jnp.concatenate([d_query.reshape(rows, width), d_keys, d_values], axis=1).astype(
        jnp.bfloat16
    )
    g_bias_q = jnp.sum(d_projected[:, :width].astype(jnp.float32), axis=0)
    g_bias_v = jnp.sum(d_projected[:, 2 * width :].astype(jnp.float32), axis=0)
    g_w_qkv = contract_rows(normed_low, d_projected)
    d_normed = contract_cols(d_projected, w_qkv)
    d_input_norm, g_gain_one, g_shift_one = norm_one_pull(d_normed)
    d_inputs = d_mid + d_input_norm
    g_vectors = jnp.concatenate(
        [
            g_gain_one,
            g_shift_one,
            g_bias_q,
            g_bias_v,
            g_bias_o,
            g_scale_one,
            g_gain_two,
            g_shift_two,
            g_bias_d,
            g_scale_two,
            g_bias_up,
        ]
    )
    column_sums = (
        lax.psum_scatter(
            g_w_qkv.astype(jnp.bfloat16), "dp", scatter_dimension=1, tiled=True
        ).astype(jnp.float32),
        lax.psum_scatter(
            g_w_out.astype(jnp.bfloat16), "dp", scatter_dimension=1, tiled=True
        ).astype(jnp.float32),
        lax.psum_scatter(g_w_up.astype(jnp.bfloat16), "dp", scatter_dimension=1, tiled=True).astype(
            jnp.float32
        ),
        lax.psum_scatter(
            g_w_down.astype(jnp.bfloat16), "dp", scatter_dimension=1, tiled=True
        ).astype(jnp.float32),
        lax.psum_scatter(
            g_vectors.astype(jnp.bfloat16), "dp", scatter_dimension=0, tiled=True
        ).astype(jnp.float32),
    )
    g_w_qkv, g_w_out, g_w_up, g_w_down, g_vectors = (
        lax.psum_scatter(
            column_sums[0].astype(jnp.bfloat16), "blk", scatter_dimension=0, tiled=True
        ).astype(jnp.float32),
        lax.psum_scatter(
            column_sums[1].astype(jnp.bfloat16), "blk", scatter_dimension=0, tiled=True
        ).astype(jnp.float32),
        lax.psum_scatter(
            column_sums[2].astype(jnp.bfloat16), "blk", scatter_dimension=0, tiled=True
        ).astype(jnp.float32),
        lax.psum_scatter(
            column_sums[3].astype(jnp.bfloat16), "blk", scatter_dimension=0, tiled=True
        ).astype(jnp.float32),
        lax.psum_scatter(
            column_sums[4].astype(jnp.bfloat16), "blk", scatter_dimension=0, tiled=True
        ).astype(jnp.float32),
    )
    return (
        out[None],
        d_inputs.astype(jnp.bfloat16)[None],
        g_w_qkv,
        g_w_out,
        g_w_up,
        g_w_down,
        g_vectors,
    )


BF = jnp.bfloat16
F32 = jnp.float32
MASKED = -1e30
GRANT = 60 * 1024 * 1024
STEP_GRANT = 20 * 1024 * 1024
WIDE_CHUNK = 128


def unit_tables():
    lists, places = np.zeros((2, 2, 2, 6), np.int32), np.zeros((2, 2, 4, 3), np.int32)
    units = {core: [unit for unit in range(24) if unit // 4 % 2 == core] for core in range(2)}
    for y in range(2):
        for low_z in range(2):
            first = {}
            for core in range(2):
                own = [unit for unit in units[core] if unit // 3 % 2 == y]
                first[core] = [unit for unit in own if unit // 6 % 2 == low_z]
                rest = [unit for unit in own if unit // 6 % 2 != low_z]
                lists[core, y, low_z] = [units[core].index(unit) for unit in first[core] + rest]
            for core in range(2):
                held = first[core] + first[1 - core]
                for z in (low_z, low_z + 2):
                    places[core, y, z] = [held.index(3 * (2 * z + y) + index) for index in range(3)]
    return np.concatenate([lists.reshape(-1), places.reshape(-1)])


UNIT_TABLE = unit_tables()
UNIT_LIST = 4
ENDS = UNIT_LIST + UNIT_TABLE.size


def dot_nn(left, right):
    return lax.dot_general(left, right, (((1,), (0,)), ((), ())), preferred_element_type=F32)


def dot_nt(left, right):
    return lax.dot_general(left, right, (((1,), (1,)), ((), ())), preferred_element_type=F32)


def dot_tn(left, right):
    return lax.dot_general(left, right, (((0,), (0,)), ((), ())), preferred_element_type=F32)


def standardise(values):
    centred = values - jnp.mean(values, axis=-1, keepdims=True)
    inverse = lax.rsqrt(jnp.mean(centred * centred, axis=-1, keepdims=True) + EPSILON)
    return centred * inverse, inverse


def standardise_grad(grad, xhat, inverse):
    first = jnp.mean(grad, axis=-1, keepdims=True)
    second = jnp.mean(grad * xhat, axis=-1, keepdims=True)
    return (grad - first - xhat * second) * inverse


def column_sum(values):
    return jnp.sum(values, axis=0, keepdims=True)


def item_at(place, where_ref, items):
    found = jnp.zeros_like(place)
    for index in range(items):
        found = found + (place >= where_ref[ENDS + index]).astype(jnp.int32)
    return found


def own_block(where_ref, rel_x, rel_c):
    return 2 * (where_ref[0] ^ rel_x) + (where_ref[1] ^ rel_c)


def low(*shape):
    return jax.ShapeDtypeStruct(shape, BF)


def full(*shape):
    return jax.ShapeDtypeStruct(shape, F32)


def lanes_at(index, size):
    return pl.ds(pl.multiple_of(index * size, size), size)


class Stage:
    def __init__(self, reads, places, writes):
        self.reads, self.places, self.writes = reads, places, writes
        self.started, self.waited, self.begun = set(), set(), []

    def start(self, *indices):
        for index in indices:
            if index not in self.started:
                self.started.add(index)
                for copy in self.reads[index]:
                    copy.start()

    def __getitem__(self, index):
        self.start(index)
        if index not in self.waited:
            self.waited.add(index)
            for copy in self.reads[index]:
                copy.wait()
        return self.places[index]

    def out(self, index):
        return self.writes[index][0]

    def put(self, *indices):
        for index in indices:
            self.writes[index][1].start()
            self.begun.append(index)

    def finish(self):
        for index in range(len(self.reads)):
            self[index]
        self.put(*(index for index in range(len(self.writes)) if index not in self.begun))
        for place, copy in self.writes:
            copy.wait()


class Place:
    def __init__(self, lengths_ref, table_ref):
        position, turn = lax.axis_index("blk"), lax.axis_index("dp")
        self.four = (position // 2, position % 2, turn // 2, turn % 2)
        self.table_ref = table_ref
        self.ends, end = [], jnp.int32(0)
        for index in range(lengths_ref.shape[1]):
            end = end + lengths_ref[0, index]
            self.ends.append(end)

    def __getitem__(self, index):
        if isinstance(index, int) and index < UNIT_LIST:
            return self.four[index]
        if isinstance(index, int) and index >= ENDS:
            return self.ends[index - ENDS]
        return self.table_ref[index - UNIT_LIST]


def unpack_rows(raw_ref, vec_ref):
    count = vec_ref.shape[1] // 128
    for row in range(vec_ref.shape[0]):
        for part in range(count):
            vec_ref[row : row + 1, part * 128 : (part + 1) * 128] = raw_ref[row * count + part : row * count + part + 1]


def staged_call(body, where, operands, out_shape, cuts=None, scratch=(), late=(), pairs=(), tables=False, grant=GRANT):
    cuts = cuts or {}
    count, results = len(operands), len(out_shape)
    shapes, parts = [], []
    for index, operand in enumerate(operands):
        shape, pieces = (operand.shape, 1) if index not in cuts else cuts[index][:2]
        shapes.append(pltpu.VMEM(shape, operand.dtype))
        parts.append(pieces)
    held_shapes, held_at = [], {}
    for index, item in enumerate(out_shape):
        if index - 1 in pairs:
            held_at[index] = (len(held_shapes) - 1, 1)
        elif index in pairs:
            held_at[index] = (len(held_shapes), 0)
            held_shapes.append(pltpu.VMEM((2, *item.shape), item.dtype))
        else:
            held_at[index] = (len(held_shapes), None)
            held_shapes.append(pltpu.VMEM(item.shape, item.dtype))

    def kernel(*refs):
        where_ref = Place(refs[0], refs[1] if tables else None)
        refs = refs[2 if tables else 1 :]
        ins, outs = refs[:count], refs[count : count + results]
        places = refs[count + results : 2 * count + results]
        held = refs[2 * count + results : 2 * count + results + len(held_shapes)]
        read_sem, write_sem, *rest = refs[2 * count + results + len(held_shapes) :]
        reads, used = [], 0
        for index in range(count):
            moves = [(ins[index], places[index])] if index not in cuts else cuts[index][2](where_ref, ins[index], places[index])
            reads.append([])
            for source, target in moves:
                reads[-1].append(pltpu.make_async_copy(source, target, read_sem.at[used]))
                used += 1
        writes = []
        for index in range(results):
            place, entry = held_at[index]
            source = held[place] if entry is None else held[place].at[entry]
            writes.append((held[place], pltpu.make_async_copy(source, outs[index], write_sem.at[index])))
        stage = Stage(reads, places, writes)
        stage.start(*(index for index in range(count) if index not in late))
        body(where_ref, stage, *rest)
        stage.finish()

    return pl.pallas_call(
        kernel,
        in_specs=[pl.BlockSpec(memory_space=pltpu.SMEM)] * (2 if tables else 1)
        + [pl.BlockSpec(memory_space=pl.ANY)] * count,
        out_specs=[pl.BlockSpec(memory_space=pl.ANY)] * results,
        out_shape=out_shape,
        scratch_shapes=shapes
        + held_shapes
        + [pltpu.SemaphoreType.DMA((sum(parts),)), pltpu.SemaphoreType.DMA((results,))]
        + list(scratch),
        compiler_params=pltpu.CompilerParams(vmem_limit_bytes=grant),
    )(where, *((UNIT_TABLE,) if tables else ()), *operands)


def each(count, body):
    def step(index, carry):
        body(index)
        return carry

    lax.fori_loop(0, count, step, 0)


def hidden_unit(where_ref, rel_x, side):
    return 4 * (where_ref[0] ^ rel_x) + 2 * where_ref[1] + side


def lanes_below(shape, count):
    return lax.broadcasted_iota(jnp.int32, shape, 1) < count


def stack_heads(pair):
    first = lanes_below(pair.shape, HEAD_SIZE)
    zero = jnp.zeros_like(pair)
    return jnp.concatenate([jnp.where(first, pair, zero), jnp.where(first, zero, pair)], axis=0)


def turn(source, target):
    each(source.shape[1] // 128, lambda index: target.__setitem__(lanes_at(index, 128), source[:, lanes_at(index, 128)].T))


def valid_at(where_ref, rel_c, first, count, parts, items):
    row = first + lax.broadcasted_iota(jnp.int32, (count, 1), 0)
    item = item_at(row * parts + own_block(where_ref, 0, rel_c), where_ref, items)
    return (item < items).astype(F32)


def normed_rows(xhat, vec_ref, first):
    return (xhat.astype(F32) * vec_ref[first : first + 1] + vec_ref[first + 1 : first + 2]).astype(BF)


def prepare_kernel(parts, items, where_ref, stage, vec_ref, held, normed_ref, row_ref):
    unpack_rows(stage[2], vec_ref)
    own_ref, sib_ref = stage[0], stage[1]
    stage.start(3, 4, 5, 6)
    xhat_ref, qkv_ref, dact_ref, turned_ref, sum_ref = (stage.out(index) for index in range(5))
    rows, width = own_ref.shape
    half = width // 2
    core = where_ref[1]
    for rel_c, ref in enumerate((own_ref, sib_ref)):

        def norm(index, rel_c=rel_c, ref=ref):
            xhat, unused = standardise(ref[lanes_at(index, WIDE_CHUNK)].astype(F32))
            to = lanes_at(index + rel_c * (rows // WIDE_CHUNK), WIDE_CHUNK)
            xhat_ref[to] = xhat.astype(BF)
            normed_ref[to] = (xhat * vec_ref[0:1] + vec_ref[1:2]).astype(BF)

        each(rows // WIDE_CHUNK, norm)
    stage.put(0)
    sum_ref[...] = jnp.zeros_like(sum_ref)
    for rel_c in range(2):

        def grad(index, rel_c=rel_c, ref=stage[4 + rel_c]):
            valid = valid_at(where_ref, rel_c, index * WIDE_CHUNK, WIDE_CHUNK, parts, items)
            part = (vec_ref[9:10] * (ref[lanes_at(index, WIDE_CHUNK)].astype(F32) * valid)).astype(BF)
            held[lanes_at(index + rel_c * (rows // WIDE_CHUNK), WIDE_CHUNK)] = part
            if rel_c == 0:
                sum_ref[...] += column_sum(part.astype(F32))

        each(rows // WIDE_CHUNK, grad)
    turn(held, turned_ref)
    stage.put(3, 4)
    row_ref[0:1, :half] = vec_ref[2:3, lanes_at(core, half)]
    row_ref[0:1, half : 2 * half] = jnp.zeros((1, half), F32)
    row_ref[0:1, 2 * half :] = vec_ref[3:4, lanes_at(core, half)]
    row_ref[1:2, :half] = jnp.full((1, half), HEAD_SIZE ** (-0.5), F32)
    row_ref[1:2, half:] = jnp.ones((1, 2 * half), F32)
    weight_ref = stage[3]

    def project(index):
        lanes = lanes_at(index, half)
        part = dot_nn(normed_ref[...], weight_ref[:, lanes]) + row_ref[0:1, lanes]
        qkv_ref[:, lanes] = (part.astype(BF).astype(F32) * row_ref[1:2, lanes]).astype(BF)

    each(3, project)
    stage.put(1)
    down_ref = stage[6]
    piece = dact_ref.shape[1] // 4

    def back(index):
        dact_ref[:, lanes_at(index, piece)] = dot_nt(held[...], down_ref[lanes_at(index, piece)]).astype(BF)

    each(4, back)


def item_of_place(where_ref, place, items):
    found = jnp.int32(0)
    for index in range(items):
        found = found + (place >= where_ref[ENDS + index]).astype(jnp.int32)
    return found


def tiles_meet(where_ref, one, other, parts, items):
    span = TILE * parts
    first, last = min(one, other), max(one, other)
    return item_of_place(where_ref, first * span + span - 1, items) >= item_of_place(
        where_ref, last * span, items
    )


def near_tiles(tile, tiles):
    return max(0, tile - 1), min(tiles, tile + 2)


def far_pairs(tiles):
    return [(one, other) for one in range(tiles) for other in range(tiles) if abs(one - other) > 1]


def any_far(where_ref, tiles, parts, items):
    found = jnp.bool_(False)
    for one, other in far_pairs(tiles):
        if one < other:
            found = found | tiles_meet(where_ref, one, other, parts, items)
    return found


def attend_kernel(parts, items, where_ref, stage, vec_ref, wide_ref, normed_ref, asks_ref):
    unpack_rows(stage[2], vec_ref)
    xhat_ref, kv_ref, attended_ref, logsum_ref = (stage.out(index) for index in range(4))
    far_a_ref, far_b_ref = stage[0], stage[1]
    stage.start(3, 4)
    rows, width = far_a_ref.shape
    tiles = rows // TILE
    span = parts * TILE
    both = 2 * HEAD_SIZE
    half = width // 2
    core = where_ref[1]
    for rel_c, ref in enumerate((far_a_ref, far_b_ref)):
        xhat, unused = standardise(ref[...].astype(F32))
        xhat_ref[rel_c * rows : (rel_c + 1) * rows] = xhat.astype(BF)
        normed_ref[rel_c * rows : (rel_c + 1) * rows] = normed_rows(xhat, vec_ref, 0)
    stage.put(0)
    row = lax.broadcasted_iota(jnp.int32, (2 * TILE, 2 * TILE), 0)
    block = 2 * where_ref[0] + (where_ref[1] ^ (row // TILE))
    for tile in range(tiles):
        asks_ref[tile] = item_at((tile * TILE + row % TILE) * parts + block, where_ref, items)
    lane = lax.broadcasted_iota(jnp.int32, (1, span), 1)
    slot = lane // TILE
    block = 2 * (where_ref[0] ^ (slot // 2)) + (where_ref[1] ^ (slot % 2))
    key_item = [item_at((tile * TILE + lane % TILE) * parts + block, where_ref, items) for tile in range(tiles)]
    weight_ref = stage[3]
    row_ref = jnp.concatenate([jnp.zeros((1, half), F32), vec_ref[3:4, lanes_at(core, half)]], axis=1)
    far_kv = (dot_nn(normed_ref[...], weight_ref[...]) + row_ref).astype(BF)
    qkv_ref = stage[4]
    for tile in range(tiles):
        for slot in range(2):
            at = slice(slot * rows + tile * TILE, slot * rows + (tile + 1) * TILE)
            kv_ref[tile * span + slot * TILE : tile * span + (slot + 1) * TILE] = qkv_ref[at, half:]
            kv_ref[tile * span + (slot + 2) * TILE : tile * span + (slot + 3) * TILE] = far_kv[at]
    stage.put(1)
    for index in range(half // both):
        wide_ref[:, 2 * index * both : (2 * index + 1) * both] = kv_ref[:, half + index * both : half + (index + 1) * both]
        wide_ref[:, (2 * index + 1) * both : (2 * index + 2) * both] = jnp.ones((tiles * span, both), BF)

    def attend(index, tile, first, last):
        lanes = lanes_at(index, both)
        at = slice(first * span, last * span)
        places = [pl.ds(pl.multiple_of(rel_c * rows + tile * TILE, TILE), TILE) for rel_c in range(2)]
        query = stack_heads(jnp.concatenate([qkv_ref[place, lanes] for place in places], axis=0))
        score = dot_nt(query, kv_ref[at, lanes])
        asked = asks_ref[tile][:, :1]
        allowed = jnp.concatenate([asked == key_item[other] for other in range(first, last)], axis=1)
        score = jnp.where(jnp.concatenate([allowed, allowed], axis=0), score, MASKED)
        best = jnp.max(score, axis=1, keepdims=True)
        weight = jnp.exp(score - best).astype(BF)
        mixed = dot_nn(weight, wide_ref[at, lanes_at(index, 2 * both)])
        total = mixed[:, both:]
        logsum_ref[index, pl.ds(tile, 1)] = (best + jnp.log(total)).T[:1]
        mixed = mixed[:, :both] / total
        attended = jnp.where(lanes_below((both, both), HEAD_SIZE), mixed[:both], mixed[both:]).astype(BF)
        for rel_c, place in enumerate(places):
            attended_ref[place, lanes] = attended[rel_c * TILE : (rel_c + 1) * TILE]

    def pair(index):
        for tile in range(tiles):
            attend(index, tile, *near_tiles(tile, tiles))

    each(half // both, pair)

    @pl.when(any_far(where_ref, tiles, parts, items))
    def far():
        def again(step):
            tile = step % tiles
            found = jnp.bool_(False)
            for one, other in far_pairs(tiles):
                found = found | ((tile == one) & tiles_meet(where_ref, one, other, parts, items))
            pl.when(found)(lambda: attend(step // tiles, tile, 0, tiles))

        each(half // both * tiles, again)


def gelu_with_slope(values):
    bell = jnp.exp(-0.5 * values * values)
    inverse = 1.0 / (1.0 + (0.3275911 * 0.5**0.5) * jnp.abs(values))
    series = 1.061405429
    for coefficient in (-1.453152027, 1.421413741, -0.284496736, 0.254829592):
        series = series * inverse + coefficient
    tail = 0.5 * (series * inverse) * bell
    normal = jnp.where(values >= 0, 1.0 - tail, tail)
    return values * normal, normal + values * bell * ((2.0 * math.pi) ** -0.5)


def set_block(where_ref, rel_y, low_z, high_z):
    return 2 * (where_ref[2] ^ (low_z + 2 * high_z)) + (where_ref[3] ^ rel_y)


def mlp_kernel(where_ref, stage, vec_ref, bias_ref, mid_ref, joined, normed, grad, turned, dbefore_ref):
    py_ref, ux_ref, dz_ref = stage.out(0), stage.out(2), stage.out(4)
    xhat_ref, inverse_ref, mid_own_ref, branch_ref, swap_ref, act_ref, bias_sum_ref = (
        stage.out(index) for index in range(6, 13)
    )
    unpack_rows(stage[4], vec_ref)
    att_own_ref, att_sib_ref, own_ref, sib_ref, raw_ref, out_ref = (stage[index] for index in range(6))
    stage.start(6, 7, 8)
    x, core, z, y = (where_ref[index] for index in range(4))
    rows, width = own_ref.shape
    half = width // 2
    piece = act_ref.shape[1] // 4
    joined[:, :half] = att_own_ref[...]
    joined[:rows, half:] = att_sib_ref[rows:]
    joined[rows:, half:] = att_sib_ref[:rows]

    def project(index):
        lanes = lanes_at(index, 256)
        branch = dot_nn(joined[...], out_ref[:, lanes]) + vec_ref[4:5, lanes]
        branch_ref[:, lanes] = branch[:rows].astype(BF)
        branch = vec_ref[5:6, lanes] * branch
        mid_ref[:rows, lanes] = own_ref[:, lanes].astype(F32) + branch[:rows]
        mid_ref[rows:, lanes] = sib_ref[:, lanes].astype(F32) + branch[rows:]

    each(width // 256, project)

    mid_own_ref[...] = mid_ref[:rows]

    def norm(index):
        at = lanes_at(index, WIDE_CHUNK)
        xhat, inverse = standardise(mid_ref[at])
        normed[at] = (xhat * vec_ref[6:7] + vec_ref[7:8]).astype(BF)
        xhat_ref[at] = xhat.astype(BF)
        inverse_ref[at] = inverse

    each(2 * rows // WIDE_CHUNK, norm)
    stage.put(6, 7, 8, 9)
    count = piece // 128
    for unit in range(8):
        for part in range(count):
            row = 10 * width // 128 + unit * count + part
            bias_ref[unit : unit + 1, part * 128 : (part + 1) * 128] = raw_ref[row : row + 1]
    up_ref, dact_ref, turned_ref = stage[6], stage[7], stage[8]
    size = grad.shape[0] // 8

    def hidden(index):
        rel_x = 1 - index
        for side in range(2):
            at = lanes_at(2 * rel_x + side, piece)
            before = dot_nn(normed[...], up_ref[:, at]) + bias_ref[pl.ds(hidden_unit(where_ref, rel_x, side), 1)]
            act, slope = gelu_with_slope(before)
            act_ref[:, at] = act.astype(BF)
            dbefore = (dact_ref[:, at].astype(F32) * slope).astype(BF)
            dbefore_ref[:, at] = dbefore
            bias_sum_ref[:, at] = column_sum(dbefore.astype(F32))
            grad[:, side * piece : (side + 1) * piece] = dot_nn(turned_ref[...], act_ref[:, at]).astype(BF)

        def lay(index):
            low_z, high_z, rel_y = index // 4, index // 2 % 2, index % 2
            first = set_block(where_ref, rel_y, low_z, high_z) * size
            most = dz_ref.shape[4] - size
            dz_ref[low_z, high_z, rel_x, rel_y, :size] = grad[pl.ds(pl.multiple_of(first, size), size), :piece]
            dz_ref[low_z, high_z, rel_x, rel_y, size:] = grad[pl.ds(pl.multiple_of(first, size), most), piece:]
            py_ref[rel_y, rel_x, lanes_at(2 * low_z + high_z, size - most)] = grad[
                pl.ds(pl.multiple_of(first + most, size - most), size - most), piece:
            ]

        each(8, lay)

    each(2, hidden)
    stage.put(4, 5, 11, 12)
    turn(normed, turned)
    block = 2 * size

    def up(index):
        rel_y, high_z = index // 2, index % 2
        unit = 2 * (x ^ (z // 2) ^ high_z) + (y ^ rel_y)
        grad[:, :piece] = dot_nn(turned[...], dbefore_ref[:, lanes_at(unit, piece)]).astype(BF)
        for rel_x in range(2):
            to = pl.ds(pl.multiple_of(py_ref.shape[2] - 2 * block + high_z * block, 64), block)
            py_ref[rel_y, rel_x, to] = grad[lanes_at(own_block(where_ref, rel_x, 0), block), :piece]
            ux_ref[rel_x, rel_y, high_z] = grad[lanes_at(own_block(where_ref, rel_x, 1), block), :piece]

    each(4, up)
    stage.put(0, 1, 2, 3)

    def back(index):
        lanes = lanes_at(index, 256)
        total = dot_nt(dbefore_ref[...], up_ref[lanes])
        swap_ref[:, lanes] = total.astype(BF)

    each(width // 256, back)


def middle(parts, items, where_ref, stage, vec_ref, sum_ref, datt_ref, held, chosen, packed):
    dmid_ref, a_ref, o_ref = stage.out(0), stage.out(1), stage.out(5)
    keep_ref, got_ref, xhat_ref, inverse_ref, own_ref, sib_ref, raw_ref = (stage[index] for index in range(7))
    stage.start(10, 9, 7, 8, 11, 12, 13)
    unpack_rows(raw_ref, vec_ref)
    rows, width = own_ref.shape
    half = width // 2
    core = where_ref[1]
    left_is_own = lanes_below((rows, half), half // 2) == (core == 0)
    for rel_c, ref in enumerate((own_ref, sib_ref)):
        here = slice(rel_c * rows, (rel_c + 1) * rows)
        there = slice((1 - rel_c) * rows, (2 - rel_c) * rows)
        valid = valid_at(where_ref, rel_c, 0, rows, parts, items)
        dnormed = keep_ref[here].astype(F32) + got_ref[there].astype(F32)
        xhat, inverse = xhat_ref[here].astype(F32), inverse_ref[here]
        dmid = ref[...].astype(F32) * valid + standardise_grad(vec_ref[6:7] * dnormed, xhat, inverse)
        dbranch = (vec_ref[5:6] * dmid).astype(BF)
        held[here] = dbranch
        if rel_c == 0:
            dmid_ref[...] = dmid
            sum_ref[0:1] = column_sum(dbranch.astype(F32))
            sum_ref[1:2] = column_sum(dmid * stage[10][...].astype(F32))
            sum_ref[2:3] = column_sum(dnormed * xhat)
            sum_ref[3:4] = column_sum(dnormed)
    stage.put(0)
    stage.start(14, 15)
    datt_ref[...] = dot_nt(held[...], stage[9][...]).astype(BF)
    att_own_ref, att_sib_ref = stage[7], stage[8]
    for rel_c in range(2):
        here = slice(rel_c * rows, (rel_c + 1) * rows)
        there = slice((1 - rel_c) * rows, (2 - rel_c) * rows)
        other = pltpu.roll(att_sib_ref[there].astype(F32), half // 2, 1)
        chosen[here] = jnp.where(left_is_own, att_own_ref[here].astype(F32), other).astype(BF)
    grad = dot_tn(held[...], chosen[...])
    count, unit_rows = packed.shape[1:3]
    for index in range(count):
        left, right = pack_unit(grad[2 * index * unit_rows : 2 * (index + 1) * unit_rows])
        packed[0, index] = left.astype(BF)
        packed[1, index] = right.astype(BF)

    units = 6 * unit_rows

    def lay(index):
        rel_x, rel_y, block = index // 8, index // 4 % 2, index % 4
        here = packed.at[where_ref[0] ^ rel_x, set_block(where_ref, rel_y, block // 2, block % 2)]
        a_ref[rel_x, rel_y, pl.ds(pl.multiple_of(units + 16 * block, 16), 16)] = here[:16]
        o_ref[rel_y, rel_x, lanes_at(block, unit_rows - 16)] = here[16:]

    each(16, lay)
    stage.put(5, 6)


def pack_unit(unit):
    half = unit.shape[0] // 2
    width = unit.shape[1]
    top, bottom = unit[:half], unit[half:]
    first = lanes_below((half, width), width // 2)
    left = jnp.where(first, top, pltpu.roll(bottom, width // 2, 1))
    right = jnp.where(first, pltpu.roll(top, width // 2, 1), bottom)
    return left, right


def join_heads(stacked_turned):
    stacked = stacked_turned.T
    count = stacked.shape[0] // 2
    return jnp.where(
        lanes_below((count, stacked.shape[1]), HEAD_SIZE), stacked[:count], stacked[count:]
    )


def query_items(where_ref, tile, parts, items):
    lane = lax.broadcasted_iota(jnp.int32, (1, 4 * TILE), 1)
    rel_c = (lane // TILE) % 2
    block = 2 * where_ref[0] + (where_ref[1] ^ rel_c)
    return item_at((tile * TILE + lane % TILE) * parts + block, where_ref, items)


def fill_key_items(where_ref, item_ref, tiles, parts, items):
    row = lax.broadcasted_iota(jnp.int32, (TILE, item_ref.shape[1]), 0)
    for tile in range(tiles):
        for slot in range(parts):
            block = own_block(where_ref, slot // 2, slot % 2)
            at = (tile * parts + slot) * TILE
            item_ref[at : at + TILE] = item_at((tile * TILE + row) * parts + block, where_ref, items)


def both_heads(array):
    return jnp.concatenate([array, array], axis=1)


def attend_grad(
    parts, items, where_ref, stage, datt_ref, dquery_ref, dkeys_ref, dvalues_ref, asks_ref, item_ref, turned_ref, dk, dv, dq
):
    attended_ref, qkv_ref, kv_ref, logsum_ref = stage[7], stage[11], stage[12], stage[13]
    half = datt_ref.shape[1]
    rows = datt_ref.shape[0] // 2
    tiles = rows // TILE
    span = parts * TILE
    scale = HEAD_SIZE ** (-0.5)
    turned_ref[...] = kv_ref[:, :half].T
    fill_key_items(where_ref, item_ref, tiles, parts, items)
    for tile in range(tiles):
        asks_ref[tile : tile + 1] = query_items(where_ref, tile, parts, items)
    some_far = any_far(where_ref, tiles, parts, items)

    def pair(index, carry):
        lanes = lanes_at(index, 2 * HEAD_SIZE)
        value_lanes = pl.ds(pl.multiple_of(half + index * 2 * HEAD_SIZE, 2 * HEAD_SIZE), 2 * HEAD_SIZE)
        dk[...] = jnp.zeros_like(dk)
        dv[...] = jnp.zeros_like(dv)

        def places(tile):
            return [pl.ds(pl.multiple_of(rel_c * rows + tile * TILE, TILE), TILE) for rel_c in range(2)]

        def visit(tile, at):
            query = stack_heads(jnp.concatenate([qkv_ref[place, lanes] for place in places(tile)], axis=0))
            grad = jnp.concatenate([datt_ref[place, lanes] for place in places(tile)], axis=0)
            attended = jnp.concatenate([attended_ref[place, lanes] for place in places(tile)], axis=0)
            product = (grad.astype(F32) * attended.astype(F32)).T
            delta = jnp.concatenate([column_sum(product[:HEAD_SIZE]), column_sum(product[HEAD_SIZE:])], axis=1)
            grad = stack_heads(grad)
            score = dot_nt(kv_ref[at, lanes], query)
            allowed = both_heads(item_ref[at]) == asks_ref[pl.ds(tile, 1)]
            prob = jnp.exp(jnp.where(allowed, score, MASKED) - logsum_ref[index, pl.ds(tile, 1)])
            dprob = dot_nt(kv_ref[at, value_lanes], grad)
            dscore = (prob * (dprob - delta)).astype(BF)
            dv[at] += dot_nn(prob.astype(BF), grad)
            dk[at] += dot_nn(dscore, query)
            return dot_nn(turned_ref[lanes, at], dscore)

        for tile in range(tiles):
            first, last = near_tiles(tile, tiles)
            dq[tile] = visit(tile, slice(first * span, last * span))

        @pl.when(some_far)
        def far():
            def add(step):
                tile, other = step // tiles, step % tiles
                found = jnp.bool_(False)
                for one, two in far_pairs(tiles):
                    found = found | ((step == one * tiles + two) & tiles_meet(where_ref, one, two, parts, items))

                @pl.when(found)
                def meet():
                    at = pl.ds(pl.multiple_of(other * span, span), span)
                    dq[tile] += visit(tile, at)

            each(tiles * tiles, add)

        for tile in range(tiles):
            dquery = (join_heads(dq[tile]) * scale).astype(BF)
            for rel_c, place in enumerate(places(tile)):
                dquery_ref[place, lanes] = dquery[rel_c * TILE : (rel_c + 1) * TILE]
            for slot in range(parts):
                to = slice(slot * rows + tile * TILE, slot * rows + (tile + 1) * TILE)
                at = slice(tile * span + slot * TILE, tile * span + (slot + 1) * TILE)
                dkeys_ref[to, lanes] = dk[at].astype(BF)
                dvalues_ref[to, lanes] = dv[at].astype(BF)
        return carry

    lax.fori_loop(0, half // (2 * HEAD_SIZE), pair, 0)


def twice(half_row, where_ref):
    row = both_heads(half_row)
    return jnp.where(lanes_below(row.shape, half_row.shape[1]) == (where_ref[1] == 0), row, 0.0)


def qkv_grad(where_ref, stage, vec_ref, sum_ref, dquery_ref, dkeys_ref, dvalues_ref, normed_ref, packed):
    a_ref, b_ref = stage.out(1), stage.out(3)
    near_ref, far_ref = stage[14], stage[15]
    rows, width = near_ref.shape
    core, z, y = where_ref[1], where_ref[2], where_ref[3]
    normed_ref[:rows] = normed_rows(near_ref[...], vec_ref, 0)
    normed_ref[rows:] = normed_rows(far_ref[...], vec_ref, 0)
    sum_ref[4:5] = twice(column_sum(dquery_ref[...].astype(F32)), where_ref)
    sum_ref[5:6] = twice(column_sum(dvalues_ref[...].astype(F32)), where_ref)
    for part, ref in enumerate((dquery_ref, dkeys_ref, dvalues_ref)):
        grad = dot_tn(ref[...], normed_ref[: ref.shape[0]])
        size = grad.shape[0] // 4
        for unit in range(4):
            for at_x in range(2):
                left, right = pack_unit(
                    grad[unit * size : (unit + 1) * size, at_x * width // 2 : (at_x + 1) * width // 2]
                )
                packed[2 * at_x, 4 * part + unit] = left.astype(BF)
                packed[2 * at_x + 1, 4 * part + unit] = right.astype(BF)

    def lay(index):
        rel_x, rel_y, at = index // 12, index // 6 % 2, index % 6
        unit = where_ref[UNIT_LIST + 24 * core + 12 * (y ^ rel_y) + 6 * (z % 2) + at]
        a_ref[rel_x, rel_y, lanes_at(at, packed.shape[2])] = packed[own_block(where_ref, rel_x, 0), unit]
        b_ref[rel_y, rel_x, at] = packed[own_block(where_ref, rel_x, 1), unit]

    each(24, lay)
    stage.put(1, 2, 3, 4)


def backward_kernel(
    parts, items, where_ref, stage, vec_ref, datt_ref, held, chosen, gpacked, normed_ref, packed, asks_ref, item_ref,
    turned_ref, dk, dv, dq,
):
    sum_ref, dquery_ref, dkeys_ref, dvalues_ref = (stage.out(index) for index in (10, 7, 8, 9))
    middle(parts, items, where_ref, stage, vec_ref, sum_ref, datt_ref, held, chosen, gpacked)
    attend_grad(
        parts, items, where_ref, stage, datt_ref, dquery_ref, dkeys_ref, dvalues_ref, asks_ref, item_ref, turned_ref,
        dk, dv, dq,
    )
    stage.put(7, 8, 9)
    qkv_grad(where_ref, stage, vec_ref, sum_ref, dquery_ref, dkeys_ref, dvalues_ref, normed_ref, packed)


def tokens_grad_kernel(parts, items, where_ref, stage, vec_ref):
    own_ref, far_ref, send_ref, keep_ref, sum_ref = (stage.out(index) for index in range(5))
    dquery_ref, dkeys_ref, dvalues_ref, weight_ref, near_ref, beyond_ref = (stage[index] for index in range(6))
    rows, width = own_ref.shape
    half = dquery_ref.shape[1]
    gain = jnp.zeros((1, width), F32)
    shift = gain
    for slot in (1, 3, 2, 0):
        at = slice(slot * rows, (slot + 1) * rows)
        part = dot_nt(dkeys_ref[at], weight_ref[:, half : 2 * half]) + dot_nt(dvalues_ref[at], weight_ref[:, 2 * half :])
        if slot < 2:
            part = part + dot_nt(dquery_ref[at], weight_ref[:, :half])
        xhat = (near_ref if slot < 2 else beyond_ref)[(slot % 2) * rows : (slot % 2 + 1) * rows].astype(F32)
        gain = gain + column_sum(part * xhat)
        shift = shift + column_sum(part)
        if slot % 2:
            send_ref[slot // 2 * rows : (slot // 2 + 1) * rows] = part.astype(BF)
        elif slot:
            far_ref[...] = part.astype(BF)
        else:
            own_ref[...] = part.astype(BF)
    stage.put(0, 1)
    unpack_rows(stage[6], vec_ref)
    act_ref, down_ref, cot_ref, cot_sib_ref, back_ref, bias_d_ref, bias_up_ref = (stage[index] for index in range(7, 14))
    feed = dot_nn(act_ref[...], down_ref[...])
    keep_ref[...] = feed[:rows] + vec_ref[8:9]
    send_ref[2 * rows :] = feed[rows:].astype(BF)
    stage.put(2, 3)
    scale = column_sum(cot_ref[...].astype(F32) * valid_at(where_ref, 0, 0, rows, parts, items) * keep_ref[...])
    scale = scale + column_sum(cot_sib_ref[...].astype(F32) * valid_at(where_ref, 1, 0, rows, parts, items) * feed[rows:])
    sum_ref[0:1] = gain
    sum_ref[1:2] = shift
    sum_ref[2:4] = back_ref[4:6]
    sum_ref[4:8] = back_ref[0:4]
    sum_ref[8:9] = bias_d_ref[...]
    sum_ref[9:10] = scale
    for at_x in range(2):
        one = bias_up_ref[:, at_x * width : (at_x + 1) * width]
        two = bias_up_ref[:, (1 - at_x) * width : (2 - at_x) * width]
        here = jnp.where(where_ref[0] == 0, one, two)
        for at_c in range(2):
            at = 10 + 2 * at_x + at_c
            sum_ref[at : at + 1] = jnp.where(where_ref[1] == at_c, here, 0.0)
    sum_ref[14:] = jnp.zeros((2, width), F32)


def unpack_unit(unit, target, first):
    half, lanes = unit.shape
    target[first : first + half] = unit[:, : target.shape[1]]
    target[first + half : first + 2 * half] = pltpu.roll(unit, lanes // 2, 1)[:, : target.shape[1]]


def sum_of(*terms):
    total = terms[0].astype(F32)
    for term in terms[1:]:
        total = total + term.astype(F32)
    return total


def fold_sums(sums):
    lanes = sums.shape[1] // 2
    return jnp.concatenate([sums[:, :lanes], sums[:, lanes:]], axis=0)


def second_step_kernel(where_ref, stage):
    dz_keep, dz_got, py_keep, py_got, a_ref, ux_keep, ux_got, b_got, o_ref = (stage[index] for index in range(9))
    dz_ref, x_ref, y_ref = (stage.out(index) for index in range(3))
    dz_ref[...] = sum_of(dz_keep[...], dz_got[...]).astype(BF)
    stage.put(0)
    count, rows = py_keep.shape[0], a_ref.shape[1]
    x_ref[:count] = sum_of(py_keep[...], py_got[...]).astype(BF)
    for rel_y in range(2):
        x_ref[count + rel_y * rows : count + (rel_y + 1) * rows] = a_ref[rel_y]
    stage.put(1)
    block = ux_keep.shape[1]
    for high_z in range(2):
        y_ref[high_z * block : (high_z + 1) * block] = sum_of(ux_keep[high_z], ux_got[high_z]).astype(BF)
    unit_rows = b_got.shape[2]
    first = 2 * block
    for rel_x in range(2):
        for index in range(6):
            y_ref[first : first + unit_rows] = b_got[rel_x, index]
            first += unit_rows
    rows = o_ref.shape[1]
    for rel_x in range(2):
        y_ref[first : first + rows] = o_ref[rel_x]
        first += rows


def third_step_kernel(where_ref, stage):
    ux_keep, ux_got, y_got, py_keep, py_got, x_got, b_keep, o_keep = (stage[index] for index in range(8))
    sum_refs, a_keep = [stage[index] for index in range(8, 12)], stage[12]
    send_ref, x_ref, a_ref, keep_ref = (stage.out(index) for index in range(4))
    count = py_keep.shape[0]
    block = ux_keep.shape[1]
    lead = send_ref.shape[1] - block
    same = where_ref[2] % 2 == where_ref[1]
    for high_z in range(2):
        at = slice(4 * lead + high_z * block, 4 * lead + (high_z + 1) * block)
        own = sum_of(py_keep[at], py_got[at], x_got[at])
        sib = sum_of(ux_keep[high_z], ux_got[high_z], y_got[high_z * block : (high_z + 1) * block])
        for side, ref in enumerate((keep_ref, send_ref)):
            at = slice((2 * side + high_z) * lead, (2 * side + high_z + 1) * lead)
            ref[high_z, :lead] = sum_of(py_keep[at], py_got[at], x_got[at]).astype(BF)
            here = jnp.where(same, sib, own) if side else jnp.where(same, own, sib)
            ref[high_z, lead:] = here.astype(BF)
    stage.put(0)
    unit_rows, rows = b_keep.shape[1], o_keep.shape[0]
    units = 6 * unit_rows
    first = 2 * block + units
    for index in range(6):
        at = slice(index * unit_rows, (index + 1) * unit_rows)
        x_ref[at] = sum_of(b_keep[index], y_got[first + index * unit_rows : first + (index + 1) * unit_rows]).astype(BF)
    first += units + rows
    x_ref[units : units + rows] = sum_of(o_keep[...], y_got[first : first + rows]).astype(BF)
    x_ref[units + rows :] = fold_sums(sum_of(*(ref[...] for ref in sum_refs))).astype(BF)
    stage.put(1)
    a_ref[...] = sum_of(a_keep[...], x_got[count + a_keep.shape[0] :]).astype(BF)


def fourth_step_kernel(where_ref, stage):
    a_keep, x_got, a_far, b_keep, y_got, b_far, o_keep, y_rest, x_ref, mlp_keep, mlp_got, dz_keep, dz_got, dz_far = (
        stage[index] for index in range(14)
    )
    send_ref, mlp_ref, dz_ref, mlp_kept, kept_ref, dz_kept, dtok_ref = (stage.out(index) for index in range(7))
    unit_rows, rows = b_keep.shape[1], o_keep.shape[0]
    units, most = 6 * unit_rows, rows // 4
    own = sum_of(a_keep[...], x_got[...], a_far[...]).astype(BF)
    rest = sum_of(o_keep[...], y_rest[...], b_far[units : units + rows]).astype(BF)
    sums = sum_of(x_ref[...], b_far[units + rows :]).astype(BF)
    for side, ref in enumerate((kept_ref, send_ref)):
        ref[: units // 2] = own[side * units // 2 : (side + 1) * units // 2]
        for index in range(3):
            unit = 3 * side + index
            at = slice(unit * unit_rows, (unit + 1) * unit_rows)
            to = slice((3 + index) * unit_rows, (4 + index) * unit_rows)
            ref[to] = sum_of(b_keep[unit], y_got[at], b_far[at]).astype(BF)
        for high_z in range(2):
            first, block = units + high_z * unit_rows, 2 * side + high_z
            ref[first : first + 16] = own[units + 16 * block : units + 16 * (block + 1)]
            ref[first + 16 : first + unit_rows] = rest[block * most : (block + 1) * most]
        ref[units + 2 * unit_rows :] = sums
    stage.put(0)
    mlp_ref[...] = sum_of(mlp_keep[1], mlp_got[1]).astype(BF)
    stage.put(1)
    for side, ref in enumerate((dz_kept, dz_ref)):
        ref[...] = sum_of(dz_keep[side], dz_got[side], dz_far[side]).astype(BF)
    stage.put(2)
    dtok_ref[...] = sum_of(stage[14][...], stage[15][...]).astype(BF)
    stage.put(6)
    mlp_kept[...] = sum_of(mlp_keep[0], mlp_got[0]).astype(BF)


def fifth_step_kernel(where_ref, stage, held):
    kept_ref, last_got, dz_kept, dz_got = (stage[index] for index in range(4))
    send_ref, dz_ref, keep_ref, dz_low_ref = (stage.out(index) for index in range(4))
    core, z, y = where_ref[1], where_ref[2], where_ref[3]
    unit_rows = held.shape[1]
    for index in range(6):
        at = slice(index * unit_rows, (index + 1) * unit_rows)
        held[index] = sum_of(kept_ref[at], last_got[at]).astype(BF)
    rest = sum_of(kept_ref[6 * unit_rows :], last_got[6 * unit_rows :]).astype(BF)
    for side, ref, owner_z in ((1, send_ref, z ^ 2), (0, keep_ref, z)):
        for index in range(3):
            at = where_ref[UNIT_LIST + 48 + ((core * 2 + y) * 4 + owner_z) * 3 + index]
            ref[index * unit_rows : (index + 1) * unit_rows] = held[at]
        ref[3 * unit_rows : 4 * unit_rows] = rest[side * unit_rows : (side + 1) * unit_rows]
        ref[4 * unit_rows :] = rest[2 * unit_rows :]
    stage.put(0)
    for side, ref in enumerate((dz_low_ref, dz_ref)):
        ref[...] = sum_of(dz_kept[side], dz_got[side]).astype(BF)


def finish_kernel(where_ref, stage, rows_ref, out_rows_ref, flat):
    mlp_kept, mlp_far, dz_low, dz_far, last_keep, last_far = (stage[index] for index in range(6))
    down_ref, up_ref, out_ref, vec_ref, qkv_ref = (stage.out(index) for index in range(5))
    size, block = down_ref.shape[0], up_ref.shape[0]
    lanes = up_ref.shape[1]
    mlp, dz = sum_of(mlp_kept[...], mlp_far[...]), sum_of(dz_low[...], dz_far[...])
    lead = mlp.shape[0] - block
    most = size - lead
    up_ref[...] = mlp[lead:]
    down_ref[:, :lanes] = dz[:size]
    down_ref[:most, lanes:] = dz[size : size + most]
    down_ref[most:, lanes:] = mlp[:lead]
    stage.put(0, 1)
    out_rows_ref[...] = jnp.zeros_like(out_rows_ref)
    last = sum_of(last_keep[...], last_far[...])
    half = size // 2
    unpack_unit(last[3 * half : 4 * half], out_rows_ref, 0)
    out_ref[...] = out_rows_ref[...].T[: out_ref.shape[0], : out_ref.shape[1]]
    sums = last[4 * half :]
    count = sums.shape[0] // 2
    for row in range(count):
        flat[:, 2 * row * lanes : (2 * row + 1) * lanes] = sums[row : row + 1]
        flat[:, (2 * row + 1) * lanes : (2 * row + 2) * lanes] = sums[count + row : count + row + 1]
    share = vec_ref.shape[1]
    start = (4 * set_block(where_ref, 0, 0, 0) + own_block(where_ref, 0, 0)) * share
    window = flat[:, pl.ds(pl.multiple_of(start // 128 * 128, 128), 512)]
    window = pltpu.roll(jnp.broadcast_to(window, (8, 512)), (512 - start % 128) % 512, 1)
    vec_ref[...] = window[:1, :share]
    stage.put(2, 3)
    rows_ref[...] = jnp.zeros_like(rows_ref)
    for unit in range(3):
        unpack_unit(last[unit * half : (unit + 1) * half], rows_ref, 2 * unit * half)
    qkv_ref[...] = rows_ref[...].T[: qkv_ref.shape[0], : qkv_ref.shape[1]]


def rows_kernel(parts, items, where_ref, stage, vec_ref):
    keep_ref, late_ref, far_ref, own_ref, dmid_ref, raw_ref, feed_ref, mid_ref = (stage[index] for index in range(8))
    unpack_rows(raw_ref, vec_ref)
    rows = own_ref.shape[0]
    dnormed = sum_of(keep_ref[...], late_ref[:rows], far_ref[...])
    xhat, inverse = standardise(own_ref[...].astype(F32))
    stage.out(0)[...] = (dmid_ref[...] + standardise_grad(vec_ref[0:1] * dnormed, xhat, inverse)).astype(BF)
    stage.put(0)
    valid = valid_at(where_ref, 0, 0, rows, parts, items)
    feed = sum_of(feed_ref[...], late_ref[rows:])
    stage.out(1)[...] = (valid * (mid_ref[...] + vec_ref[9:10] * feed)).astype(BF)


def swapped(array, axis, bit):
    length = lax.axis_size(axis)
    return lax.ppermute(array, axis, [(i, i ^ bit) for i in range(length)])


def to_core(array):
    return swapped(array, "blk", 1)


def to_x(array):
    return swapped(array, "blk", 2)


def to_y(array):
    return swapped(array, "dp", 1)


def to_z(array):
    return swapped(array, "dp", 2)


def to_zz(array):
    return swapped(array, "dp", 4)


def after(done, *arrays):
    return lax.optimization_barrier((done, *arrays))[1:]


def first_rows(count):
    def cut(where_ref, source, target):
        return [(source.at[:count], target)]

    return cut


def entry(array, index):
    def cut(where_ref, source, target):
        return [(source.at[index], target)]

    return (array.shape[1:], 1, cut)


def first_and_last_rows(count):
    def cut(where_ref, source, target):
        return [(source.at[:count], target.at[:count]), (source.at[2 * count :], target.at[count:])]

    return cut


def some_rows(array, first, last):
    def cut(where_ref, source, target):
        return [(source.at[first:last], target)]

    return ((last - first, *array.shape[1:]), 1, cut)


def own_columns(first):
    def cut(where_ref, source, target):
        half = source.shape[0] // 2
        return [
            (source.at[:, lanes_at(where_ref[1] + 2 * part, half)], target.at[:, (part - first) * half : (part - first + 1) * half])
            for part in range(first, 3)
        ]

    return cut


def own_hidden(axis):
    def cut(where_ref, source, target):
        pairs = []
        piece = target.shape[axis] // 4
        for rel_x in range(2):
            for side in range(2):
                at = lanes_at(hidden_unit(where_ref, rel_x, side), piece)
                to = slice((2 * rel_x + side) * piece, (2 * rel_x + side + 1) * piece)
                pairs.append((source.at[at], target.at[to]) if axis == 0 else (source.at[:, at], target.at[:, to]))
        return pairs

    return cut


def both_head_rows(where_ref, source, target):
    half = target.shape[0] // 2
    return [
        (source.at[lanes_at(where_ref[1], half), :], target.at[:half]),
        (source.at[lanes_at(1 - where_ref[1], half), :], target.at[half:]),
    ]


def own_head_rows(where_ref, source, target):
    return [(source.at[lanes_at(where_ref[1], target.shape[0]), :], target)]


def on_device_aligned(tokens, lengths, w_qkv, w_out, w_up, w_down, vectors, cotangent):
    tokens, cotangent = tokens[0], cotangent[0]
    rows, width = tokens.shape
    hidden = w_up.shape[1]
    items = lengths.shape[1]
    parts = lax.axis_size("blk")
    sets = lax.axis_size("dp")
    position, turn = lax.axis_index("blk"), lax.axis_index("dp")
    x, core, z, y = position // 2, position % 2, turn // 2, turn % 2
    where = lengths
    half = width // 2
    inner = hidden // 2
    piece = hidden // sets
    both = 2 * rows
    total_rows = parts * rows
    block = width // parts
    share = width // sets
    names = (parts, items)
    zs = sets // 2
    all_columns = ((width, 3 * half), 3, own_columns(0))
    kv_columns = ((width, 2 * half), 2, own_columns(1))
    up_columns = ((width, inner), 4, own_hidden(1))
    down_rows = ((inner, width), 4, own_hidden(0))
    head_rows = ((half, width), 1, own_head_rows)
    out_rows = ((width, width), 2, both_head_rows)

    far_a = to_x(tokens)
    sib = to_core(tokens)
    cot_sib = to_core(cotangent)

    vec = vectors.reshape(-1, 128)
    rows_of_vec = pltpu.VMEM((10, width), F32)

    xhat_near, qkv_near, dact, dfeed_turned, bias_d_sum = staged_call(
        functools.partial(prepare_kernel, *names),
        where,
        (tokens, sib, vec, w_qkv, cotangent, cot_sib, w_down),
        [low(both, width), low(both, 3 * half), low(both, inner), low(width, both), full(1, width)],
        cuts={3: all_columns, 6: down_rows},
        scratch=[rows_of_vec, pltpu.VMEM((both, width), BF), pltpu.VMEM((both, width), BF), pltpu.VMEM((2, 3 * half), F32)],
    )

    far_a, qkv_near, dact = lax.optimization_barrier((far_a, qkv_near, dact))
    far_b = to_core(far_a)

    xhat_far, kv, attended, logsum = staged_call(
        functools.partial(attend_kernel, *names),
        where,
        (far_a, far_b, vec, w_qkv, qkv_near),
        [low(both, width), low(total_rows, width), low(both, half), full(half // (2 * HEAD_SIZE), rows // TILE, 4 * TILE)],
        cuts={3: kv_columns},
        scratch=[
            rows_of_vec,
            pltpu.VMEM((total_rows, 2 * half), BF),
            pltpu.VMEM((both, width), BF),
            pltpu.VMEM((rows // TILE, 2 * TILE, 2 * TILE), jnp.int32),
        ],
    )
    attended_sib = to_core(attended)

    unit_rows = share // 2
    lead = 32
    py, us, dz = low(2, 4 * lead + 2 * block, piece), low(2, 2, block, piece), low(2, 2, 2, 2 * share - lead, piece)
    (py_keep, py_send, ux_keep, ux_send, dz_keep, dz_send, xhat_two, inverse_two, mid, branch, swap, act,
     bias_up_sum) = staged_call(
        mlp_kernel,
        where,
        (attended, attended_sib, tokens, sib, vec, w_out, w_up, dact, dfeed_turned),
        [py, py, us, us, dz, dz, low(both, width), full(both, 1), full(rows, width), low(rows, width), low(both, width),
         low(both, inner), full(1, inner)],
        cuts={5: out_rows, 6: up_columns},
        late=(6, 7, 8),
        pairs=(0, 2, 4),
        scratch=[rows_of_vec, pltpu.VMEM((sets, piece), F32), pltpu.VMEM((both, width), F32),
                 pltpu.VMEM((both, width), BF), pltpu.VMEM((both, width), BF), pltpu.VMEM((width, 2 * piece), BF),
                 pltpu.VMEM((width, both), BF), pltpu.VMEM((both, inner), BF)],
    )
    swap_got = to_core(swap)
    ux_send, ux_keep = to_core(ux_send), to_core(ux_keep)
    py_got = to_y(py_send)
    ux_got = to_x(ux_send)
    dz_got = to_z(dz_send)

    dmid, a_keep, a_send, b_keep, b_send, o_keep, o_send, dquery, dkeys, dvalues, back_sums = staged_call(
        functools.partial(backward_kernel, *names),
        where,
        (swap, swap_got, xhat_two, inverse_two, cotangent, cot_sib, vec, attended, attended_sib, w_out, branch,
         qkv_near, kv, logsum, xhat_near, xhat_far),
        [full(rows, width)] + [low(2, 6 * unit_rows + 64, half)] * 2 + [low(2, 6, unit_rows, half)] * 2
        + [low(2, 4 * unit_rows - 64, half)] * 2
        + [low(both, half), low(total_rows, half), low(total_rows, half), full(8, width)],
        cuts={9: head_rows},
        late=tuple(range(7, 16)),
        pairs=(1, 3, 5),
        tables=True,
        scratch=[rows_of_vec, pltpu.VMEM((both, half), BF), pltpu.VMEM((both, width), BF),
                 pltpu.VMEM((both, half), BF), pltpu.VMEM((2, sets, unit_rows, half), BF),
                 pltpu.VMEM((total_rows, width), BF), pltpu.VMEM((4, 12, unit_rows, half), BF),
                 pltpu.VMEM((rows // TILE, 4 * TILE), jnp.int32), pltpu.VMEM((total_rows, 2 * TILE), jnp.int32),
                 pltpu.VMEM((half, total_rows), BF), pltpu.VMEM((total_rows, 2 * HEAD_SIZE), F32),
                 pltpu.VMEM((total_rows, 2 * HEAD_SIZE), F32),
                 pltpu.VMEM((rows // TILE, 2 * HEAD_SIZE, 4 * TILE), F32)],
    )
    six, top = 6 * unit_rows, 2 * share - lead
    step = functools.partial(staged_call, grant=STEP_GRANT)
    b_send, b_keep = to_core(b_send), to_core(b_keep)
    py_got, ux_got, dz_got, b_send, b_keep = after(back_sums, py_got, ux_got, dz_got, b_send, b_keep)
    count = py_keep.shape[1]
    dz_step, x_step, y_step = staged_call(
        second_step_kernel,
        where,
        (dz_keep, dz_got, py_keep, py_got, a_send, ux_keep, ux_got, b_send, o_send),
        [low(*dz_keep.shape[1:]), low(count + 2 * six + 128, half), low(2 * block + 2 * six + 8 * unit_rows - 128, half)],
        cuts={index: entry(array, 1)
              for index, array in ((0, dz_keep), (1, dz_got), (2, py_keep), (3, py_got), (5, ux_keep), (6, ux_got))},
    )
    dz_far, x_got, y_got = to_zz(dz_step), to_x(x_step), to_y(y_step)
    (back_sums,) = after(y_step, back_sums)
    dtok_own, dtok_far, late_send, feed_keep, sums = staged_call(
        functools.partial(tokens_grad_kernel, *names),
        where,
        (dquery, dkeys, dvalues, w_qkv, xhat_near, xhat_far, vec, act, w_down, cotangent, cot_sib, back_sums,
         bias_d_sum, bias_up_sum),
        [low(rows, width), low(rows, width), low(3 * rows, width), full(rows, width), full(16, width)],
        cuts={3: all_columns, 8: down_rows},
        scratch=[rows_of_vec],
    )
    sums_core, sums_y = to_core(sums), to_y(sums)
    sums_far = to_core(sums_y)
    dz_far, x_got, y_got, sums_core, sums_y, sums_far = lax.optimization_barrier(
        (dz_far, x_got, y_got, sums_core, sums_y, sums_far)
    )

    rest = 4 * unit_rows - 64
    mlp_send, b_step, a_step, mlp_keep = staged_call(
        third_step_kernel,
        where,
        (ux_keep, ux_got, y_got, py_keep, py_got, x_got, b_keep, o_keep, sums, sums_core, sums_y, sums_far, a_keep),
        [low(2, lead + block, piece), low(six + rest + 32, half), low(six + 64, half), low(2, lead + block, piece)],
        cuts={index: entry(array, 0) for index, array in ((0, ux_keep), (1, ux_got), (3, py_keep), (4, py_got))}
        | {index: entry(array, 1) for index, array in ((6, b_keep), (7, o_keep), (12, a_keep))},
    )
    mlp_got, b_far, a_far = to_z(mlp_send), to_x(b_step), to_y(a_step)
    (late_send,) = after(mlp_keep, late_send)
    late_got = to_core(late_send)
    mlp_got, b_far, a_far, late_got = lax.optimization_barrier((mlp_got, b_far, a_far, late_got))

    first = 2 * block + 2 * six
    last_send, mlp_step, dz_step, mlp_kept, last_keep, dz_kept, dtok_step = staged_call(
        fourth_step_kernel,
        where,
        (a_keep, x_got, a_far, b_keep, y_got, b_far, o_keep, y_got, b_step, mlp_keep, mlp_got, dz_keep, dz_got, dz_far,
         dtok_far, late_got),
        [low(six + 2 * unit_rows + 32, half), low(lead + block, piece), low(2, top, piece), low(lead + block, piece),
         low(six + 2 * unit_rows + 32, half), low(2, top, piece), low(rows, width)],
        cuts={0: entry(a_keep, 0), 1: some_rows(x_got, count, count + six + 64), 3: entry(b_keep, 0),
              4: some_rows(y_got, 2 * block, 2 * block + six), 6: entry(o_keep, 0), 7: some_rows(y_got, first, first + rest),
              8: some_rows(b_step, six + rest, six + rest + 32), 11: entry(dz_keep, 0), 12: entry(dz_got, 0),
              15: some_rows(late_got, rows, both)},
    )
    last_got, mlp_far, dz_x, dtok_x = to_z(last_send), to_zz(mlp_step), to_x(dz_step), to_x(dtok_step)
    last_send, dz_y, last_kept, dz_low = step(
        fifth_step_kernel,
        where,
        (last_keep, last_got, dz_kept, dz_x),
        [low(4 * unit_rows + 32, half), low(top, piece), low(4 * unit_rows + 32, half), low(top, piece)],
        scratch=[pltpu.VMEM((6, unit_rows, half), BF)],
        tables=True,
    )
    last_far, dz_y = to_zz(last_send), to_y(dz_y)

    (dtok_x,) = after(dz_low, dtok_x)
    grad_tokens, out = staged_call(
        functools.partial(rows_kernel, *names),
        where,
        (dtok_own, late_got, dtok_x, tokens, dmid, vec, feed_keep, mid),
        [low(rows, width), low(rows, width)],
        cuts={1: ((both, width), 2, first_and_last_rows(rows))},
        scratch=[rows_of_vec],
    )

    mlp_far, dz_y, last_far = after(grad_tokens, mlp_far, dz_y, last_far)
    g_w_down, g_w_up, g_w_out, g_vec, g_w_qkv = step(
        finish_kernel,
        where,
        (mlp_kept, mlp_far, dz_low, dz_y, last_kept, last_far),
        [full(share, 2 * piece), full(block, piece), full(block, share), full(1, vectors.shape[0] // (sets * parts)),
         full(block, 3 * share)],
        scratch=[pltpu.VMEM((384, 256), F32), pltpu.VMEM((128, 256), F32), pltpu.VMEM((1, 16 * width + 512), F32)],
    )
    return (out[None], grad_tokens[None], g_w_qkv, g_w_out, g_w_up, g_w_down.T, g_vec.reshape(-1))


def is_aligned(mesh, tokens, w_up):
    parts, sets = mesh.shape["blk"], mesh.shape["dp"]
    width, hidden = w_up.shape
    rows = tokens.shape[1] // parts
    return (
        parts == 4
        and sets == 2 * parts
        and rows == 4 * TILE
        and (hidden // sets) % 128 == 0
        and (width // 2) % 128 == 0
        and (width // sets) % 32 == 0
        and width == H * HEAD_SIZE
    )


def solution(mesh):
    def run(tokens, lengths, w_qkv, w_out, w_up, w_down, vectors, cotangent):
        body = on_device_aligned if is_aligned(mesh, tokens, w_up) else on_device
        return jax.shard_map(
            body,
            mesh=mesh,
            in_specs=(
                P("dp", "blk", None),
                P("dp", None),
                P(),
                P(),
                P(),
                P(),
                P(),
                P("dp", "blk", None),
            ),
            out_specs=(
                P("dp", "blk", None),
                P("dp", "blk", None),
                P("blk", "dp"),
                P("blk", "dp"),
                P("blk", "dp"),
                P("blk", "dp"),
                P(("dp", "blk")),
            ),
            check_vma=False,
        )(tokens, lengths, w_qkv, w_out, w_up, w_down, vectors, cotangent)

    return run
```

```python
import functools
import math

import jax
import jax.numpy as jnp
import numpy as np
from jax import lax
from jax.experimental import pallas as pl
from jax.experimental.pallas import tpu as pltpu
from jax.sharding import PartitionSpec as P

H = 12
HEAD_SIZE = 64
TILE = 64


EPSILON = 1e-06
FLOOR_SCORE = -1e30


def passed_along(array, axis, by):
    length = lax.axis_size(axis)
    return lax.ppermute(array, axis, [(i, (i + by) % length) for i in range(length)])


def norm_rows(values, gain, shift):
    centre = jnp.mean(values, axis=-1, keepdims=True)
    centred = values - centre
    spread = jnp.mean(centred * centred, axis=-1, keepdims=True)
    return centred * lax.rsqrt(spread + EPSILON) * gain + shift


def exact_gelu(values):
    return jax.nn.gelu(values, approximate=False)


def segment_of(rows_index, rows, parts, ends):
    place = rows_index % rows * parts + rows_index // rows
    return jnp.sum((place[:, None] >= ends[None, :]).astype(jnp.int32), axis=1)


def contract_rows(left, right):
    return lax.dot_general(
        left, right, (((0,), (0,)), ((), ())), preferred_element_type=jnp.float32
    )


def contract_cols(left, right):
    return lax.dot_general(
        left, right, (((1,), (1,)), ((), ())), preferred_element_type=jnp.float32
    )


def attend_block(query, query_item, keys, values, key_item, scale, carry):
    best, total, weighted = carry
    count = keys.shape[0]
    heads = query.shape[1]
    key_heads = keys.reshape(count, heads, -1)
    value_heads = values.reshape(count, heads, -1)
    allowed = (query_item[:, None] == key_item[None, :])[None]
    score = jnp.einsum("qhd,khd->hqk", query, key_heads, preferred_element_type=jnp.float32) * scale
    score = jnp.where(allowed, score, FLOOR_SCORE)
    newbest = jnp.maximum(best, jnp.max(score, axis=-1))
    weight = jnp.where(allowed, jnp.exp(score - newbest[..., None]), 0.0)
    factor = jnp.exp(best - newbest)
    total = total * factor + jnp.sum(weight, axis=-1)
    weighted = weighted * factor[..., None] + jnp.einsum(
        "hqk,khd->hqd", weight.astype(jnp.bfloat16), value_heads, preferred_element_type=jnp.float32
    )
    return (newbest, total, weighted)


def grad_block(query, d_out, logsum, delta, query_item, keys, values, key_item, scale):
    count = keys.shape[0]
    heads = query.shape[1]
    key_heads = keys.reshape(count, heads, -1)
    value_heads = values.reshape(count, heads, -1)
    allowed = (query_item[:, None] == key_item[None, :])[None]
    score = jnp.einsum("qhd,khd->hqk", query, key_heads, preferred_element_type=jnp.float32) * scale
    prob = jnp.where(allowed, jnp.exp(score - logsum[..., None]), 0.0)
    d_prob = jnp.einsum("qhd,khd->hqk", d_out, value_heads, preferred_element_type=jnp.float32)
    d_score = (prob * (d_prob - delta[..., None])).astype(jnp.bfloat16)
    d_query = (
        jnp.einsum("hqk,khd->qhd", d_score, key_heads, preferred_element_type=jnp.float32) * scale
    )
    d_keys = jnp.einsum("hqk,qhd->khd", d_score, query, preferred_element_type=jnp.float32) * scale
    d_values = jnp.einsum(
        "hqk,qhd->khd", prob.astype(jnp.bfloat16), d_out, preferred_element_type=jnp.float32
    )
    return (d_query, d_keys.reshape(count, -1), d_values.reshape(count, -1))


def on_device(tokens, lengths, w_qkv, w_out, w_up, w_down, vectors, cotangent):
    inputs = tokens[0].astype(jnp.float32)
    rows, width = inputs.shape
    heads = H
    head_size = width // heads
    scale = head_size ** (-0.5)
    items = lengths.shape[1]
    ends = jnp.cumsum(lengths[0])
    parts = lax.axis_size("blk")
    position = lax.axis_index("blk")
    query_item = segment_of(position * rows + lax.iota(jnp.int32, rows), rows, parts, ends)
    valid = (query_item < items).astype(jnp.float32)[:, None]
    pieces = [vectors[index * width : (index + 1) * width] for index in range(10)]
    (
        gain_one,
        shift_one,
        bias_q,
        bias_v,
        bias_o,
        scale_one,
        gain_two,
        shift_two,
        bias_d,
        scale_two,
    ) = pieces
    bias_up = vectors[10 * width :]
    normed, norm_one_pull = jax.vjp(norm_rows, inputs, gain_one, shift_one)
    normed_low = normed.astype(jnp.bfloat16)
    qkv_bias = jnp.concatenate([bias_q, jnp.zeros_like(bias_q), bias_v])
    projected = (jnp.dot(normed_low, w_qkv, preferred_element_type=jnp.float32) + qkv_bias).astype(
        jnp.bfloat16
    )
    query = projected[:, :width].reshape(rows, heads, head_size)
    keys = projected[:, width : 2 * width]
    values = projected[:, 2 * width :]
    start_state = (
        jnp.full((heads, rows), FLOOR_SCORE, jnp.float32),
        jnp.zeros((heads, rows), jnp.float32),
        jnp.zeros((heads, rows, head_size), jnp.float32),
    )
    carry = start_state
    piece = (
        lax.all_gather(keys, "blk", axis=0, tiled=True),
        lax.all_gather(values, "blk", axis=0, tiled=True),
    )
    count = piece[0].shape[0]
    size = math.gcd(count, 512)
    steps = count // size
    key_blocks = piece[0].reshape(steps, size, width)
    value_blocks = piece[1].reshape(steps, size, width)

    def inner(state, item):
        block_keys, block_values, offset = item
        key_item = segment_of(offset + lax.iota(jnp.int32, size), rows, parts, ends)
        return (
            attend_block(query, query_item, block_keys, block_values, key_item, scale, state),
            None,
        )

    carry, unused = lax.scan(
        inner, carry, (key_blocks, value_blocks, lax.iota(jnp.int32, steps) * size)
    )
    best, total, weighted = carry
    logsum = best + jnp.log(total)
    attended = (weighted / total[..., None]).transpose(1, 0, 2).reshape(rows, width)
    attended_low = attended.astype(jnp.bfloat16)
    branch = jnp.dot(attended_low, w_out, preferred_element_type=jnp.float32) + bias_o
    mid = inputs + scale_one * branch
    normed_two, norm_two_pull = jax.vjp(norm_rows, mid, gain_two, shift_two)
    normed_two_low = normed_two.astype(jnp.bfloat16)
    before = jnp.dot(normed_two_low, w_up, preferred_element_type=jnp.float32) + bias_up
    activated, gelu_pull = jax.vjp(exact_gelu, before)
    activated_low = activated.astype(jnp.bfloat16)
    feed = jnp.dot(activated_low, w_down, preferred_element_type=jnp.float32) + bias_d
    result = mid + scale_two * feed
    out = (result * valid).astype(jnp.bfloat16)
    d_result = cotangent[0].astype(jnp.float32) * valid
    d_feed = (scale_two * d_result).astype(jnp.bfloat16)
    g_scale_two = jnp.sum(d_result * feed, axis=0)
    g_bias_d = jnp.sum(d_feed.astype(jnp.float32), axis=0)
    g_w_down = contract_rows(activated_low, d_feed)
    d_activated = contract_cols(d_feed, w_down)
    d_before = gelu_pull(d_activated)[0].astype(jnp.bfloat16)
    g_bias_up = jnp.sum(d_before.astype(jnp.float32), axis=0)
    g_w_up = contract_rows(normed_two_low, d_before)
    d_normed_two = contract_cols(d_before, w_up)
    d_mid_norm, g_gain_two, g_shift_two = norm_two_pull(d_normed_two)
    d_mid = d_result + d_mid_norm
    d_branch = (scale_one * d_mid).astype(jnp.bfloat16)
    g_scale_one = jnp.sum(d_mid * branch, axis=0)
    g_bias_o = jnp.sum(d_branch.astype(jnp.float32), axis=0)
    g_w_out = contract_rows(attended_low, d_branch)
    d_attended = contract_cols(d_branch, w_out).astype(jnp.bfloat16)
    d_heads = d_attended.reshape(rows, heads, head_size)
    delta = jnp.sum(
        (d_attended.astype(jnp.float32) * attended).reshape(rows, heads, head_size), axis=-1
    ).T
    zero_query = jnp.zeros((rows, heads, head_size), jnp.float32)

    def visit_block(block_keys, block_values, owner):
        key_item = segment_of(owner * rows + lax.iota(jnp.int32, rows), rows, parts, ends)
        return grad_block(
            query, d_heads, logsum, delta, query_item, block_keys, block_values, key_item, scale
        )

    def send_back(d_keys, d_values):
        return (
            passed_along(d_keys.astype(jnp.bfloat16), "blk", 1).astype(d_keys.dtype),
            passed_along(d_values.astype(jnp.bfloat16), "blk", 1).astype(d_values.dtype),
        )

    def accumulate(state, owner):
        d_query, block_keys, block_values, d_keys, d_values = state
        dq_part, dk_part, dv_part = visit_block(block_keys, block_values, owner)
        d_keys, d_values = send_back(d_keys + dk_part, d_values + dv_part)
        return (d_query + dq_part, d_keys, d_values)

    def turn(step, state):
        owner = (position - step) % parts
        d_query, d_keys, d_values = accumulate(state, owner)
        block_keys, block_values = passed_along((state[1], state[2]), "blk", 1)
        return (d_query, block_keys, block_values, d_keys, d_values)

    zero_rows = jnp.zeros((rows, width), jnp.float32)
    state = lax.fori_loop(0, parts - 1, turn, (zero_query, keys, values, zero_rows, zero_rows))
    d_query, d_keys, d_values = accumulate(state, (position + 1) % parts)
    d_projected = jnp.concatenate([d_query.reshape(rows, width), d_keys, d_values], axis=1).astype(
        jnp.bfloat16
    )
    g_bias_q = jnp.sum(d_projected[:, :width].astype(jnp.float32), axis=0)
    g_bias_v = jnp.sum(d_projected[:, 2 * width :].astype(jnp.float32), axis=0)
    g_w_qkv = contract_rows(normed_low, d_projected)
    d_normed = contract_cols(d_projected, w_qkv)
    d_input_norm, g_gain_one, g_shift_one = norm_one_pull(d_normed)
    d_inputs = d_mid + d_input_norm
    g_vectors = jnp.concatenate(
        [
            g_gain_one,
            g_shift_one,
            g_bias_q,
            g_bias_v,
            g_bias_o,
            g_scale_one,
            g_gain_two,
            g_shift_two,
            g_bias_d,
            g_scale_two,
            g_bias_up,
        ]
    )
    column_sums = (
        lax.psum_scatter(
            g_w_qkv.astype(jnp.bfloat16), "dp", scatter_dimension=1, tiled=True
        ).astype(jnp.float32),
        lax.psum_scatter(
            g_w_out.astype(jnp.bfloat16), "dp", scatter_dimension=1, tiled=True
        ).astype(jnp.float32),
        lax.psum_scatter(g_w_up.astype(jnp.bfloat16), "dp", scatter_dimension=1, tiled=True).astype(
            jnp.float32
        ),
        lax.psum_scatter(
            g_w_down.astype(jnp.bfloat16), "dp", scatter_dimension=1, tiled=True
        ).astype(jnp.float32),
        lax.psum_scatter(
            g_vectors.astype(jnp.bfloat16), "dp", scatter_dimension=0, tiled=True
        ).astype(jnp.float32),
    )
    g_w_qkv, g_w_out, g_w_up, g_w_down, g_vectors = (
        lax.psum_scatter(
            column_sums[0].astype(jnp.bfloat16), "blk", scatter_dimension=0, tiled=True
        ).astype(jnp.float32),
        lax.psum_scatter(
            column_sums[1].astype(jnp.bfloat16), "blk", scatter_dimension=0, tiled=True
        ).astype(jnp.float32),
        lax.psum_scatter(
            column_sums[2].astype(jnp.bfloat16), "blk", scatter_dimension=0, tiled=True
        ).astype(jnp.float32),
        lax.psum_scatter(
            column_sums[3].astype(jnp.bfloat16), "blk", scatter_dimension=0, tiled=True
        ).astype(jnp.float32),
        lax.psum_scatter(
            column_sums[4].astype(jnp.bfloat16), "blk", scatter_dimension=0, tiled=True
        ).astype(jnp.float32),
    )
    return (
        out[None],
        d_inputs.astype(jnp.bfloat16)[None],
        g_w_qkv,
        g_w_out,
        g_w_up,
        g_w_down,
        g_vectors,
    )


BF = jnp.bfloat16
F32 = jnp.float32
MASKED = -1e30
GRANT = 60 * 1024 * 1024
STEP_GRANT = 20 * 1024 * 1024
LATE_GRANT = 32 * 1024 * 1024
WIDE_CHUNK = 128


def unit_tables():
    lists, places = np.zeros((2, 2, 2, 6), np.int32), np.zeros((2, 2, 4, 3), np.int32)
    units = {core: [unit for unit in range(24) if unit // 4 % 2 == core] for core in range(2)}
    for y in range(2):
        for low_z in range(2):
            first = {}
            for core in range(2):
                own = [unit for unit in units[core] if unit // 3 % 2 == y]
                first[core] = [unit for unit in own if unit // 6 % 2 == low_z]
                rest = [unit for unit in own if unit // 6 % 2 != low_z]
                lists[core, y, low_z] = [units[core].index(unit) for unit in first[core] + rest]
            for core in range(2):
                held = first[core] + first[1 - core]
                for z in (low_z, low_z + 2):
                    places[core, y, z] = [held.index(3 * (2 * z + y) + index) for index in range(3)]
    return np.concatenate([lists.reshape(-1), places.reshape(-1)])


UNIT_TABLE = unit_tables()
UNIT_LIST = 4
ENDS = UNIT_LIST + UNIT_TABLE.size


def dot_nn(left, right):
    return lax.dot_general(left, right, (((1,), (0,)), ((), ())), preferred_element_type=F32)


def dot_nt(left, right):
    return lax.dot_general(left, right, (((1,), (1,)), ((), ())), preferred_element_type=F32)


def dot_tn(left, right):
    return lax.dot_general(left, right, (((0,), (0,)), ((), ())), preferred_element_type=F32)


def standardise(values):
    centred = values - jnp.mean(values, axis=-1, keepdims=True)
    inverse = lax.rsqrt(jnp.mean(centred * centred, axis=-1, keepdims=True) + EPSILON)
    return centred * inverse, inverse


def standardise_grad(grad, xhat, inverse):
    first = jnp.mean(grad, axis=-1, keepdims=True)
    second = jnp.mean(grad * xhat, axis=-1, keepdims=True)
    return (grad - first - xhat * second) * inverse


def column_sum(values):
    return jnp.sum(values, axis=0, keepdims=True)


def item_at(place, where_ref, items):
    found = jnp.zeros_like(place)
    for index in range(items):
        found = found + (place >= where_ref[ENDS + index]).astype(jnp.int32)
    return found


def own_block(where_ref, rel_x, rel_c):
    return 2 * (where_ref[0] ^ rel_x) + (where_ref[1] ^ rel_c)


def low(*shape):
    return jax.ShapeDtypeStruct(shape, BF)


def full(*shape):
    return jax.ShapeDtypeStruct(shape, F32)


def lanes_at(index, size):
    return pl.ds(pl.multiple_of(index * size, size), size)


class Stage:
    def __init__(self, reads, places, writes):
        self.reads, self.places, self.writes = reads, places, writes
        self.started, self.waited, self.begun = set(), set(), []

    def start(self, *indices):
        for index in indices:
            if index not in self.started:
                self.started.add(index)
                for copy in self.reads[index]:
                    copy.start()

    def __getitem__(self, index):
        self.start(index)
        if index not in self.waited:
            self.waited.add(index)
            for copy in self.reads[index]:
                copy.wait()
        return self.places[index]

    def out(self, index):
        return self.writes[index][0]

    def put(self, *indices):
        for index in indices:
            self.writes[index][1].start()
            self.begun.append(index)

    def finish(self):
        for index in range(len(self.reads)):
            self[index]
        self.put(*(index for index in range(len(self.writes)) if index not in self.begun))
        for place, copy in self.writes:
            copy.wait()


class Place:
    def __init__(self, lengths_ref, table_ref):
        position, turn = lax.axis_index("blk"), lax.axis_index("dp")
        self.four = (position // 2, position % 2, turn // 2, turn % 2)
        self.table_ref = table_ref
        self.ends, end = [], jnp.int32(0)
        for index in range(lengths_ref.shape[1]):
            end = end + lengths_ref[0, index]
            self.ends.append(end)

    def __getitem__(self, index):
        if isinstance(index, int) and index < UNIT_LIST:
            return self.four[index]
        if isinstance(index, int) and index >= ENDS:
            return self.ends[index - ENDS]
        return self.table_ref[index - UNIT_LIST]


def unpack_rows(raw_ref, vec_ref):
    count = vec_ref.shape[1] // 128
    for row in range(vec_ref.shape[0]):
        for part in range(count):
            vec_ref[row : row + 1, part * 128 : (part + 1) * 128] = raw_ref[row * count + part : row * count + part + 1]


def staged_call(body, where, operands, out_shape, cuts=None, scratch=(), late=(), pairs=(), tables=False, grant=GRANT):
    cuts = cuts or {}
    count, results = len(operands), len(out_shape)
    shapes, parts = [], []
    for index, operand in enumerate(operands):
        shape, pieces = (operand.shape, 1) if index not in cuts else cuts[index][:2]
        shapes.append(pltpu.VMEM(shape, operand.dtype))
        parts.append(pieces)
    held_shapes, held_at = [], {}
    for index, item in enumerate(out_shape):
        if index - 1 in pairs:
            held_at[index] = (len(held_shapes) - 1, 1)
        elif index in pairs:
            held_at[index] = (len(held_shapes), 0)
            held_shapes.append(pltpu.VMEM((2, *item.shape), item.dtype))
        else:
            held_at[index] = (len(held_shapes), None)
            held_shapes.append(pltpu.VMEM(item.shape, item.dtype))

    def kernel(*refs):
        where_ref = Place(refs[0], refs[1] if tables else None)
        refs = refs[2 if tables else 1 :]
        ins, outs = refs[:count], refs[count : count + results]
        places = refs[count + results : 2 * count + results]
        held = refs[2 * count + results : 2 * count + results + len(held_shapes)]
        read_sem, write_sem, *rest = refs[2 * count + results + len(held_shapes) :]
        reads, used = [], 0
        for index in range(count):
            moves = [(ins[index], places[index])] if index not in cuts else cuts[index][2](where_ref, ins[index], places[index])
            reads.append([])
            for source, target in moves:
                reads[-1].append(pltpu.make_async_copy(source, target, read_sem.at[used]))
                used += 1
        writes = []
        for index in range(results):
            place, entry = held_at[index]
            source = held[place] if entry is None else held[place].at[entry]
            writes.append((held[place], pltpu.make_async_copy(source, outs[index], write_sem.at[index])))
        stage = Stage(reads, places, writes)
        stage.start(*(index for index in range(count) if index not in late))
        body(where_ref, stage, *rest)
        stage.finish()

    return pl.pallas_call(
        kernel,
        in_specs=[pl.BlockSpec(memory_space=pltpu.SMEM)] * (2 if tables else 1)
        + [pl.BlockSpec(memory_space=pl.ANY)] * count,
        out_specs=[pl.BlockSpec(memory_space=pl.ANY)] * results,
        out_shape=out_shape,
        scratch_shapes=shapes
        + held_shapes
        + [pltpu.SemaphoreType.DMA((sum(parts),)), pltpu.SemaphoreType.DMA((results,))]
        + list(scratch),
        compiler_params=pltpu.CompilerParams(vmem_limit_bytes=grant),
    )(where, *((UNIT_TABLE,) if tables else ()), *operands)


def each(count, body):
    def step(index, carry):
        body(index)
        return carry

    lax.fori_loop(0, count, step, 0)


def hidden_unit(where_ref, rel_x, side):
    return 4 * (where_ref[0] ^ rel_x) + 2 * where_ref[1] + side


def lanes_below(shape, count):
    return lax.broadcasted_iota(jnp.int32, shape, 1) < count


def stack_heads(pair):
    first = lanes_below(pair.shape, HEAD_SIZE)
    zero = jnp.zeros_like(pair)
    return jnp.concatenate([jnp.where(first, pair, zero), jnp.where(first, zero, pair)], axis=0)


def turn(source, target):
    each(source.shape[1] // 128, lambda index: target.__setitem__(lanes_at(index, 128), source[:, lanes_at(index, 128)].T))


def valid_at(where_ref, rel_c, first, count, parts, items):
    row = first + lax.broadcasted_iota(jnp.int32, (count, 1), 0)
    item = item_at(row * parts + own_block(where_ref, 0, rel_c), where_ref, items)
    return (item < items).astype(F32)


def normed_rows(xhat, vec_ref, first):
    return (xhat.astype(F32) * vec_ref[first : first + 1] + vec_ref[first + 1 : first + 2]).astype(BF)


def prepare_kernel(parts, items, where_ref, stage, vec_ref, held, normed_ref, row_ref):
    unpack_rows(stage[2], vec_ref)
    own_ref, sib_ref = stage[0], stage[1]
    stage.start(3, 4, 5, 6)
    xhat_ref, qkv_ref, dact_ref, turned_ref, sum_ref = (stage.out(index) for index in range(5))
    rows, width = own_ref.shape
    half = width // 2
    core = where_ref[1]
    for rel_c, ref in enumerate((own_ref, sib_ref)):

        def norm(index, rel_c=rel_c, ref=ref):
            xhat, unused = standardise(ref[lanes_at(index, WIDE_CHUNK)].astype(F32))
            to = lanes_at(index + rel_c * (rows // WIDE_CHUNK), WIDE_CHUNK)
            xhat_ref[to] = xhat.astype(BF)
            normed_ref[to] = (xhat * vec_ref[0:1] + vec_ref[1:2]).astype(BF)

        each(rows // WIDE_CHUNK, norm)
    stage.put(0)
    sum_ref[...] = jnp.zeros_like(sum_ref)
    for rel_c in range(2):

        def grad(index, rel_c=rel_c, ref=stage[4 + rel_c]):
            valid = valid_at(where_ref, rel_c, index * WIDE_CHUNK, WIDE_CHUNK, parts, items)
            part = (vec_ref[9:10] * (ref[lanes_at(index, WIDE_CHUNK)].astype(F32) * valid)).astype(BF)
            held[lanes_at(index + rel_c * (rows // WIDE_CHUNK), WIDE_CHUNK)] = part
            if rel_c == 0:
                sum_ref[...] += column_sum(part.astype(F32))

        each(rows // WIDE_CHUNK, grad)
    turn(held, turned_ref)
    stage.put(3, 4)
    row_ref[0:1, :half] = vec_ref[2:3, lanes_at(core, half)]
    row_ref[0:1, half : 2 * half] = jnp.zeros((1, half), F32)
    row_ref[0:1, 2 * half :] = vec_ref[3:4, lanes_at(core, half)]
    row_ref[1:2, :half] = jnp.full((1, half), HEAD_SIZE ** (-0.5), F32)
    row_ref[1:2, half:] = jnp.ones((1, 2 * half), F32)
    weight_ref = stage[3]

    def project(index):
        lanes = lanes_at(index, half)
        part = dot_nn(normed_ref[...], weight_ref[:, lanes]) + row_ref[0:1, lanes]
        qkv_ref[:, lanes] = (part.astype(BF).astype(F32) * row_ref[1:2, lanes]).astype(BF)

    each(3, project)
    stage.put(1)
    down_ref = stage[6]
    piece = dact_ref.shape[1] // 4

    def back(index):
        dact_ref[:, lanes_at(index, piece)] = dot_nt(held[...], down_ref[lanes_at(index, piece)]).astype(BF)

    each(4, back)


def item_of_place(where_ref, place, items):
    found = jnp.int32(0)
    for index in range(items):
        found = found + (place >= where_ref[ENDS + index]).astype(jnp.int32)
    return found


def tiles_meet(where_ref, one, other, parts, items):
    span = TILE * parts
    first, last = min(one, other), max(one, other)
    return item_of_place(where_ref, first * span + span - 1, items) >= item_of_place(
        where_ref, last * span, items
    )


def near_tiles(tile, tiles):
    return max(0, tile - 1), min(tiles, tile + 2)


def far_pairs(tiles):
    return [(one, other) for one in range(tiles) for other in range(tiles) if abs(one - other) > 1]


def any_far(where_ref, tiles, parts, items):
    found = jnp.bool_(False)
    for one, other in far_pairs(tiles):
        if one < other:
            found = found | tiles_meet(where_ref, one, other, parts, items)
    return found


def attend_kernel(parts, items, where_ref, stage, vec_ref, wide_ref, normed_ref, asks_ref):
    unpack_rows(stage[2], vec_ref)
    xhat_ref, kv_ref, attended_ref, logsum_ref = (stage.out(index) for index in range(4))
    far_a_ref, far_b_ref = stage[0], stage[1]
    stage.start(3, 4)
    rows, width = far_a_ref.shape
    tiles = rows // TILE
    span = parts * TILE
    both = 2 * HEAD_SIZE
    half = width // 2
    core = where_ref[1]
    for rel_c, ref in enumerate((far_a_ref, far_b_ref)):
        xhat, unused = standardise(ref[...].astype(F32))
        xhat_ref[rel_c * rows : (rel_c + 1) * rows] = xhat.astype(BF)
        normed_ref[rel_c * rows : (rel_c + 1) * rows] = normed_rows(xhat, vec_ref, 0)
    stage.put(0)
    row = lax.broadcasted_iota(jnp.int32, (2 * TILE, 2 * TILE), 0)
    block = 2 * where_ref[0] + (where_ref[1] ^ (row // TILE))
    for tile in range(tiles):
        asks_ref[tile] = item_at((tile * TILE + row % TILE) * parts + block, where_ref, items)
    lane = lax.broadcasted_iota(jnp.int32, (1, span), 1)
    slot = lane // TILE
    block = 2 * (where_ref[0] ^ (slot // 2)) + (where_ref[1] ^ (slot % 2))
    key_item = [item_at((tile * TILE + lane % TILE) * parts + block, where_ref, items) for tile in range(tiles)]
    weight_ref = stage[3]
    row_ref = jnp.concatenate([jnp.zeros((1, half), F32), vec_ref[3:4, lanes_at(core, half)]], axis=1)
    far_kv = (dot_nn(normed_ref[...], weight_ref[...]) + row_ref).astype(BF)
    qkv_ref = stage[4]
    for tile in range(tiles):
        for slot in range(2):
            at = slice(slot * rows + tile * TILE, slot * rows + (tile + 1) * TILE)
            kv_ref[tile * span + slot * TILE : tile * span + (slot + 1) * TILE] = qkv_ref[at, half:]
            kv_ref[tile * span + (slot + 2) * TILE : tile * span + (slot + 3) * TILE] = far_kv[at]
    stage.put(1)
    for index in range(half // both):
        wide_ref[:, 2 * index * both : (2 * index + 1) * both] = kv_ref[:, half + index * both : half + (index + 1) * both]
        wide_ref[:, (2 * index + 1) * both : (2 * index + 2) * both] = jnp.ones((tiles * span, both), BF)

    def attend(index, tile, first, last):
        lanes = lanes_at(index, both)
        at = slice(first * span, last * span)
        places = [pl.ds(pl.multiple_of(rel_c * rows + tile * TILE, TILE), TILE) for rel_c in range(2)]
        query = stack_heads(jnp.concatenate([qkv_ref[place, lanes] for place in places], axis=0))
        score = dot_nt(query, kv_ref[at, lanes])
        asked = asks_ref[tile][:, :1]
        allowed = jnp.concatenate([asked == key_item[other] for other in range(first, last)], axis=1)
        score = jnp.where(jnp.concatenate([allowed, allowed], axis=0), score, MASKED)
        best = jnp.max(score, axis=1, keepdims=True)
        weight = jnp.exp(score - best).astype(BF)
        mixed = dot_nn(weight, wide_ref[at, lanes_at(index, 2 * both)])
        total = mixed[:, both:]
        logsum_ref[index, pl.ds(tile, 1)] = (best + jnp.log(total)).T[:1]
        mixed = mixed[:, :both] / total
        attended = jnp.where(lanes_below((both, both), HEAD_SIZE), mixed[:both], mixed[both:]).astype(BF)
        for rel_c, place in enumerate(places):
            attended_ref[place, lanes] = attended[rel_c * TILE : (rel_c + 1) * TILE]

    def pair(index):
        for tile in range(tiles):
            attend(index, tile, *near_tiles(tile, tiles))

    each(half // both, pair)

    @pl.when(any_far(where_ref, tiles, parts, items))
    def far():
        def again(step):
            tile = step % tiles
            found = jnp.bool_(False)
            for one, other in far_pairs(tiles):
                found = found | ((tile == one) & tiles_meet(where_ref, one, other, parts, items))
            pl.when(found)(lambda: attend(step // tiles, tile, 0, tiles))

        each(half // both * tiles, again)


def gelu_with_slope(values):
    bell = jnp.exp(-0.5 * values * values)
    inverse = 1.0 / (1.0 + (0.3275911 * 0.5**0.5) * jnp.abs(values))
    series = 1.061405429
    for coefficient in (-1.453152027, 1.421413741, -0.284496736, 0.254829592):
        series = series * inverse + coefficient
    tail = 0.5 * (series * inverse) * bell
    normal = jnp.where(values >= 0, 1.0 - tail, tail)
    return values * normal, normal + values * bell * ((2.0 * math.pi) ** -0.5)


def set_block(where_ref, rel_y, low_z, high_z):
    return 2 * (where_ref[2] ^ (low_z + 2 * high_z)) + (where_ref[3] ^ rel_y)


def mlp_kernel(where_ref, stage, vec_ref, bias_ref, mid_ref, joined, normed, grad, turned, dbefore_ref):
    py_ref, ux_ref, dz_ref = stage.out(0), stage.out(2), stage.out(4)
    xhat_ref, inverse_ref, mid_own_ref, branch_ref, swap_ref, act_ref, bias_sum_ref = (
        stage.out(index) for index in range(6, 13)
    )
    unpack_rows(stage[4], vec_ref)
    att_own_ref, att_sib_ref, own_ref, sib_ref, raw_ref, out_ref = (stage[index] for index in range(6))
    stage.start(6, 7, 8)
    x, core, z, y = (where_ref[index] for index in range(4))
    rows, width = own_ref.shape
    half = width // 2
    piece = act_ref.shape[1] // 4
    joined[:, :half] = att_own_ref[...]
    joined[:rows, half:] = att_sib_ref[rows:]
    joined[rows:, half:] = att_sib_ref[:rows]

    def project(index):
        lanes = lanes_at(index, 256)
        branch = dot_nn(joined[...], out_ref[:, lanes]) + vec_ref[4:5, lanes]
        branch_ref[:, lanes] = branch[:rows].astype(BF)
        branch = vec_ref[5:6, lanes] * branch
        mid_ref[:rows, lanes] = own_ref[:, lanes].astype(F32) + branch[:rows]
        mid_ref[rows:, lanes] = sib_ref[:, lanes].astype(F32) + branch[rows:]

    each(width // 256, project)

    mid_own_ref[...] = mid_ref[:rows]

    def norm(index):
        at = lanes_at(index, WIDE_CHUNK)
        xhat, inverse = standardise(mid_ref[at])
        normed[at] = (xhat * vec_ref[6:7] + vec_ref[7:8]).astype(BF)
        xhat_ref[at] = xhat.astype(BF)
        inverse_ref[at] = inverse

    each(2 * rows // WIDE_CHUNK, norm)
    stage.put(6, 7, 8, 9)
    count = piece // 128
    for unit in range(8):
        for part in range(count):
            row = 10 * width // 128 + unit * count + part
            bias_ref[unit : unit + 1, part * 128 : (part + 1) * 128] = raw_ref[row : row + 1]
    up_ref, dact_ref, turned_ref = stage[6], stage[7], stage[8]
    size = grad.shape[0] // 8

    def hidden(index):
        rel_x = 1 - index
        count = normed.shape[0] // 2
        for side in range(2):
            at = lanes_at(2 * rel_x + side, piece)
            bias = bias_ref[pl.ds(hidden_unit(where_ref, rel_x, side), 1)]
            total = jnp.zeros((1, piece), F32)
            for part in range(2):
                here = slice(part * count, (part + 1) * count)
                act, slope = gelu_with_slope(dot_nn(normed[here], up_ref[:, at]) + bias)
                act_ref[here, at] = act.astype(BF)
                dbefore = (dact_ref[here, at].astype(F32) * slope).astype(BF)
                dbefore_ref[here, at] = dbefore
                total = total + column_sum(dbefore.astype(F32))
            bias_sum_ref[:, at] = total
            grad[:, side * piece : (side + 1) * piece] = dot_nn(turned_ref[...], act_ref[:, at]).astype(BF)

        def lay(index):
            low_z, high_z, rel_y = index // 4, index // 2 % 2, index % 2
            first = set_block(where_ref, rel_y, low_z, high_z) * size
            most = dz_ref.shape[4] - size
            dz_ref[low_z, high_z, rel_x, rel_y, :size] = grad[pl.ds(pl.multiple_of(first, size), size), :piece]
            dz_ref[low_z, high_z, rel_x, rel_y, size:] = grad[pl.ds(pl.multiple_of(first, size), most), piece:]
            py_ref[rel_y, rel_x, lanes_at(2 * low_z + high_z, size - most)] = grad[
                pl.ds(pl.multiple_of(first + most, size - most), size - most), piece:
            ]

        each(8, lay)

    each(2, hidden)
    stage.put(4, 5, 11, 12)
    turn(normed, turned)
    block = 2 * size

    def up(index):
        rel_y, high_z = index // 2, index % 2
        unit = 2 * (x ^ (z // 2) ^ high_z) + (y ^ rel_y)
        grad[:, :piece] = dot_nn(turned[...], dbefore_ref[:, lanes_at(unit, piece)]).astype(BF)
        for rel_x in range(2):
            to = pl.ds(pl.multiple_of(py_ref.shape[2] - 2 * block + high_z * block, 64), block)
            py_ref[rel_y, rel_x, to] = grad[lanes_at(own_block(where_ref, rel_x, 0), block), :piece]
            ux_ref[rel_x, rel_y, high_z] = grad[lanes_at(own_block(where_ref, rel_x, 1), block), :piece]

    for index in range(4):
        up(index)
    stage.put(0, 1, 2, 3)

    def back(index):
        lanes = lanes_at(index, 256)
        total = dot_nt(dbefore_ref[...], up_ref[lanes])
        swap_ref[:, lanes] = total.astype(BF)

    each(width // 256, back)


def middle(parts, items, where_ref, stage, vec_ref, sum_ref, datt_ref, held, chosen, packed):
    dmid_ref, a_ref, o_ref = stage.out(0), stage.out(1), stage.out(5)
    keep_ref, got_ref, xhat_ref, inverse_ref, own_ref, sib_ref, raw_ref = (stage[index] for index in range(7))
    stage.start(10, 9, 7, 8, 11, 12, 13)
    unpack_rows(raw_ref, vec_ref)
    rows, width = own_ref.shape
    half = width // 2
    core = where_ref[1]
    left_is_own = lanes_below((rows, half), half // 2) == (core == 0)
    for rel_c, ref in enumerate((own_ref, sib_ref)):
        here = slice(rel_c * rows, (rel_c + 1) * rows)
        there = slice((1 - rel_c) * rows, (2 - rel_c) * rows)
        valid = valid_at(where_ref, rel_c, 0, rows, parts, items)
        dnormed = keep_ref[here].astype(F32) + got_ref[there].astype(F32)
        xhat, inverse = xhat_ref[here].astype(F32), inverse_ref[here]
        dmid = ref[...].astype(F32) * valid + standardise_grad(vec_ref[6:7] * dnormed, xhat, inverse)
        dbranch = (vec_ref[5:6] * dmid).astype(BF)
        held[here] = dbranch
        if rel_c == 0:
            dmid_ref[...] = dmid
            sum_ref[0:1] = column_sum(dbranch.astype(F32))
            sum_ref[1:2] = column_sum(dmid * stage[10][...].astype(F32))
            sum_ref[2:3] = column_sum(dnormed * xhat)
            sum_ref[3:4] = column_sum(dnormed)
    stage.put(0)
    stage.start(14, 15)
    datt_ref[...] = dot_nt(held[...], stage[9][...]).astype(BF)
    att_own_ref, att_sib_ref = stage[7], stage[8]
    for rel_c in range(2):
        here = slice(rel_c * rows, (rel_c + 1) * rows)
        there = slice((1 - rel_c) * rows, (2 - rel_c) * rows)
        other = pltpu.roll(att_sib_ref[there].astype(F32), half // 2, 1)
        chosen[here] = jnp.where(left_is_own, att_own_ref[here].astype(F32), other).astype(BF)
    grad = dot_tn(held[...], chosen[...])
    count, unit_rows = packed.shape[1:3]
    for index in range(count):
        left, right = pack_unit(grad[2 * index * unit_rows : 2 * (index + 1) * unit_rows])
        packed[0, index] = left.astype(BF)
        packed[1, index] = right.astype(BF)

    units = 6 * unit_rows

    def lay(index):
        rel_x, rel_y, block = index // 8, index // 4 % 2, index % 4
        here = packed.at[where_ref[0] ^ rel_x, set_block(where_ref, rel_y, block // 2, block % 2)]
        a_ref[rel_x, rel_y, pl.ds(pl.multiple_of(units + 16 * block, 16), 16)] = here[:16]
        o_ref[rel_y, rel_x, lanes_at(block, unit_rows - 16)] = here[16:]

    each(16, lay)
    stage.put(5, 6)


def pack_unit(unit):
    half = unit.shape[0] // 2
    width = unit.shape[1]
    top, bottom = unit[:half], unit[half:]
    first = lanes_below((half, width), width // 2)
    left = jnp.where(first, top, pltpu.roll(bottom, width // 2, 1))
    right = jnp.where(first, pltpu.roll(top, width // 2, 1), bottom)
    return left, right


def join_heads(stacked_turned):
    stacked = stacked_turned.T
    count = stacked.shape[0] // 2
    return jnp.where(
        lanes_below((count, stacked.shape[1]), HEAD_SIZE), stacked[:count], stacked[count:]
    )


def query_items(where_ref, tile, parts, items):
    lane = lax.broadcasted_iota(jnp.int32, (1, 4 * TILE), 1)
    rel_c = (lane // TILE) % 2
    block = 2 * where_ref[0] + (where_ref[1] ^ rel_c)
    return item_at((tile * TILE + lane % TILE) * parts + block, where_ref, items)


def fill_key_items(where_ref, item_ref, tiles, parts, items):
    row = lax.broadcasted_iota(jnp.int32, (TILE, item_ref.shape[1]), 0)
    for tile in range(tiles):
        for slot in range(parts):
            block = own_block(where_ref, slot // 2, slot % 2)
            at = (tile * parts + slot) * TILE
            item_ref[at : at + TILE] = item_at((tile * TILE + row) * parts + block, where_ref, items)


def both_heads(array):
    return jnp.concatenate([array, array], axis=1)


def attend_grad(
    parts, items, where_ref, stage, datt_ref, dquery_ref, dkeys_ref, dvalues_ref, asks_ref, item_ref, turned_ref, dk, dv, dq
):
    attended_ref, qkv_ref, kv_ref, logsum_ref = stage[7], stage[11], stage[12], stage[13]
    half = datt_ref.shape[1]
    rows = datt_ref.shape[0] // 2
    tiles = rows // TILE
    span = parts * TILE
    scale = HEAD_SIZE ** (-0.5)
    turned_ref[...] = kv_ref[:, :half].T
    fill_key_items(where_ref, item_ref, tiles, parts, items)
    for tile in range(tiles):
        asks_ref[tile : tile + 1] = query_items(where_ref, tile, parts, items)
    some_far = any_far(where_ref, tiles, parts, items)

    def pair(index, carry):
        lanes = lanes_at(index, 2 * HEAD_SIZE)
        value_lanes = pl.ds(pl.multiple_of(half + index * 2 * HEAD_SIZE, 2 * HEAD_SIZE), 2 * HEAD_SIZE)
        dk[...] = jnp.zeros_like(dk)
        dv[...] = jnp.zeros_like(dv)

        def places(tile):
            return [pl.ds(pl.multiple_of(rel_c * rows + tile * TILE, TILE), TILE) for rel_c in range(2)]

        def visit(tile, at):
            query = stack_heads(jnp.concatenate([qkv_ref[place, lanes] for place in places(tile)], axis=0))
            grad = jnp.concatenate([datt_ref[place, lanes] for place in places(tile)], axis=0)
            attended = jnp.concatenate([attended_ref[place, lanes] for place in places(tile)], axis=0)
            product = (grad.astype(F32) * attended.astype(F32)).T
            delta = jnp.concatenate([column_sum(product[:HEAD_SIZE]), column_sum(product[HEAD_SIZE:])], axis=1)
            grad = stack_heads(grad)
            score = dot_nt(kv_ref[at, lanes], query)
            allowed = both_heads(item_ref[at]) == asks_ref[pl.ds(tile, 1)]
            prob = jnp.exp(jnp.where(allowed, score, MASKED) - logsum_ref[index, pl.ds(tile, 1)])
            dprob = dot_nt(kv_ref[at, value_lanes], grad)
            dscore = (prob * (dprob - delta)).astype(BF)
            dv[at] += dot_nn(prob.astype(BF), grad)
            dk[at] += dot_nn(dscore, query)
            return dot_nn(turned_ref[lanes, at], dscore)

        for tile in range(tiles):
            first, last = near_tiles(tile, tiles)
            dq[tile] = visit(tile, slice(first * span, last * span))

        @pl.when(some_far)
        def far():
            def add(step):
                tile, other = step // tiles, step % tiles
                found = jnp.bool_(False)
                for one, two in far_pairs(tiles):
                    found = found | ((step == one * tiles + two) & tiles_meet(where_ref, one, two, parts, items))

                @pl.when(found)
                def meet():
                    at = pl.ds(pl.multiple_of(other * span, span), span)
                    dq[tile] += visit(tile, at)

            each(tiles * tiles, add)

        for tile in range(tiles):
            dquery = (join_heads(dq[tile]) * scale).astype(BF)
            for rel_c, place in enumerate(places(tile)):
                dquery_ref[place, lanes] = dquery[rel_c * TILE : (rel_c + 1) * TILE]
            for slot in range(parts):
                to = slice(slot * rows + tile * TILE, slot * rows + (tile + 1) * TILE)
                at = slice(tile * span + slot * TILE, tile * span + (slot + 1) * TILE)
                dkeys_ref[to, lanes] = dk[at].astype(BF)
                dvalues_ref[to, lanes] = dv[at].astype(BF)
        return carry

    for index in range(half // (2 * HEAD_SIZE)):
        pair(index, 0)


def twice(half_row, where_ref):
    row = both_heads(half_row)
    return jnp.where(lanes_below(row.shape, half_row.shape[1]) == (where_ref[1] == 0), row, 0.0)


def qkv_grad(where_ref, stage, vec_ref, sum_ref, dquery_ref, dkeys_ref, dvalues_ref, normed_ref, packed):
    a_ref, b_ref = stage.out(1), stage.out(3)
    near_ref, far_ref = stage[14], stage[15]
    rows, width = near_ref.shape
    core, z, y = where_ref[1], where_ref[2], where_ref[3]
    normed_ref[:rows] = normed_rows(near_ref[...], vec_ref, 0)
    normed_ref[rows:] = normed_rows(far_ref[...], vec_ref, 0)
    sum_ref[4:5] = twice(column_sum(dquery_ref[...].astype(F32)), where_ref)
    sum_ref[5:6] = twice(column_sum(dvalues_ref[...].astype(F32)), where_ref)
    for part, ref in enumerate((dquery_ref, dkeys_ref, dvalues_ref)):
        grad = dot_tn(ref[...], normed_ref[: ref.shape[0]])
        size = grad.shape[0] // 4
        for unit in range(4):
            for at_x in range(2):
                left, right = pack_unit(
                    grad[unit * size : (unit + 1) * size, at_x * width // 2 : (at_x + 1) * width // 2]
                )
                packed[2 * at_x, 4 * part + unit] = left.astype(BF)
                packed[2 * at_x + 1, 4 * part + unit] = right.astype(BF)

    def lay(index):
        rel_x, rel_y, at = index // 12, index // 6 % 2, index % 6
        unit = where_ref[UNIT_LIST + 24 * core + 12 * (y ^ rel_y) + 6 * (z % 2) + at]
        a_ref[rel_x, rel_y, lanes_at(at, packed.shape[2])] = packed[own_block(where_ref, rel_x, 0), unit]
        b_ref[rel_y, rel_x, at] = packed[own_block(where_ref, rel_x, 1), unit]

    each(24, lay)
    stage.put(1, 2, 3, 4)


def backward_kernel(
    parts, items, where_ref, stage, vec_ref, datt_ref, held, chosen, gpacked, normed_ref, packed, asks_ref, item_ref,
    turned_ref, dk, dv, dq,
):
    sum_ref, dquery_ref, dkeys_ref, dvalues_ref = (stage.out(index) for index in (10, 7, 8, 9))
    middle(parts, items, where_ref, stage, vec_ref, sum_ref, datt_ref, held, chosen, gpacked)
    attend_grad(
        parts, items, where_ref, stage, datt_ref, dquery_ref, dkeys_ref, dvalues_ref, asks_ref, item_ref, turned_ref,
        dk, dv, dq,
    )
    stage.put(7, 8, 9)
    qkv_grad(where_ref, stage, vec_ref, sum_ref, dquery_ref, dkeys_ref, dvalues_ref, normed_ref, packed)


def tokens_grad_kernel(parts, items, where_ref, stage, vec_ref):
    own_ref, far_ref, send_ref, keep_ref, sum_ref = (stage.out(index) for index in range(5))
    dquery_ref, dkeys_ref, dvalues_ref, weight_ref, near_ref, beyond_ref = (stage[index] for index in range(6))
    rows, width = own_ref.shape
    half = dquery_ref.shape[1]
    gain = jnp.zeros((1, width), F32)
    shift = gain
    for slot in (1, 3, 2, 0):
        at = slice(slot * rows, (slot + 1) * rows)
        part = dot_nt(dkeys_ref[at], weight_ref[:, half : 2 * half]) + dot_nt(dvalues_ref[at], weight_ref[:, 2 * half :])
        if slot < 2:
            part = part + dot_nt(dquery_ref[at], weight_ref[:, :half])
        xhat = (near_ref if slot < 2 else beyond_ref)[(slot % 2) * rows : (slot % 2 + 1) * rows].astype(F32)
        gain = gain + column_sum(part * xhat)
        shift = shift + column_sum(part)
        if slot % 2:
            send_ref[slot // 2 * rows : (slot // 2 + 1) * rows] = part.astype(BF)
        elif slot:
            far_ref[...] = part.astype(BF)
        else:
            own_ref[...] = part.astype(BF)
    stage.put(0, 1)
    unpack_rows(stage[6], vec_ref)
    act_ref, down_ref, cot_ref, cot_sib_ref, back_ref, bias_d_ref, bias_up_ref = (stage[index] for index in range(7, 14))
    feed = dot_nn(act_ref[...], down_ref[...])
    keep_ref[...] = feed[:rows] + vec_ref[8:9]
    send_ref[2 * rows :] = feed[rows:].astype(BF)
    stage.put(2, 3)
    scale = column_sum(cot_ref[...].astype(F32) * valid_at(where_ref, 0, 0, rows, parts, items) * keep_ref[...])
    scale = scale + column_sum(cot_sib_ref[...].astype(F32) * valid_at(where_ref, 1, 0, rows, parts, items) * feed[rows:])
    sum_ref[0:1] = gain
    sum_ref[1:2] = shift
    sum_ref[2:4] = back_ref[4:6]
    sum_ref[4:8] = back_ref[0:4]
    sum_ref[8:9] = bias_d_ref[...]
    sum_ref[9:10] = scale
    for at_x in range(2):
        one = bias_up_ref[:, at_x * width : (at_x + 1) * width]
        two = bias_up_ref[:, (1 - at_x) * width : (2 - at_x) * width]
        here = jnp.where(where_ref[0] == 0, one, two)
        for at_c in range(2):
            at = 10 + 2 * at_x + at_c
            sum_ref[at : at + 1] = jnp.where(where_ref[1] == at_c, here, 0.0)
    sum_ref[14:] = jnp.zeros((2, width), F32)


def unpack_unit(unit, target, first):
    half, lanes = unit.shape
    target[first : first + half] = unit[:, : target.shape[1]]
    target[first + half : first + 2 * half] = pltpu.roll(unit, lanes // 2, 1)[:, : target.shape[1]]


def sum_of(*terms):
    total = terms[0].astype(F32)
    for term in terms[1:]:
        total = total + term.astype(F32)
    return total


def fold_sums(sums):
    lanes = sums.shape[1] // 2
    return jnp.concatenate([sums[:, :lanes], sums[:, lanes:]], axis=0)


def second_step_kernel(where_ref, stage):
    dz_keep, dz_got, py_keep, py_got, a_ref, ux_keep, ux_got, b_got, o_ref = (stage[index] for index in range(9))
    dz_ref, x_ref, y_ref = (stage.out(index) for index in range(3))
    dz_ref[...] = sum_of(dz_keep[...], dz_got[...]).astype(BF)
    stage.put(0)
    count, rows = py_keep.shape[0], a_ref.shape[1]
    x_ref[:count] = sum_of(py_keep[...], py_got[...]).astype(BF)
    for rel_y in range(2):
        x_ref[count + rel_y * rows : count + (rel_y + 1) * rows] = a_ref[rel_y]
    stage.put(1)
    block = ux_keep.shape[1]
    for high_z in range(2):
        y_ref[high_z * block : (high_z + 1) * block] = sum_of(ux_keep[high_z], ux_got[high_z]).astype(BF)
    unit_rows = b_got.shape[2]
    first = 2 * block
    for rel_x in range(2):
        for index in range(6):
            y_ref[first : first + unit_rows] = b_got[rel_x, index]
            first += unit_rows
    rows = o_ref.shape[1]
    for rel_x in range(2):
        y_ref[first : first + rows] = o_ref[rel_x]
        first += rows


def third_step_kernel(where_ref, stage):
    ux_keep, ux_got, y_got, py_keep, py_got, x_got, b_keep, o_keep = (stage[index] for index in range(8))
    sum_refs, a_keep = [stage[index] for index in range(8, 12)], stage[12]
    send_ref, x_ref, a_ref, keep_ref = (stage.out(index) for index in range(4))
    count = py_keep.shape[0]
    block = ux_keep.shape[1]
    lead = send_ref.shape[1] - block
    same = where_ref[2] % 2 == where_ref[1]
    for high_z in range(2):
        at = slice(4 * lead + high_z * block, 4 * lead + (high_z + 1) * block)
        own = sum_of(py_keep[at], py_got[at], x_got[at])
        sib = sum_of(ux_keep[high_z], ux_got[high_z], y_got[high_z * block : (high_z + 1) * block])
        for side, ref in enumerate((keep_ref, send_ref)):
            at = slice((2 * side + high_z) * lead, (2 * side + high_z + 1) * lead)
            ref[high_z, :lead] = sum_of(py_keep[at], py_got[at], x_got[at]).astype(BF)
            here = jnp.where(same, sib, own) if side else jnp.where(same, own, sib)
            ref[high_z, lead:] = here.astype(BF)
    stage.put(0)
    unit_rows, rows = b_keep.shape[1], o_keep.shape[0]
    units = 6 * unit_rows
    first = 2 * block + units
    for index in range(6):
        at = slice(index * unit_rows, (index + 1) * unit_rows)
        x_ref[at] = sum_of(b_keep[index], y_got[first + index * unit_rows : first + (index + 1) * unit_rows]).astype(BF)
    first += units + rows
    x_ref[units : units + rows] = sum_of(o_keep[...], y_got[first : first + rows]).astype(BF)
    x_ref[units + rows :] = fold_sums(sum_of(*(ref[...] for ref in sum_refs))).astype(BF)
    stage.put(1)
    a_ref[...] = sum_of(a_keep[...], x_got[count + a_keep.shape[0] :]).astype(BF)


def fourth_step_kernel(where_ref, stage):
    a_keep, x_got, a_far, b_keep, y_got, b_far, o_keep, y_rest, x_ref, mlp_keep, mlp_got, dz_keep, dz_got, dz_far = (
        stage[index] for index in range(14)
    )
    send_ref, mlp_ref, dz_ref, mlp_kept, kept_ref, dz_kept, dtok_ref = (stage.out(index) for index in range(7))
    unit_rows, rows = b_keep.shape[1], o_keep.shape[0]
    units, most = 6 * unit_rows, rows // 4
    own = sum_of(a_keep[...], x_got[...], a_far[...]).astype(BF)
    rest = sum_of(o_keep[...], y_rest[...], b_far[units : units + rows]).astype(BF)
    sums = sum_of(x_ref[...], b_far[units + rows :]).astype(BF)
    for side, ref in enumerate((kept_ref, send_ref)):
        ref[: units // 2] = own[side * units // 2 : (side + 1) * units // 2]
        for index in range(3):
            unit = 3 * side + index
            at = slice(unit * unit_rows, (unit + 1) * unit_rows)
            to = slice((3 + index) * unit_rows, (4 + index) * unit_rows)
            ref[to] = sum_of(b_keep[unit], y_got[at], b_far[at]).astype(BF)
        for high_z in range(2):
            first, block = units + high_z * unit_rows, 2 * side + high_z
            ref[first : first + 16] = own[units + 16 * block : units + 16 * (block + 1)]
            ref[first + 16 : first + unit_rows] = rest[block * most : (block + 1) * most]
        ref[units + 2 * unit_rows :] = sums
    stage.put(0)
    mlp_ref[...] = sum_of(mlp_keep[1], mlp_got[1]).astype(BF)
    stage.put(1)
    for side, ref in enumerate((dz_kept, dz_ref)):
        ref[...] = sum_of(dz_keep[side], dz_got[side], dz_far[side]).astype(BF)
    stage.put(2)
    dtok_ref[...] = sum_of(stage[14][...], stage[15][...]).astype(BF)
    stage.put(6)
    mlp_kept[...] = sum_of(mlp_keep[0], mlp_got[0]).astype(BF)


def fifth_step_kernel(where_ref, stage, held):
    kept_ref, last_got, dz_kept, dz_got = (stage[index] for index in range(4))
    send_ref, dz_ref, keep_ref, dz_low_ref = (stage.out(index) for index in range(4))
    core, z, y = where_ref[1], where_ref[2], where_ref[3]
    unit_rows = held.shape[1]
    for index in range(6):
        at = slice(index * unit_rows, (index + 1) * unit_rows)
        held[index] = sum_of(kept_ref[at], last_got[at]).astype(BF)
    rest = sum_of(kept_ref[6 * unit_rows :], last_got[6 * unit_rows :]).astype(BF)
    for side, ref, owner_z in ((1, send_ref, z ^ 2), (0, keep_ref, z)):
        for index in range(3):
            at = where_ref[UNIT_LIST + 48 + ((core * 2 + y) * 4 + owner_z) * 3 + index]
            ref[index * unit_rows : (index + 1) * unit_rows] = held[at]
        ref[3 * unit_rows : 4 * unit_rows] = rest[side * unit_rows : (side + 1) * unit_rows]
        ref[4 * unit_rows :] = rest[2 * unit_rows :]
    stage.put(0)
    for side, ref in enumerate((dz_low_ref, dz_ref)):
        ref[...] = sum_of(dz_kept[side], dz_got[side]).astype(BF)


def finish_kernel(where_ref, stage, rows_ref, out_rows_ref, flat):
    mlp_kept, mlp_far, dz_low, dz_far, last_keep, last_far = (stage[index] for index in range(6))
    down_ref, up_ref, out_ref, vec_ref, qkv_ref = (stage.out(index) for index in range(5))
    size, block = down_ref.shape[0], up_ref.shape[0]
    lanes = up_ref.shape[1]
    mlp, dz = sum_of(mlp_kept[...], mlp_far[...]), sum_of(dz_low[...], dz_far[...])
    lead = mlp.shape[0] - block
    most = size - lead
    up_ref[...] = mlp[lead:]
    down_ref[:, :lanes] = dz[:size]
    down_ref[:most, lanes:] = dz[size : size + most]
    down_ref[most:, lanes:] = mlp[:lead]
    stage.put(0, 1)
    out_rows_ref[...] = jnp.zeros_like(out_rows_ref)
    last = sum_of(last_keep[...], last_far[...])
    half = size // 2
    unpack_unit(last[3 * half : 4 * half], out_rows_ref, 0)
    out_ref[...] = out_rows_ref[...].T[: out_ref.shape[0], : out_ref.shape[1]]
    sums = last[4 * half :]
    count = sums.shape[0] // 2
    for row in range(count):
        flat[:, 2 * row * lanes : (2 * row + 1) * lanes] = sums[row : row + 1]
        flat[:, (2 * row + 1) * lanes : (2 * row + 2) * lanes] = sums[count + row : count + row + 1]
    share = vec_ref.shape[1]
    start = (4 * set_block(where_ref, 0, 0, 0) + own_block(where_ref, 0, 0)) * share
    window = flat[:, pl.ds(pl.multiple_of(start // 128 * 128, 128), 512)]
    window = pltpu.roll(jnp.broadcast_to(window, (8, 512)), (512 - start % 128) % 512, 1)
    vec_ref[...] = window[:1, :share]
    stage.put(2, 3)
    rows_ref[...] = jnp.zeros_like(rows_ref)
    for unit in range(3):
        unpack_unit(last[unit * half : (unit + 1) * half], rows_ref, 2 * unit * half)
    qkv_ref[...] = rows_ref[...].T[: qkv_ref.shape[0], : qkv_ref.shape[1]]


def rows_kernel(parts, items, where_ref, stage, vec_ref):
    keep_ref, late_ref, far_ref, own_ref, dmid_ref, raw_ref, feed_ref, mid_ref = (stage[index] for index in range(8))
    unpack_rows(raw_ref, vec_ref)
    rows = own_ref.shape[0]
    dnormed = sum_of(keep_ref[...], late_ref[:rows], far_ref[...])
    xhat, inverse = standardise(own_ref[...].astype(F32))
    stage.out(0)[...] = (dmid_ref[...] + standardise_grad(vec_ref[0:1] * dnormed, xhat, inverse)).astype(BF)
    stage.put(0)
    valid = valid_at(where_ref, 0, 0, rows, parts, items)
    feed = sum_of(feed_ref[...], late_ref[rows:])
    stage.out(1)[...] = (valid * (mid_ref[...] + vec_ref[9:10] * feed)).astype(BF)


def swapped(array, axis, bit):
    length = lax.axis_size(axis)
    return lax.ppermute(array, axis, [(i, i ^ bit) for i in range(length)])


def to_core(array):
    return swapped(array, "blk", 1)


def to_x(array):
    return swapped(array, "blk", 2)


def to_y(array):
    return swapped(array, "dp", 1)


def to_z(array):
    return swapped(array, "dp", 2)


def to_zz(array):
    return swapped(array, "dp", 4)


def after(done, *arrays):
    return lax.optimization_barrier((done, *arrays))[1:]


def first_rows(count):
    def cut(where_ref, source, target):
        return [(source.at[:count], target)]

    return cut


def entry(array, index):
    def cut(where_ref, source, target):
        return [(source.at[index], target)]

    return (array.shape[1:], 1, cut)


def first_and_last_rows(count):
    def cut(where_ref, source, target):
        return [(source.at[:count], target.at[:count]), (source.at[2 * count :], target.at[count:])]

    return cut


def some_rows(array, first, last):
    def cut(where_ref, source, target):
        return [(source.at[first:last], target)]

    return ((last - first, *array.shape[1:]), 1, cut)


def own_columns(first):
    def cut(where_ref, source, target):
        half = source.shape[0] // 2
        return [
            (source.at[:, lanes_at(where_ref[1] + 2 * part, half)], target.at[:, (part - first) * half : (part - first + 1) * half])
            for part in range(first, 3)
        ]

    return cut


def own_hidden(axis):
    def cut(where_ref, source, target):
        pairs = []
        piece = target.shape[axis] // 4
        for rel_x in range(2):
            for side in range(2):
                at = lanes_at(hidden_unit(where_ref, rel_x, side), piece)
                to = slice((2 * rel_x + side) * piece, (2 * rel_x + side + 1) * piece)
                pairs.append((source.at[at], target.at[to]) if axis == 0 else (source.at[:, at], target.at[:, to]))
        return pairs

    return cut


def both_head_rows(where_ref, source, target):
    half = target.shape[0] // 2
    return [
        (source.at[lanes_at(where_ref[1], half), :], target.at[:half]),
        (source.at[lanes_at(1 - where_ref[1], half), :], target.at[half:]),
    ]


def own_head_rows(where_ref, source, target):
    return [(source.at[lanes_at(where_ref[1], target.shape[0]), :], target)]


def on_device_aligned(tokens, lengths, w_qkv, w_out, w_up, w_down, vectors, cotangent):
    tokens, cotangent = tokens[0], cotangent[0]
    rows, width = tokens.shape
    hidden = w_up.shape[1]
    items = lengths.shape[1]
    parts = lax.axis_size("blk")
    sets = lax.axis_size("dp")
    position, turn = lax.axis_index("blk"), lax.axis_index("dp")
    x, core, z, y = position // 2, position % 2, turn // 2, turn % 2
    where = lengths
    half = width // 2
    inner = hidden // 2
    piece = hidden // sets
    both = 2 * rows
    total_rows = parts * rows
    block = width // parts
    share = width // sets
    names = (parts, items)
    zs = sets // 2
    all_columns = ((width, 3 * half), 3, own_columns(0))
    kv_columns = ((width, 2 * half), 2, own_columns(1))
    up_columns = ((width, inner), 4, own_hidden(1))
    down_rows = ((inner, width), 4, own_hidden(0))
    head_rows = ((half, width), 1, own_head_rows)
    out_rows = ((width, width), 2, both_head_rows)

    far_a = to_x(tokens)
    sib = to_core(tokens)
    cot_sib = to_core(cotangent)

    vec = vectors.reshape(-1, 128)
    rows_of_vec = pltpu.VMEM((10, width), F32)

    xhat_near, qkv_near, dact, dfeed_turned, bias_d_sum = staged_call(
        functools.partial(prepare_kernel, *names),
        where,
        (tokens, sib, vec, w_qkv, cotangent, cot_sib, w_down),
        [low(both, width), low(both, 3 * half), low(both, inner), low(width, both), full(1, width)],
        cuts={3: all_columns, 6: down_rows},
        scratch=[rows_of_vec, pltpu.VMEM((both, width), BF), pltpu.VMEM((both, width), BF), pltpu.VMEM((2, 3 * half), F32)],
    )

    far_a, qkv_near, dact = lax.optimization_barrier((far_a, qkv_near, dact))
    far_b = to_core(far_a)

    xhat_far, kv, attended, logsum = staged_call(
        functools.partial(attend_kernel, *names),
        where,
        (far_a, far_b, vec, w_qkv, qkv_near),
        [low(both, width), low(total_rows, width), low(both, half), full(half // (2 * HEAD_SIZE), rows // TILE, 4 * TILE)],
        cuts={3: kv_columns},
        scratch=[
            rows_of_vec,
            pltpu.VMEM((total_rows, 2 * half), BF),
            pltpu.VMEM((both, width), BF),
            pltpu.VMEM((rows // TILE, 2 * TILE, 2 * TILE), jnp.int32),
        ],
    )
    attended_sib = to_core(attended)

    unit_rows = share // 2
    lead = 32
    py, us, dz = low(2, 4 * lead + 2 * block, piece), low(2, 2, block, piece), low(2, 2, 2, 2 * share - lead, piece)
    (py_keep, py_send, ux_keep, ux_send, dz_keep, dz_send, xhat_two, inverse_two, mid, branch, swap, act,
     bias_up_sum) = staged_call(
        mlp_kernel,
        where,
        (attended, attended_sib, tokens, sib, vec, w_out, w_up, dact, dfeed_turned),
        [py, py, us, us, dz, dz, low(both, width), full(both, 1), full(rows, width), low(rows, width), low(both, width),
         low(both, inner), full(1, inner)],
        cuts={5: out_rows, 6: up_columns},
        late=(6, 7, 8),
        pairs=(0, 2, 4),
        scratch=[rows_of_vec, pltpu.VMEM((sets, piece), F32), pltpu.VMEM((both, width), F32),
                 pltpu.VMEM((both, width), BF), pltpu.VMEM((both, width), BF), pltpu.VMEM((width, 2 * piece), BF),
                 pltpu.VMEM((width, both), BF), pltpu.VMEM((both, inner), BF)],
    )
    swap_got = to_core(swap)
    ux_send, ux_keep = to_core(ux_send), to_core(ux_keep)
    py_got = to_y(py_send)
    ux_got = to_x(ux_send)
    dz_got = to_z(dz_send)

    dmid, a_keep, a_send, b_keep, b_send, o_keep, o_send, dquery, dkeys, dvalues, back_sums = staged_call(
        functools.partial(backward_kernel, *names),
        where,
        (swap, swap_got, xhat_two, inverse_two, cotangent, cot_sib, vec, attended, attended_sib, w_out, branch,
         qkv_near, kv, logsum, xhat_near, xhat_far),
        [full(rows, width)] + [low(2, 6 * unit_rows + 64, half)] * 2 + [low(2, 6, unit_rows, half)] * 2
        + [low(2, 4 * unit_rows - 64, half)] * 2
        + [low(both, half), low(total_rows, half), low(total_rows, half), full(8, width)],
        cuts={9: head_rows},
        late=tuple(range(7, 16)),
        pairs=(1, 3, 5),
        tables=True,
        scratch=[rows_of_vec, pltpu.VMEM((both, half), BF), pltpu.VMEM((both, width), BF),
                 pltpu.VMEM((both, half), BF), pltpu.VMEM((2, sets, unit_rows, half), BF),
                 pltpu.VMEM((total_rows, width), BF), pltpu.VMEM((4, 12, unit_rows, half), BF),
                 pltpu.VMEM((rows // TILE, 4 * TILE), jnp.int32), pltpu.VMEM((total_rows, 2 * TILE), jnp.int32),
                 pltpu.VMEM((half, total_rows), BF), pltpu.VMEM((total_rows, 2 * HEAD_SIZE), F32),
                 pltpu.VMEM((total_rows, 2 * HEAD_SIZE), F32),
                 pltpu.VMEM((rows // TILE, 2 * HEAD_SIZE, 4 * TILE), F32)],
    )
    six, top = 6 * unit_rows, 2 * share - lead
    step = functools.partial(staged_call, grant=STEP_GRANT)
    b_send, b_keep = to_core(b_send), to_core(b_keep)
    py_got, ux_got, dz_got, b_send, b_keep = after(back_sums, py_got, ux_got, dz_got, b_send, b_keep)
    count = py_keep.shape[1]
    dz_step, x_step, y_step = staged_call(
        second_step_kernel,
        where,
        (dz_keep, dz_got, py_keep, py_got, a_send, ux_keep, ux_got, b_send, o_send),
        [low(*dz_keep.shape[1:]), low(count + 2 * six + 128, half), low(2 * block + 2 * six + 8 * unit_rows - 128, half)],
        cuts={index: entry(array, 1)
              for index, array in ((0, dz_keep), (1, dz_got), (2, py_keep), (3, py_got), (5, ux_keep), (6, ux_got))},
    )
    dz_far, x_got, y_got = to_zz(dz_step), to_x(x_step), to_y(y_step)
    (back_sums,) = after(y_step, back_sums)
    dtok_own, dtok_far, late_send, feed_keep, sums = staged_call(
        functools.partial(tokens_grad_kernel, *names),
        where,
        (dquery, dkeys, dvalues, w_qkv, xhat_near, xhat_far, vec, act, w_down, cotangent, cot_sib, back_sums,
         bias_d_sum, bias_up_sum),
        [low(rows, width), low(rows, width), low(3 * rows, width), full(rows, width), full(16, width)],
        cuts={3: all_columns, 8: down_rows},
        scratch=[rows_of_vec],
        grant=LATE_GRANT,
    )
    sums_core, sums_y = to_core(sums), to_y(sums)
    sums_far = to_core(sums_y)
    dz_far, x_got, y_got, sums_core, sums_y, sums_far = lax.optimization_barrier(
        (dz_far, x_got, y_got, sums_core, sums_y, sums_far)
    )

    rest = 4 * unit_rows - 64
    mlp_send, b_step, a_step, mlp_keep = step(
        third_step_kernel,
        where,
        (ux_keep, ux_got, y_got, py_keep, py_got, x_got, b_keep, o_keep, sums, sums_core, sums_y, sums_far, a_keep),
        [low(2, lead + block, piece), low(six + rest + 32, half), low(six + 64, half), low(2, lead + block, piece)],
        cuts={index: entry(array, 0) for index, array in ((0, ux_keep), (1, ux_got), (3, py_keep), (4, py_got))}
        | {index: entry(array, 1) for index, array in ((6, b_keep), (7, o_keep), (12, a_keep))},
    )
    mlp_got, b_far, a_far = to_z(mlp_send), to_x(b_step), to_y(a_step)
    (late_send,) = after(mlp_keep, late_send)
    late_got = to_core(late_send)
    mlp_got, b_far, a_far, late_got = lax.optimization_barrier((mlp_got, b_far, a_far, late_got))

    first = 2 * block + 2 * six
    last_send, mlp_step, dz_step, mlp_kept, last_keep, dz_kept, dtok_step = step(
        fourth_step_kernel,
        where,
        (a_keep, x_got, a_far, b_keep, y_got, b_far, o_keep, y_got, b_step, mlp_keep, mlp_got, dz_keep, dz_got, dz_far,
         dtok_far, late_got),
        [low(six + 2 * unit_rows + 32, half), low(lead + block, piece), low(2, top, piece), low(lead + block, piece),
         low(six + 2 * unit_rows + 32, half), low(2, top, piece), low(rows, width)],
        cuts={0: entry(a_keep, 0), 1: some_rows(x_got, count, count + six + 64), 3: entry(b_keep, 0),
              4: some_rows(y_got, 2 * block, 2 * block + six), 6: entry(o_keep, 0), 7: some_rows(y_got, first, first + rest),
              8: some_rows(b_step, six + rest, six + rest + 32), 11: entry(dz_keep, 0), 12: entry(dz_got, 0),
              15: some_rows(late_got, rows, both)},
    )
    last_got, mlp_far, dz_x, dtok_x = to_z(last_send), to_zz(mlp_step), to_x(dz_step), to_x(dtok_step)
    last_send, dz_y, last_kept, dz_low = step(
        fifth_step_kernel,
        where,
        (last_keep, last_got, dz_kept, dz_x),
        [low(4 * unit_rows + 32, half), low(top, piece), low(4 * unit_rows + 32, half), low(top, piece)],
        scratch=[pltpu.VMEM((6, unit_rows, half), BF)],
        tables=True,
    )
    last_far, dz_y = to_zz(last_send), to_y(dz_y)

    (dtok_x,) = after(dz_low, dtok_x)
    grad_tokens, out = staged_call(
        functools.partial(rows_kernel, *names),
        where,
        (dtok_own, late_got, dtok_x, tokens, dmid, vec, feed_keep, mid),
        [low(rows, width), low(rows, width)],
        cuts={1: ((both, width), 2, first_and_last_rows(rows))},
        scratch=[rows_of_vec],
        grant=STEP_GRANT,
    )

    mlp_far, dz_y, last_far = after(grad_tokens, mlp_far, dz_y, last_far)
    g_w_down, g_w_up, g_w_out, g_vec, g_w_qkv = step(
        finish_kernel,
        where,
        (mlp_kept, mlp_far, dz_low, dz_y, last_kept, last_far),
        [full(share, 2 * piece), full(block, piece), full(block, share), full(1, vectors.shape[0] // (sets * parts)),
         full(block, 3 * share)],
        scratch=[pltpu.VMEM((384, 256), F32), pltpu.VMEM((128, 256), F32), pltpu.VMEM((1, 16 * width + 512), F32)],
    )
    return (out[None], grad_tokens[None], g_w_qkv, g_w_out, g_w_up, g_w_down.T, g_vec.reshape(-1))


def is_aligned(mesh, tokens, w_up):
    parts, sets = mesh.shape["blk"], mesh.shape["dp"]
    width, hidden = w_up.shape
    rows = tokens.shape[1] // parts
    return (
        parts == 4
        and sets == 2 * parts
        and rows == 4 * TILE
        and (hidden // sets) % 128 == 0
        and (width // 2) % 128 == 0
        and (width // sets) % 32 == 0
        and width == H * HEAD_SIZE
    )


def solution(mesh):
    def run(tokens, lengths, w_qkv, w_out, w_up, w_down, vectors, cotangent):
        body = on_device_aligned if is_aligned(mesh, tokens, w_up) else on_device
        return jax.shard_map(
            body,
            mesh=mesh,
            in_specs=(
                P("dp", "blk", None),
                P("dp", None),
                P(),
                P(),
                P(),
                P(),
                P(),
                P("dp", "blk", None),
            ),
            out_specs=(
                P("dp", "blk", None),
                P("dp", "blk", None),
                P("blk", "dp"),
                P("blk", "dp"),
                P("blk", "dp"),
                P("blk", "dp"),
                P(("dp", "blk")),
            ),
            check_vma=False,
        )(tokens, lengths, w_qkv, w_out, w_up, w_down, vectors, cotangent)

    return run
```

```python
import functools
import math

import jax
import jax.numpy as jnp
import numpy as np
from jax import lax
from jax.experimental import pallas as pl
from jax.experimental.pallas import tpu as pltpu
from jax.sharding import PartitionSpec as P

H = 12
HEAD_SIZE = 64
TILE = 64


EPSILON = 1e-06
FLOOR_SCORE = -1e30


def passed_along(array, axis, by):
    length = lax.axis_size(axis)
    return lax.ppermute(array, axis, [(i, (i + by) % length) for i in range(length)])


def norm_rows(values, gain, shift):
    centre = jnp.mean(values, axis=-1, keepdims=True)
    centred = values - centre
    spread = jnp.mean(centred * centred, axis=-1, keepdims=True)
    return centred * lax.rsqrt(spread + EPSILON) * gain + shift


def exact_gelu(values):
    return jax.nn.gelu(values, approximate=False)


def segment_of(rows_index, rows, parts, ends):
    place = rows_index % rows * parts + rows_index // rows
    return jnp.sum((place[:, None] >= ends[None, :]).astype(jnp.int32), axis=1)


def contract_rows(left, right):
    return lax.dot_general(
        left, right, (((0,), (0,)), ((), ())), preferred_element_type=jnp.float32
    )


def contract_cols(left, right):
    return lax.dot_general(
        left, right, (((1,), (1,)), ((), ())), preferred_element_type=jnp.float32
    )


def attend_block(query, query_item, keys, values, key_item, scale, carry):
    best, total, weighted = carry
    count = keys.shape[0]
    heads = query.shape[1]
    key_heads = keys.reshape(count, heads, -1)
    value_heads = values.reshape(count, heads, -1)
    allowed = (query_item[:, None] == key_item[None, :])[None]
    score = jnp.einsum("qhd,khd->hqk", query, key_heads, preferred_element_type=jnp.float32) * scale
    score = jnp.where(allowed, score, FLOOR_SCORE)
    newbest = jnp.maximum(best, jnp.max(score, axis=-1))
    weight = jnp.where(allowed, jnp.exp(score - newbest[..., None]), 0.0)
    factor = jnp.exp(best - newbest)
    total = total * factor + jnp.sum(weight, axis=-1)
    weighted = weighted * factor[..., None] + jnp.einsum(
        "hqk,khd->hqd", weight.astype(jnp.bfloat16), value_heads, preferred_element_type=jnp.float32
    )
    return (newbest, total, weighted)


def grad_block(query, d_out, logsum, delta, query_item, keys, values, key_item, scale):
    count = keys.shape[0]
    heads = query.shape[1]
    key_heads = keys.reshape(count, heads, -1)
    value_heads = values.reshape(count, heads, -1)
    allowed = (query_item[:, None] == key_item[None, :])[None]
    score = jnp.einsum("qhd,khd->hqk", query, key_heads, preferred_element_type=jnp.float32) * scale
    prob = jnp.where(allowed, jnp.exp(score - logsum[..., None]), 0.0)
    d_prob = jnp.einsum("qhd,khd->hqk", d_out, value_heads, preferred_element_type=jnp.float32)
    d_score = (prob * (d_prob - delta[..., None])).astype(jnp.bfloat16)
    d_query = (
        jnp.einsum("hqk,khd->qhd", d_score, key_heads, preferred_element_type=jnp.float32) * scale
    )
    d_keys = jnp.einsum("hqk,qhd->khd", d_score, query, preferred_element_type=jnp.float32) * scale
    d_values = jnp.einsum(
        "hqk,qhd->khd", prob.astype(jnp.bfloat16), d_out, preferred_element_type=jnp.float32
    )
    return (d_query, d_keys.reshape(count, -1), d_values.reshape(count, -1))


def on_device(tokens, lengths, w_qkv, w_out, w_up, w_down, vectors, cotangent):
    inputs = tokens[0].astype(jnp.float32)
    rows, width = inputs.shape
    heads = H
    head_size = width // heads
    scale = head_size ** (-0.5)
    items = lengths.shape[1]
    ends = jnp.cumsum(lengths[0])
    parts = lax.axis_size("blk")
    position = lax.axis_index("blk")
    query_item = segment_of(position * rows + lax.iota(jnp.int32, rows), rows, parts, ends)
    valid = (query_item < items).astype(jnp.float32)[:, None]
    pieces = [vectors[index * width : (index + 1) * width] for index in range(10)]
    (
        gain_one,
        shift_one,
        bias_q,
        bias_v,
        bias_o,
        scale_one,
        gain_two,
        shift_two,
        bias_d,
        scale_two,
    ) = pieces
    bias_up = vectors[10 * width :]
    normed, norm_one_pull = jax.vjp(norm_rows, inputs, gain_one, shift_one)
    normed_low = normed.astype(jnp.bfloat16)
    qkv_bias = jnp.concatenate([bias_q, jnp.zeros_like(bias_q), bias_v])
    projected = (jnp.dot(normed_low, w_qkv, preferred_element_type=jnp.float32) + qkv_bias).astype(
        jnp.bfloat16
    )
    query = projected[:, :width].reshape(rows, heads, head_size)
    keys = projected[:, width : 2 * width]
    values = projected[:, 2 * width :]
    start_state = (
        jnp.full((heads, rows), FLOOR_SCORE, jnp.float32),
        jnp.zeros((heads, rows), jnp.float32),
        jnp.zeros((heads, rows, head_size), jnp.float32),
    )
    carry = start_state
    piece = (
        lax.all_gather(keys, "blk", axis=0, tiled=True),
        lax.all_gather(values, "blk", axis=0, tiled=True),
    )
    count = piece[0].shape[0]
    size = math.gcd(count, 512)
    steps = count // size
    key_blocks = piece[0].reshape(steps, size, width)
    value_blocks = piece[1].reshape(steps, size, width)

    def inner(state, item):
        block_keys, block_values, offset = item
        key_item = segment_of(offset + lax.iota(jnp.int32, size), rows, parts, ends)
        return (
            attend_block(query, query_item, block_keys, block_values, key_item, scale, state),
            None,
        )

    carry, unused = lax.scan(
        inner, carry, (key_blocks, value_blocks, lax.iota(jnp.int32, steps) * size)
    )
    best, total, weighted = carry
    logsum = best + jnp.log(total)
    attended = (weighted / total[..., None]).transpose(1, 0, 2).reshape(rows, width)
    attended_low = attended.astype(jnp.bfloat16)
    branch = jnp.dot(attended_low, w_out, preferred_element_type=jnp.float32) + bias_o
    mid = inputs + scale_one * branch
    normed_two, norm_two_pull = jax.vjp(norm_rows, mid, gain_two, shift_two)
    normed_two_low = normed_two.astype(jnp.bfloat16)
    before = jnp.dot(normed_two_low, w_up, preferred_element_type=jnp.float32) + bias_up
    activated, gelu_pull = jax.vjp(exact_gelu, before)
    activated_low = activated.astype(jnp.bfloat16)
    feed = jnp.dot(activated_low, w_down, preferred_element_type=jnp.float32) + bias_d
    result = mid + scale_two * feed
    out = (result * valid).astype(jnp.bfloat16)
    d_result = cotangent[0].astype(jnp.float32) * valid
    d_feed = (scale_two * d_result).astype(jnp.bfloat16)
    g_scale_two = jnp.sum(d_result * feed, axis=0)
    g_bias_d = jnp.sum(d_feed.astype(jnp.float32), axis=0)
    g_w_down = contract_rows(activated_low, d_feed)
    d_activated = contract_cols(d_feed, w_down)
    d_before = gelu_pull(d_activated)[0].astype(jnp.bfloat16)
    g_bias_up = jnp.sum(d_before.astype(jnp.float32), axis=0)
    g_w_up = contract_rows(normed_two_low, d_before)
    d_normed_two = contract_cols(d_before, w_up)
    d_mid_norm, g_gain_two, g_shift_two = norm_two_pull(d_normed_two)
    d_mid = d_result + d_mid_norm
    d_branch = (scale_one * d_mid).astype(jnp.bfloat16)
    g_scale_one = jnp.sum(d_mid * branch, axis=0)
    g_bias_o = jnp.sum(d_branch.astype(jnp.float32), axis=0)
    g_w_out = contract_rows(attended_low, d_branch)
    d_attended = contract_cols(d_branch, w_out).astype(jnp.bfloat16)
    d_heads = d_attended.reshape(rows, heads, head_size)
    delta = jnp.sum(
        (d_attended.astype(jnp.float32) * attended).reshape(rows, heads, head_size), axis=-1
    ).T
    zero_query = jnp.zeros((rows, heads, head_size), jnp.float32)

    def visit_block(block_keys, block_values, owner):
        key_item = segment_of(owner * rows + lax.iota(jnp.int32, rows), rows, parts, ends)
        return grad_block(
            query, d_heads, logsum, delta, query_item, block_keys, block_values, key_item, scale
        )

    def send_back(d_keys, d_values):
        return (
            passed_along(d_keys.astype(jnp.bfloat16), "blk", 1).astype(d_keys.dtype),
            passed_along(d_values.astype(jnp.bfloat16), "blk", 1).astype(d_values.dtype),
        )

    def accumulate(state, owner):
        d_query, block_keys, block_values, d_keys, d_values = state
        dq_part, dk_part, dv_part = visit_block(block_keys, block_values, owner)
        d_keys, d_values = send_back(d_keys + dk_part, d_values + dv_part)
        return (d_query + dq_part, d_keys, d_values)

    def turn(step, state):
        owner = (position - step) % parts
        d_query, d_keys, d_values = accumulate(state, owner)
        block_keys, block_values = passed_along((state[1], state[2]), "blk", 1)
        return (d_query, block_keys, block_values, d_keys, d_values)

    zero_rows = jnp.zeros((rows, width), jnp.float32)
    state = lax.fori_loop(0, parts - 1, turn, (zero_query, keys, values, zero_rows, zero_rows))
    d_query, d_keys, d_values = accumulate(state, (position + 1) % parts)
    d_projected = jnp.concatenate([d_query.reshape(rows, width), d_keys, d_values], axis=1).astype(
        jnp.bfloat16
    )
    g_bias_q = jnp.sum(d_projected[:, :width].astype(jnp.float32), axis=0)
    g_bias_v = jnp.sum(d_projected[:, 2 * width :].astype(jnp.float32), axis=0)
    g_w_qkv = contract_rows(normed_low, d_projected)
    d_normed = contract_cols(d_projected, w_qkv)
    d_input_norm, g_gain_one, g_shift_one = norm_one_pull(d_normed)
    d_inputs = d_mid + d_input_norm
    g_vectors = jnp.concatenate(
        [
            g_gain_one,
            g_shift_one,
            g_bias_q,
            g_bias_v,
            g_bias_o,
            g_scale_one,
            g_gain_two,
            g_shift_two,
            g_bias_d,
            g_scale_two,
            g_bias_up,
        ]
    )
    column_sums = (
        lax.psum_scatter(
            g_w_qkv.astype(jnp.bfloat16), "dp", scatter_dimension=1, tiled=True
        ).astype(jnp.float32),
        lax.psum_scatter(
            g_w_out.astype(jnp.bfloat16), "dp", scatter_dimension=1, tiled=True
        ).astype(jnp.float32),
        lax.psum_scatter(g_w_up.astype(jnp.bfloat16), "dp", scatter_dimension=1, tiled=True).astype(
            jnp.float32
        ),
        lax.psum_scatter(
            g_w_down.astype(jnp.bfloat16), "dp", scatter_dimension=1, tiled=True
        ).astype(jnp.float32),
        lax.psum_scatter(
            g_vectors.astype(jnp.bfloat16), "dp", scatter_dimension=0, tiled=True
        ).astype(jnp.float32),
    )
    g_w_qkv, g_w_out, g_w_up, g_w_down, g_vectors = (
        lax.psum_scatter(
            column_sums[0].astype(jnp.bfloat16), "blk", scatter_dimension=0, tiled=True
        ).astype(jnp.float32),
        lax.psum_scatter(
            column_sums[1].astype(jnp.bfloat16), "blk", scatter_dimension=0, tiled=True
        ).astype(jnp.float32),
        lax.psum_scatter(
            column_sums[2].astype(jnp.bfloat16), "blk", scatter_dimension=0, tiled=True
        ).astype(jnp.float32),
        lax.psum_scatter(
            column_sums[3].astype(jnp.bfloat16), "blk", scatter_dimension=0, tiled=True
        ).astype(jnp.float32),
        lax.psum_scatter(
            column_sums[4].astype(jnp.bfloat16), "blk", scatter_dimension=0, tiled=True
        ).astype(jnp.float32),
    )
    return (
        out[None],
        d_inputs.astype(jnp.bfloat16)[None],
        g_w_qkv,
        g_w_out,
        g_w_up,
        g_w_down,
        g_vectors,
    )


BF = jnp.bfloat16
F32 = jnp.float32
MASKED = -1e30
GRANT = 60 * 1024 * 1024
STEP_GRANT = 20 * 1024 * 1024
LATE_GRANT = 48 * 1024 * 1024
WIDE_CHUNK = 128


def unit_tables():
    lists, places = np.zeros((2, 2, 2, 6), np.int32), np.zeros((2, 2, 4, 3), np.int32)
    units = {core: [unit for unit in range(24) if unit // 4 % 2 == core] for core in range(2)}
    for y in range(2):
        for low_z in range(2):
            first = {}
            for core in range(2):
                own = [unit for unit in units[core] if unit // 3 % 2 == y]
                first[core] = [unit for unit in own if unit // 6 % 2 == low_z]
                rest = [unit for unit in own if unit // 6 % 2 != low_z]
                lists[core, y, low_z] = [units[core].index(unit) for unit in first[core] + rest]
            for core in range(2):
                held = first[core] + first[1 - core]
                for z in (low_z, low_z + 2):
                    places[core, y, z] = [held.index(3 * (2 * z + y) + index) for index in range(3)]
    return np.concatenate([lists.reshape(-1), places.reshape(-1)])


UNIT_TABLE = unit_tables()
UNIT_LIST = 4
ENDS = UNIT_LIST + UNIT_TABLE.size


def dot_nn(left, right):
    return lax.dot_general(left, right, (((1,), (0,)), ((), ())), preferred_element_type=F32)


def dot_nt(left, right):
    return lax.dot_general(left, right, (((1,), (1,)), ((), ())), preferred_element_type=F32)


def dot_tn(left, right):
    return lax.dot_general(left, right, (((0,), (0,)), ((), ())), preferred_element_type=F32)


def standardise(values):
    centred = values - jnp.mean(values, axis=-1, keepdims=True)
    inverse = lax.rsqrt(jnp.mean(centred * centred, axis=-1, keepdims=True) + EPSILON)
    return centred * inverse, inverse


def standardise_grad(grad, xhat, inverse):
    first = jnp.mean(grad, axis=-1, keepdims=True)
    second = jnp.mean(grad * xhat, axis=-1, keepdims=True)
    return (grad - first - xhat * second) * inverse


def column_sum(values):
    return jnp.sum(values, axis=0, keepdims=True)


def item_at(place, where_ref, items):
    found = jnp.zeros_like(place)
    for index in range(items):
        found = found + (place >= where_ref[ENDS + index]).astype(jnp.int32)
    return found


def own_block(where_ref, rel_x, rel_c):
    return 2 * (where_ref[0] ^ rel_x) + (where_ref[1] ^ rel_c)


def low(*shape):
    return jax.ShapeDtypeStruct(shape, BF)


def full(*shape):
    return jax.ShapeDtypeStruct(shape, F32)


def lanes_at(index, size):
    return pl.ds(pl.multiple_of(index * size, size), size)


class Stage:
    def __init__(self, reads, places, writes):
        self.reads, self.places, self.writes = reads, places, writes
        self.started, self.waited, self.begun = set(), set(), []

    def start(self, *indices):
        for index in indices:
            if index not in self.started:
                self.started.add(index)
                for copy in self.reads[index]:
                    copy.start()

    def __getitem__(self, index):
        self.start(index)
        if index not in self.waited:
            self.waited.add(index)
            for copy in self.reads[index]:
                copy.wait()
        return self.places[index]

    def out(self, index):
        return self.writes[index][0]

    def put(self, *indices):
        for index in indices:
            self.writes[index][1].start()
            self.begun.append(index)

    def finish(self):
        for index in range(len(self.reads)):
            self[index]
        self.put(*(index for index in range(len(self.writes)) if index not in self.begun))
        for place, copy in self.writes:
            copy.wait()


class Place:
    def __init__(self, lengths_ref, table_ref):
        position, turn = lax.axis_index("blk"), lax.axis_index("dp")
        self.four = (position // 2, position % 2, turn // 2, turn % 2)
        self.table_ref = table_ref
        self.ends, end = [], jnp.int32(0)
        for index in range(lengths_ref.shape[1]):
            end = end + lengths_ref[0, index]
            self.ends.append(end)

    def __getitem__(self, index):
        if isinstance(index, int) and index < UNIT_LIST:
            return self.four[index]
        if isinstance(index, int) and index >= ENDS:
            return self.ends[index - ENDS]
        return self.table_ref[index - UNIT_LIST]


def unpack_rows(raw_ref, vec_ref):
    count = vec_ref.shape[1] // 128
    for row in range(vec_ref.shape[0]):
        for part in range(count):
            vec_ref[row : row + 1, part * 128 : (part + 1) * 128] = raw_ref[row * count + part : row * count + part + 1]


def staged_call(body, where, operands, out_shape, cuts=None, scratch=(), late=(), pairs=(), tables=False, grant=GRANT):
    cuts = cuts or {}
    count, results = len(operands), len(out_shape)
    shapes, parts = [], []
    for index, operand in enumerate(operands):
        shape, pieces = (operand.shape, 1) if index not in cuts else cuts[index][:2]
        shapes.append(pltpu.VMEM(shape, operand.dtype))
        parts.append(pieces)
    held_shapes, held_at = [], {}
    for index, item in enumerate(out_shape):
        if index - 1 in pairs:
            held_at[index] = (len(held_shapes) - 1, 1)
        elif index in pairs:
            held_at[index] = (len(held_shapes), 0)
            held_shapes.append(pltpu.VMEM((2, *item.shape), item.dtype))
        else:
            held_at[index] = (len(held_shapes), None)
            held_shapes.append(pltpu.VMEM(item.shape, item.dtype))

    def kernel(*refs):
        where_ref = Place(refs[0], refs[1] if tables else None)
        refs = refs[2 if tables else 1 :]
        ins, outs = refs[:count], refs[count : count + results]
        places = refs[count + results : 2 * count + results]
        held = refs[2 * count + results : 2 * count + results + len(held_shapes)]
        read_sem, write_sem, *rest = refs[2 * count + results + len(held_shapes) :]
        reads, used = [], 0
        for index in range(count):
            moves = [(ins[index], places[index])] if index not in cuts else cuts[index][2](where_ref, ins[index], places[index])
            reads.append([])
            for source, target in moves:
                reads[-1].append(pltpu.make_async_copy(source, target, read_sem.at[used]))
                used += 1
        writes = []
        for index in range(results):
            place, entry = held_at[index]
            source = held[place] if entry is None else held[place].at[entry]
            writes.append((held[place], pltpu.make_async_copy(source, outs[index], write_sem.at[index])))
        stage = Stage(reads, places, writes)
        stage.start(*(index for index in range(count) if index not in late))
        body(where_ref, stage, *rest)
        stage.finish()

    return pl.pallas_call(
        kernel,
        in_specs=[pl.BlockSpec(memory_space=pltpu.SMEM)] * (2 if tables else 1)
        + [pl.BlockSpec(memory_space=pl.ANY)] * count,
        out_specs=[pl.BlockSpec(memory_space=pl.ANY)] * results,
        out_shape=out_shape,
        scratch_shapes=shapes
        + held_shapes
        + [pltpu.SemaphoreType.DMA((sum(parts),)), pltpu.SemaphoreType.DMA((results,))]
        + list(scratch),
        compiler_params=pltpu.CompilerParams(vmem_limit_bytes=grant),
    )(where, *((UNIT_TABLE,) if tables else ()), *operands)


def each(count, body):
    def step(index, carry):
        body(index)
        return carry

    lax.fori_loop(0, count, step, 0)


def hidden_unit(where_ref, rel_x, side):
    return 4 * (where_ref[0] ^ rel_x) + 2 * where_ref[1] + side


def lanes_below(shape, count):
    return lax.broadcasted_iota(jnp.int32, shape, 1) < count


def stack_heads(pair):
    first = lanes_below(pair.shape, HEAD_SIZE)
    zero = jnp.zeros_like(pair)
    return jnp.concatenate([jnp.where(first, pair, zero), jnp.where(first, zero, pair)], axis=0)


def turn(source, target):
    each(source.shape[1] // 128, lambda index: target.__setitem__(lanes_at(index, 128), source[:, lanes_at(index, 128)].T))


def valid_at(where_ref, rel_c, first, count, parts, items):
    row = first + lax.broadcasted_iota(jnp.int32, (count, 1), 0)
    item = item_at(row * parts + own_block(where_ref, 0, rel_c), where_ref, items)
    return (item < items).astype(F32)


def normed_rows(xhat, vec_ref, first):
    return (xhat.astype(F32) * vec_ref[first : first + 1] + vec_ref[first + 1 : first + 2]).astype(BF)


def prepare_kernel(parts, items, where_ref, stage, vec_ref, held, normed_ref, row_ref):
    unpack_rows(stage[2], vec_ref)
    own_ref, sib_ref = stage[0], stage[1]
    stage.start(3, 4, 5, 6)
    xhat_ref, qkv_ref, dact_ref, turned_ref, sum_ref = (stage.out(index) for index in range(5))
    rows, width = own_ref.shape
    half = width // 2
    core = where_ref[1]
    for rel_c, ref in enumerate((own_ref, sib_ref)):

        def norm(index, rel_c=rel_c, ref=ref):
            xhat, unused = standardise(ref[lanes_at(index, WIDE_CHUNK)].astype(F32))
            to = lanes_at(index + rel_c * (rows // WIDE_CHUNK), WIDE_CHUNK)
            xhat_ref[to] = xhat.astype(BF)
            normed_ref[to] = (xhat * vec_ref[0:1] + vec_ref[1:2]).astype(BF)

        each(rows // WIDE_CHUNK, norm)
    stage.put(0)
    sum_ref[...] = jnp.zeros_like(sum_ref)
    for rel_c in range(2):

        def grad(index, rel_c=rel_c, ref=stage[4 + rel_c]):
            valid = valid_at(where_ref, rel_c, index * WIDE_CHUNK, WIDE_CHUNK, parts, items)
            part = (vec_ref[9:10] * (ref[lanes_at(index, WIDE_CHUNK)].astype(F32) * valid)).astype(BF)
            held[lanes_at(index + rel_c * (rows // WIDE_CHUNK), WIDE_CHUNK)] = part
            if rel_c == 0:
                sum_ref[...] += column_sum(part.astype(F32))

        each(rows // WIDE_CHUNK, grad)
    turn(held, turned_ref)
    stage.put(3, 4)
    row_ref[0:1, :half] = vec_ref[2:3, lanes_at(core, half)]
    row_ref[0:1, half : 2 * half] = jnp.zeros((1, half), F32)
    row_ref[0:1, 2 * half :] = vec_ref[3:4, lanes_at(core, half)]
    row_ref[1:2, :half] = jnp.full((1, half), HEAD_SIZE ** (-0.5), F32)
    row_ref[1:2, half:] = jnp.ones((1, 2 * half), F32)
    weight_ref = stage[3]

    def project(index):
        lanes = lanes_at(index, half)
        part = dot_nn(normed_ref[...], weight_ref[:, lanes]) + row_ref[0:1, lanes]
        qkv_ref[:, lanes] = (part.astype(BF).astype(F32) * row_ref[1:2, lanes]).astype(BF)

    each(3, project)
    stage.put(1)
    down_ref = stage[6]
    piece = dact_ref.shape[1] // 4

    def back(index):
        dact_ref[:, lanes_at(index, piece)] = dot_nt(held[...], down_ref[lanes_at(index, piece)]).astype(BF)

    each(4, back)


def item_of_place(where_ref, place, items):
    found = jnp.int32(0)
    for index in range(items):
        found = found + (place >= where_ref[ENDS + index]).astype(jnp.int32)
    return found


def tiles_meet(where_ref, one, other, parts, items):
    span = TILE * parts
    first, last = min(one, other), max(one, other)
    return item_of_place(where_ref, first * span + span - 1, items) >= item_of_place(
        where_ref, last * span, items
    )


def near_tiles(tile, tiles):
    return max(0, tile - 1), min(tiles, tile + 2)


def far_pairs(tiles):
    return [(one, other) for one in range(tiles) for other in range(tiles) if abs(one - other) > 1]


def any_far(where_ref, tiles, parts, items):
    found = jnp.bool_(False)
    for one, other in far_pairs(tiles):
        if one < other:
            found = found | tiles_meet(where_ref, one, other, parts, items)
    return found


def attend_kernel(parts, items, where_ref, stage, vec_ref, wide_ref, normed_ref, asks_ref):
    unpack_rows(stage[2], vec_ref)
    xhat_ref, kv_ref, attended_ref, logsum_ref = (stage.out(index) for index in range(4))
    far_a_ref, far_b_ref = stage[0], stage[1]
    stage.start(3, 4)
    rows, width = far_a_ref.shape
    tiles = rows // TILE
    span = parts * TILE
    both = 2 * HEAD_SIZE
    half = width // 2
    core = where_ref[1]
    for rel_c, ref in enumerate((far_a_ref, far_b_ref)):
        xhat, unused = standardise(ref[...].astype(F32))
        xhat_ref[rel_c * rows : (rel_c + 1) * rows] = xhat.astype(BF)
        normed_ref[rel_c * rows : (rel_c + 1) * rows] = normed_rows(xhat, vec_ref, 0)
    stage.put(0)
    row = lax.broadcasted_iota(jnp.int32, (2 * TILE, 2 * TILE), 0)
    block = 2 * where_ref[0] + (where_ref[1] ^ (row // TILE))
    for tile in range(tiles):
        asks_ref[tile] = item_at((tile * TILE + row % TILE) * parts + block, where_ref, items)
    lane = lax.broadcasted_iota(jnp.int32, (1, span), 1)
    slot = lane // TILE
    block = 2 * (where_ref[0] ^ (slot // 2)) + (where_ref[1] ^ (slot % 2))
    key_item = [item_at((tile * TILE + lane % TILE) * parts + block, where_ref, items) for tile in range(tiles)]
    weight_ref = stage[3]
    row_ref = jnp.concatenate([jnp.zeros((1, half), F32), vec_ref[3:4, lanes_at(core, half)]], axis=1)
    far_kv = (dot_nn(normed_ref[...], weight_ref[...]) + row_ref).astype(BF)
    qkv_ref = stage[4]
    for tile in range(tiles):
        for slot in range(2):
            at = slice(slot * rows + tile * TILE, slot * rows + (tile + 1) * TILE)
            kv_ref[tile * span + slot * TILE : tile * span + (slot + 1) * TILE] = qkv_ref[at, half:]
            kv_ref[tile * span + (slot + 2) * TILE : tile * span + (slot + 3) * TILE] = far_kv[at]
    stage.put(1)
    for index in range(half // both):
        wide_ref[:, 2 * index * both : (2 * index + 1) * both] = kv_ref[:, half + index * both : half + (index + 1) * both]
        wide_ref[:, (2 * index + 1) * both : (2 * index + 2) * both] = jnp.ones((tiles * span, both), BF)

    def attend(index, tile, first, last):
        lanes = lanes_at(index, both)
        at = slice(first * span, last * span)
        places = [pl.ds(pl.multiple_of(rel_c * rows + tile * TILE, TILE), TILE) for rel_c in range(2)]
        query = stack_heads(jnp.concatenate([qkv_ref[place, lanes] for place in places], axis=0))
        score = dot_nt(query, kv_ref[at, lanes])
        asked = asks_ref[tile][:, :1]
        allowed = jnp.concatenate([asked == key_item[other] for other in range(first, last)], axis=1)
        score = jnp.where(jnp.concatenate([allowed, allowed], axis=0), score, MASKED)
        best = jnp.max(score, axis=1, keepdims=True)
        weight = jnp.exp(score - best).astype(BF)
        mixed = dot_nn(weight, wide_ref[at, lanes_at(index, 2 * both)])
        total = mixed[:, both:]
        logsum_ref[index, pl.ds(tile, 1)] = (best + jnp.log(total)).T[:1]
        mixed = mixed[:, :both] / total
        attended = jnp.where(lanes_below((both, both), HEAD_SIZE), mixed[:both], mixed[both:]).astype(BF)
        for rel_c, place in enumerate(places):
            attended_ref[place, lanes] = attended[rel_c * TILE : (rel_c + 1) * TILE]

    def pair(index):
        for tile in range(tiles):
            attend(index, tile, *near_tiles(tile, tiles))

    each(half // both, pair)

    @pl.when(any_far(where_ref, tiles, parts, items))
    def far():
        def again(step):
            tile = step % tiles
            found = jnp.bool_(False)
            for one, other in far_pairs(tiles):
                found = found | ((tile == one) & tiles_meet(where_ref, one, other, parts, items))
            pl.when(found)(lambda: attend(step // tiles, tile, 0, tiles))

        each(half // both * tiles, again)


def gelu_with_slope(values):
    bell = jnp.exp(-0.5 * values * values)
    inverse = 1.0 / (1.0 + (0.3275911 * 0.5**0.5) * jnp.abs(values))
    series = 1.061405429
    for coefficient in (-1.453152027, 1.421413741, -0.284496736, 0.254829592):
        series = series * inverse + coefficient
    tail = 0.5 * (series * inverse) * bell
    normal = jnp.where(values >= 0, 1.0 - tail, tail)
    return values * normal, normal + values * bell * ((2.0 * math.pi) ** -0.5)


def set_block(where_ref, rel_y, low_z, high_z):
    return 2 * (where_ref[2] ^ (low_z + 2 * high_z)) + (where_ref[3] ^ rel_y)


def mlp_kernel(where_ref, stage, vec_ref, bias_ref, mid_ref, joined, normed, grad, turned, dbefore_ref):
    py_ref, ux_ref, dz_ref = stage.out(0), stage.out(2), stage.out(4)
    xhat_ref, inverse_ref, mid_own_ref, branch_ref, swap_ref, act_ref, bias_sum_ref = (
        stage.out(index) for index in range(6, 13)
    )
    unpack_rows(stage[4], vec_ref)
    att_own_ref, att_sib_ref, own_ref, sib_ref, raw_ref, out_ref = (stage[index] for index in range(6))
    stage.start(6, 7, 8)
    x, core, z, y = (where_ref[index] for index in range(4))
    rows, width = own_ref.shape
    half = width // 2
    piece = act_ref.shape[1] // 4
    joined[:, :half] = att_own_ref[...]
    joined[:rows, half:] = att_sib_ref[rows:]
    joined[rows:, half:] = att_sib_ref[:rows]

    def project(index):
        lanes = lanes_at(index, 256)
        branch = dot_nn(joined[...], out_ref[:, lanes]) + vec_ref[4:5, lanes]
        branch_ref[:, lanes] = branch[:rows].astype(BF)
        branch = vec_ref[5:6, lanes] * branch
        mid_ref[:rows, lanes] = own_ref[:, lanes].astype(F32) + branch[:rows]
        mid_ref[rows:, lanes] = sib_ref[:, lanes].astype(F32) + branch[rows:]

    each(width // 256, project)

    mid_own_ref[...] = mid_ref[:rows]

    def norm(index):
        at = lanes_at(index, WIDE_CHUNK)
        xhat, inverse = standardise(mid_ref[at])
        normed[at] = (xhat * vec_ref[6:7] + vec_ref[7:8]).astype(BF)
        xhat_ref[at] = xhat.astype(BF)
        inverse_ref[at] = inverse

    each(2 * rows // WIDE_CHUNK, norm)
    stage.put(6, 7, 8, 9)
    count = piece // 128
    for unit in range(8):
        for part in range(count):
            row = 10 * width // 128 + unit * count + part
            bias_ref[unit : unit + 1, part * 128 : (part + 1) * 128] = raw_ref[row : row + 1]
    up_ref, dact_ref, turned_ref = stage[6], stage[7], stage[8]
    size = grad.shape[0] // 8

    def hidden(index):
        rel_x = 1 - index
        count = normed.shape[0] // 2
        for side in range(2):
            at = lanes_at(2 * rel_x + side, piece)
            bias = bias_ref[pl.ds(hidden_unit(where_ref, rel_x, side), 1)]
            total = jnp.zeros((1, piece), F32)
            for part in range(2):
                here = slice(part * count, (part + 1) * count)
                act, slope = gelu_with_slope(dot_nn(normed[here], up_ref[:, at]) + bias)
                act_ref[here, at] = act.astype(BF)
                dbefore = (dact_ref[here, at].astype(F32) * slope).astype(BF)
                dbefore_ref[here, at] = dbefore
                total = total + column_sum(dbefore.astype(F32))
            bias_sum_ref[:, at] = total
            grad[:, side * piece : (side + 1) * piece] = dot_nn(turned_ref[...], act_ref[:, at]).astype(BF)

        def lay(index):
            low_z, high_z, rel_y = index // 4, index // 2 % 2, index % 2
            first = set_block(where_ref, rel_y, low_z, high_z) * size
            most = dz_ref.shape[4] - size
            dz_ref[low_z, high_z, rel_x, rel_y, :size] = grad[pl.ds(pl.multiple_of(first, size), size), :piece]
            dz_ref[low_z, high_z, rel_x, rel_y, size:] = grad[pl.ds(pl.multiple_of(first, size), most), piece:]
            py_ref[rel_y, rel_x, lanes_at(2 * low_z + high_z, size - most)] = grad[
                pl.ds(pl.multiple_of(first + most, size - most), size - most), piece:
            ]

        each(8, lay)

    each(2, hidden)
    stage.put(4, 5, 11, 12)
    turn(normed, turned)
    block = 2 * size

    def up(index):
        rel_y, high_z = index // 2, index % 2
        unit = 2 * (x ^ (z // 2) ^ high_z) + (y ^ rel_y)
        grad[:, :piece] = dot_nn(turned[...], dbefore_ref[:, lanes_at(unit, piece)]).astype(BF)
        for rel_x in range(2):
            to = pl.ds(pl.multiple_of(py_ref.shape[2] - 2 * block + high_z * block, 64), block)
            py_ref[rel_y, rel_x, to] = grad[lanes_at(own_block(where_ref, rel_x, 0), block), :piece]
            ux_ref[rel_x, rel_y, high_z] = grad[lanes_at(own_block(where_ref, rel_x, 1), block), :piece]

    for index in range(4):
        up(index)
    stage.put(0, 1, 2, 3)

    def back(index):
        lanes = lanes_at(index, 256)
        total = dot_nt(dbefore_ref[...], up_ref[lanes])
        swap_ref[:, lanes] = total.astype(BF)

    each(width // 256, back)


def middle(parts, items, where_ref, stage, vec_ref, sum_ref, datt_ref, held, chosen, packed):
    dmid_ref, a_ref, o_ref = stage.out(0), stage.out(1), stage.out(5)
    keep_ref, got_ref, xhat_ref, inverse_ref, own_ref, sib_ref, raw_ref = (stage[index] for index in range(7))
    stage.start(10, 9, 7, 8, 11, 12, 13)
    unpack_rows(raw_ref, vec_ref)
    rows, width = own_ref.shape
    half = width // 2
    core = where_ref[1]
    left_is_own = lanes_below((rows, half), half // 2) == (core == 0)
    for rel_c, ref in enumerate((own_ref, sib_ref)):
        here = slice(rel_c * rows, (rel_c + 1) * rows)
        there = slice((1 - rel_c) * rows, (2 - rel_c) * rows)
        valid = valid_at(where_ref, rel_c, 0, rows, parts, items)
        dnormed = keep_ref[here].astype(F32) + got_ref[there].astype(F32)
        xhat, inverse = xhat_ref[here].astype(F32), inverse_ref[here]
        dmid = ref[...].astype(F32) * valid + standardise_grad(vec_ref[6:7] * dnormed, xhat, inverse)
        dbranch = (vec_ref[5:6] * dmid).astype(BF)
        held[here] = dbranch
        if rel_c == 0:
            dmid_ref[...] = dmid
            sum_ref[0:1] = column_sum(dbranch.astype(F32))
            sum_ref[1:2] = column_sum(dmid * stage[10][...].astype(F32))
            sum_ref[2:3] = column_sum(dnormed * xhat)
            sum_ref[3:4] = column_sum(dnormed)
    stage.put(0)
    stage.start(14, 15)
    datt_ref[...] = dot_nt(held[...], stage[9][...]).astype(BF)
    att_own_ref, att_sib_ref = stage[7], stage[8]
    for rel_c in range(2):
        here = slice(rel_c * rows, (rel_c + 1) * rows)
        there = slice((1 - rel_c) * rows, (2 - rel_c) * rows)
        other = pltpu.roll(att_sib_ref[there].astype(F32), half // 2, 1)
        chosen[here] = jnp.where(left_is_own, att_own_ref[here].astype(F32), other).astype(BF)
    grad = dot_tn(held[...], chosen[...])
    count, unit_rows = packed.shape[1:3]
    for index in range(count):
        left, right = pack_unit(grad[2 * index * unit_rows : 2 * (index + 1) * unit_rows])
        packed[0, index] = left.astype(BF)
        packed[1, index] = right.astype(BF)

    units = 6 * unit_rows

    def lay(index):
        rel_x, rel_y, block = index // 8, index // 4 % 2, index % 4
        here = packed.at[where_ref[0] ^ rel_x, set_block(where_ref, rel_y, block // 2, block % 2)]
        a_ref[rel_x, rel_y, pl.ds(pl.multiple_of(units + 16 * block, 16), 16)] = here[:16]
        o_ref[rel_y, rel_x, lanes_at(block, unit_rows - 16)] = here[16:]

    each(16, lay)
    stage.put(5, 6)


def pack_unit(unit):
    half = unit.shape[0] // 2
    width = unit.shape[1]
    top, bottom = unit[:half], unit[half:]
    first = lanes_below((half, width), width // 2)
    left = jnp.where(first, top, pltpu.roll(bottom, width // 2, 1))
    right = jnp.where(first, pltpu.roll(top, width // 2, 1), bottom)
    return left, right


def join_heads(stacked_turned):
    stacked = stacked_turned.T
    count = stacked.shape[0] // 2
    return jnp.where(
        lanes_below((count, stacked.shape[1]), HEAD_SIZE), stacked[:count], stacked[count:]
    )


def query_items(where_ref, tile, parts, items):
    lane = lax.broadcasted_iota(jnp.int32, (1, 4 * TILE), 1)
    rel_c = (lane // TILE) % 2
    block = 2 * where_ref[0] + (where_ref[1] ^ rel_c)
    return item_at((tile * TILE + lane % TILE) * parts + block, where_ref, items)


def fill_key_items(where_ref, item_ref, tiles, parts, items):
    row = lax.broadcasted_iota(jnp.int32, (TILE, item_ref.shape[1]), 0)
    for tile in range(tiles):
        for slot in range(parts):
            block = own_block(where_ref, slot // 2, slot % 2)
            at = (tile * parts + slot) * TILE
            item_ref[at : at + TILE] = item_at((tile * TILE + row) * parts + block, where_ref, items)


def both_heads(array):
    return jnp.concatenate([array, array], axis=1)


def attend_grad(
    parts, items, where_ref, stage, datt_ref, dquery_ref, dkeys_ref, dvalues_ref, asks_ref, item_ref, turned_ref, dk, dv, dq
):
    attended_ref, qkv_ref, kv_ref, logsum_ref = stage[7], stage[11], stage[12], stage[13]
    half = datt_ref.shape[1]
    rows = datt_ref.shape[0] // 2
    tiles = rows // TILE
    span = parts * TILE
    scale = HEAD_SIZE ** (-0.5)
    turned_ref[...] = kv_ref[:, :half].T
    fill_key_items(where_ref, item_ref, tiles, parts, items)
    for tile in range(tiles):
        asks_ref[tile : tile + 1] = query_items(where_ref, tile, parts, items)
    some_far = any_far(where_ref, tiles, parts, items)

    def pair(index, carry):
        lanes = lanes_at(index, 2 * HEAD_SIZE)
        value_lanes = pl.ds(pl.multiple_of(half + index * 2 * HEAD_SIZE, 2 * HEAD_SIZE), 2 * HEAD_SIZE)
        dk[...] = jnp.zeros_like(dk)
        dv[...] = jnp.zeros_like(dv)

        def places(tile):
            return [pl.ds(pl.multiple_of(rel_c * rows + tile * TILE, TILE), TILE) for rel_c in range(2)]

        def visit(tile, at):
            query = stack_heads(jnp.concatenate([qkv_ref[place, lanes] for place in places(tile)], axis=0))
            grad = jnp.concatenate([datt_ref[place, lanes] for place in places(tile)], axis=0)
            attended = jnp.concatenate([attended_ref[place, lanes] for place in places(tile)], axis=0)
            product = (grad.astype(F32) * attended.astype(F32)).T
            delta = jnp.concatenate([column_sum(product[:HEAD_SIZE]), column_sum(product[HEAD_SIZE:])], axis=1)
            grad = stack_heads(grad)
            score = dot_nt(kv_ref[at, lanes], query)
            allowed = both_heads(item_ref[at]) == asks_ref[pl.ds(tile, 1)]
            prob = jnp.exp(jnp.where(allowed, score, MASKED) - logsum_ref[index, pl.ds(tile, 1)])
            dprob = dot_nt(kv_ref[at, value_lanes], grad)
            dscore = (prob * (dprob - delta)).astype(BF)
            dv[at] += dot_nn(prob.astype(BF), grad)
            dk[at] += dot_nn(dscore, query)
            return dot_nn(turned_ref[lanes, at], dscore)

        for tile in range(tiles):
            first, last = near_tiles(tile, tiles)
            dq[tile] = visit(tile, slice(first * span, last * span))

        @pl.when(some_far)
        def far():
            def add(step):
                tile, other = step // tiles, step % tiles
                found = jnp.bool_(False)
                for one, two in far_pairs(tiles):
                    found = found | ((step == one * tiles + two) & tiles_meet(where_ref, one, two, parts, items))

                @pl.when(found)
                def meet():
                    at = pl.ds(pl.multiple_of(other * span, span), span)
                    dq[tile] += visit(tile, at)

            each(tiles * tiles, add)

        for tile in range(tiles):
            dquery = (join_heads(dq[tile]) * scale).astype(BF)
            for rel_c, place in enumerate(places(tile)):
                dquery_ref[place, lanes] = dquery[rel_c * TILE : (rel_c + 1) * TILE]
            for slot in range(parts):
                to = slice(slot * rows + tile * TILE, slot * rows + (tile + 1) * TILE)
                at = slice(tile * span + slot * TILE, tile * span + (slot + 1) * TILE)
                dkeys_ref[to, lanes] = dk[at].astype(BF)
                dvalues_ref[to, lanes] = dv[at].astype(BF)
        return carry

    for index in range(half // (2 * HEAD_SIZE)):
        pair(index, 0)


def twice(half_row, where_ref):
    row = both_heads(half_row)
    return jnp.where(lanes_below(row.shape, half_row.shape[1]) == (where_ref[1] == 0), row, 0.0)


def qkv_grad(where_ref, stage, vec_ref, sum_ref, dquery_ref, dkeys_ref, dvalues_ref, normed_ref, packed):
    a_ref, b_ref = stage.out(1), stage.out(3)
    near_ref, far_ref = stage[14], stage[15]
    rows, width = near_ref.shape
    core, z, y = where_ref[1], where_ref[2], where_ref[3]
    normed_ref[:rows] = normed_rows(near_ref[...], vec_ref, 0)
    normed_ref[rows:] = normed_rows(far_ref[...], vec_ref, 0)
    sum_ref[4:5] = twice(column_sum(dquery_ref[...].astype(F32)), where_ref)
    sum_ref[5:6] = twice(column_sum(dvalues_ref[...].astype(F32)), where_ref)
    for part, ref in enumerate((dquery_ref, dkeys_ref, dvalues_ref)):
        grad = dot_tn(ref[...], normed_ref[: ref.shape[0]])
        size = grad.shape[0] // 4
        for unit in range(4):
            for at_x in range(2):
                left, right = pack_unit(
                    grad[unit * size : (unit + 1) * size, at_x * width // 2 : (at_x + 1) * width // 2]
                )
                packed[2 * at_x, 4 * part + unit] = left.astype(BF)
                packed[2 * at_x + 1, 4 * part + unit] = right.astype(BF)

    def lay(index):
        rel_x, rel_y, at = index // 12, index // 6 % 2, index % 6
        unit = where_ref[UNIT_LIST + 24 * core + 12 * (y ^ rel_y) + 6 * (z % 2) + at]
        a_ref[rel_x, rel_y, lanes_at(at, packed.shape[2])] = packed[own_block(where_ref, rel_x, 0), unit]
        b_ref[rel_y, rel_x, at] = packed[own_block(where_ref, rel_x, 1), unit]

    each(24, lay)
    stage.put(1, 2, 3, 4)


def backward_kernel(
    parts, items, where_ref, stage, vec_ref, datt_ref, held, chosen, gpacked, normed_ref, packed, asks_ref, item_ref,
    turned_ref, dk, dv, dq,
):
    sum_ref, dquery_ref, dkeys_ref, dvalues_ref = (stage.out(index) for index in (10, 7, 8, 9))
    middle(parts, items, where_ref, stage, vec_ref, sum_ref, datt_ref, held, chosen, gpacked)
    attend_grad(
        parts, items, where_ref, stage, datt_ref, dquery_ref, dkeys_ref, dvalues_ref, asks_ref, item_ref, turned_ref,
        dk, dv, dq,
    )
    stage.put(7, 8, 9)
    qkv_grad(where_ref, stage, vec_ref, sum_ref, dquery_ref, dkeys_ref, dvalues_ref, normed_ref, packed)


def tokens_grad_kernel(parts, items, where_ref, stage, vec_ref):
    own_ref, far_ref, send_ref, keep_ref, sum_ref = (stage.out(index) for index in range(5))
    dquery_ref, dkeys_ref, dvalues_ref, weight_ref, near_ref, beyond_ref = (stage[index] for index in range(6))
    rows, width = own_ref.shape
    half = dquery_ref.shape[1]
    gain = jnp.zeros((1, width), F32)
    shift = gain
    for slot in (1, 3, 2, 0):
        at = slice(slot * rows, (slot + 1) * rows)
        part = dot_nt(dkeys_ref[at], weight_ref[:, half : 2 * half]) + dot_nt(dvalues_ref[at], weight_ref[:, 2 * half :])
        if slot < 2:
            part = part + dot_nt(dquery_ref[at], weight_ref[:, :half])
        xhat = (near_ref if slot < 2 else beyond_ref)[(slot % 2) * rows : (slot % 2 + 1) * rows].astype(F32)
        gain = gain + column_sum(part * xhat)
        shift = shift + column_sum(part)
        if slot % 2:
            send_ref[slot // 2 * rows : (slot // 2 + 1) * rows] = part.astype(BF)
        elif slot:
            far_ref[...] = part.astype(BF)
        else:
            own_ref[...] = part.astype(BF)
    stage.put(0, 1)
    unpack_rows(stage[6], vec_ref)
    act_ref, down_ref, cot_ref, cot_sib_ref, back_ref, bias_d_ref, bias_up_ref = (stage[index] for index in range(7, 14))
    feed = dot_nn(act_ref[...], down_ref[...])
    keep_ref[...] = feed[:rows] + vec_ref[8:9]
    send_ref[2 * rows :] = feed[rows:].astype(BF)
    stage.put(2, 3)
    scale = column_sum(cot_ref[...].astype(F32) * valid_at(where_ref, 0, 0, rows, parts, items) * keep_ref[...])
    scale = scale + column_sum(cot_sib_ref[...].astype(F32) * valid_at(where_ref, 1, 0, rows, parts, items) * feed[rows:])
    sum_ref[0:1] = gain
    sum_ref[1:2] = shift
    sum_ref[2:4] = back_ref[4:6]
    sum_ref[4:8] = back_ref[0:4]
    sum_ref[8:9] = bias_d_ref[...]
    sum_ref[9:10] = scale
    for at_x in range(2):
        one = bias_up_ref[:, at_x * width : (at_x + 1) * width]
        two = bias_up_ref[:, (1 - at_x) * width : (2 - at_x) * width]
        here = jnp.where(where_ref[0] == 0, one, two)
        for at_c in range(2):
            at = 10 + 2 * at_x + at_c
            sum_ref[at : at + 1] = jnp.where(where_ref[1] == at_c, here, 0.0)
    sum_ref[14:] = jnp.zeros((2, width), F32)


def unpack_unit(unit, target, first):
    half, lanes = unit.shape
    target[first : first + half] = unit[:, : target.shape[1]]
    target[first + half : first + 2 * half] = pltpu.roll(unit, lanes // 2, 1)[:, : target.shape[1]]


def sum_of(*terms):
    total = terms[0].astype(F32)
    for term in terms[1:]:
        total = total + term.astype(F32)
    return total


def fold_sums(sums):
    lanes = sums.shape[1] // 2
    return jnp.concatenate([sums[:, :lanes], sums[:, lanes:]], axis=0)


def second_step_kernel(where_ref, stage):
    dz_keep, dz_got, py_keep, py_got, a_ref, ux_keep, ux_got, b_got, o_ref = (stage[index] for index in range(9))
    dz_ref, x_ref, y_ref = (stage.out(index) for index in range(3))
    dz_ref[...] = sum_of(dz_keep[...], dz_got[...]).astype(BF)
    stage.put(0)
    count, rows = py_keep.shape[0], a_ref.shape[1]
    x_ref[:count] = sum_of(py_keep[...], py_got[...]).astype(BF)
    for rel_y in range(2):
        x_ref[count + rel_y * rows : count + (rel_y + 1) * rows] = a_ref[rel_y]
    stage.put(1)
    block = ux_keep.shape[1]
    for high_z in range(2):
        y_ref[high_z * block : (high_z + 1) * block] = sum_of(ux_keep[high_z], ux_got[high_z]).astype(BF)
    unit_rows = b_got.shape[2]
    first = 2 * block
    for rel_x in range(2):
        for index in range(6):
            y_ref[first : first + unit_rows] = b_got[rel_x, index]
            first += unit_rows
    rows = o_ref.shape[1]
    for rel_x in range(2):
        y_ref[first : first + rows] = o_ref[rel_x]
        first += rows


def third_step_kernel(where_ref, stage):
    ux_keep, ux_got, y_got, py_keep, py_got, x_got, b_keep, o_keep = (stage[index] for index in range(8))
    sum_refs, a_keep = [stage[index] for index in range(8, 12)], stage[12]
    send_ref, x_ref, a_ref, keep_ref = (stage.out(index) for index in range(4))
    count = py_keep.shape[0]
    block = ux_keep.shape[1]
    lead = send_ref.shape[1] - block
    same = where_ref[2] % 2 == where_ref[1]
    for high_z in range(2):
        at = slice(4 * lead + high_z * block, 4 * lead + (high_z + 1) * block)
        own = sum_of(py_keep[at], py_got[at], x_got[at])
        sib = sum_of(ux_keep[high_z], ux_got[high_z], y_got[high_z * block : (high_z + 1) * block])
        for side, ref in enumerate((keep_ref, send_ref)):
            at = slice((2 * side + high_z) * lead, (2 * side + high_z + 1) * lead)
            ref[high_z, :lead] = sum_of(py_keep[at], py_got[at], x_got[at]).astype(BF)
            here = jnp.where(same, sib, own) if side else jnp.where(same, own, sib)
            ref[high_z, lead:] = here.astype(BF)
    stage.put(0)
    unit_rows, rows = b_keep.shape[1], o_keep.shape[0]
    units = 6 * unit_rows
    first = 2 * block + units
    for index in range(6):
        at = slice(index * unit_rows, (index + 1) * unit_rows)
        x_ref[at] = sum_of(b_keep[index], y_got[first + index * unit_rows : first + (index + 1) * unit_rows]).astype(BF)
    first += units + rows
    x_ref[units : units + rows] = sum_of(o_keep[...], y_got[first : first + rows]).astype(BF)
    x_ref[units + rows :] = fold_sums(sum_of(*(ref[...] for ref in sum_refs))).astype(BF)
    stage.put(1)
    a_ref[...] = sum_of(a_keep[...], x_got[count + a_keep.shape[0] :]).astype(BF)


def last_rows(side, a_keep, a_got, a_far, b_keep, y_got, b_far, o_keep, y_rest, x_ref, ref):
    unit_rows, rows = b_keep.shape[1], o_keep.shape[0]
    units, most = 6 * unit_rows, rows // 2
    half = units // 2
    at = slice(side * half, (side + 1) * half)
    ref[:half] = sum_of(a_keep[at], a_got[at], a_far[at]).astype(BF)
    for index in range(3):
        at = slice(index * unit_rows, (index + 1) * unit_rows)
        far = slice(side * half + index * unit_rows, side * half + (index + 1) * unit_rows)
        ref[half + index * unit_rows : half + (index + 1) * unit_rows] = sum_of(
            b_keep[index], y_got[at], b_far[far]
        ).astype(BF)
    for high_z in range(2):
        first, block = units + high_z * unit_rows, 2 * side + high_z
        at = slice(units + 16 * block, units + 16 * (block + 1))
        ref[first : first + 16] = sum_of(a_keep[at], a_got[at], a_far[at]).astype(BF)
        at = slice(high_z * most, (high_z + 1) * most)
        far = units + side * rows + high_z * most
        ref[first + 16 : first + unit_rows] = sum_of(o_keep[at], y_rest[at], b_far[far : far + most]).astype(BF)
    ref[units + 2 * unit_rows :] = sum_of(x_ref[...], b_far[units + 2 * rows :]).astype(BF)


def fourth_step_kernel(where_ref, stage):
    send_ref, mlp_ref, dz_ref, dtok_ref = (stage.out(index) for index in range(4))
    last_rows(1, *(stage[index] for index in range(9)), send_ref)
    stage.put(0)
    dz_ref[...] = sum_of(stage[11][...], stage[12][...], stage[13][...]).astype(BF)
    stage.put(2)
    dtok_ref[...] = sum_of(stage[14][...], stage[15][...]).astype(BF)
    stage.put(3)
    mlp_ref[...] = sum_of(stage[9][...], stage[10][...]).astype(BF)


def kept_kernel(where_ref, stage):
    mlp_ref, kept_ref, dz_ref = (stage.out(index) for index in range(3))
    last_rows(0, *(stage[index] for index in range(9)), kept_ref)
    stage.put(1)
    dz_ref[...] = sum_of(stage[11][...], stage[12][...], stage[13][...]).astype(BF)
    stage.put(2)
    mlp_ref[...] = sum_of(stage[9][...], stage[10][...]).astype(BF)


def fifth_step_kernel(where_ref, stage, held):
    kept_ref, last_got, dz_kept, dz_got = (stage[index] for index in range(4))
    send_ref, dz_ref, keep_ref, dz_low_ref = (stage.out(index) for index in range(4))
    core, z, y = where_ref[1], where_ref[2], where_ref[3]
    unit_rows = held.shape[1]
    for index in range(6):
        at = slice(index * unit_rows, (index + 1) * unit_rows)
        held[index] = sum_of(kept_ref[at], last_got[at]).astype(BF)
    rest = sum_of(kept_ref[6 * unit_rows :], last_got[6 * unit_rows :]).astype(BF)
    for side, ref, owner_z in ((1, send_ref, z ^ 2), (0, keep_ref, z)):
        for index in range(3):
            at = where_ref[UNIT_LIST + 48 + ((core * 2 + y) * 4 + owner_z) * 3 + index]
            ref[index * unit_rows : (index + 1) * unit_rows] = held[at]
        ref[3 * unit_rows : 4 * unit_rows] = rest[side * unit_rows : (side + 1) * unit_rows]
        ref[4 * unit_rows :] = rest[2 * unit_rows :]
    stage.put(0)
    for side, ref in enumerate((dz_low_ref, dz_ref)):
        ref[...] = sum_of(dz_kept[0, side], dz_got[0, side]).astype(BF)


def finish_kernel(where_ref, stage, rows_ref, out_rows_ref, flat):
    mlp_kept, mlp_far, dz_low, dz_far, last_keep, last_far = (stage[index] for index in range(6))
    down_ref, up_ref, out_ref, vec_ref, qkv_ref = (stage.out(index) for index in range(5))
    size, block = down_ref.shape[0], up_ref.shape[0]
    lanes = up_ref.shape[1]
    mlp, dz = sum_of(mlp_kept[...], mlp_far[...]), sum_of(dz_low[...], dz_far[...])
    lead = mlp.shape[0] - block
    most = size - lead
    up_ref[...] = mlp[lead:]
    down_ref[:, :lanes] = dz[:size]
    down_ref[:most, lanes:] = dz[size : size + most]
    down_ref[most:, lanes:] = mlp[:lead]
    stage.put(0, 1)
    out_rows_ref[...] = jnp.zeros_like(out_rows_ref)
    last = sum_of(last_keep[...], last_far[...])
    half = size // 2
    unpack_unit(last[3 * half : 4 * half], out_rows_ref, 0)
    out_ref[...] = out_rows_ref[...].T[: out_ref.shape[0], : out_ref.shape[1]]
    sums = last[4 * half :]
    count = sums.shape[0] // 2
    for row in range(count):
        flat[:, 2 * row * lanes : (2 * row + 1) * lanes] = sums[row : row + 1]
        flat[:, (2 * row + 1) * lanes : (2 * row + 2) * lanes] = sums[count + row : count + row + 1]
    share = vec_ref.shape[1]
    start = (4 * set_block(where_ref, 0, 0, 0) + own_block(where_ref, 0, 0)) * share
    window = flat[:, pl.ds(pl.multiple_of(start // 128 * 128, 128), 512)]
    window = pltpu.roll(jnp.broadcast_to(window, (8, 512)), (512 - start % 128) % 512, 1)
    vec_ref[...] = window[:1, :share]
    stage.put(2, 3)
    rows_ref[...] = jnp.zeros_like(rows_ref)
    for unit in range(3):
        unpack_unit(last[unit * half : (unit + 1) * half], rows_ref, 2 * unit * half)
    qkv_ref[...] = rows_ref[...].T[: qkv_ref.shape[0], : qkv_ref.shape[1]]


def rows_kernel(parts, items, where_ref, stage, vec_ref):
    keep_ref, late_ref, far_ref, own_ref, dmid_ref, raw_ref, feed_ref, mid_ref = (stage[index] for index in range(8))
    unpack_rows(raw_ref, vec_ref)
    rows = own_ref.shape[0]
    dnormed = sum_of(keep_ref[...], late_ref[:rows], far_ref[...])
    xhat, inverse = standardise(own_ref[...].astype(F32))
    stage.out(0)[...] = (dmid_ref[...] + standardise_grad(vec_ref[0:1] * dnormed, xhat, inverse)).astype(BF)
    stage.put(0)
    valid = valid_at(where_ref, 0, 0, rows, parts, items)
    feed = sum_of(feed_ref[...], late_ref[rows:])
    stage.out(1)[...] = (valid * (mid_ref[...] + vec_ref[9:10] * feed)).astype(BF)


def swapped(array, axis, bit):
    length = lax.axis_size(axis)
    return lax.ppermute(array, axis, [(i, i ^ bit) for i in range(length)])


def to_core(array):
    return swapped(array, "blk", 1)


def to_x(array):
    return swapped(array, "blk", 2)


def to_y(array):
    return swapped(array, "dp", 1)


def to_z(array):
    return swapped(array, "dp", 2)


def to_zz(array):
    return swapped(array, "dp", 4)


def after(done, *arrays):
    return lax.optimization_barrier((done, *arrays))[1:]


def first_rows(count):
    def cut(where_ref, source, target):
        return [(source.at[:count], target)]

    return cut


def entry(array, index):
    def cut(where_ref, source, target):
        return [(source.at[index], target)]

    return (array.shape[1:], 1, cut)


def first_and_last_rows(count):
    def cut(where_ref, source, target):
        return [(source.at[:count], target.at[:count]), (source.at[2 * count :], target.at[count:])]

    return cut


def rows_of_entry(array, index, first, last):
    def cut(where_ref, source, target):
        return [(source.at[index, first:last], target)]

    return ((last - first, *array.shape[2:]), 1, cut)


def some_rows(array, first, last):
    def cut(where_ref, source, target):
        return [(source.at[first:last], target)]

    return ((last - first, *array.shape[1:]), 1, cut)


def own_columns(first):
    def cut(where_ref, source, target):
        half = source.shape[0] // 2
        return [
            (source.at[:, lanes_at(where_ref[1] + 2 * part, half)], target.at[:, (part - first) * half : (part - first + 1) * half])
            for part in range(first, 3)
        ]

    return cut


def own_hidden(axis):
    def cut(where_ref, source, target):
        pairs = []
        piece = target.shape[axis] // 4
        for rel_x in range(2):
            for side in range(2):
                at = lanes_at(hidden_unit(where_ref, rel_x, side), piece)
                to = slice((2 * rel_x + side) * piece, (2 * rel_x + side + 1) * piece)
                pairs.append((source.at[at], target.at[to]) if axis == 0 else (source.at[:, at], target.at[:, to]))
        return pairs

    return cut


def both_head_rows(where_ref, source, target):
    half = target.shape[0] // 2
    return [
        (source.at[lanes_at(where_ref[1], half), :], target.at[:half]),
        (source.at[lanes_at(1 - where_ref[1], half), :], target.at[half:]),
    ]


def own_head_rows(where_ref, source, target):
    return [(source.at[lanes_at(where_ref[1], target.shape[0]), :], target)]


def on_device_aligned(tokens, lengths, w_qkv, w_out, w_up, w_down, vectors, cotangent):
    tokens, cotangent = tokens[0], cotangent[0]
    rows, width = tokens.shape
    hidden = w_up.shape[1]
    items = lengths.shape[1]
    parts = lax.axis_size("blk")
    sets = lax.axis_size("dp")
    position, turn = lax.axis_index("blk"), lax.axis_index("dp")
    x, core, z, y = position // 2, position % 2, turn // 2, turn % 2
    where = lengths
    half = width // 2
    inner = hidden // 2
    piece = hidden // sets
    both = 2 * rows
    total_rows = parts * rows
    block = width // parts
    share = width // sets
    names = (parts, items)
    zs = sets // 2
    all_columns = ((width, 3 * half), 3, own_columns(0))
    kv_columns = ((width, 2 * half), 2, own_columns(1))
    up_columns = ((width, inner), 4, own_hidden(1))
    down_rows = ((inner, width), 4, own_hidden(0))
    head_rows = ((half, width), 1, own_head_rows)
    out_rows = ((width, width), 2, both_head_rows)

    far_a = to_x(tokens)
    sib = to_core(tokens)
    cot_sib = to_core(cotangent)

    vec = vectors.reshape(-1, 128)
    rows_of_vec = pltpu.VMEM((10, width), F32)

    xhat_near, qkv_near, dact, dfeed_turned, bias_d_sum = staged_call(
        functools.partial(prepare_kernel, *names),
        where,
        (tokens, sib, vec, w_qkv, cotangent, cot_sib, w_down),
        [low(both, width), low(both, 3 * half), low(both, inner), low(width, both), full(1, width)],
        cuts={3: all_columns, 6: down_rows},
        scratch=[rows_of_vec, pltpu.VMEM((both, width), BF), pltpu.VMEM((both, width), BF), pltpu.VMEM((2, 3 * half), F32)],
    )

    far_a, qkv_near, dact = lax.optimization_barrier((far_a, qkv_near, dact))
    far_b = to_core(far_a)

    xhat_far, kv, attended, logsum = staged_call(
        functools.partial(attend_kernel, *names),
        where,
        (far_a, far_b, vec, w_qkv, qkv_near),
        [low(both, width), low(total_rows, width), low(both, half), full(half // (2 * HEAD_SIZE), rows // TILE, 4 * TILE)],
        cuts={3: kv_columns},
        scratch=[
            rows_of_vec,
            pltpu.VMEM((total_rows, 2 * half), BF),
            pltpu.VMEM((both, width), BF),
            pltpu.VMEM((rows // TILE, 2 * TILE, 2 * TILE), jnp.int32),
        ],
    )
    attended_sib = to_core(attended)

    unit_rows = share // 2
    lead = 32
    py, us, dz = low(2, 4 * lead + 2 * block, piece), low(2, 2, block, piece), low(2, 2, 2, 2 * share - lead, piece)
    (py_keep, py_send, ux_keep, ux_send, dz_keep, dz_send, xhat_two, inverse_two, mid, branch, swap, act,
     bias_up_sum) = staged_call(
        mlp_kernel,
        where,
        (attended, attended_sib, tokens, sib, vec, w_out, w_up, dact, dfeed_turned),
        [py, py, us, us, dz, dz, low(both, width), full(both, 1), full(rows, width), low(rows, width), low(both, width),
         low(both, inner), full(1, inner)],
        cuts={5: out_rows, 6: up_columns},
        late=(6, 7, 8),
        pairs=(0, 2, 4),
        scratch=[rows_of_vec, pltpu.VMEM((sets, piece), F32), pltpu.VMEM((both, width), F32),
                 pltpu.VMEM((both, width), BF), pltpu.VMEM((both, width), BF), pltpu.VMEM((width, 2 * piece), BF),
                 pltpu.VMEM((width, both), BF), pltpu.VMEM((both, inner), BF)],
    )
    swap_got = to_core(swap)
    ux_send, ux_keep = to_core(ux_send), to_core(ux_keep)
    py_got = to_y(py_send)
    ux_got = to_x(ux_send)
    dz_got = to_z(dz_send)

    dmid, a_keep, a_send, b_keep, b_send, o_keep, o_send, dquery, dkeys, dvalues, back_sums = staged_call(
        functools.partial(backward_kernel, *names),
        where,
        (swap, swap_got, xhat_two, inverse_two, cotangent, cot_sib, vec, attended, attended_sib, w_out, branch,
         qkv_near, kv, logsum, xhat_near, xhat_far),
        [full(rows, width)] + [low(2, 6 * unit_rows + 64, half)] * 2 + [low(2, 6, unit_rows, half)] * 2
        + [low(2, 4 * unit_rows - 64, half)] * 2
        + [low(both, half), low(total_rows, half), low(total_rows, half), full(8, width)],
        cuts={9: head_rows},
        late=tuple(range(7, 16)),
        pairs=(1, 3, 5),
        tables=True,
        scratch=[rows_of_vec, pltpu.VMEM((both, half), BF), pltpu.VMEM((both, width), BF),
                 pltpu.VMEM((both, half), BF), pltpu.VMEM((2, sets, unit_rows, half), BF),
                 pltpu.VMEM((total_rows, width), BF), pltpu.VMEM((4, 12, unit_rows, half), BF),
                 pltpu.VMEM((rows // TILE, 4 * TILE), jnp.int32), pltpu.VMEM((total_rows, 2 * TILE), jnp.int32),
                 pltpu.VMEM((half, total_rows), BF), pltpu.VMEM((total_rows, 2 * HEAD_SIZE), F32),
                 pltpu.VMEM((total_rows, 2 * HEAD_SIZE), F32),
                 pltpu.VMEM((rows // TILE, 2 * HEAD_SIZE, 4 * TILE), F32)],
    )
    six, top = 6 * unit_rows, 2 * share - lead
    step = functools.partial(staged_call, grant=STEP_GRANT)
    b_send, b_keep = to_core(b_send), to_core(b_keep)
    py_got, ux_got, dz_got, b_send, b_keep = after(back_sums, py_got, ux_got, dz_got, b_send, b_keep)
    count = py_keep.shape[1]
    dz_step, x_step, y_step = staged_call(
        second_step_kernel,
        where,
        (dz_keep, dz_got, py_keep, py_got, a_send, ux_keep, ux_got, b_send, o_send),
        [low(*dz_keep.shape[1:]), low(count + 2 * six + 128, half), low(2 * block + 2 * six + 8 * unit_rows - 128, half)],
        cuts={index: entry(array, 1)
              for index, array in ((0, dz_keep), (1, dz_got), (2, py_keep), (3, py_got), (5, ux_keep), (6, ux_got))},
    )
    dz_far, x_got, y_got = to_zz(dz_step), to_x(x_step), to_y(y_step)
    (back_sums,) = after(y_step, back_sums)
    dtok_own, dtok_far, late_send, feed_keep, sums = staged_call(
        functools.partial(tokens_grad_kernel, *names),
        where,
        (dquery, dkeys, dvalues, w_qkv, xhat_near, xhat_far, vec, act, w_down, cotangent, cot_sib, back_sums,
         bias_d_sum, bias_up_sum),
        [low(rows, width), low(rows, width), low(3 * rows, width), full(rows, width), full(16, width)],
        cuts={3: all_columns, 8: down_rows},
        scratch=[rows_of_vec],
        grant=LATE_GRANT,
    )
    sums_core, sums_y = to_core(sums), to_y(sums)
    sums_far = to_core(sums_y)
    dz_far, x_got, y_got, sums_core, sums_y, sums_far = lax.optimization_barrier(
        (dz_far, x_got, y_got, sums_core, sums_y, sums_far)
    )

    rest = 4 * unit_rows - 64
    mlp_send, b_step, a_step, mlp_keep = step(
        third_step_kernel,
        where,
        (ux_keep, ux_got, y_got, py_keep, py_got, x_got, b_keep, o_keep, sums, sums_core, sums_y, sums_far, a_keep),
        [low(2, lead + block, piece), low(six + rest + 32, half), low(six + 64, half), low(2, lead + block, piece)],
        cuts={index: entry(array, 0) for index, array in ((0, ux_keep), (1, ux_got), (3, py_keep), (4, py_got))}
        | {index: entry(array, 1) for index, array in ((6, b_keep), (7, o_keep), (12, a_keep))},
    )
    mlp_got, b_far, a_far = to_z(mlp_send), to_x(b_step), to_y(a_step)
    (late_send,) = after(mlp_keep, late_send)
    late_got = to_core(late_send)
    mlp_got, b_far, a_far, late_got = lax.optimization_barrier((mlp_got, b_far, a_far, late_got))

    first, part = 2 * block + 2 * six, rest // 2

    def side_cuts(side):
        start = 2 * block + side * six // 2
        return {
            0: entry(a_keep, 0), 1: some_rows(x_got, count, count + six + 64),
            3: rows_of_entry(b_keep, 0, 3 * side, 3 * side + 3),
            4: some_rows(y_got, start, start + six // 2),
            6: rows_of_entry(o_keep, 0, side * part, (side + 1) * part),
            7: some_rows(y_got, first + side * part, first + (side + 1) * part),
            8: some_rows(b_step, six + rest, six + rest + 32),
            9: entry(mlp_keep, side), 10: entry(mlp_got, side),
            11: rows_of_entry(dz_keep, 0, side, side + 1), 12: rows_of_entry(dz_got, 0, side, side + 1),
            13: some_rows(dz_far, side, side + 1),
        }

    operands = (a_keep, x_got, a_far, b_keep, y_got, b_far, o_keep, y_got, b_step, mlp_keep, mlp_got, dz_keep, dz_got, dz_far)
    last = low(six + 2 * unit_rows + 32, half)
    last_send, mlp_step, dz_step, dtok_step = step(
        fourth_step_kernel,
        where,
        (*operands, dtok_far, late_got),
        [last, low(lead + block, piece), low(1, 2, top, piece), low(rows, width)],
        cuts=side_cuts(1) | {15: some_rows(late_got, rows, both)},
    )
    last_got, mlp_far, dz_x, dtok_x = to_z(last_send), to_zz(mlp_step), to_x(dz_step), to_x(dtok_step)
    mlp_kept, last_keep, dz_kept = step(
        kept_kernel,
        where,
        after(last_send, *operands),
        [low(lead + block, piece), last, low(1, 2, top, piece)],
        cuts=side_cuts(0),
    )
    last_send, dz_y, last_kept, dz_low = step(
        fifth_step_kernel,
        where,
        (last_keep, last_got, dz_kept, dz_x),
        [low(4 * unit_rows + 32, half), low(top, piece), low(4 * unit_rows + 32, half), low(top, piece)],
        scratch=[pltpu.VMEM((6, unit_rows, half), BF)],
        tables=True,
    )
    last_far, dz_y = to_zz(last_send), to_y(dz_y)

    (dtok_x,) = after(dz_low, dtok_x)
    grad_tokens, out = staged_call(
        functools.partial(rows_kernel, *names),
        where,
        (dtok_own, late_got, dtok_x, tokens, dmid, vec, feed_keep, mid),
        [low(rows, width), low(rows, width)],
        cuts={1: ((both, width), 2, first_and_last_rows(rows))},
        scratch=[rows_of_vec],
        grant=STEP_GRANT,
    )

    mlp_far, dz_y, last_far = after(grad_tokens, mlp_far, dz_y, last_far)
    g_w_down, g_w_up, g_w_out, g_vec, g_w_qkv = step(
        finish_kernel,
        where,
        (mlp_kept, mlp_far, dz_low, dz_y, last_kept, last_far),
        [full(share, 2 * piece), full(block, piece), full(block, share), full(1, vectors.shape[0] // (sets * parts)),
         full(block, 3 * share)],
        scratch=[pltpu.VMEM((384, 256), F32), pltpu.VMEM((128, 256), F32), pltpu.VMEM((1, 16 * width + 512), F32)],
    )
    return (out[None], grad_tokens[None], g_w_qkv, g_w_out, g_w_up, g_w_down.T, g_vec.reshape(-1))


def is_aligned(mesh, tokens, w_up):
    parts, sets = mesh.shape["blk"], mesh.shape["dp"]
    width, hidden = w_up.shape
    rows = tokens.shape[1] // parts
    return (
        parts == 4
        and sets == 2 * parts
        and rows == 4 * TILE
        and (hidden // sets) % 128 == 0
        and (width // 2) % 128 == 0
        and (width // sets) % 32 == 0
        and width == H * HEAD_SIZE
    )


def solution(mesh):
    def run(tokens, lengths, w_qkv, w_out, w_up, w_down, vectors, cotangent):
        body = on_device_aligned if is_aligned(mesh, tokens, w_up) else on_device
        return jax.shard_map(
            body,
            mesh=mesh,
            in_specs=(
                P("dp", "blk", None),
                P("dp", None),
                P(),
                P(),
                P(),
                P(),
                P(),
                P("dp", "blk", None),
            ),
            out_specs=(
                P("dp", "blk", None),
                P("dp", "blk", None),
                P("blk", "dp"),
                P("blk", "dp"),
                P("blk", "dp"),
                P("blk", "dp"),
                P(("dp", "blk")),
            ),
            check_vma=False,
        )(tokens, lengths, w_qkv, w_out, w_up, w_down, vectors, cotangent)

    return run
```

```python
import functools
import math

import jax
import jax.numpy as jnp
import numpy as np
from jax import lax
from jax.experimental import pallas as pl
from jax.experimental.pallas import tpu as pltpu
from jax.sharding import PartitionSpec as P

H = 12
HEAD_SIZE = 64
TILE = 64


EPSILON = 1e-06
FLOOR_SCORE = -1e30


def passed_along(array, axis, by):
    length = lax.axis_size(axis)
    return lax.ppermute(array, axis, [(i, (i + by) % length) for i in range(length)])


def norm_rows(values, gain, shift):
    centre = jnp.mean(values, axis=-1, keepdims=True)
    centred = values - centre
    spread = jnp.mean(centred * centred, axis=-1, keepdims=True)
    return centred * lax.rsqrt(spread + EPSILON) * gain + shift


def exact_gelu(values):
    return jax.nn.gelu(values, approximate=False)


def segment_of(rows_index, rows, parts, ends):
    place = rows_index % rows * parts + rows_index // rows
    return jnp.sum((place[:, None] >= ends[None, :]).astype(jnp.int32), axis=1)


def contract_rows(left, right):
    return lax.dot_general(
        left, right, (((0,), (0,)), ((), ())), preferred_element_type=jnp.float32
    )


def contract_cols(left, right):
    return lax.dot_general(
        left, right, (((1,), (1,)), ((), ())), preferred_element_type=jnp.float32
    )


def attend_block(query, query_item, keys, values, key_item, scale, carry):
    best, total, weighted = carry
    count = keys.shape[0]
    heads = query.shape[1]
    key_heads = keys.reshape(count, heads, -1)
    value_heads = values.reshape(count, heads, -1)
    allowed = (query_item[:, None] == key_item[None, :])[None]
    score = jnp.einsum("qhd,khd->hqk", query, key_heads, preferred_element_type=jnp.float32) * scale
    score = jnp.where(allowed, score, FLOOR_SCORE)
    newbest = jnp.maximum(best, jnp.max(score, axis=-1))
    weight = jnp.where(allowed, jnp.exp(score - newbest[..., None]), 0.0)
    factor = jnp.exp(best - newbest)
    total = total * factor + jnp.sum(weight, axis=-1)
    weighted = weighted * factor[..., None] + jnp.einsum(
        "hqk,khd->hqd", weight.astype(jnp.bfloat16), value_heads, preferred_element_type=jnp.float32
    )
    return (newbest, total, weighted)


def grad_block(query, d_out, logsum, delta, query_item, keys, values, key_item, scale):
    count = keys.shape[0]
    heads = query.shape[1]
    key_heads = keys.reshape(count, heads, -1)
    value_heads = values.reshape(count, heads, -1)
    allowed = (query_item[:, None] == key_item[None, :])[None]
    score = jnp.einsum("qhd,khd->hqk", query, key_heads, preferred_element_type=jnp.float32) * scale
    prob = jnp.where(allowed, jnp.exp(score - logsum[..., None]), 0.0)
    d_prob = jnp.einsum("qhd,khd->hqk", d_out, value_heads, preferred_element_type=jnp.float32)
    d_score = (prob * (d_prob - delta[..., None])).astype(jnp.bfloat16)
    d_query = (
        jnp.einsum("hqk,khd->qhd", d_score, key_heads, preferred_element_type=jnp.float32) * scale
    )
    d_keys = jnp.einsum("hqk,qhd->khd", d_score, query, preferred_element_type=jnp.float32) * scale
    d_values = jnp.einsum(
        "hqk,qhd->khd", prob.astype(jnp.bfloat16), d_out, preferred_element_type=jnp.float32
    )
    return (d_query, d_keys.reshape(count, -1), d_values.reshape(count, -1))


def on_device(tokens, lengths, w_qkv, w_out, w_up, w_down, vectors, cotangent):
    inputs = tokens[0].astype(jnp.float32)
    rows, width = inputs.shape
    heads = H
    head_size = width // heads
    scale = head_size ** (-0.5)
    items = lengths.shape[1]
    ends = jnp.cumsum(lengths[0])
    parts = lax.axis_size("blk")
    position = lax.axis_index("blk")
    query_item = segment_of(position * rows + lax.iota(jnp.int32, rows), rows, parts, ends)
    valid = (query_item < items).astype(jnp.float32)[:, None]
    pieces = [vectors[index * width : (index + 1) * width] for index in range(10)]
    (
        gain_one,
        shift_one,
        bias_q,
        bias_v,
        bias_o,
        scale_one,
        gain_two,
        shift_two,
        bias_d,
        scale_two,
    ) = pieces
    bias_up = vectors[10 * width :]
    normed, norm_one_pull = jax.vjp(norm_rows, inputs, gain_one, shift_one)
    normed_low = normed.astype(jnp.bfloat16)
    qkv_bias = jnp.concatenate([bias_q, jnp.zeros_like(bias_q), bias_v])
    projected = (jnp.dot(normed_low, w_qkv, preferred_element_type=jnp.float32) + qkv_bias).astype(
        jnp.bfloat16
    )
    query = projected[:, :width].reshape(rows, heads, head_size)
    keys = projected[:, width : 2 * width]
    values = projected[:, 2 * width :]
    start_state = (
        jnp.full((heads, rows), FLOOR_SCORE, jnp.float32),
        jnp.zeros((heads, rows), jnp.float32),
        jnp.zeros((heads, rows, head_size), jnp.float32),
    )
    carry = start_state
    piece = (
        lax.all_gather(keys, "blk", axis=0, tiled=True),
        lax.all_gather(values, "blk", axis=0, tiled=True),
    )
    count = piece[0].shape[0]
    size = math.gcd(count, 512)
    steps = count // size
    key_blocks = piece[0].reshape(steps, size, width)
    value_blocks = piece[1].reshape(steps, size, width)

    def inner(state, item):
        block_keys, block_values, offset = item
        key_item = segment_of(offset + lax.iota(jnp.int32, size), rows, parts, ends)
        return (
            attend_block(query, query_item, block_keys, block_values, key_item, scale, state),
            None,
        )

    carry, unused = lax.scan(
        inner, carry, (key_blocks, value_blocks, lax.iota(jnp.int32, steps) * size)
    )
    best, total, weighted = carry
    logsum = best + jnp.log(total)
    attended = (weighted / total[..., None]).transpose(1, 0, 2).reshape(rows, width)
    attended_low = attended.astype(jnp.bfloat16)
    branch = jnp.dot(attended_low, w_out, preferred_element_type=jnp.float32) + bias_o
    mid = inputs + scale_one * branch
    normed_two, norm_two_pull = jax.vjp(norm_rows, mid, gain_two, shift_two)
    normed_two_low = normed_two.astype(jnp.bfloat16)
    before = jnp.dot(normed_two_low, w_up, preferred_element_type=jnp.float32) + bias_up
    activated, gelu_pull = jax.vjp(exact_gelu, before)
    activated_low = activated.astype(jnp.bfloat16)
    feed = jnp.dot(activated_low, w_down, preferred_element_type=jnp.float32) + bias_d
    result = mid + scale_two * feed
    out = (result * valid).astype(jnp.bfloat16)
    d_result = cotangent[0].astype(jnp.float32) * valid
    d_feed = (scale_two * d_result).astype(jnp.bfloat16)
    g_scale_two = jnp.sum(d_result * feed, axis=0)
    g_bias_d = jnp.sum(d_feed.astype(jnp.float32), axis=0)
    g_w_down = contract_rows(activated_low, d_feed)
    d_activated = contract_cols(d_feed, w_down)
    d_before = gelu_pull(d_activated)[0].astype(jnp.bfloat16)
    g_bias_up = jnp.sum(d_before.astype(jnp.float32), axis=0)
    g_w_up = contract_rows(normed_two_low, d_before)
    d_normed_two = contract_cols(d_before, w_up)
    d_mid_norm, g_gain_two, g_shift_two = norm_two_pull(d_normed_two)
    d_mid = d_result + d_mid_norm
    d_branch = (scale_one * d_mid).astype(jnp.bfloat16)
    g_scale_one = jnp.sum(d_mid * branch, axis=0)
    g_bias_o = jnp.sum(d_branch.astype(jnp.float32), axis=0)
    g_w_out = contract_rows(attended_low, d_branch)
    d_attended = contract_cols(d_branch, w_out).astype(jnp.bfloat16)
    d_heads = d_attended.reshape(rows, heads, head_size)
    delta = jnp.sum(
        (d_attended.astype(jnp.float32) * attended).reshape(rows, heads, head_size), axis=-1
    ).T
    zero_query = jnp.zeros((rows, heads, head_size), jnp.float32)

    def visit_block(block_keys, block_values, owner):
        key_item = segment_of(owner * rows + lax.iota(jnp.int32, rows), rows, parts, ends)
        return grad_block(
            query, d_heads, logsum, delta, query_item, block_keys, block_values, key_item, scale
        )

    def send_back(d_keys, d_values):
        return (
            passed_along(d_keys.astype(jnp.bfloat16), "blk", 1).astype(d_keys.dtype),
            passed_along(d_values.astype(jnp.bfloat16), "blk", 1).astype(d_values.dtype),
        )

    def accumulate(state, owner):
        d_query, block_keys, block_values, d_keys, d_values = state
        dq_part, dk_part, dv_part = visit_block(block_keys, block_values, owner)
        d_keys, d_values = send_back(d_keys + dk_part, d_values + dv_part)
        return (d_query + dq_part, d_keys, d_values)

    def turn(step, state):
        owner = (position - step) % parts
        d_query, d_keys, d_values = accumulate(state, owner)
        block_keys, block_values = passed_along((state[1], state[2]), "blk", 1)
        return (d_query, block_keys, block_values, d_keys, d_values)

    zero_rows = jnp.zeros((rows, width), jnp.float32)
    state = lax.fori_loop(0, parts - 1, turn, (zero_query, keys, values, zero_rows, zero_rows))
    d_query, d_keys, d_values = accumulate(state, (position + 1) % parts)
    d_projected = jnp.concatenate([d_query.reshape(rows, width), d_keys, d_values], axis=1).astype(
        jnp.bfloat16
    )
    g_bias_q = jnp.sum(d_projected[:, :width].astype(jnp.float32), axis=0)
    g_bias_v = jnp.sum(d_projected[:, 2 * width :].astype(jnp.float32), axis=0)
    g_w_qkv = contract_rows(normed_low, d_projected)
    d_normed = contract_cols(d_projected, w_qkv)
    d_input_norm, g_gain_one, g_shift_one = norm_one_pull(d_normed)
    d_inputs = d_mid + d_input_norm
    g_vectors = jnp.concatenate(
        [
            g_gain_one,
            g_shift_one,
            g_bias_q,
            g_bias_v,
            g_bias_o,
            g_scale_one,
            g_gain_two,
            g_shift_two,
            g_bias_d,
            g_scale_two,
            g_bias_up,
        ]
    )
    column_sums = (
        lax.psum_scatter(
            g_w_qkv.astype(jnp.bfloat16), "dp", scatter_dimension=1, tiled=True
        ).astype(jnp.float32),
        lax.psum_scatter(
            g_w_out.astype(jnp.bfloat16), "dp", scatter_dimension=1, tiled=True
        ).astype(jnp.float32),
        lax.psum_scatter(g_w_up.astype(jnp.bfloat16), "dp", scatter_dimension=1, tiled=True).astype(
            jnp.float32
        ),
        lax.psum_scatter(
            g_w_down.astype(jnp.bfloat16), "dp", scatter_dimension=1, tiled=True
        ).astype(jnp.float32),
        lax.psum_scatter(
            g_vectors.astype(jnp.bfloat16), "dp", scatter_dimension=0, tiled=True
        ).astype(jnp.float32),
    )
    g_w_qkv, g_w_out, g_w_up, g_w_down, g_vectors = (
        lax.psum_scatter(
            column_sums[0].astype(jnp.bfloat16), "blk", scatter_dimension=0, tiled=True
        ).astype(jnp.float32),
        lax.psum_scatter(
            column_sums[1].astype(jnp.bfloat16), "blk", scatter_dimension=0, tiled=True
        ).astype(jnp.float32),
        lax.psum_scatter(
            column_sums[2].astype(jnp.bfloat16), "blk", scatter_dimension=0, tiled=True
        ).astype(jnp.float32),
        lax.psum_scatter(
            column_sums[3].astype(jnp.bfloat16), "blk", scatter_dimension=0, tiled=True
        ).astype(jnp.float32),
        lax.psum_scatter(
            column_sums[4].astype(jnp.bfloat16), "blk", scatter_dimension=0, tiled=True
        ).astype(jnp.float32),
    )
    return (
        out[None],
        d_inputs.astype(jnp.bfloat16)[None],
        g_w_qkv,
        g_w_out,
        g_w_up,
        g_w_down,
        g_vectors,
    )


BF = jnp.bfloat16
F32 = jnp.float32
MASKED = -1e30
GRANT = 60 * 1024 * 1024
STEP_GRANT = 20 * 1024 * 1024
LATE_GRANT = 48 * 1024 * 1024
WIDE_CHUNK = 128


def unit_tables():
    lists, places = np.zeros((2, 2, 2, 6), np.int32), np.zeros((2, 2, 4, 3), np.int32)
    units = {core: [unit for unit in range(24) if unit // 4 % 2 == core] for core in range(2)}
    for y in range(2):
        for low_z in range(2):
            first = {}
            for core in range(2):
                own = [unit for unit in units[core] if unit // 3 % 2 == y]
                first[core] = [unit for unit in own if unit // 6 % 2 == low_z]
                rest = [unit for unit in own if unit // 6 % 2 != low_z]
                lists[core, y, low_z] = [units[core].index(unit) for unit in first[core] + rest]
            for core in range(2):
                held = first[core] + first[1 - core]
                for z in (low_z, low_z + 2):
                    places[core, y, z] = [held.index(3 * (2 * z + y) + index) for index in range(3)]
    return np.concatenate([lists.reshape(-1), places.reshape(-1)])


UNIT_TABLE = unit_tables()
UNIT_LIST = 4
ENDS = UNIT_LIST + UNIT_TABLE.size


def dot_nn(left, right):
    return lax.dot_general(left, right, (((1,), (0,)), ((), ())), preferred_element_type=F32)


def dot_nt(left, right):
    return lax.dot_general(left, right, (((1,), (1,)), ((), ())), preferred_element_type=F32)


def dot_tn(left, right):
    return lax.dot_general(left, right, (((0,), (0,)), ((), ())), preferred_element_type=F32)


def standardise(values):
    centred = values - jnp.mean(values, axis=-1, keepdims=True)
    inverse = lax.rsqrt(jnp.mean(centred * centred, axis=-1, keepdims=True) + EPSILON)
    return centred * inverse, inverse


def standardise_grad(grad, xhat, inverse):
    first = jnp.mean(grad, axis=-1, keepdims=True)
    second = jnp.mean(grad * xhat, axis=-1, keepdims=True)
    return (grad - first - xhat * second) * inverse


def column_sum(values):
    return jnp.sum(values, axis=0, keepdims=True)


def item_at(place, where_ref, items):
    found = jnp.zeros_like(place)
    for index in range(items):
        found = found + (place >= where_ref[ENDS + index]).astype(jnp.int32)
    return found


def own_block(where_ref, rel_x, rel_c):
    return 2 * (where_ref[0] ^ rel_x) + (where_ref[1] ^ rel_c)


def low(*shape):
    return jax.ShapeDtypeStruct(shape, BF)


def full(*shape):
    return jax.ShapeDtypeStruct(shape, F32)


def lanes_at(index, size):
    return pl.ds(pl.multiple_of(index * size, size), size)


class Stage:
    def __init__(self, reads, places, writes):
        self.reads, self.places, self.writes = reads, places, writes
        self.started, self.waited, self.begun = set(), set(), []

    def start(self, *indices):
        for index in indices:
            if index not in self.started:
                self.started.add(index)
                for copy in self.reads[index]:
                    copy.start()

    def __getitem__(self, index):
        self.start(index)
        if index not in self.waited:
            self.waited.add(index)
            for copy in self.reads[index]:
                copy.wait()
        return self.places[index]

    def out(self, index):
        return self.writes[index][0]

    def put(self, *indices):
        for index in indices:
            self.writes[index][1].start()
            self.begun.append(index)

    def finish(self):
        for index in range(len(self.reads)):
            self[index]
        self.put(*(index for index in range(len(self.writes)) if index not in self.begun))
        for place, copy in self.writes:
            copy.wait()


class Place:
    def __init__(self, lengths_ref, table_ref):
        position, turn = lax.axis_index("blk"), lax.axis_index("dp")
        self.four = (position // 2, position % 2, turn // 2, turn % 2)
        self.table_ref = table_ref
        self.ends, end = [], jnp.int32(0)
        for index in range(lengths_ref.shape[1]):
            end = end + lengths_ref[0, index]
            self.ends.append(end)

    def __getitem__(self, index):
        if isinstance(index, int) and index < UNIT_LIST:
            return self.four[index]
        if isinstance(index, int) and index >= ENDS:
            return self.ends[index - ENDS]
        return self.table_ref[index - UNIT_LIST]


def unpack_rows(raw_ref, vec_ref):
    count = vec_ref.shape[1] // 128
    for row in range(vec_ref.shape[0]):
        for part in range(count):
            vec_ref[row : row + 1, part * 128 : (part + 1) * 128] = raw_ref[row * count + part : row * count + part + 1]


def staged_call(body, where, operands, out_shape, cuts=None, scratch=(), late=(), pairs=(), tables=False, grant=GRANT):
    cuts = cuts or {}
    count, results = len(operands), len(out_shape)
    shapes, parts = [], []
    for index, operand in enumerate(operands):
        shape, pieces = (operand.shape, 1) if index not in cuts else cuts[index][:2]
        shapes.append(pltpu.VMEM(shape, operand.dtype))
        parts.append(pieces)
    held_shapes, held_at = [], {}
    for index, item in enumerate(out_shape):
        if index - 1 in pairs:
            held_at[index] = (len(held_shapes) - 1, 1)
        elif index in pairs:
            held_at[index] = (len(held_shapes), 0)
            held_shapes.append(pltpu.VMEM((2, *item.shape), item.dtype))
        else:
            held_at[index] = (len(held_shapes), None)
            held_shapes.append(pltpu.VMEM(item.shape, item.dtype))

    def kernel(*refs):
        where_ref = Place(refs[0], refs[1] if tables else None)
        refs = refs[2 if tables else 1 :]
        ins, outs = refs[:count], refs[count : count + results]
        places = refs[count + results : 2 * count + results]
        held = refs[2 * count + results : 2 * count + results + len(held_shapes)]
        read_sem, write_sem, *rest = refs[2 * count + results + len(held_shapes) :]
        reads, used = [], 0
        for index in range(count):
            moves = [(ins[index], places[index])] if index not in cuts else cuts[index][2](where_ref, ins[index], places[index])
            reads.append([])
            for source, target in moves:
                reads[-1].append(pltpu.make_async_copy(source, target, read_sem.at[used]))
                used += 1
        writes = []
        for index in range(results):
            place, entry = held_at[index]
            source = held[place] if entry is None else held[place].at[entry]
            writes.append((held[place], pltpu.make_async_copy(source, outs[index], write_sem.at[index])))
        stage = Stage(reads, places, writes)
        stage.start(*(index for index in range(count) if index not in late))
        body(where_ref, stage, *rest)
        stage.finish()

    return pl.pallas_call(
        kernel,
        in_specs=[pl.BlockSpec(memory_space=pltpu.SMEM)] * (2 if tables else 1)
        + [pl.BlockSpec(memory_space=pl.ANY)] * count,
        out_specs=[pl.BlockSpec(memory_space=pl.ANY)] * results,
        out_shape=out_shape,
        scratch_shapes=shapes
        + held_shapes
        + [pltpu.SemaphoreType.DMA((sum(parts),)), pltpu.SemaphoreType.DMA((results,))]
        + list(scratch),
        compiler_params=pltpu.CompilerParams(vmem_limit_bytes=grant),
    )(where, *((UNIT_TABLE,) if tables else ()), *operands)


def each(count, body):
    def step(index, carry):
        body(index)
        return carry

    lax.fori_loop(0, count, step, 0)


def hidden_unit(where_ref, rel_x, side):
    return 4 * (where_ref[0] ^ rel_x) + 2 * where_ref[1] + side


def lanes_below(shape, count):
    return lax.broadcasted_iota(jnp.int32, shape, 1) < count


def stack_heads(pair):
    first = lanes_below(pair.shape, HEAD_SIZE)
    zero = jnp.zeros_like(pair)
    return jnp.concatenate([jnp.where(first, pair, zero), jnp.where(first, zero, pair)], axis=0)


def turn(source, target):
    each(source.shape[1] // 128, lambda index: target.__setitem__(lanes_at(index, 128), source[:, lanes_at(index, 128)].T))


def valid_at(where_ref, rel_c, first, count, parts, items):
    row = first + lax.broadcasted_iota(jnp.int32, (count, 1), 0)
    item = item_at(row * parts + own_block(where_ref, 0, rel_c), where_ref, items)
    return (item < items).astype(F32)


def normed_rows(xhat, vec_ref, first):
    return (xhat.astype(F32) * vec_ref[first : first + 1] + vec_ref[first + 1 : first + 2]).astype(BF)


def prepare_kernel(parts, items, where_ref, stage, vec_ref, held, normed_ref, row_ref):
    unpack_rows(stage[2], vec_ref)
    own_ref, sib_ref = stage[0], stage[1]
    stage.start(3, 4, 5, 6)
    xhat_ref, qkv_ref, dact_ref, turned_ref, sum_ref = (stage.out(index) for index in range(5))
    rows, width = own_ref.shape
    half = width // 2
    core = where_ref[1]
    for rel_c, ref in enumerate((own_ref, sib_ref)):

        def norm(index, rel_c=rel_c, ref=ref):
            xhat, unused = standardise(ref[lanes_at(index, WIDE_CHUNK)].astype(F32))
            to = lanes_at(index + rel_c * (rows // WIDE_CHUNK), WIDE_CHUNK)
            xhat_ref[to] = xhat.astype(BF)
            normed_ref[to] = (xhat * vec_ref[0:1] + vec_ref[1:2]).astype(BF)

        each(rows // WIDE_CHUNK, norm)
    stage.put(0)
    sum_ref[...] = jnp.zeros_like(sum_ref)
    for rel_c in range(2):

        def grad(index, rel_c=rel_c, ref=stage[4 + rel_c]):
            valid = valid_at(where_ref, rel_c, index * WIDE_CHUNK, WIDE_CHUNK, parts, items)
            part = (vec_ref[9:10] * (ref[lanes_at(index, WIDE_CHUNK)].astype(F32) * valid)).astype(BF)
            held[lanes_at(index + rel_c * (rows // WIDE_CHUNK), WIDE_CHUNK)] = part
            if rel_c == 0:
                sum_ref[...] += column_sum(part.astype(F32))

        each(rows // WIDE_CHUNK, grad)
    turn(held, turned_ref)
    stage.put(3, 4)
    row_ref[0:1, :half] = vec_ref[2:3, lanes_at(core, half)]
    row_ref[0:1, half : 2 * half] = jnp.zeros((1, half), F32)
    row_ref[0:1, 2 * half :] = vec_ref[3:4, lanes_at(core, half)]
    row_ref[1:2, :half] = jnp.full((1, half), HEAD_SIZE ** (-0.5), F32)
    row_ref[1:2, half:] = jnp.ones((1, 2 * half), F32)
    weight_ref = stage[3]

    def project(index):
        lanes = lanes_at(index, half)
        part = dot_nn(normed_ref[...], weight_ref[:, lanes]) + row_ref[0:1, lanes]
        qkv_ref[:, lanes] = (part.astype(BF).astype(F32) * row_ref[1:2, lanes]).astype(BF)

    each(3, project)
    stage.put(1)
    down_ref = stage[6]
    piece = dact_ref.shape[1] // 4

    def back(index):
        dact_ref[:, lanes_at(index, piece)] = dot_nt(held[...], down_ref[lanes_at(index, piece)]).astype(BF)

    each(4, back)


def item_of_place(where_ref, place, items):
    found = jnp.int32(0)
    for index in range(items):
        found = found + (place >= where_ref[ENDS + index]).astype(jnp.int32)
    return found


def tiles_meet(where_ref, one, other, parts, items):
    span = TILE * parts
    first, last = min(one, other), max(one, other)
    return item_of_place(where_ref, first * span + span - 1, items) >= item_of_place(
        where_ref, last * span, items
    )


def near_tiles(tile, tiles):
    return max(0, tile - 1), min(tiles, tile + 2)


def far_pairs(tiles):
    return [(one, other) for one in range(tiles) for other in range(tiles) if abs(one - other) > 1]


def any_far(where_ref, tiles, parts, items):
    found = jnp.bool_(False)
    for one, other in far_pairs(tiles):
        if one < other:
            found = found | tiles_meet(where_ref, one, other, parts, items)
    return found


def attend_kernel(parts, items, where_ref, stage, vec_ref, wide_ref, normed_ref, asks_ref):
    unpack_rows(stage[2], vec_ref)
    xhat_ref, kv_ref, attended_ref, logsum_ref = (stage.out(index) for index in range(4))
    far_a_ref, far_b_ref = stage[0], stage[1]
    stage.start(3, 4)
    rows, width = far_a_ref.shape
    tiles = rows // TILE
    span = parts * TILE
    both = 2 * HEAD_SIZE
    half = width // 2
    core = where_ref[1]
    for rel_c, ref in enumerate((far_a_ref, far_b_ref)):
        xhat, unused = standardise(ref[...].astype(F32))
        xhat_ref[rel_c * rows : (rel_c + 1) * rows] = xhat.astype(BF)
        normed_ref[rel_c * rows : (rel_c + 1) * rows] = normed_rows(xhat, vec_ref, 0)
    stage.put(0)
    row = lax.broadcasted_iota(jnp.int32, (2 * TILE, 2 * TILE), 0)
    block = 2 * where_ref[0] + (where_ref[1] ^ (row // TILE))
    for tile in range(tiles):
        asks_ref[tile] = item_at((tile * TILE + row % TILE) * parts + block, where_ref, items)
    lane = lax.broadcasted_iota(jnp.int32, (1, span), 1)
    slot = lane // TILE
    block = 2 * (where_ref[0] ^ (slot // 2)) + (where_ref[1] ^ (slot % 2))
    key_item = [item_at((tile * TILE + lane % TILE) * parts + block, where_ref, items) for tile in range(tiles)]
    weight_ref = stage[3]
    row_ref = jnp.concatenate([jnp.zeros((1, half), F32), vec_ref[3:4, lanes_at(core, half)]], axis=1)
    far_kv = (dot_nn(normed_ref[...], weight_ref[...]) + row_ref).astype(BF)
    qkv_ref = stage[4]
    for tile in range(tiles):
        for slot in range(2):
            at = slice(slot * rows + tile * TILE, slot * rows + (tile + 1) * TILE)
            kv_ref[tile * span + slot * TILE : tile * span + (slot + 1) * TILE] = qkv_ref[at, half:]
            kv_ref[tile * span + (slot + 2) * TILE : tile * span + (slot + 3) * TILE] = far_kv[at]
    stage.put(1)
    for index in range(half // both):
        wide_ref[:, 2 * index * both : (2 * index + 1) * both] = kv_ref[:, half + index * both : half + (index + 1) * both]
        wide_ref[:, (2 * index + 1) * both : (2 * index + 2) * both] = jnp.ones((tiles * span, both), BF)

    def attend(index, tile, first, last):
        lanes = lanes_at(index, both)
        at = slice(first * span, last * span)
        places = [pl.ds(pl.multiple_of(rel_c * rows + tile * TILE, TILE), TILE) for rel_c in range(2)]
        query = stack_heads(jnp.concatenate([qkv_ref[place, lanes] for place in places], axis=0))
        score = dot_nt(query, kv_ref[at, lanes])
        asked = asks_ref[tile][:, :1]
        allowed = jnp.concatenate([asked == key_item[other] for other in range(first, last)], axis=1)
        score = jnp.where(jnp.concatenate([allowed, allowed], axis=0), score, MASKED)
        best = jnp.max(score, axis=1, keepdims=True)
        weight = jnp.exp(score - best).astype(BF)
        mixed = dot_nn(weight, wide_ref[at, lanes_at(index, 2 * both)])
        total = mixed[:, both:]
        logsum_ref[index, pl.ds(tile, 1)] = (best + jnp.log(total)).T[:1]
        mixed = mixed[:, :both] / total
        attended = jnp.where(lanes_below((both, both), HEAD_SIZE), mixed[:both], mixed[both:]).astype(BF)
        for rel_c, place in enumerate(places):
            attended_ref[place, lanes] = attended[rel_c * TILE : (rel_c + 1) * TILE]

    def pair(index):
        for tile in range(tiles):
            attend(index, tile, *near_tiles(tile, tiles))

    each(half // both, pair)

    @pl.when(any_far(where_ref, tiles, parts, items))
    def far():
        def again(step):
            tile = step % tiles
            found = jnp.bool_(False)
            for one, other in far_pairs(tiles):
                found = found | ((tile == one) & tiles_meet(where_ref, one, other, parts, items))
            pl.when(found)(lambda: attend(step // tiles, tile, 0, tiles))

        each(half // both * tiles, again)


def gelu_with_slope(values):
    bell = jnp.exp(-0.5 * values * values)
    inverse = 1.0 / (1.0 + (0.3275911 * 0.5**0.5) * jnp.abs(values))
    series = 1.061405429
    for coefficient in (-1.453152027, 1.421413741, -0.284496736, 0.254829592):
        series = series * inverse + coefficient
    tail = 0.5 * (series * inverse) * bell
    normal = jnp.where(values >= 0, 1.0 - tail, tail)
    return values * normal, normal + values * bell * ((2.0 * math.pi) ** -0.5)


def set_block(where_ref, rel_y, low_z, high_z):
    return 2 * (where_ref[2] ^ (low_z + 2 * high_z)) + (where_ref[3] ^ rel_y)


def mlp_kernel(where_ref, stage, vec_ref, bias_ref, mid_ref, joined, normed, grad, turned, dbefore_ref):
    py_ref, ux_ref, dz_ref = stage.out(0), stage.out(2), stage.out(4)
    xhat_ref, inverse_ref, mid_own_ref, branch_ref, swap_ref, act_ref, bias_sum_ref = (
        stage.out(index) for index in range(6, 13)
    )
    unpack_rows(stage[4], vec_ref)
    att_own_ref, att_sib_ref, own_ref, sib_ref, raw_ref, out_ref = (stage[index] for index in range(6))
    stage.start(6, 7, 8)
    x, core, z, y = (where_ref[index] for index in range(4))
    rows, width = own_ref.shape
    half = width // 2
    piece = act_ref.shape[1] // 4
    joined[:, :half] = att_own_ref[...]
    joined[:rows, half:] = att_sib_ref[rows:]
    joined[rows:, half:] = att_sib_ref[:rows]

    def project(index):
        lanes = lanes_at(index, 256)
        branch = dot_nn(joined[...], out_ref[:, lanes]) + vec_ref[4:5, lanes]
        branch_ref[:, lanes] = branch[:rows].astype(BF)
        branch = vec_ref[5:6, lanes] * branch
        mid_ref[:rows, lanes] = own_ref[:, lanes].astype(F32) + branch[:rows]
        mid_ref[rows:, lanes] = sib_ref[:, lanes].astype(F32) + branch[rows:]

    each(width // 256, project)

    mid_own_ref[...] = mid_ref[:rows]

    def norm(index):
        at = lanes_at(index, WIDE_CHUNK)
        xhat, inverse = standardise(mid_ref[at])
        normed[at] = (xhat * vec_ref[6:7] + vec_ref[7:8]).astype(BF)
        xhat_ref[at] = xhat.astype(BF)
        inverse_ref[at] = inverse

    each(2 * rows // WIDE_CHUNK, norm)
    stage.put(6, 7, 8, 9)
    count = piece // 128
    for unit in range(8):
        for part in range(count):
            row = 10 * width // 128 + unit * count + part
            bias_ref[unit : unit + 1, part * 128 : (part + 1) * 128] = raw_ref[row : row + 1]
    up_ref, dact_ref, turned_ref = stage[6], stage[7], stage[8]
    size = grad.shape[0] // 8

    def hidden(index):
        rel_x = 1 - index
        count = normed.shape[0] // 2
        for side in range(2):
            at = lanes_at(2 * rel_x + side, piece)
            bias = bias_ref[pl.ds(hidden_unit(where_ref, rel_x, side), 1)]
            total = jnp.zeros((1, piece), F32)
            for part in range(2):
                here = slice(part * count, (part + 1) * count)
                act, slope = gelu_with_slope(dot_nn(normed[here], up_ref[:, at]) + bias)
                act_ref[here, at] = act.astype(BF)
                dbefore = (dact_ref[here, at].astype(F32) * slope).astype(BF)
                dbefore_ref[here, at] = dbefore
                total = total + column_sum(dbefore.astype(F32))
            bias_sum_ref[:, at] = total
            grad[:, side * piece : (side + 1) * piece] = dot_nn(turned_ref[...], act_ref[:, at]).astype(BF)

        def lay(index):
            low_z, high_z, rel_y = index // 4, index // 2 % 2, index % 2
            first = set_block(where_ref, rel_y, low_z, high_z) * size
            most = dz_ref.shape[4] - size
            dz_ref[low_z, high_z, rel_x, rel_y, :size] = grad[pl.ds(pl.multiple_of(first, size), size), :piece]
            dz_ref[low_z, high_z, rel_x, rel_y, size:] = grad[pl.ds(pl.multiple_of(first, size), most), piece:]
            py_ref[rel_y, rel_x, lanes_at(2 * low_z + high_z, size - most)] = grad[
                pl.ds(pl.multiple_of(first + most, size - most), size - most), piece:
            ]

        each(8, lay)

    each(2, hidden)
    stage.put(4, 5, 11, 12)
    turn(normed, turned)
    block = 2 * size

    def up(index):
        rel_y, high_z = index // 2, index % 2
        unit = 2 * (x ^ (z // 2) ^ high_z) + (y ^ rel_y)
        grad[:, :piece] = dot_nn(turned[...], dbefore_ref[:, lanes_at(unit, piece)]).astype(BF)
        for rel_x in range(2):
            to = pl.ds(pl.multiple_of(py_ref.shape[2] - 2 * block + high_z * block, 64), block)
            py_ref[rel_y, rel_x, to] = grad[lanes_at(own_block(where_ref, rel_x, 0), block), :piece]
            ux_ref[rel_x, rel_y, high_z] = grad[lanes_at(own_block(where_ref, rel_x, 1), block), :piece]

    for index in range(4):
        up(index)
    stage.put(0, 1, 2, 3)

    def back(index):
        lanes = lanes_at(index, 256)
        total = dot_nt(dbefore_ref[...], up_ref[lanes])
        swap_ref[:, lanes] = total.astype(BF)

    each(width // 256, back)


def middle(parts, items, where_ref, stage, vec_ref, sum_ref, datt_ref, held, chosen, packed):
    dmid_ref, a_ref, o_ref = stage.out(0), stage.out(1), stage.out(5)
    keep_ref, got_ref, xhat_ref, inverse_ref, own_ref, sib_ref, raw_ref = (stage[index] for index in range(7))
    stage.start(10, 9, 7, 8, 11, 12, 13)
    unpack_rows(raw_ref, vec_ref)
    rows, width = own_ref.shape
    half = width // 2
    core = where_ref[1]
    left_is_own = lanes_below((rows, half), half // 2) == (core == 0)
    for rel_c, ref in enumerate((own_ref, sib_ref)):
        here = slice(rel_c * rows, (rel_c + 1) * rows)
        there = slice((1 - rel_c) * rows, (2 - rel_c) * rows)
        valid = valid_at(where_ref, rel_c, 0, rows, parts, items)
        dnormed = keep_ref[here].astype(F32) + got_ref[there].astype(F32)
        xhat, inverse = xhat_ref[here].astype(F32), inverse_ref[here]
        dmid = ref[...].astype(F32) * valid + standardise_grad(vec_ref[6:7] * dnormed, xhat, inverse)
        dbranch = (vec_ref[5:6] * dmid).astype(BF)
        held[here] = dbranch
        if rel_c == 0:
            dmid_ref[...] = dmid
            sum_ref[0:1] = column_sum(dbranch.astype(F32))
            sum_ref[1:2] = column_sum(dmid * stage[10][...].astype(F32))
            sum_ref[2:3] = column_sum(dnormed * xhat)
            sum_ref[3:4] = column_sum(dnormed)
    stage.put(0)
    stage.start(14, 15)
    datt_ref[...] = dot_nt(held[...], stage[9][...]).astype(BF)
    att_own_ref, att_sib_ref = stage[7], stage[8]
    for rel_c in range(2):
        here = slice(rel_c * rows, (rel_c + 1) * rows)
        there = slice((1 - rel_c) * rows, (2 - rel_c) * rows)
        other = pltpu.roll(att_sib_ref[there].astype(F32), half // 2, 1)
        chosen[here] = jnp.where(left_is_own, att_own_ref[here].astype(F32), other).astype(BF)
    grad = dot_tn(held[...], chosen[...])
    count, unit_rows = packed.shape[1:3]
    for index in range(count):
        left, right = pack_unit(grad[2 * index * unit_rows : 2 * (index + 1) * unit_rows])
        packed[0, index] = left.astype(BF)
        packed[1, index] = right.astype(BF)

    units = 6 * unit_rows

    def lay(index):
        rel_x, rel_y, block = index // 8, index // 4 % 2, index % 4
        here = packed.at[where_ref[0] ^ rel_x, set_block(where_ref, rel_y, block // 2, block % 2)]
        a_ref[rel_x, rel_y, pl.ds(pl.multiple_of(units + 16 * block, 16), 16)] = here[:16]
        o_ref[rel_y, rel_x, lanes_at(block, unit_rows - 16)] = here[16:]

    each(16, lay)
    stage.put(5, 6)


def pack_unit(unit):
    half = unit.shape[0] // 2
    width = unit.shape[1]
    top, bottom = unit[:half], unit[half:]
    first = lanes_below((half, width), width // 2)
    left = jnp.where(first, top, pltpu.roll(bottom, width // 2, 1))
    right = jnp.where(first, pltpu.roll(top, width // 2, 1), bottom)
    return left, right


def join_heads(stacked_turned):
    stacked = stacked_turned.T
    count = stacked.shape[0] // 2
    return jnp.where(
        lanes_below((count, stacked.shape[1]), HEAD_SIZE), stacked[:count], stacked[count:]
    )


def query_items(where_ref, tile, parts, items):
    lane = lax.broadcasted_iota(jnp.int32, (1, 4 * TILE), 1)
    rel_c = (lane // TILE) % 2
    block = 2 * where_ref[0] + (where_ref[1] ^ rel_c)
    return item_at((tile * TILE + lane % TILE) * parts + block, where_ref, items)


def fill_key_items(where_ref, item_ref, tiles, parts, items):
    row = lax.broadcasted_iota(jnp.int32, (TILE, item_ref.shape[1]), 0)
    for tile in range(tiles):
        for slot in range(parts):
            block = own_block(where_ref, slot // 2, slot % 2)
            at = (tile * parts + slot) * TILE
            item_ref[at : at + TILE] = item_at((tile * TILE + row) * parts + block, where_ref, items)


def both_heads(array):
    return jnp.concatenate([array, array], axis=1)


def attend_grad(
    parts, items, where_ref, stage, datt_ref, dquery_ref, dkeys_ref, dvalues_ref, asks_ref, item_ref, turned_ref, dk, dv, dq
):
    attended_ref, qkv_ref, kv_ref, logsum_ref = stage[7], stage[11], stage[12], stage[13]
    half = datt_ref.shape[1]
    rows = datt_ref.shape[0] // 2
    tiles = rows // TILE
    span = parts * TILE
    scale = HEAD_SIZE ** (-0.5)
    turned_ref[...] = kv_ref[:, :half].T
    fill_key_items(where_ref, item_ref, tiles, parts, items)
    for tile in range(tiles):
        asks_ref[tile : tile + 1] = query_items(where_ref, tile, parts, items)
    some_far = any_far(where_ref, tiles, parts, items)

    def pair(index, carry):
        lanes = lanes_at(index, 2 * HEAD_SIZE)
        value_lanes = pl.ds(pl.multiple_of(half + index * 2 * HEAD_SIZE, 2 * HEAD_SIZE), 2 * HEAD_SIZE)
        dk[...] = jnp.zeros_like(dk)
        dv[...] = jnp.zeros_like(dv)

        def places(tile):
            return [pl.ds(pl.multiple_of(rel_c * rows + tile * TILE, TILE), TILE) for rel_c in range(2)]

        def visit(tile, at):
            query = stack_heads(jnp.concatenate([qkv_ref[place, lanes] for place in places(tile)], axis=0))
            grad = jnp.concatenate([datt_ref[place, lanes] for place in places(tile)], axis=0)
            attended = jnp.concatenate([attended_ref[place, lanes] for place in places(tile)], axis=0)
            product = (grad.astype(F32) * attended.astype(F32)).T
            delta = jnp.concatenate([column_sum(product[:HEAD_SIZE]), column_sum(product[HEAD_SIZE:])], axis=1)
            grad = stack_heads(grad)
            score = dot_nt(kv_ref[at, lanes], query)
            allowed = both_heads(item_ref[at]) == asks_ref[pl.ds(tile, 1)]
            prob = jnp.exp(jnp.where(allowed, score, MASKED) - logsum_ref[index, pl.ds(tile, 1)])
            dprob = dot_nt(kv_ref[at, value_lanes], grad)
            dscore = (prob * (dprob - delta)).astype(BF)
            dv[at] += dot_nn(prob.astype(BF), grad)
            dk[at] += dot_nn(dscore, query)
            return dot_nn(turned_ref[lanes, at], dscore)

        for tile in range(tiles):
            first, last = near_tiles(tile, tiles)
            dq[tile] = visit(tile, slice(first * span, last * span))

        @pl.when(some_far)
        def far():
            def add(step):
                tile, other = step // tiles, step % tiles
                found = jnp.bool_(False)
                for one, two in far_pairs(tiles):
                    found = found | ((step == one * tiles + two) & tiles_meet(where_ref, one, two, parts, items))

                @pl.when(found)
                def meet():
                    at = pl.ds(pl.multiple_of(other * span, span), span)
                    dq[tile] += visit(tile, at)

            each(tiles * tiles, add)

        for tile in range(tiles):
            dquery = (join_heads(dq[tile]) * scale).astype(BF)
            for rel_c, place in enumerate(places(tile)):
                dquery_ref[place, lanes] = dquery[rel_c * TILE : (rel_c + 1) * TILE]
            for slot in range(parts):
                to = slice(slot * rows + tile * TILE, slot * rows + (tile + 1) * TILE)
                at = slice(tile * span + slot * TILE, tile * span + (slot + 1) * TILE)
                dkeys_ref[to, lanes] = dk[at].astype(BF)
                dvalues_ref[to, lanes] = dv[at].astype(BF)
        return carry

    for index in range(half // (2 * HEAD_SIZE)):
        pair(index, 0)


def twice(half_row, where_ref):
    row = both_heads(half_row)
    return jnp.where(lanes_below(row.shape, half_row.shape[1]) == (where_ref[1] == 0), row, 0.0)


def qkv_grad(where_ref, stage, vec_ref, sum_ref, dquery_ref, dkeys_ref, dvalues_ref, normed_ref, packed):
    a_ref, b_ref = stage.out(1), stage.out(3)
    near_ref, far_ref = stage[14], stage[15]
    rows, width = near_ref.shape
    core, z, y = where_ref[1], where_ref[2], where_ref[3]
    normed_ref[:rows] = normed_rows(near_ref[...], vec_ref, 0)
    normed_ref[rows:] = normed_rows(far_ref[...], vec_ref, 0)
    sum_ref[4:5] = twice(column_sum(dquery_ref[...].astype(F32)), where_ref)
    sum_ref[5:6] = twice(column_sum(dvalues_ref[...].astype(F32)), where_ref)
    for part, ref in enumerate((dquery_ref, dkeys_ref, dvalues_ref)):
        grad = dot_tn(ref[...], normed_ref[: ref.shape[0]])
        size = grad.shape[0] // 4
        for unit in range(4):
            for at_x in range(2):
                left, right = pack_unit(
                    grad[unit * size : (unit + 1) * size, at_x * width // 2 : (at_x + 1) * width // 2]
                )
                packed[2 * at_x, 4 * part + unit] = left.astype(BF)
                packed[2 * at_x + 1, 4 * part + unit] = right.astype(BF)

    def lay(index):
        rel_x, rel_y, at = index // 12, index // 6 % 2, index % 6
        unit = where_ref[UNIT_LIST + 24 * core + 12 * (y ^ rel_y) + 6 * (z % 2) + at]
        a_ref[rel_x, rel_y, lanes_at(at, packed.shape[2])] = packed[own_block(where_ref, rel_x, 0), unit]
        b_ref[rel_y, rel_x, at] = packed[own_block(where_ref, rel_x, 1), unit]

    each(24, lay)
    stage.put(1, 2, 3, 4)


def backward_kernel(
    parts, items, where_ref, stage, vec_ref, datt_ref, held, chosen, gpacked, normed_ref, packed, asks_ref, item_ref,
    turned_ref, dk, dv, dq,
):
    sum_ref, dquery_ref, dkeys_ref, dvalues_ref = (stage.out(index) for index in (10, 7, 8, 9))
    middle(parts, items, where_ref, stage, vec_ref, sum_ref, datt_ref, held, chosen, gpacked)
    attend_grad(
        parts, items, where_ref, stage, datt_ref, dquery_ref, dkeys_ref, dvalues_ref, asks_ref, item_ref, turned_ref,
        dk, dv, dq,
    )
    stage.put(7, 8, 9)
    qkv_grad(where_ref, stage, vec_ref, sum_ref, dquery_ref, dkeys_ref, dvalues_ref, normed_ref, packed)


def tokens_grad_kernel(parts, items, where_ref, stage, vec_ref):
    own_ref, far_ref, send_ref, keep_ref, sum_ref = (stage.out(index) for index in range(5))
    dquery_ref, dkeys_ref, dvalues_ref, weight_ref, near_ref, beyond_ref = (stage[index] for index in range(6))
    rows, width = own_ref.shape
    half = dquery_ref.shape[1]
    gain = jnp.zeros((1, width), F32)
    shift = gain
    for slot in (1, 3, 2, 0):
        at = slice(slot * rows, (slot + 1) * rows)
        part = dot_nt(dkeys_ref[at], weight_ref[:, half : 2 * half]) + dot_nt(dvalues_ref[at], weight_ref[:, 2 * half :])
        if slot < 2:
            part = part + dot_nt(dquery_ref[at], weight_ref[:, :half])
        xhat = (near_ref if slot < 2 else beyond_ref)[(slot % 2) * rows : (slot % 2 + 1) * rows].astype(F32)
        gain = gain + column_sum(part * xhat)
        shift = shift + column_sum(part)
        if slot % 2:
            send_ref[slot // 2 * rows : (slot // 2 + 1) * rows] = part.astype(BF)
        elif slot:
            far_ref[...] = part.astype(BF)
        else:
            own_ref[...] = part.astype(BF)
    stage.put(0, 1)
    unpack_rows(stage[6], vec_ref)
    act_ref, down_ref, cot_ref, cot_sib_ref, back_ref, bias_d_ref, bias_up_ref = (stage[index] for index in range(7, 14))
    feed = dot_nn(act_ref[...], down_ref[...])
    keep_ref[...] = feed[:rows] + vec_ref[8:9]
    send_ref[2 * rows :] = feed[rows:].astype(BF)
    stage.put(2, 3)
    scale = column_sum(cot_ref[...].astype(F32) * valid_at(where_ref, 0, 0, rows, parts, items) * keep_ref[...])
    scale = scale + column_sum(cot_sib_ref[...].astype(F32) * valid_at(where_ref, 1, 0, rows, parts, items) * feed[rows:])
    sum_ref[0:1] = gain
    sum_ref[1:2] = shift
    sum_ref[2:4] = back_ref[4:6]
    sum_ref[4:8] = back_ref[0:4]
    sum_ref[8:9] = bias_d_ref[...]
    sum_ref[9:10] = scale
    for at_x in range(2):
        one = bias_up_ref[:, at_x * width : (at_x + 1) * width]
        two = bias_up_ref[:, (1 - at_x) * width : (2 - at_x) * width]
        here = jnp.where(where_ref[0] == 0, one, two)
        for at_c in range(2):
            at = 10 + 2 * at_x + at_c
            sum_ref[at : at + 1] = jnp.where(where_ref[1] == at_c, here, 0.0)
    sum_ref[14:] = jnp.zeros((2, width), F32)


def unpack_unit(unit, target, first):
    half, lanes = unit.shape
    target[first : first + half] = unit[:, : target.shape[1]]
    target[first + half : first + 2 * half] = pltpu.roll(unit, lanes // 2, 1)[:, : target.shape[1]]


def sum_of(*terms):
    total = terms[0].astype(F32)
    for term in terms[1:]:
        total = total + term.astype(F32)
    return total


def fold_sums(sums):
    lanes = sums.shape[1] // 2
    return jnp.concatenate([sums[:, :lanes], sums[:, lanes:]], axis=0)


def second_step_kernel(where_ref, stage):
    dz_keep, dz_got, py_keep, py_got, a_ref, ux_keep, ux_got, b_got, o_ref = (stage[index] for index in range(9))
    dz_ref, x_ref, y_ref = (stage.out(index) for index in range(3))
    dz_ref[...] = sum_of(dz_keep[...], dz_got[...]).astype(BF)
    stage.put(0)
    count, rows = py_keep.shape[0], a_ref.shape[1]
    x_ref[:count] = sum_of(py_keep[...], py_got[...]).astype(BF)
    for rel_y in range(2):
        x_ref[count + rel_y * rows : count + (rel_y + 1) * rows] = a_ref[rel_y]
    stage.put(1)
    block = ux_keep.shape[1]
    for high_z in range(2):
        y_ref[high_z * block : (high_z + 1) * block] = sum_of(ux_keep[high_z], ux_got[high_z]).astype(BF)
    unit_rows = b_got.shape[2]
    first = 2 * block
    for rel_x in range(2):
        for index in range(6):
            y_ref[first : first + unit_rows] = b_got[rel_x, index]
            first += unit_rows
    rows = o_ref.shape[1]
    for rel_x in range(2):
        y_ref[first : first + rows] = o_ref[rel_x]
        first += rows


def mlp_rows(side, where_ref, ux_keep, ux_got, y_got, py_keep, py_got, x_got, ref):
    block = ux_keep.shape[1]
    lead = ref.shape[1] - block
    same = where_ref[2] % 2 == where_ref[1]
    for high_z in range(2):
        at = slice(2 * lead + high_z * block, 2 * lead + (high_z + 1) * block)
        own = sum_of(py_keep[at], py_got[at], x_got[at])
        sib = sum_of(ux_keep[high_z], ux_got[high_z], y_got[high_z * block : (high_z + 1) * block])
        at = slice(high_z * lead, (high_z + 1) * lead)
        ref[high_z, :lead] = sum_of(py_keep[at], py_got[at], x_got[at]).astype(BF)
        here = jnp.where(same, sib, own) if side else jnp.where(same, own, sib)
        ref[high_z, lead:] = here.astype(BF)


def third_step_kernel(where_ref, stage):
    send_ref, x_ref, a_ref = (stage.out(index) for index in range(3))
    mlp_rows(1, where_ref, *(stage[index] for index in range(6)), send_ref)
    stage.put(0)
    b_keep, b_got, o_keep, o_got = (stage[index] for index in range(6, 10))
    sum_refs, a_keep, a_got = [stage[index] for index in range(10, 14)], stage[14], stage[15]
    unit_rows, rows = b_keep.shape[1], o_keep.shape[0]
    units = 6 * unit_rows
    for index in range(6):
        at = slice(index * unit_rows, (index + 1) * unit_rows)
        x_ref[at] = sum_of(b_keep[index], b_got[at]).astype(BF)
    x_ref[units : units + rows] = sum_of(o_keep[...], o_got[...]).astype(BF)
    x_ref[units + rows :] = fold_sums(sum_of(*(ref[...] for ref in sum_refs))).astype(BF)
    stage.put(1)
    a_ref[...] = sum_of(a_keep[...], a_got[...]).astype(BF)


def mlp_kept_kernel(where_ref, stage):
    mlp_rows(0, where_ref, *(stage[index] for index in range(6)), stage.out(0))


def last_rows(side, a_keep, a_got, a_far, b_keep, y_got, b_far, o_keep, y_rest, x_ref, ref):
    unit_rows, rows = b_keep.shape[1], o_keep.shape[0]
    units, most = 6 * unit_rows, rows // 2
    half = units // 2
    at = slice(side * half, (side + 1) * half)
    ref[:half] = sum_of(a_keep[at], a_got[at], a_far[at]).astype(BF)
    for index in range(3):
        at = slice(index * unit_rows, (index + 1) * unit_rows)
        far = slice(side * half + index * unit_rows, side * half + (index + 1) * unit_rows)
        ref[half + index * unit_rows : half + (index + 1) * unit_rows] = sum_of(
            b_keep[index], y_got[at], b_far[far]
        ).astype(BF)
    for high_z in range(2):
        first, block = units + high_z * unit_rows, 2 * side + high_z
        at = slice(units + 16 * block, units + 16 * (block + 1))
        ref[first : first + 16] = sum_of(a_keep[at], a_got[at], a_far[at]).astype(BF)
        at = slice(high_z * most, (high_z + 1) * most)
        far = units + side * rows + high_z * most
        ref[first + 16 : first + unit_rows] = sum_of(o_keep[at], y_rest[at], b_far[far : far + most]).astype(BF)
    ref[units + 2 * unit_rows :] = sum_of(x_ref[...], b_far[units + 2 * rows :]).astype(BF)


def fourth_step_kernel(where_ref, stage):
    send_ref, dz_ref, dtok_ref = (stage.out(index) for index in range(3))
    last_rows(1, *(stage[index] for index in range(9)), send_ref)
    stage.put(0)
    dz_ref[...] = sum_of(stage[9][...], stage[10][...], stage[11][...]).astype(BF)
    stage.put(1)
    dtok_ref[...] = sum_of(stage[12][...], stage[13][...]).astype(BF)


def kept_kernel(where_ref, stage):
    mlp_ref, mlp_kept, kept_ref, dz_ref = (stage.out(index) for index in range(4))
    mlp_ref[...] = sum_of(stage[12][1], stage[13][1]).astype(BF)
    mlp_kept[...] = sum_of(stage[12][0], stage[13][0]).astype(BF)
    stage.put(0, 1)
    last_rows(0, *(stage[index] for index in range(9)), kept_ref)
    stage.put(2)
    dz_ref[...] = sum_of(stage[9][...], stage[10][...], stage[11][...]).astype(BF)


def fifth_step_kernel(where_ref, stage, held):
    kept_ref, last_got, dz_kept, dz_got = (stage[index] for index in range(4))
    send_ref, dz_ref, keep_ref, dz_low_ref = (stage.out(index) for index in range(4))
    core, z, y = where_ref[1], where_ref[2], where_ref[3]
    unit_rows = held.shape[1]
    for index in range(6):
        at = slice(index * unit_rows, (index + 1) * unit_rows)
        held[index] = sum_of(kept_ref[at], last_got[at]).astype(BF)
    rest = sum_of(kept_ref[6 * unit_rows :], last_got[6 * unit_rows :]).astype(BF)
    for side, ref, owner_z in ((1, send_ref, z ^ 2), (0, keep_ref, z)):
        for index in range(3):
            at = where_ref[UNIT_LIST + 48 + ((core * 2 + y) * 4 + owner_z) * 3 + index]
            ref[index * unit_rows : (index + 1) * unit_rows] = held[at]
        ref[3 * unit_rows : 4 * unit_rows] = rest[side * unit_rows : (side + 1) * unit_rows]
        ref[4 * unit_rows :] = rest[2 * unit_rows :]
    stage.put(0)
    for side, ref in enumerate((dz_low_ref, dz_ref)):
        ref[...] = sum_of(dz_kept[0, side], dz_got[0, side]).astype(BF)


def finish_kernel(where_ref, stage, rows_ref, out_rows_ref, flat):
    mlp_kept, mlp_far, dz_low, dz_far, last_keep, last_far = (stage[index] for index in range(6))
    down_ref, up_ref, out_ref, vec_ref, qkv_ref = (stage.out(index) for index in range(5))
    size, block = down_ref.shape[0], up_ref.shape[0]
    lanes = up_ref.shape[1]
    mlp, dz = sum_of(mlp_kept[...], mlp_far[...]), sum_of(dz_low[...], dz_far[...])
    lead = mlp.shape[0] - block
    most = size - lead
    up_ref[...] = mlp[lead:]
    down_ref[:, :lanes] = dz[:size]
    down_ref[:most, lanes:] = dz[size : size + most]
    down_ref[most:, lanes:] = mlp[:lead]
    stage.put(0, 1)
    out_rows_ref[...] = jnp.zeros_like(out_rows_ref)
    last = sum_of(last_keep[...], last_far[...])
    half = size // 2
    unpack_unit(last[3 * half : 4 * half], out_rows_ref, 0)
    out_ref[...] = out_rows_ref[...].T[: out_ref.shape[0], : out_ref.shape[1]]
    sums = last[4 * half :]
    count = sums.shape[0] // 2
    for row in range(count):
        flat[:, 2 * row * lanes : (2 * row + 1) * lanes] = sums[row : row + 1]
        flat[:, (2 * row + 1) * lanes : (2 * row + 2) * lanes] = sums[count + row : count + row + 1]
    share = vec_ref.shape[1]
    start = (4 * set_block(where_ref, 0, 0, 0) + own_block(where_ref, 0, 0)) * share
    window = flat[:, pl.ds(pl.multiple_of(start // 128 * 128, 128), 512)]
    window = pltpu.roll(jnp.broadcast_to(window, (8, 512)), (512 - start % 128) % 512, 1)
    vec_ref[...] = window[:1, :share]
    stage.put(2, 3)
    rows_ref[...] = jnp.zeros_like(rows_ref)
    for unit in range(3):
        unpack_unit(last[unit * half : (unit + 1) * half], rows_ref, 2 * unit * half)
    qkv_ref[...] = rows_ref[...].T[: qkv_ref.shape[0], : qkv_ref.shape[1]]


def rows_kernel(parts, items, where_ref, stage, vec_ref):
    keep_ref, late_ref, far_ref, own_ref, dmid_ref, raw_ref, feed_ref, mid_ref = (stage[index] for index in range(8))
    unpack_rows(raw_ref, vec_ref)
    rows = own_ref.shape[0]
    dnormed = sum_of(keep_ref[...], late_ref[:rows], far_ref[...])
    xhat, inverse = standardise(own_ref[...].astype(F32))
    stage.out(0)[...] = (dmid_ref[...] + standardise_grad(vec_ref[0:1] * dnormed, xhat, inverse)).astype(BF)
    stage.put(0)
    valid = valid_at(where_ref, 0, 0, rows, parts, items)
    feed = sum_of(feed_ref[...], late_ref[rows:])
    stage.out(1)[...] = (valid * (mid_ref[...] + vec_ref[9:10] * feed)).astype(BF)


def swapped(array, axis, bit):
    length = lax.axis_size(axis)
    return lax.ppermute(array, axis, [(i, i ^ bit) for i in range(length)])


def to_core(array):
    return swapped(array, "blk", 1)


def to_x(array):
    return swapped(array, "blk", 2)


def to_y(array):
    return swapped(array, "dp", 1)


def to_z(array):
    return swapped(array, "dp", 2)


def to_zz(array):
    return swapped(array, "dp", 4)


def after(done, *arrays):
    return lax.optimization_barrier((done, *arrays))[1:]


def first_rows(count):
    def cut(where_ref, source, target):
        return [(source.at[:count], target)]

    return cut


def entry(array, index):
    def cut(where_ref, source, target):
        return [(source.at[index], target)]

    return (array.shape[1:], 1, cut)


def first_and_last_rows(count):
    def cut(where_ref, source, target):
        return [(source.at[:count], target.at[:count]), (source.at[2 * count :], target.at[count:])]

    return cut


def rows_of_entry(array, index, first, last):
    def cut(where_ref, source, target):
        return [(source.at[index, first:last], target)]

    return ((last - first, *array.shape[2:]), 1, cut)


def joined_rows(array, index, pieces):
    def cut(where_ref, source, target):
        moves, to = [], 0
        for first, last in pieces:
            at = source.at[first:last] if index is None else source.at[index, first:last]
            moves.append((at, target.at[to : to + last - first]))
            to += last - first
        return moves

    count = sum(last - first for first, last in pieces)
    return ((count, array.shape[-1]), len(pieces), cut)


def some_rows(array, first, last):
    def cut(where_ref, source, target):
        return [(source.at[first:last], target)]

    return ((last - first, *array.shape[1:]), 1, cut)


def own_columns(first):
    def cut(where_ref, source, target):
        half = source.shape[0] // 2
        return [
            (source.at[:, lanes_at(where_ref[1] + 2 * part, half)], target.at[:, (part - first) * half : (part - first + 1) * half])
            for part in range(first, 3)
        ]

    return cut


def own_hidden(axis):
    def cut(where_ref, source, target):
        pairs = []
        piece = target.shape[axis] // 4
        for rel_x in range(2):
            for side in range(2):
                at = lanes_at(hidden_unit(where_ref, rel_x, side), piece)
                to = slice((2 * rel_x + side) * piece, (2 * rel_x + side + 1) * piece)
                pairs.append((source.at[at], target.at[to]) if axis == 0 else (source.at[:, at], target.at[:, to]))
        return pairs

    return cut


def both_head_rows(where_ref, source, target):
    half = target.shape[0] // 2
    return [
        (source.at[lanes_at(where_ref[1], half), :], target.at[:half]),
        (source.at[lanes_at(1 - where_ref[1], half), :], target.at[half:]),
    ]


def own_head_rows(where_ref, source, target):
    return [(source.at[lanes_at(where_ref[1], target.shape[0]), :], target)]


def on_device_aligned(tokens, lengths, w_qkv, w_out, w_up, w_down, vectors, cotangent):
    tokens, cotangent = tokens[0], cotangent[0]
    rows, width = tokens.shape
    hidden = w_up.shape[1]
    items = lengths.shape[1]
    parts = lax.axis_size("blk")
    sets = lax.axis_size("dp")
    position, turn = lax.axis_index("blk"), lax.axis_index("dp")
    x, core, z, y = position // 2, position % 2, turn // 2, turn % 2
    where = lengths
    half = width // 2
    inner = hidden // 2
    piece = hidden // sets
    both = 2 * rows
    total_rows = parts * rows
    block = width // parts
    share = width // sets
    names = (parts, items)
    zs = sets // 2
    all_columns = ((width, 3 * half), 3, own_columns(0))
    kv_columns = ((width, 2 * half), 2, own_columns(1))
    up_columns = ((width, inner), 4, own_hidden(1))
    down_rows = ((inner, width), 4, own_hidden(0))
    head_rows = ((half, width), 1, own_head_rows)
    out_rows = ((width, width), 2, both_head_rows)

    far_a = to_x(tokens)
    sib = to_core(tokens)
    cot_sib = to_core(cotangent)

    vec = vectors.reshape(-1, 128)
    rows_of_vec = pltpu.VMEM((10, width), F32)

    xhat_near, qkv_near, dact, dfeed_turned, bias_d_sum = staged_call(
        functools.partial(prepare_kernel, *names),
        where,
        (tokens, sib, vec, w_qkv, cotangent, cot_sib, w_down),
        [low(both, width), low(both, 3 * half), low(both, inner), low(width, both), full(1, width)],
        cuts={3: all_columns, 6: down_rows},
        scratch=[rows_of_vec, pltpu.VMEM((both, width), BF), pltpu.VMEM((both, width), BF), pltpu.VMEM((2, 3 * half), F32)],
    )

    far_a, qkv_near, dact = lax.optimization_barrier((far_a, qkv_near, dact))
    far_b = to_core(far_a)

    xhat_far, kv, attended, logsum = staged_call(
        functools.partial(attend_kernel, *names),
        where,
        (far_a, far_b, vec, w_qkv, qkv_near),
        [low(both, width), low(total_rows, width), low(both, half), full(half // (2 * HEAD_SIZE), rows // TILE, 4 * TILE)],
        cuts={3: kv_columns},
        scratch=[
            rows_of_vec,
            pltpu.VMEM((total_rows, 2 * half), BF),
            pltpu.VMEM((both, width), BF),
            pltpu.VMEM((rows // TILE, 2 * TILE, 2 * TILE), jnp.int32),
        ],
    )
    attended_sib = to_core(attended)

    unit_rows = share // 2
    lead = 32
    py, us, dz = low(2, 4 * lead + 2 * block, piece), low(2, 2, block, piece), low(2, 2, 2, 2 * share - lead, piece)
    (py_keep, py_send, ux_keep, ux_send, dz_keep, dz_send, xhat_two, inverse_two, mid, branch, swap, act,
     bias_up_sum) = staged_call(
        mlp_kernel,
        where,
        (attended, attended_sib, tokens, sib, vec, w_out, w_up, dact, dfeed_turned),
        [py, py, us, us, dz, dz, low(both, width), full(both, 1), full(rows, width), low(rows, width), low(both, width),
         low(both, inner), full(1, inner)],
        cuts={5: out_rows, 6: up_columns},
        late=(6, 7, 8),
        pairs=(0, 2, 4),
        scratch=[rows_of_vec, pltpu.VMEM((sets, piece), F32), pltpu.VMEM((both, width), F32),
                 pltpu.VMEM((both, width), BF), pltpu.VMEM((both, width), BF), pltpu.VMEM((width, 2 * piece), BF),
                 pltpu.VMEM((width, both), BF), pltpu.VMEM((both, inner), BF)],
    )
    swap_got = to_core(swap)
    ux_send, ux_keep = to_core(ux_send), to_core(ux_keep)
    py_got = to_y(py_send)
    ux_got = to_x(ux_send)
    dz_got = to_z(dz_send)

    dmid, a_keep, a_send, b_keep, b_send, o_keep, o_send, dquery, dkeys, dvalues, back_sums = staged_call(
        functools.partial(backward_kernel, *names),
        where,
        (swap, swap_got, xhat_two, inverse_two, cotangent, cot_sib, vec, attended, attended_sib, w_out, branch,
         qkv_near, kv, logsum, xhat_near, xhat_far),
        [full(rows, width)] + [low(2, 6 * unit_rows + 64, half)] * 2 + [low(2, 6, unit_rows, half)] * 2
        + [low(2, 4 * unit_rows - 64, half)] * 2
        + [low(both, half), low(total_rows, half), low(total_rows, half), full(8, width)],
        cuts={9: head_rows},
        late=tuple(range(7, 16)),
        pairs=(1, 3, 5),
        tables=True,
        scratch=[rows_of_vec, pltpu.VMEM((both, half), BF), pltpu.VMEM((both, width), BF),
                 pltpu.VMEM((both, half), BF), pltpu.VMEM((2, sets, unit_rows, half), BF),
                 pltpu.VMEM((total_rows, width), BF), pltpu.VMEM((4, 12, unit_rows, half), BF),
                 pltpu.VMEM((rows // TILE, 4 * TILE), jnp.int32), pltpu.VMEM((total_rows, 2 * TILE), jnp.int32),
                 pltpu.VMEM((half, total_rows), BF), pltpu.VMEM((total_rows, 2 * HEAD_SIZE), F32),
                 pltpu.VMEM((total_rows, 2 * HEAD_SIZE), F32),
                 pltpu.VMEM((rows // TILE, 2 * HEAD_SIZE, 4 * TILE), F32)],
    )
    six, top = 6 * unit_rows, 2 * share - lead
    step = functools.partial(staged_call, grant=STEP_GRANT)
    b_send, b_keep = to_core(b_send), to_core(b_keep)
    py_got, ux_got, dz_got, b_send, b_keep = after(back_sums, py_got, ux_got, dz_got, b_send, b_keep)
    count = py_keep.shape[1]
    dz_step, x_step, y_step = staged_call(
        second_step_kernel,
        where,
        (dz_keep, dz_got, py_keep, py_got, a_send, ux_keep, ux_got, b_send, o_send),
        [low(*dz_keep.shape[1:]), low(count + 2 * six + 128, half), low(2 * block + 2 * six + 8 * unit_rows - 128, half)],
        cuts={index: entry(array, 1)
              for index, array in ((0, dz_keep), (1, dz_got), (2, py_keep), (3, py_got), (5, ux_keep), (6, ux_got))},
    )
    dz_far, x_got, y_got = to_zz(dz_step), to_x(x_step), to_y(y_step)
    (back_sums,) = after(y_step, back_sums)
    dtok_own, dtok_far, late_send, feed_keep, sums = staged_call(
        functools.partial(tokens_grad_kernel, *names),
        where,
        (dquery, dkeys, dvalues, w_qkv, xhat_near, xhat_far, vec, act, w_down, cotangent, cot_sib, back_sums,
         bias_d_sum, bias_up_sum),
        [low(rows, width), low(rows, width), low(3 * rows, width), full(rows, width), full(16, width)],
        cuts={3: all_columns, 8: down_rows},
        scratch=[rows_of_vec],
        grant=LATE_GRANT,
    )
    sums_core, sums_y = to_core(sums), to_y(sums)
    sums_far = to_core(sums_y)
    dz_far, x_got, y_got, sums_core, sums_y, sums_far = lax.optimization_barrier(
        (dz_far, x_got, y_got, sums_core, sums_y, sums_far)
    )

    rest = 4 * unit_rows - 64
    first = 2 * block + 2 * six

    def mlp_cuts(side):
        pieces = [(side * 2 * lead, (side + 1) * 2 * lead), (4 * lead, 4 * lead + 2 * block)]
        return {0: entry(ux_keep, 0), 1: entry(ux_got, 0), 2: some_rows(y_got, 0, 2 * block),
                3: joined_rows(py_keep, 0, pieces), 4: joined_rows(py_got, 0, pieces), 5: joined_rows(x_got, None, pieces)}

    operands = (ux_keep, ux_got, y_got, py_keep, py_got, x_got)
    mlp_send, b_step, a_step = step(
        third_step_kernel,
        where,
        (*operands, b_keep, y_got, o_keep, y_got, sums, sums_core, sums_y, sums_far, a_keep, x_got),
        [low(2, lead + block, piece), low(six + rest + 32, half), low(six + 64, half)],
        cuts=mlp_cuts(1)
        | {6: entry(b_keep, 1), 7: some_rows(y_got, 2 * block + six, first), 8: entry(o_keep, 1),
           9: some_rows(y_got, first + rest, first + 2 * rest), 14: entry(a_keep, 1),
           15: some_rows(x_got, count + six + 64, count + 2 * (six + 64))},
    )
    mlp_got, b_far, a_far = to_z(mlp_send), to_x(b_step), to_y(a_step)
    (mlp_keep,) = step(
        mlp_kept_kernel, where, after(mlp_send, *operands), [low(2, lead + block, piece)], cuts=mlp_cuts(0)
    )
    (late_send,) = after(mlp_send, late_send)
    late_got = to_core(late_send)
    mlp_got, b_far, a_far, late_got, mlp_keep = lax.optimization_barrier((mlp_got, b_far, a_far, late_got, mlp_keep))

    first, part = 2 * block + 2 * six, rest // 2

    def side_cuts(side):
        start = 2 * block + side * six // 2
        return {
            0: entry(a_keep, 0), 1: some_rows(x_got, count, count + six + 64),
            3: rows_of_entry(b_keep, 0, 3 * side, 3 * side + 3),
            4: some_rows(y_got, start, start + six // 2),
            6: rows_of_entry(o_keep, 0, side * part, (side + 1) * part),
            7: some_rows(y_got, first + side * part, first + (side + 1) * part),
            8: some_rows(b_step, six + rest, six + rest + 32),
            9: rows_of_entry(dz_keep, 0, side, side + 1), 10: rows_of_entry(dz_got, 0, side, side + 1),
            11: some_rows(dz_far, side, side + 1),
        }

    operands = (a_keep, x_got, a_far, b_keep, y_got, b_far, o_keep, y_got, b_step, dz_keep, dz_got, dz_far)
    last = low(six + 2 * unit_rows + 32, half)
    last_send, dz_step, dtok_step = step(
        fourth_step_kernel,
        where,
        (*operands, dtok_far, late_got),
        [last, low(1, 2, top, piece), low(rows, width)],
        cuts=side_cuts(1) | {13: some_rows(late_got, rows, both)},
    )
    last_got, dz_x, dtok_x = to_z(last_send), to_x(dz_step), to_x(dtok_step)
    mlp_step, mlp_kept, last_keep, dz_kept = step(
        kept_kernel,
        where,
        after(last_send, *operands, mlp_keep, mlp_got),
        [low(lead + block, piece)] * 2 + [last, low(1, 2, top, piece)],
        cuts=side_cuts(0),
    )
    mlp_far = to_zz(mlp_step)
    last_send, dz_y, last_kept, dz_low = step(
        fifth_step_kernel,
        where,
        (last_keep, last_got, dz_kept, dz_x),
        [low(4 * unit_rows + 32, half), low(top, piece), low(4 * unit_rows + 32, half), low(top, piece)],
        scratch=[pltpu.VMEM((6, unit_rows, half), BF)],
        tables=True,
    )
    last_far, dz_y = to_zz(last_send), to_y(dz_y)

    (dtok_x,) = after(dz_low, dtok_x)
    grad_tokens, out = staged_call(
        functools.partial(rows_kernel, *names),
        where,
        (dtok_own, late_got, dtok_x, tokens, dmid, vec, feed_keep, mid),
        [low(rows, width), low(rows, width)],
        cuts={1: ((both, width), 2, first_and_last_rows(rows))},
        scratch=[rows_of_vec],
        grant=STEP_GRANT,
    )

    mlp_far, dz_y, last_far = after(grad_tokens, mlp_far, dz_y, last_far)
    g_w_down, g_w_up, g_w_out, g_vec, g_w_qkv = step(
        finish_kernel,
        where,
        (mlp_kept, mlp_far, dz_low, dz_y, last_kept, last_far),
        [full(share, 2 * piece), full(block, piece), full(block, share), full(1, vectors.shape[0] // (sets * parts)),
         full(block, 3 * share)],
        scratch=[pltpu.VMEM((384, 256), F32), pltpu.VMEM((128, 256), F32), pltpu.VMEM((1, 16 * width + 512), F32)],
    )
    return (out[None], grad_tokens[None], g_w_qkv, g_w_out, g_w_up, g_w_down.T, g_vec.reshape(-1))


def is_aligned(mesh, tokens, w_up):
    parts, sets = mesh.shape["blk"], mesh.shape["dp"]
    width, hidden = w_up.shape
    rows = tokens.shape[1] // parts
    return (
        parts == 4
        and sets == 2 * parts
        and rows == 4 * TILE
        and (hidden // sets) % 128 == 0
        and (width // 2) % 128 == 0
        and (width // sets) % 32 == 0
        and width == H * HEAD_SIZE
    )


def solution(mesh):
    def run(tokens, lengths, w_qkv, w_out, w_up, w_down, vectors, cotangent):
        body = on_device_aligned if is_aligned(mesh, tokens, w_up) else on_device
        return jax.shard_map(
            body,
            mesh=mesh,
            in_specs=(
                P("dp", "blk", None),
                P("dp", None),
                P(),
                P(),
                P(),
                P(),
                P(),
                P("dp", "blk", None),
            ),
            out_specs=(
                P("dp", "blk", None),
                P("dp", "blk", None),
                P("blk", "dp"),
                P("blk", "dp"),
                P("blk", "dp"),
                P("blk", "dp"),
                P(("dp", "blk")),
            ),
            check_vma=False,
        )(tokens, lengths, w_qkv, w_out, w_up, w_down, vectors, cotangent)

    return run
```

```python
import functools
import math

import jax
import jax.numpy as jnp
import numpy as np
from jax import lax
from jax.experimental import pallas as pl
from jax.experimental.pallas import tpu as pltpu
from jax.sharding import PartitionSpec as P

H = 12
HEAD_SIZE = 64
TILE = 64


EPSILON = 1e-06
FLOOR_SCORE = -1e30


def passed_along(array, axis, by):
    length = lax.axis_size(axis)
    return lax.ppermute(array, axis, [(i, (i + by) % length) for i in range(length)])


def norm_rows(values, gain, shift):
    centre = jnp.mean(values, axis=-1, keepdims=True)
    centred = values - centre
    spread = jnp.mean(centred * centred, axis=-1, keepdims=True)
    return centred * lax.rsqrt(spread + EPSILON) * gain + shift


def exact_gelu(values):
    return jax.nn.gelu(values, approximate=False)


def segment_of(rows_index, rows, parts, ends):
    place = rows_index % rows * parts + rows_index // rows
    return jnp.sum((place[:, None] >= ends[None, :]).astype(jnp.int32), axis=1)


def contract_rows(left, right):
    return lax.dot_general(
        left, right, (((0,), (0,)), ((), ())), preferred_element_type=jnp.float32
    )


def contract_cols(left, right):
    return lax.dot_general(
        left, right, (((1,), (1,)), ((), ())), preferred_element_type=jnp.float32
    )


def attend_block(query, query_item, keys, values, key_item, scale, carry):
    best, total, weighted = carry
    count = keys.shape[0]
    heads = query.shape[1]
    key_heads = keys.reshape(count, heads, -1)
    value_heads = values.reshape(count, heads, -1)
    allowed = (query_item[:, None] == key_item[None, :])[None]
    score = jnp.einsum("qhd,khd->hqk", query, key_heads, preferred_element_type=jnp.float32) * scale
    score = jnp.where(allowed, score, FLOOR_SCORE)
    newbest = jnp.maximum(best, jnp.max(score, axis=-1))
    weight = jnp.where(allowed, jnp.exp(score - newbest[..., None]), 0.0)
    factor = jnp.exp(best - newbest)
    total = total * factor + jnp.sum(weight, axis=-1)
    weighted = weighted * factor[..., None] + jnp.einsum(
        "hqk,khd->hqd", weight.astype(jnp.bfloat16), value_heads, preferred_element_type=jnp.float32
    )
    return (newbest, total, weighted)


def grad_block(query, d_out, logsum, delta, query_item, keys, values, key_item, scale):
    count = keys.shape[0]
    heads = query.shape[1]
    key_heads = keys.reshape(count, heads, -1)
    value_heads = values.reshape(count, heads, -1)
    allowed = (query_item[:, None] == key_item[None, :])[None]
    score = jnp.einsum("qhd,khd->hqk", query, key_heads, preferred_element_type=jnp.float32) * scale
    prob = jnp.where(allowed, jnp.exp(score - logsum[..., None]), 0.0)
    d_prob = jnp.einsum("qhd,khd->hqk", d_out, value_heads, preferred_element_type=jnp.float32)
    d_score = (prob * (d_prob - delta[..., None])).astype(jnp.bfloat16)
    d_query = (
        jnp.einsum("hqk,khd->qhd", d_score, key_heads, preferred_element_type=jnp.float32) * scale
    )
    d_keys = jnp.einsum("hqk,qhd->khd", d_score, query, preferred_element_type=jnp.float32) * scale
    d_values = jnp.einsum(
        "hqk,qhd->khd", prob.astype(jnp.bfloat16), d_out, preferred_element_type=jnp.float32
    )
    return (d_query, d_keys.reshape(count, -1), d_values.reshape(count, -1))


def on_device(tokens, lengths, w_qkv, w_out, w_up, w_down, vectors, cotangent):
    inputs = tokens[0].astype(jnp.float32)
    rows, width = inputs.shape
    heads = H
    head_size = width // heads
    scale = head_size ** (-0.5)
    items = lengths.shape[1]
    ends = jnp.cumsum(lengths[0])
    parts = lax.axis_size("blk")
    position = lax.axis_index("blk")
    query_item = segment_of(position * rows + lax.iota(jnp.int32, rows), rows, parts, ends)
    valid = (query_item < items).astype(jnp.float32)[:, None]
    pieces = [vectors[index * width : (index + 1) * width] for index in range(10)]
    (
        gain_one,
        shift_one,
        bias_q,
        bias_v,
        bias_o,
        scale_one,
        gain_two,
        shift_two,
        bias_d,
        scale_two,
    ) = pieces
    bias_up = vectors[10 * width :]
    normed, norm_one_pull = jax.vjp(norm_rows, inputs, gain_one, shift_one)
    normed_low = normed.astype(jnp.bfloat16)
    qkv_bias = jnp.concatenate([bias_q, jnp.zeros_like(bias_q), bias_v])
    projected = (jnp.dot(normed_low, w_qkv, preferred_element_type=jnp.float32) + qkv_bias).astype(
        jnp.bfloat16
    )
    query = projected[:, :width].reshape(rows, heads, head_size)
    keys = projected[:, width : 2 * width]
    values = projected[:, 2 * width :]
    start_state = (
        jnp.full((heads, rows), FLOOR_SCORE, jnp.float32),
        jnp.zeros((heads, rows), jnp.float32),
        jnp.zeros((heads, rows, head_size), jnp.float32),
    )
    carry = start_state
    piece = (
        lax.all_gather(keys, "blk", axis=0, tiled=True),
        lax.all_gather(values, "blk", axis=0, tiled=True),
    )
    count = piece[0].shape[0]
    size = math.gcd(count, 512)
    steps = count // size
    key_blocks = piece[0].reshape(steps, size, width)
    value_blocks = piece[1].reshape(steps, size, width)

    def inner(state, item):
        block_keys, block_values, offset = item
        key_item = segment_of(offset + lax.iota(jnp.int32, size), rows, parts, ends)
        return (
            attend_block(query, query_item, block_keys, block_values, key_item, scale, state),
            None,
        )

    carry, unused = lax.scan(
        inner, carry, (key_blocks, value_blocks, lax.iota(jnp.int32, steps) * size)
    )
    best, total, weighted = carry
    logsum = best + jnp.log(total)
    attended = (weighted / total[..., None]).transpose(1, 0, 2).reshape(rows, width)
    attended_low = attended.astype(jnp.bfloat16)
    branch = jnp.dot(attended_low, w_out, preferred_element_type=jnp.float32) + bias_o
    mid = inputs + scale_one * branch
    normed_two, norm_two_pull = jax.vjp(norm_rows, mid, gain_two, shift_two)
    normed_two_low = normed_two.astype(jnp.bfloat16)
    before = jnp.dot(normed_two_low, w_up, preferred_element_type=jnp.float32) + bias_up
    activated, gelu_pull = jax.vjp(exact_gelu, before)
    activated_low = activated.astype(jnp.bfloat16)
    feed = jnp.dot(activated_low, w_down, preferred_element_type=jnp.float32) + bias_d
    result = mid + scale_two * feed
    out = (result * valid).astype(jnp.bfloat16)
    d_result = cotangent[0].astype(jnp.float32) * valid
    d_feed = (scale_two * d_result).astype(jnp.bfloat16)
    g_scale_two = jnp.sum(d_result * feed, axis=0)
    g_bias_d = jnp.sum(d_feed.astype(jnp.float32), axis=0)
    g_w_down = contract_rows(activated_low, d_feed)
    d_activated = contract_cols(d_feed, w_down)
    d_before = gelu_pull(d_activated)[0].astype(jnp.bfloat16)
    g_bias_up = jnp.sum(d_before.astype(jnp.float32), axis=0)
    g_w_up = contract_rows(normed_two_low, d_before)
    d_normed_two = contract_cols(d_before, w_up)
    d_mid_norm, g_gain_two, g_shift_two = norm_two_pull(d_normed_two)
    d_mid = d_result + d_mid_norm
    d_branch = (scale_one * d_mid).astype(jnp.bfloat16)
    g_scale_one = jnp.sum(d_mid * branch, axis=0)
    g_bias_o = jnp.sum(d_branch.astype(jnp.float32), axis=0)
    g_w_out = contract_rows(attended_low, d_branch)
    d_attended = contract_cols(d_branch, w_out).astype(jnp.bfloat16)
    d_heads = d_attended.reshape(rows, heads, head_size)
    delta = jnp.sum(
        (d_attended.astype(jnp.float32) * attended).reshape(rows, heads, head_size), axis=-1
    ).T
    zero_query = jnp.zeros((rows, heads, head_size), jnp.float32)

    def visit_block(block_keys, block_values, owner):
        key_item = segment_of(owner * rows + lax.iota(jnp.int32, rows), rows, parts, ends)
        return grad_block(
            query, d_heads, logsum, delta, query_item, block_keys, block_values, key_item, scale
        )

    def send_back(d_keys, d_values):
        return (
            passed_along(d_keys.astype(jnp.bfloat16), "blk", 1).astype(d_keys.dtype),
            passed_along(d_values.astype(jnp.bfloat16), "blk", 1).astype(d_values.dtype),
        )

    def accumulate(state, owner):
        d_query, block_keys, block_values, d_keys, d_values = state
        dq_part, dk_part, dv_part = visit_block(block_keys, block_values, owner)
        d_keys, d_values = send_back(d_keys + dk_part, d_values + dv_part)
        return (d_query + dq_part, d_keys, d_values)

    def turn(step, state):
        owner = (position - step) % parts
        d_query, d_keys, d_values = accumulate(state, owner)
        block_keys, block_values = passed_along((state[1], state[2]), "blk", 1)
        return (d_query, block_keys, block_values, d_keys, d_values)

    zero_rows = jnp.zeros((rows, width), jnp.float32)
    state = lax.fori_loop(0, parts - 1, turn, (zero_query, keys, values, zero_rows, zero_rows))
    d_query, d_keys, d_values = accumulate(state, (position + 1) % parts)
    d_projected = jnp.concatenate([d_query.reshape(rows, width), d_keys, d_values], axis=1).astype(
        jnp.bfloat16
    )
    g_bias_q = jnp.sum(d_projected[:, :width].astype(jnp.float32), axis=0)
    g_bias_v = jnp.sum(d_projected[:, 2 * width :].astype(jnp.float32), axis=0)
    g_w_qkv = contract_rows(normed_low, d_projected)
    d_normed = contract_cols(d_projected, w_qkv)
    d_input_norm, g_gain_one, g_shift_one = norm_one_pull(d_normed)
    d_inputs = d_mid + d_input_norm
    g_vectors = jnp.concatenate(
        [
            g_gain_one,
            g_shift_one,
            g_bias_q,
            g_bias_v,
            g_bias_o,
            g_scale_one,
            g_gain_two,
            g_shift_two,
            g_bias_d,
            g_scale_two,
            g_bias_up,
        ]
    )
    column_sums = (
        lax.psum_scatter(
            g_w_qkv.astype(jnp.bfloat16), "dp", scatter_dimension=1, tiled=True
        ).astype(jnp.float32),
        lax.psum_scatter(
            g_w_out.astype(jnp.bfloat16), "dp", scatter_dimension=1, tiled=True
        ).astype(jnp.float32),
        lax.psum_scatter(g_w_up.astype(jnp.bfloat16), "dp", scatter_dimension=1, tiled=True).astype(
            jnp.float32
        ),
        lax.psum_scatter(
            g_w_down.astype(jnp.bfloat16), "dp", scatter_dimension=1, tiled=True
        ).astype(jnp.float32),
        lax.psum_scatter(
            g_vectors.astype(jnp.bfloat16), "dp", scatter_dimension=0, tiled=True
        ).astype(jnp.float32),
    )
    g_w_qkv, g_w_out, g_w_up, g_w_down, g_vectors = (
        lax.psum_scatter(
            column_sums[0].astype(jnp.bfloat16), "blk", scatter_dimension=0, tiled=True
        ).astype(jnp.float32),
        lax.psum_scatter(
            column_sums[1].astype(jnp.bfloat16), "blk", scatter_dimension=0, tiled=True
        ).astype(jnp.float32),
        lax.psum_scatter(
            column_sums[2].astype(jnp.bfloat16), "blk", scatter_dimension=0, tiled=True
        ).astype(jnp.float32),
        lax.psum_scatter(
            column_sums[3].astype(jnp.bfloat16), "blk", scatter_dimension=0, tiled=True
        ).astype(jnp.float32),
        lax.psum_scatter(
            column_sums[4].astype(jnp.bfloat16), "blk", scatter_dimension=0, tiled=True
        ).astype(jnp.float32),
    )
    return (
        out[None],
        d_inputs.astype(jnp.bfloat16)[None],
        g_w_qkv,
        g_w_out,
        g_w_up,
        g_w_down,
        g_vectors,
    )


BF = jnp.bfloat16
F32 = jnp.float32
MASKED = -1e30
GRANT = 60 * 1024 * 1024
STEP_GRANT = 20 * 1024 * 1024
LATE_GRANT = 48 * 1024 * 1024
WIDE_CHUNK = 128


def unit_tables():
    lists, places = np.zeros((2, 2, 2, 6), np.int32), np.zeros((2, 2, 4, 3), np.int32)
    units = {core: [unit for unit in range(24) if unit // 4 % 2 == core] for core in range(2)}
    for y in range(2):
        for low_z in range(2):
            first = {}
            for core in range(2):
                own = [unit for unit in units[core] if unit // 3 % 2 == y]
                first[core] = [unit for unit in own if unit // 6 % 2 == low_z]
                rest = [unit for unit in own if unit // 6 % 2 != low_z]
                lists[core, y, low_z] = [units[core].index(unit) for unit in first[core] + rest]
            for core in range(2):
                held = first[core] + first[1 - core]
                for z in (low_z, low_z + 2):
                    places[core, y, z] = [held.index(3 * (2 * z + y) + index) for index in range(3)]
    return np.concatenate([lists.reshape(-1), places.reshape(-1)])


UNIT_TABLE = unit_tables()
UNIT_LIST = 4
ENDS = UNIT_LIST + UNIT_TABLE.size


def dot_nn(left, right):
    return lax.dot_general(left, right, (((1,), (0,)), ((), ())), preferred_element_type=F32)


def dot_nt(left, right):
    return lax.dot_general(left, right, (((1,), (1,)), ((), ())), preferred_element_type=F32)


def dot_tn(left, right):
    return lax.dot_general(left, right, (((0,), (0,)), ((), ())), preferred_element_type=F32)


def standardise(values):
    centred = values - jnp.mean(values, axis=-1, keepdims=True)
    inverse = lax.rsqrt(jnp.mean(centred * centred, axis=-1, keepdims=True) + EPSILON)
    return centred * inverse, inverse


def standardise_grad(grad, xhat, inverse):
    first = jnp.mean(grad, axis=-1, keepdims=True)
    second = jnp.mean(grad * xhat, axis=-1, keepdims=True)
    return (grad - first - xhat * second) * inverse


def column_sum(values):
    return jnp.sum(values, axis=0, keepdims=True)


def item_at(place, where_ref, items):
    found = jnp.zeros_like(place)
    for index in range(items):
        found = found + (place >= where_ref[ENDS + index]).astype(jnp.int32)
    return found


def own_block(where_ref, rel_x, rel_c):
    return 2 * (where_ref[0] ^ rel_x) + (where_ref[1] ^ rel_c)


def low(*shape):
    return jax.ShapeDtypeStruct(shape, BF)


def full(*shape):
    return jax.ShapeDtypeStruct(shape, F32)


def lanes_at(index, size):
    return pl.ds(pl.multiple_of(index * size, size), size)


class Stage:
    def __init__(self, reads, places, writes):
        self.reads, self.places, self.writes = reads, places, writes
        self.started, self.waited, self.begun = set(), set(), []

    def start(self, *indices):
        for index in indices:
            if index not in self.started:
                self.started.add(index)
                for copy in self.reads[index]:
                    copy.start()

    def __getitem__(self, index):
        self.start(index)
        if index not in self.waited:
            self.waited.add(index)
            for copy in self.reads[index]:
                copy.wait()
        return self.places[index]

    def out(self, index):
        return self.writes[index][0]

    def put(self, *indices):
        for index in indices:
            self.writes[index][1].start()
            self.begun.append(index)

    def finish(self):
        for index in range(len(self.reads)):
            self[index]
        self.put(*(index for index in range(len(self.writes)) if index not in self.begun))
        for place, copy in self.writes:
            copy.wait()


class Place:
    def __init__(self, lengths_ref, table_ref):
        position, turn = lax.axis_index("blk"), lax.axis_index("dp")
        self.four = (position // 2, position % 2, turn // 2, turn % 2)
        self.table_ref = table_ref
        self.ends, end = [], jnp.int32(0)
        for index in range(lengths_ref.shape[1]):
            end = end + lengths_ref[0, index]
            self.ends.append(end)

    def __getitem__(self, index):
        if isinstance(index, int) and index < UNIT_LIST:
            return self.four[index]
        if isinstance(index, int) and index >= ENDS:
            return self.ends[index - ENDS]
        return self.table_ref[index - UNIT_LIST]


def unpack_rows(raw_ref, vec_ref):
    count = vec_ref.shape[1] // 128
    for row in range(vec_ref.shape[0]):
        for part in range(count):
            vec_ref[row : row + 1, part * 128 : (part + 1) * 128] = raw_ref[row * count + part : row * count + part + 1]


def staged_call(body, where, operands, out_shape, cuts=None, scratch=(), late=(), pairs=(), tables=False, grant=GRANT):
    cuts = cuts or {}
    count, results = len(operands), len(out_shape)
    shapes, parts = [], []
    for index, operand in enumerate(operands):
        shape, pieces = (operand.shape, 1) if index not in cuts else cuts[index][:2]
        shapes.append(pltpu.VMEM(shape, operand.dtype))
        parts.append(pieces)
    held_shapes, held_at = [], {}
    for index, item in enumerate(out_shape):
        if index - 1 in pairs:
            held_at[index] = (len(held_shapes) - 1, 1)
        elif index in pairs:
            held_at[index] = (len(held_shapes), 0)
            held_shapes.append(pltpu.VMEM((2, *item.shape), item.dtype))
        else:
            held_at[index] = (len(held_shapes), None)
            held_shapes.append(pltpu.VMEM(item.shape, item.dtype))

    def kernel(*refs):
        where_ref = Place(refs[0], refs[1] if tables else None)
        refs = refs[2 if tables else 1 :]
        ins, outs = refs[:count], refs[count : count + results]
        places = refs[count + results : 2 * count + results]
        held = refs[2 * count + results : 2 * count + results + len(held_shapes)]
        read_sem, write_sem, *rest = refs[2 * count + results + len(held_shapes) :]
        reads, used = [], 0
        for index in range(count):
            moves = [(ins[index], places[index])] if index not in cuts else cuts[index][2](where_ref, ins[index], places[index])
            reads.append([])
            for source, target in moves:
                reads[-1].append(pltpu.make_async_copy(source, target, read_sem.at[used]))
                used += 1
        writes = []
        for index in range(results):
            place, entry = held_at[index]
            source = held[place] if entry is None else held[place].at[entry]
            writes.append((held[place], pltpu.make_async_copy(source, outs[index], write_sem.at[index])))
        stage = Stage(reads, places, writes)
        stage.start(*(index for index in range(count) if index not in late))
        body(where_ref, stage, *rest)
        stage.finish()

    return pl.pallas_call(
        kernel,
        in_specs=[pl.BlockSpec(memory_space=pltpu.SMEM)] * (2 if tables else 1)
        + [pl.BlockSpec(memory_space=pl.ANY)] * count,
        out_specs=[pl.BlockSpec(memory_space=pl.ANY)] * results,
        out_shape=out_shape,
        scratch_shapes=shapes
        + held_shapes
        + [pltpu.SemaphoreType.DMA((sum(parts),)), pltpu.SemaphoreType.DMA((results,))]
        + list(scratch),
        compiler_params=pltpu.CompilerParams(vmem_limit_bytes=grant),
    )(where, *((UNIT_TABLE,) if tables else ()), *operands)


def each(count, body):
    def step(index, carry):
        body(index)
        return carry

    lax.fori_loop(0, count, step, 0)


def hidden_unit(where_ref, rel_x, side):
    return 4 * (where_ref[0] ^ rel_x) + 2 * where_ref[1] + side


def lanes_below(shape, count):
    return lax.broadcasted_iota(jnp.int32, shape, 1) < count


def stack_heads(pair):
    first = lanes_below(pair.shape, HEAD_SIZE)
    zero = jnp.zeros_like(pair)
    return jnp.concatenate([jnp.where(first, pair, zero), jnp.where(first, zero, pair)], axis=0)


def turn(source, target):
    each(source.shape[1] // 128, lambda index: target.__setitem__(lanes_at(index, 128), source[:, lanes_at(index, 128)].T))


def valid_at(where_ref, rel_c, first, count, parts, items):
    row = first + lax.broadcasted_iota(jnp.int32, (count, 1), 0)
    item = item_at(row * parts + own_block(where_ref, 0, rel_c), where_ref, items)
    return (item < items).astype(F32)


def normed_rows(xhat, vec_ref, first):
    return (xhat.astype(F32) * vec_ref[first : first + 1] + vec_ref[first + 1 : first + 2]).astype(BF)


def prepare_kernel(parts, items, where_ref, stage, vec_ref, held, normed_ref, row_ref):
    unpack_rows(stage[2], vec_ref)
    own_ref, sib_ref = stage[0], stage[1]
    stage.start(3, 4, 5, 6)
    xhat_ref, qkv_ref, dact_ref, turned_ref, sum_ref = (stage.out(index) for index in range(5))
    rows, width = own_ref.shape
    half = width // 2
    core = where_ref[1]
    for rel_c, ref in enumerate((own_ref, sib_ref)):

        def norm(index, rel_c=rel_c, ref=ref):
            xhat, unused = standardise(ref[lanes_at(index, WIDE_CHUNK)].astype(F32))
            to = lanes_at(index + rel_c * (rows // WIDE_CHUNK), WIDE_CHUNK)
            xhat_ref[to] = xhat.astype(BF)
            normed_ref[to] = (xhat * vec_ref[0:1] + vec_ref[1:2]).astype(BF)

        each(rows // WIDE_CHUNK, norm)
    stage.put(0)
    sum_ref[...] = jnp.zeros_like(sum_ref)
    for rel_c in range(2):

        def grad(index, rel_c=rel_c, ref=stage[4 + rel_c]):
            valid = valid_at(where_ref, rel_c, index * WIDE_CHUNK, WIDE_CHUNK, parts, items)
            part = (vec_ref[9:10] * (ref[lanes_at(index, WIDE_CHUNK)].astype(F32) * valid)).astype(BF)
            held[lanes_at(index + rel_c * (rows // WIDE_CHUNK), WIDE_CHUNK)] = part
            if rel_c == 0:
                sum_ref[...] += column_sum(part.astype(F32))

        each(rows // WIDE_CHUNK, grad)
    turn(held, turned_ref)
    stage.put(3, 4)
    row_ref[0:1, :half] = vec_ref[2:3, lanes_at(core, half)]
    row_ref[0:1, half : 2 * half] = jnp.zeros((1, half), F32)
    row_ref[0:1, 2 * half :] = vec_ref[3:4, lanes_at(core, half)]
    row_ref[1:2, :half] = jnp.full((1, half), HEAD_SIZE ** (-0.5), F32)
    row_ref[1:2, half:] = jnp.ones((1, 2 * half), F32)
    weight_ref = stage[3]

    def project(index):
        lanes = lanes_at(index, half)
        part = dot_nn(normed_ref[...], weight_ref[:, lanes]) + row_ref[0:1, lanes]
        qkv_ref[:, lanes] = (part.astype(BF).astype(F32) * row_ref[1:2, lanes]).astype(BF)

    each(3, project)
    stage.put(1)
    down_ref = stage[6]
    piece = dact_ref.shape[1] // 4

    def back(index):
        dact_ref[:, lanes_at(index, piece)] = dot_nt(held[...], down_ref[lanes_at(index, piece)]).astype(BF)

    each(4, back)


def item_of_place(where_ref, place, items):
    found = jnp.int32(0)
    for index in range(items):
        found = found + (place >= where_ref[ENDS + index]).astype(jnp.int32)
    return found


def tiles_meet(where_ref, one, other, parts, items):
    span = TILE * parts
    first, last = min(one, other), max(one, other)
    return item_of_place(where_ref, first * span + span - 1, items) >= item_of_place(
        where_ref, last * span, items
    )


def near_tiles(tile, tiles):
    return max(0, tile - 1), min(tiles, tile + 2)


def far_pairs(tiles):
    return [(one, other) for one in range(tiles) for other in range(tiles) if abs(one - other) > 1]


def any_far(where_ref, tiles, parts, items):
    found = jnp.bool_(False)
    for one, other in far_pairs(tiles):
        if one < other:
            found = found | tiles_meet(where_ref, one, other, parts, items)
    return found


def attend_kernel(parts, items, where_ref, stage, vec_ref, wide_ref, normed_ref, asks_ref):
    unpack_rows(stage[2], vec_ref)
    xhat_ref, kv_ref, attended_ref, logsum_ref = (stage.out(index) for index in range(4))
    far_a_ref, far_b_ref = stage[0], stage[1]
    stage.start(3, 4)
    rows, width = far_a_ref.shape
    tiles = rows // TILE
    span = parts * TILE
    both = 2 * HEAD_SIZE
    half = width // 2
    core = where_ref[1]
    for rel_c, ref in enumerate((far_a_ref, far_b_ref)):
        xhat, unused = standardise(ref[...].astype(F32))
        xhat_ref[rel_c * rows : (rel_c + 1) * rows] = xhat.astype(BF)
        normed_ref[rel_c * rows : (rel_c + 1) * rows] = normed_rows(xhat, vec_ref, 0)
    stage.put(0)
    row = lax.broadcasted_iota(jnp.int32, (2 * TILE, 2 * TILE), 0)
    block = 2 * where_ref[0] + (where_ref[1] ^ (row // TILE))
    for tile in range(tiles):
        asks_ref[tile] = item_at((tile * TILE + row % TILE) * parts + block, where_ref, items)
    lane = lax.broadcasted_iota(jnp.int32, (1, span), 1)
    slot = lane // TILE
    block = 2 * (where_ref[0] ^ (slot // 2)) + (where_ref[1] ^ (slot % 2))
    key_item = [item_at((tile * TILE + lane % TILE) * parts + block, where_ref, items) for tile in range(tiles)]
    weight_ref = stage[3]
    row_ref = jnp.concatenate([jnp.zeros((1, half), F32), vec_ref[3:4, lanes_at(core, half)]], axis=1)
    far_kv = (dot_nn(normed_ref[...], weight_ref[...]) + row_ref).astype(BF)
    qkv_ref = stage[4]
    for tile in range(tiles):
        for slot in range(2):
            at = slice(slot * rows + tile * TILE, slot * rows + (tile + 1) * TILE)
            kv_ref[tile * span + slot * TILE : tile * span + (slot + 1) * TILE] = qkv_ref[at, half:]
            kv_ref[tile * span + (slot + 2) * TILE : tile * span + (slot + 3) * TILE] = far_kv[at]
    stage.put(1)
    for index in range(half // both):
        wide_ref[:, 2 * index * both : (2 * index + 1) * both] = kv_ref[:, half + index * both : half + (index + 1) * both]
        wide_ref[:, (2 * index + 1) * both : (2 * index + 2) * both] = jnp.ones((tiles * span, both), BF)

    def attend(index, tile, first, last):
        lanes = lanes_at(index, both)
        at = slice(first * span, last * span)
        places = [pl.ds(pl.multiple_of(rel_c * rows + tile * TILE, TILE), TILE) for rel_c in range(2)]
        query = stack_heads(jnp.concatenate([qkv_ref[place, lanes] for place in places], axis=0))
        score = dot_nt(query, kv_ref[at, lanes])
        asked = asks_ref[tile][:, :1]
        allowed = jnp.concatenate([asked == key_item[other] for other in range(first, last)], axis=1)
        score = jnp.where(jnp.concatenate([allowed, allowed], axis=0), score, MASKED)
        best = jnp.max(score, axis=1, keepdims=True)
        weight = jnp.exp(score - best).astype(BF)
        mixed = dot_nn(weight, wide_ref[at, lanes_at(index, 2 * both)])
        total = mixed[:, both:]
        logsum_ref[index, pl.ds(tile, 1)] = (best + jnp.log(total)).T[:1]
        mixed = mixed[:, :both] / total
        attended = jnp.where(lanes_below((both, both), HEAD_SIZE), mixed[:both], mixed[both:]).astype(BF)
        for rel_c, place in enumerate(places):
            attended_ref[place, lanes] = attended[rel_c * TILE : (rel_c + 1) * TILE]

    def pair(index):
        for tile in range(tiles):
            attend(index, tile, *near_tiles(tile, tiles))

    each(half // both, pair)

    def widen(index, tile, other):
        lanes = lanes_at(index, both)
        at = slice(other * span, (other + 1) * span)
        places = [slice(rel_c * rows + tile * TILE, rel_c * rows + (tile + 1) * TILE) for rel_c in range(2)]
        query = stack_heads(jnp.concatenate([qkv_ref[place, lanes] for place in places], axis=0))
        allowed = asks_ref[tile][:, :1] == key_item[other]
        score = dot_nt(query, kv_ref[at, lanes])
        score = jnp.where(jnp.concatenate([allowed, allowed], axis=0), score, MASKED)
        best = jnp.max(score, axis=1, keepdims=True)
        mixed = dot_nn(jnp.exp(score - best).astype(BF), wide_ref[at, lanes_at(index, 2 * both)])
        total = mixed[:, both:]
        fresh = best + jnp.log(total)
        known = jnp.broadcast_to(logsum_ref[index, pl.ds(tile, 1)], (both, 2 * both)).T
        top = jnp.maximum(known, fresh)
        logsum = top + jnp.log(jnp.exp(known - top) + jnp.exp(fresh - top))
        logsum_ref[index, pl.ds(tile, 1)] = logsum.T[:1]
        first = lanes_below((both, both), HEAD_SIZE)
        scale, mixed = jnp.exp(known - logsum), mixed[:, :both] / total * jnp.exp(fresh - logsum)
        before = jnp.concatenate([attended_ref[place, lanes] for place in places], axis=0).astype(F32)
        after_all = before * jnp.where(first, scale[:both], scale[both:]) + jnp.where(first, mixed[:both], mixed[both:])
        for rel_c, place in enumerate(places):
            attended_ref[place, lanes] = after_all[rel_c * TILE : (rel_c + 1) * TILE].astype(BF)

    for one, two in far_pairs(tiles):
        pl.when(tiles_meet(where_ref, one, two, parts, items))(
            lambda one=one, two=two: each(half // both, lambda index: widen(index, one, two))
        )


def gelu_with_slope(values):
    bell = jnp.exp(-0.5 * values * values)
    inverse = 1.0 / (1.0 + (0.3275911 * 0.5**0.5) * jnp.abs(values))
    series = 1.061405429
    for coefficient in (-1.453152027, 1.421413741, -0.284496736, 0.254829592):
        series = series * inverse + coefficient
    tail = 0.5 * (series * inverse) * bell
    normal = jnp.where(values >= 0, 1.0 - tail, tail)
    return values * normal, normal + values * bell * ((2.0 * math.pi) ** -0.5)


def set_block(where_ref, rel_y, low_z, high_z):
    return 2 * (where_ref[2] ^ (low_z + 2 * high_z)) + (where_ref[3] ^ rel_y)


def mlp_kernel(where_ref, stage, vec_ref, bias_ref, mid_ref, joined, normed, grad, turned, dbefore_ref):
    py_ref, ux_ref, dz_ref = stage.out(0), stage.out(2), stage.out(4)
    xhat_ref, inverse_ref, mid_own_ref, branch_ref, swap_ref, act_ref, bias_sum_ref = (
        stage.out(index) for index in range(6, 13)
    )
    unpack_rows(stage[4], vec_ref)
    att_own_ref, att_sib_ref, own_ref, sib_ref, raw_ref, out_ref = (stage[index] for index in range(6))
    stage.start(6, 7, 8)
    x, core, z, y = (where_ref[index] for index in range(4))
    rows, width = own_ref.shape
    half = width // 2
    piece = act_ref.shape[1] // 4
    joined[:, :half] = att_own_ref[...]
    joined[:rows, half:] = att_sib_ref[rows:]
    joined[rows:, half:] = att_sib_ref[:rows]

    def project(index):
        lanes = lanes_at(index, 256)
        branch = dot_nn(joined[...], out_ref[:, lanes]) + vec_ref[4:5, lanes]
        branch_ref[:, lanes] = branch[:rows].astype(BF)
        branch = vec_ref[5:6, lanes] * branch
        mid_ref[:rows, lanes] = own_ref[:, lanes].astype(F32) + branch[:rows]
        mid_ref[rows:, lanes] = sib_ref[:, lanes].astype(F32) + branch[rows:]

    each(width // 256, project)

    mid_own_ref[...] = mid_ref[:rows]

    def norm(index):
        at = lanes_at(index, WIDE_CHUNK)
        xhat, inverse = standardise(mid_ref[at])
        normed[at] = (xhat * vec_ref[6:7] + vec_ref[7:8]).astype(BF)
        xhat_ref[at] = xhat.astype(BF)
        inverse_ref[at] = inverse

    each(2 * rows // WIDE_CHUNK, norm)
    stage.put(6, 7, 8, 9)
    count = piece // 128
    for unit in range(8):
        for part in range(count):
            row = 10 * width // 128 + unit * count + part
            bias_ref[unit : unit + 1, part * 128 : (part + 1) * 128] = raw_ref[row : row + 1]
    up_ref, dact_ref, turned_ref = stage[6], stage[7], stage[8]
    size = grad.shape[0] // 8

    def hidden(index):
        rel_x = 1 - index
        count = normed.shape[0] // 2
        for side in range(2):
            at = lanes_at(2 * rel_x + side, piece)
            bias = bias_ref[pl.ds(hidden_unit(where_ref, rel_x, side), 1)]
            total = jnp.zeros((1, piece), F32)
            for part in range(2):
                here = slice(part * count, (part + 1) * count)
                act, slope = gelu_with_slope(dot_nn(normed[here], up_ref[:, at]) + bias)
                act_ref[here, at] = act.astype(BF)
                dbefore = (dact_ref[here, at].astype(F32) * slope).astype(BF)
                dbefore_ref[here, at] = dbefore
                total = total + column_sum(dbefore.astype(F32))
            bias_sum_ref[:, at] = total
            grad[:, side * piece : (side + 1) * piece] = dot_nn(turned_ref[...], act_ref[:, at]).astype(BF)

        def lay(index):
            low_z, high_z, rel_y = index // 4, index // 2 % 2, index % 2
            first = set_block(where_ref, rel_y, low_z, high_z) * size
            most = dz_ref.shape[4] - size
            dz_ref[low_z, high_z, rel_x, rel_y, :size] = grad[pl.ds(pl.multiple_of(first, size), size), :piece]
            dz_ref[low_z, high_z, rel_x, rel_y, size:] = grad[pl.ds(pl.multiple_of(first, size), most), piece:]
            py_ref[rel_y, rel_x, lanes_at(2 * low_z + high_z, size - most)] = grad[
                pl.ds(pl.multiple_of(first + most, size - most), size - most), piece:
            ]

        each(8, lay)

    each(2, hidden)
    stage.put(4, 5, 11, 12)
    turn(normed, turned)
    block = 2 * size

    def up(index):
        rel_y, high_z = index // 2, index % 2
        unit = 2 * (x ^ (z // 2) ^ high_z) + (y ^ rel_y)
        grad[:, :piece] = dot_nn(turned[...], dbefore_ref[:, lanes_at(unit, piece)]).astype(BF)
        for rel_x in range(2):
            to = pl.ds(pl.multiple_of(py_ref.shape[2] - 2 * block + high_z * block, 64), block)
            py_ref[rel_y, rel_x, to] = grad[lanes_at(own_block(where_ref, rel_x, 0), block), :piece]
            ux_ref[rel_x, rel_y, high_z] = grad[lanes_at(own_block(where_ref, rel_x, 1), block), :piece]

    for index in range(4):
        up(index)
    stage.put(0, 1, 2, 3)

    def back(index):
        lanes = lanes_at(index, 256)
        total = dot_nt(dbefore_ref[...], up_ref[lanes])
        swap_ref[:, lanes] = total.astype(BF)

    each(width // 256, back)


def middle(parts, items, where_ref, stage, vec_ref, sum_ref, datt_ref, held, chosen, packed):
    dmid_ref, a_ref, o_ref = stage.out(0), stage.out(1), stage.out(5)
    keep_ref, got_ref, xhat_ref, inverse_ref, own_ref, sib_ref, raw_ref = (stage[index] for index in range(7))
    stage.start(10, 9, 7, 8, 11, 12, 13)
    unpack_rows(raw_ref, vec_ref)
    rows, width = own_ref.shape
    half = width // 2
    core = where_ref[1]
    left_is_own = lanes_below((rows, half), half // 2) == (core == 0)
    for rel_c, ref in enumerate((own_ref, sib_ref)):
        here = slice(rel_c * rows, (rel_c + 1) * rows)
        there = slice((1 - rel_c) * rows, (2 - rel_c) * rows)
        valid = valid_at(where_ref, rel_c, 0, rows, parts, items)
        dnormed = keep_ref[here].astype(F32) + got_ref[there].astype(F32)
        xhat, inverse = xhat_ref[here].astype(F32), inverse_ref[here]
        dmid = ref[...].astype(F32) * valid + standardise_grad(vec_ref[6:7] * dnormed, xhat, inverse)
        dbranch = (vec_ref[5:6] * dmid).astype(BF)
        held[here] = dbranch
        if rel_c == 0:
            dmid_ref[...] = dmid
            sum_ref[0:1] = column_sum(dbranch.astype(F32))
            sum_ref[1:2] = column_sum(dmid * stage[10][...].astype(F32))
            sum_ref[2:3] = column_sum(dnormed * xhat)
            sum_ref[3:4] = column_sum(dnormed)
    stage.put(0)
    stage.start(14, 15)
    datt_ref[...] = dot_nt(held[...], stage[9][...]).astype(BF)
    att_own_ref, att_sib_ref = stage[7], stage[8]
    for rel_c in range(2):
        here = slice(rel_c * rows, (rel_c + 1) * rows)
        there = slice((1 - rel_c) * rows, (2 - rel_c) * rows)
        other = pltpu.roll(att_sib_ref[there].astype(F32), half // 2, 1)
        chosen[here] = jnp.where(left_is_own, att_own_ref[here].astype(F32), other).astype(BF)
    grad = dot_tn(held[...], chosen[...])
    count, unit_rows = packed.shape[1:3]
    for index in range(count):
        left, right = pack_unit(grad[2 * index * unit_rows : 2 * (index + 1) * unit_rows])
        packed[0, index] = left.astype(BF)
        packed[1, index] = right.astype(BF)

    units = 6 * unit_rows

    def lay(index):
        rel_x, rel_y, block = index // 8, index // 4 % 2, index % 4
        here = packed.at[where_ref[0] ^ rel_x, set_block(where_ref, rel_y, block // 2, block % 2)]
        a_ref[rel_x, rel_y, pl.ds(pl.multiple_of(units + 16 * block, 16), 16)] = here[:16]
        o_ref[rel_y, rel_x, lanes_at(block, unit_rows - 16)] = here[16:]

    each(16, lay)
    stage.put(5, 6)


def pack_unit(unit):
    half = unit.shape[0] // 2
    width = unit.shape[1]
    top, bottom = unit[:half], unit[half:]
    first = lanes_below((half, width), width // 2)
    left = jnp.where(first, top, pltpu.roll(bottom, width // 2, 1))
    right = jnp.where(first, pltpu.roll(top, width // 2, 1), bottom)
    return left, right


def join_heads(stacked_turned):
    stacked = stacked_turned.T
    count = stacked.shape[0] // 2
    return jnp.where(
        lanes_below((count, stacked.shape[1]), HEAD_SIZE), stacked[:count], stacked[count:]
    )


def query_items(where_ref, tile, parts, items):
    lane = lax.broadcasted_iota(jnp.int32, (1, 4 * TILE), 1)
    rel_c = (lane // TILE) % 2
    block = 2 * where_ref[0] + (where_ref[1] ^ rel_c)
    return item_at((tile * TILE + lane % TILE) * parts + block, where_ref, items)


def fill_key_items(where_ref, item_ref, tiles, parts, items):
    row = lax.broadcasted_iota(jnp.int32, (TILE, item_ref.shape[1]), 0)
    for tile in range(tiles):
        for slot in range(parts):
            block = own_block(where_ref, slot // 2, slot % 2)
            at = (tile * parts + slot) * TILE
            item_ref[at : at + TILE] = item_at((tile * TILE + row) * parts + block, where_ref, items)


def both_heads(array):
    return jnp.concatenate([array, array], axis=1)


def attend_grad(
    parts, items, where_ref, stage, datt_ref, dquery_ref, dkeys_ref, dvalues_ref, asks_ref, item_ref, turned_ref, dk, dv, dq
):
    attended_ref, qkv_ref, kv_ref, logsum_ref = stage[7], stage[11], stage[12], stage[13]
    half = datt_ref.shape[1]
    rows = datt_ref.shape[0] // 2
    tiles = rows // TILE
    span = parts * TILE
    scale = HEAD_SIZE ** (-0.5)
    turned_ref[...] = kv_ref[:, :half].T
    fill_key_items(where_ref, item_ref, tiles, parts, items)
    for tile in range(tiles):
        asks_ref[tile : tile + 1] = query_items(where_ref, tile, parts, items)
    some_far = any_far(where_ref, tiles, parts, items)

    def pair(index, carry):
        lanes = lanes_at(index, 2 * HEAD_SIZE)
        value_lanes = pl.ds(pl.multiple_of(half + index * 2 * HEAD_SIZE, 2 * HEAD_SIZE), 2 * HEAD_SIZE)
        dk[...] = jnp.zeros_like(dk)
        dv[...] = jnp.zeros_like(dv)

        def places(tile):
            return [pl.ds(pl.multiple_of(rel_c * rows + tile * TILE, TILE), TILE) for rel_c in range(2)]

        def visit(tile, at):
            query = stack_heads(jnp.concatenate([qkv_ref[place, lanes] for place in places(tile)], axis=0))
            grad = jnp.concatenate([datt_ref[place, lanes] for place in places(tile)], axis=0)
            attended = jnp.concatenate([attended_ref[place, lanes] for place in places(tile)], axis=0)
            product = (grad.astype(F32) * attended.astype(F32)).T
            delta = jnp.concatenate([column_sum(product[:HEAD_SIZE]), column_sum(product[HEAD_SIZE:])], axis=1)
            grad = stack_heads(grad)
            score = dot_nt(kv_ref[at, lanes], query)
            allowed = both_heads(item_ref[at]) == asks_ref[pl.ds(tile, 1)]
            prob = jnp.exp(jnp.where(allowed, score, MASKED) - logsum_ref[index, pl.ds(tile, 1)])
            dprob = dot_nt(kv_ref[at, value_lanes], grad)
            dscore = (prob * (dprob - delta)).astype(BF)
            dv[at] += dot_nn(prob.astype(BF), grad)
            dk[at] += dot_nn(dscore, query)
            return dot_nn(turned_ref[lanes, at], dscore)

        for tile in range(tiles):
            first, last = near_tiles(tile, tiles)
            dq[tile] = visit(tile, slice(first * span, last * span))

        @pl.when(some_far)
        def far():
            def add(step):
                tile, other = step // tiles, step % tiles
                found = jnp.bool_(False)
                for one, two in far_pairs(tiles):
                    found = found | ((step == one * tiles + two) & tiles_meet(where_ref, one, two, parts, items))

                @pl.when(found)
                def meet():
                    at = pl.ds(pl.multiple_of(other * span, span), span)
                    dq[tile] += visit(tile, at)

            each(tiles * tiles, add)

        for tile in range(tiles):
            dquery = (join_heads(dq[tile]) * scale).astype(BF)
            for rel_c, place in enumerate(places(tile)):
                dquery_ref[place, lanes] = dquery[rel_c * TILE : (rel_c + 1) * TILE]
            for slot in range(parts):
                to = slice(slot * rows + tile * TILE, slot * rows + (tile + 1) * TILE)
                at = slice(tile * span + slot * TILE, tile * span + (slot + 1) * TILE)
                dkeys_ref[to, lanes] = dk[at].astype(BF)
                dvalues_ref[to, lanes] = dv[at].astype(BF)
        return carry

    for index in range(half // (2 * HEAD_SIZE)):
        pair(index, 0)


def twice(half_row, where_ref):
    row = both_heads(half_row)
    return jnp.where(lanes_below(row.shape, half_row.shape[1]) == (where_ref[1] == 0), row, 0.0)


def qkv_grad(where_ref, stage, vec_ref, sum_ref, dquery_ref, dkeys_ref, dvalues_ref, normed_ref, packed):
    a_ref, b_ref = stage.out(1), stage.out(3)
    near_ref, far_ref = stage[14], stage[15]
    rows, width = near_ref.shape
    core, z, y = where_ref[1], where_ref[2], where_ref[3]
    normed_ref[:rows] = normed_rows(near_ref[...], vec_ref, 0)
    normed_ref[rows:] = normed_rows(far_ref[...], vec_ref, 0)
    sum_ref[4:5] = twice(column_sum(dquery_ref[...].astype(F32)), where_ref)
    sum_ref[5:6] = twice(column_sum(dvalues_ref[...].astype(F32)), where_ref)
    for part, ref in enumerate((dquery_ref, dkeys_ref, dvalues_ref)):
        grad = dot_tn(ref[...], normed_ref[: ref.shape[0]])
        size = grad.shape[0] // 4
        for unit in range(4):
            for at_x in range(2):
                left, right = pack_unit(
                    grad[unit * size : (unit + 1) * size, at_x * width // 2 : (at_x + 1) * width // 2]
                )
                packed[2 * at_x, 4 * part + unit] = left.astype(BF)
                packed[2 * at_x + 1, 4 * part + unit] = right.astype(BF)

    def lay(index):
        rel_x, rel_y, at = index // 12, index // 6 % 2, index % 6
        unit = where_ref[UNIT_LIST + 24 * core + 12 * (y ^ rel_y) + 6 * (z % 2) + at]
        a_ref[rel_x, rel_y, lanes_at(at, packed.shape[2])] = packed[own_block(where_ref, rel_x, 0), unit]
        b_ref[rel_y, rel_x, at] = packed[own_block(where_ref, rel_x, 1), unit]

    each(24, lay)
    stage.put(1, 2, 3, 4)


def backward_kernel(
    parts, items, where_ref, stage, vec_ref, datt_ref, held, chosen, gpacked, normed_ref, packed, asks_ref, item_ref,
    turned_ref, dk, dv, dq,
):
    sum_ref, dquery_ref, dkeys_ref, dvalues_ref = (stage.out(index) for index in (10, 7, 8, 9))
    middle(parts, items, where_ref, stage, vec_ref, sum_ref, datt_ref, held, chosen, gpacked)
    attend_grad(
        parts, items, where_ref, stage, datt_ref, dquery_ref, dkeys_ref, dvalues_ref, asks_ref, item_ref, turned_ref,
        dk, dv, dq,
    )
    stage.put(7, 8, 9)
    qkv_grad(where_ref, stage, vec_ref, sum_ref, dquery_ref, dkeys_ref, dvalues_ref, normed_ref, packed)


def tokens_grad_kernel(parts, items, where_ref, stage, vec_ref):
    own_ref, far_ref, send_ref, keep_ref, sum_ref = (stage.out(index) for index in range(5))
    dquery_ref, dkeys_ref, dvalues_ref, weight_ref, near_ref, beyond_ref = (stage[index] for index in range(6))
    rows, width = own_ref.shape
    half = dquery_ref.shape[1]
    gain = jnp.zeros((1, width), F32)
    shift = gain
    for slot in (1, 3, 2, 0):
        at = slice(slot * rows, (slot + 1) * rows)
        part = dot_nt(dkeys_ref[at], weight_ref[:, half : 2 * half]) + dot_nt(dvalues_ref[at], weight_ref[:, 2 * half :])
        if slot < 2:
            part = part + dot_nt(dquery_ref[at], weight_ref[:, :half])
        xhat = (near_ref if slot < 2 else beyond_ref)[(slot % 2) * rows : (slot % 2 + 1) * rows].astype(F32)
        gain = gain + column_sum(part * xhat)
        shift = shift + column_sum(part)
        if slot % 2:
            send_ref[slot // 2 * rows : (slot // 2 + 1) * rows] = part.astype(BF)
        elif slot:
            far_ref[...] = part.astype(BF)
        else:
            own_ref[...] = part.astype(BF)
    stage.put(0, 1)
    unpack_rows(stage[6], vec_ref)
    act_ref, down_ref, cot_ref, cot_sib_ref, back_ref, bias_d_ref, bias_up_ref = (stage[index] for index in range(7, 14))
    feed = dot_nn(act_ref[...], down_ref[...])
    keep_ref[...] = feed[:rows] + vec_ref[8:9]
    send_ref[2 * rows :] = feed[rows:].astype(BF)
    stage.put(2, 3)
    scale = column_sum(cot_ref[...].astype(F32) * valid_at(where_ref, 0, 0, rows, parts, items) * keep_ref[...])
    scale = scale + column_sum(cot_sib_ref[...].astype(F32) * valid_at(where_ref, 1, 0, rows, parts, items) * feed[rows:])
    sum_ref[0:1] = gain
    sum_ref[1:2] = shift
    sum_ref[2:4] = back_ref[4:6]
    sum_ref[4:8] = back_ref[0:4]
    sum_ref[8:9] = bias_d_ref[...]
    sum_ref[9:10] = scale
    for at_x in range(2):
        one = bias_up_ref[:, at_x * width : (at_x + 1) * width]
        two = bias_up_ref[:, (1 - at_x) * width : (2 - at_x) * width]
        here = jnp.where(where_ref[0] == 0, one, two)
        for at_c in range(2):
            at = 10 + 2 * at_x + at_c
            sum_ref[at : at + 1] = jnp.where(where_ref[1] == at_c, here, 0.0)
    sum_ref[14:] = jnp.zeros((2, width), F32)


def unpack_unit(unit, target, first):
    half, lanes = unit.shape
    target[first : first + half] = unit[:, : target.shape[1]]
    target[first + half : first + 2 * half] = pltpu.roll(unit, lanes // 2, 1)[:, : target.shape[1]]


def sum_of(*terms):
    total = terms[0].astype(F32)
    for term in terms[1:]:
        total = total + term.astype(F32)
    return total


def fold_sums(sums):
    lanes = sums.shape[1] // 2
    return jnp.concatenate([sums[:, :lanes], sums[:, lanes:]], axis=0)


def second_step_kernel(where_ref, stage):
    dz_keep, dz_got, py_keep, py_got, a_ref, ux_keep, ux_got, b_got, o_ref = (stage[index] for index in range(9))
    dz_ref, x_ref, y_ref = (stage.out(index) for index in range(3))
    dz_ref[...] = sum_of(dz_keep[...], dz_got[...]).astype(BF)
    stage.put(0)
    count, rows = py_keep.shape[0], a_ref.shape[1]
    x_ref[:count] = sum_of(py_keep[...], py_got[...]).astype(BF)
    for rel_y in range(2):
        x_ref[count + rel_y * rows : count + (rel_y + 1) * rows] = a_ref[rel_y]
    stage.put(1)
    block = ux_keep.shape[1]
    for high_z in range(2):
        y_ref[high_z * block : (high_z + 1) * block] = sum_of(ux_keep[high_z], ux_got[high_z]).astype(BF)
    unit_rows = b_got.shape[2]
    first = 2 * block
    for rel_x in range(2):
        for index in range(6):
            y_ref[first : first + unit_rows] = b_got[rel_x, index]
            first += unit_rows
    rows = o_ref.shape[1]
    for rel_x in range(2):
        y_ref[first : first + rows] = o_ref[rel_x]
        first += rows


def mlp_rows(side, where_ref, ux_keep, ux_got, y_got, py_keep, py_got, x_got, ref):
    block = ux_keep.shape[1]
    lead = ref.shape[1] - block
    same = where_ref[2] % 2 == where_ref[1]
    for high_z in range(2):
        at = slice(2 * lead + high_z * block, 2 * lead + (high_z + 1) * block)
        own = sum_of(py_keep[at], py_got[at], x_got[at])
        sib = sum_of(ux_keep[high_z], ux_got[high_z], y_got[high_z * block : (high_z + 1) * block])
        at = slice(high_z * lead, (high_z + 1) * lead)
        ref[high_z, :lead] = sum_of(py_keep[at], py_got[at], x_got[at]).astype(BF)
        here = jnp.where(same, sib, own) if side else jnp.where(same, own, sib)
        ref[high_z, lead:] = here.astype(BF)


def third_step_kernel(where_ref, stage):
    send_ref, x_ref, a_ref = (stage.out(index) for index in range(3))
    mlp_rows(1, where_ref, *(stage[index] for index in range(6)), send_ref)
    stage.put(0)
    b_keep, b_got, o_keep, o_got = (stage[index] for index in range(6, 10))
    sum_refs, a_keep, a_got = [stage[index] for index in range(10, 14)], stage[14], stage[15]
    unit_rows, rows = b_keep.shape[1], o_keep.shape[0]
    units = 6 * unit_rows
    for index in range(6):
        at = slice(index * unit_rows, (index + 1) * unit_rows)
        x_ref[at] = sum_of(b_keep[index], b_got[at]).astype(BF)
    x_ref[units : units + rows] = sum_of(o_keep[...], o_got[...]).astype(BF)
    x_ref[units + rows :] = fold_sums(sum_of(*(ref[...] for ref in sum_refs))).astype(BF)
    stage.put(1)
    a_ref[...] = sum_of(a_keep[...], a_got[...]).astype(BF)


def mlp_kept_kernel(where_ref, stage):
    mlp_rows(0, where_ref, *(stage[index] for index in range(6)), stage.out(0))


def last_rows(side, a_keep, a_got, a_far, b_keep, y_got, b_far, o_keep, y_rest, x_ref, ref):
    unit_rows, rows = b_keep.shape[1], o_keep.shape[0]
    units, most = 6 * unit_rows, rows // 2
    half = units // 2
    at = slice(side * half, (side + 1) * half)
    ref[:half] = sum_of(a_keep[at], a_got[at], a_far[at]).astype(BF)
    for index in range(3):
        at = slice(index * unit_rows, (index + 1) * unit_rows)
        far = slice(side * half + index * unit_rows, side * half + (index + 1) * unit_rows)
        ref[half + index * unit_rows : half + (index + 1) * unit_rows] = sum_of(
            b_keep[index], y_got[at], b_far[far]
        ).astype(BF)
    for high_z in range(2):
        first, block = units + high_z * unit_rows, 2 * side + high_z
        at = slice(units + 16 * block, units + 16 * (block + 1))
        ref[first : first + 16] = sum_of(a_keep[at], a_got[at], a_far[at]).astype(BF)
        at = slice(high_z * most, (high_z + 1) * most)
        far = units + side * rows + high_z * most
        ref[first + 16 : first + unit_rows] = sum_of(o_keep[at], y_rest[at], b_far[far : far + most]).astype(BF)
    ref[units + 2 * unit_rows :] = sum_of(x_ref[...], b_far[units + 2 * rows :]).astype(BF)


def fourth_step_kernel(where_ref, stage):
    send_ref, dz_ref, dtok_ref = (stage.out(index) for index in range(3))
    last_rows(1, *(stage[index] for index in range(9)), send_ref)
    stage.put(0)
    dz_ref[...] = sum_of(stage[9][...], stage[10][...], stage[11][...]).astype(BF)
    stage.put(1)
    dtok_ref[...] = sum_of(stage[12][...], stage[13][...]).astype(BF)


def kept_kernel(where_ref, stage):
    mlp_ref, mlp_kept, kept_ref, dz_ref = (stage.out(index) for index in range(4))
    mlp_ref[...] = sum_of(stage[12][1], stage[13][1]).astype(BF)
    mlp_kept[...] = sum_of(stage[12][0], stage[13][0]).astype(BF)
    stage.put(0, 1)
    last_rows(0, *(stage[index] for index in range(9)), kept_ref)
    stage.put(2)
    dz_ref[...] = sum_of(stage[9][...], stage[10][...], stage[11][...]).astype(BF)


def fifth_step_kernel(where_ref, stage, held):
    kept_ref, last_got, dz_kept, dz_got = (stage[index] for index in range(4))
    send_ref, dz_ref, keep_ref, dz_low_ref = (stage.out(index) for index in range(4))
    core, z, y = where_ref[1], where_ref[2], where_ref[3]
    unit_rows = held.shape[1]
    for index in range(6):
        at = slice(index * unit_rows, (index + 1) * unit_rows)
        held[index] = sum_of(kept_ref[at], last_got[at]).astype(BF)
    rest = sum_of(kept_ref[6 * unit_rows :], last_got[6 * unit_rows :]).astype(BF)
    for side, ref, owner_z in ((1, send_ref, z ^ 2), (0, keep_ref, z)):
        for index in range(3):
            at = where_ref[UNIT_LIST + 48 + ((core * 2 + y) * 4 + owner_z) * 3 + index]
            ref[index * unit_rows : (index + 1) * unit_rows] = held[at]
        ref[3 * unit_rows : 4 * unit_rows] = rest[side * unit_rows : (side + 1) * unit_rows]
        ref[4 * unit_rows :] = rest[2 * unit_rows :]
    stage.put(0)
    for side, ref in enumerate((dz_low_ref, dz_ref)):
        ref[...] = sum_of(dz_kept[0, side], dz_got[0, side]).astype(BF)


def finish_kernel(where_ref, stage, rows_ref, out_rows_ref, flat):
    mlp_kept, mlp_far, dz_low, dz_far, last_keep, last_far = (stage[index] for index in range(6))
    down_ref, up_ref, out_ref, vec_ref, qkv_ref = (stage.out(index) for index in range(5))
    size, block = down_ref.shape[0], up_ref.shape[0]
    lanes = up_ref.shape[1]
    mlp, dz = sum_of(mlp_kept[...], mlp_far[...]), sum_of(dz_low[...], dz_far[...])
    lead = mlp.shape[0] - block
    most = size - lead
    up_ref[...] = mlp[lead:]
    down_ref[:, :lanes] = dz[:size]
    down_ref[:most, lanes:] = dz[size : size + most]
    down_ref[most:, lanes:] = mlp[:lead]
    stage.put(0, 1)
    out_rows_ref[...] = jnp.zeros_like(out_rows_ref)
    last = sum_of(last_keep[...], last_far[...])
    half = size // 2
    unpack_unit(last[3 * half : 4 * half], out_rows_ref, 0)
    out_ref[...] = out_rows_ref[...].T[: out_ref.shape[0], : out_ref.shape[1]]
    sums = last[4 * half :]
    count = sums.shape[0] // 2
    for row in range(count):
        flat[:, 2 * row * lanes : (2 * row + 1) * lanes] = sums[row : row + 1]
        flat[:, (2 * row + 1) * lanes : (2 * row + 2) * lanes] = sums[count + row : count + row + 1]
    share = vec_ref.shape[1]
    start = (4 * set_block(where_ref, 0, 0, 0) + own_block(where_ref, 0, 0)) * share
    window = flat[:, pl.ds(pl.multiple_of(start // 128 * 128, 128), 512)]
    window = pltpu.roll(jnp.broadcast_to(window, (8, 512)), (512 - start % 128) % 512, 1)
    vec_ref[...] = window[:1, :share]
    stage.put(2, 3)
    rows_ref[...] = jnp.zeros_like(rows_ref)
    for unit in range(3):
        unpack_unit(last[unit * half : (unit + 1) * half], rows_ref, 2 * unit * half)
    qkv_ref[...] = rows_ref[...].T[: qkv_ref.shape[0], : qkv_ref.shape[1]]


def rows_kernel(parts, items, where_ref, stage, vec_ref):
    keep_ref, late_ref, far_ref, own_ref, dmid_ref, raw_ref, feed_ref, mid_ref = (stage[index] for index in range(8))
    unpack_rows(raw_ref, vec_ref)
    rows = own_ref.shape[0]
    dnormed = sum_of(keep_ref[...], late_ref[:rows], far_ref[...])
    xhat, inverse = standardise(own_ref[...].astype(F32))
    stage.out(0)[...] = (dmid_ref[...] + standardise_grad(vec_ref[0:1] * dnormed, xhat, inverse)).astype(BF)
    stage.put(0)
    valid = valid_at(where_ref, 0, 0, rows, parts, items)
    feed = sum_of(feed_ref[...], late_ref[rows:])
    stage.out(1)[...] = (valid * (mid_ref[...] + vec_ref[9:10] * feed)).astype(BF)


def swapped(array, axis, bit):
    length = lax.axis_size(axis)
    return lax.ppermute(array, axis, [(i, i ^ bit) for i in range(length)])


def to_core(array):
    return swapped(array, "blk", 1)


def to_x(array):
    return swapped(array, "blk", 2)


def to_y(array):
    return swapped(array, "dp", 1)


def to_z(array):
    return swapped(array, "dp", 2)


def to_zz(array):
    return swapped(array, "dp", 4)


def after(done, *arrays):
    return lax.optimization_barrier((done, *arrays))[1:]


def first_rows(count):
    def cut(where_ref, source, target):
        return [(source.at[:count], target)]

    return cut


def entry(array, index):
    def cut(where_ref, source, target):
        return [(source.at[index], target)]

    return (array.shape[1:], 1, cut)


def first_and_last_rows(count):
    def cut(where_ref, source, target):
        return [(source.at[:count], target.at[:count]), (source.at[2 * count :], target.at[count:])]

    return cut


def rows_of_entry(array, index, first, last):
    def cut(where_ref, source, target):
        return [(source.at[index, first:last], target)]

    return ((last - first, *array.shape[2:]), 1, cut)


def joined_rows(array, index, pieces):
    def cut(where_ref, source, target):
        moves, to = [], 0
        for first, last in pieces:
            at = source.at[first:last] if index is None else source.at[index, first:last]
            moves.append((at, target.at[to : to + last - first]))
            to += last - first
        return moves

    count = sum(last - first for first, last in pieces)
    return ((count, array.shape[-1]), len(pieces), cut)


def some_rows(array, first, last):
    def cut(where_ref, source, target):
        return [(source.at[first:last], target)]

    return ((last - first, *array.shape[1:]), 1, cut)


def own_columns(first):
    def cut(where_ref, source, target):
        half = source.shape[0] // 2
        return [
            (source.at[:, lanes_at(where_ref[1] + 2 * part, half)], target.at[:, (part - first) * half : (part - first + 1) * half])
            for part in range(first, 3)
        ]

    return cut


def own_hidden(axis):
    def cut(where_ref, source, target):
        pairs = []
        piece = target.shape[axis] // 4
        for rel_x in range(2):
            for side in range(2):
                at = lanes_at(hidden_unit(where_ref, rel_x, side), piece)
                to = slice((2 * rel_x + side) * piece, (2 * rel_x + side + 1) * piece)
                pairs.append((source.at[at], target.at[to]) if axis == 0 else (source.at[:, at], target.at[:, to]))
        return pairs

    return cut


def both_head_rows(where_ref, source, target):
    half = target.shape[0] // 2
    return [
        (source.at[lanes_at(where_ref[1], half), :], target.at[:half]),
        (source.at[lanes_at(1 - where_ref[1], half), :], target.at[half:]),
    ]


def own_head_rows(where_ref, source, target):
    return [(source.at[lanes_at(where_ref[1], target.shape[0]), :], target)]


def on_device_aligned(tokens, lengths, w_qkv, w_out, w_up, w_down, vectors, cotangent):
    tokens, cotangent = tokens[0], cotangent[0]
    rows, width = tokens.shape
    hidden = w_up.shape[1]
    items = lengths.shape[1]
    parts = lax.axis_size("blk")
    sets = lax.axis_size("dp")
    position, turn = lax.axis_index("blk"), lax.axis_index("dp")
    x, core, z, y = position // 2, position % 2, turn // 2, turn % 2
    where = lengths
    half = width // 2
    inner = hidden // 2
    piece = hidden // sets
    both = 2 * rows
    total_rows = parts * rows
    block = width // parts
    share = width // sets
    names = (parts, items)
    zs = sets // 2
    all_columns = ((width, 3 * half), 3, own_columns(0))
    kv_columns = ((width, 2 * half), 2, own_columns(1))
    up_columns = ((width, inner), 4, own_hidden(1))
    down_rows = ((inner, width), 4, own_hidden(0))
    head_rows = ((half, width), 1, own_head_rows)
    out_rows = ((width, width), 2, both_head_rows)

    far_a = to_x(tokens)
    sib = to_core(tokens)
    cot_sib = to_core(cotangent)

    vec = vectors.reshape(-1, 128)
    rows_of_vec = pltpu.VMEM((10, width), F32)

    xhat_near, qkv_near, dact, dfeed_turned, bias_d_sum = staged_call(
        functools.partial(prepare_kernel, *names),
        where,
        (tokens, sib, vec, w_qkv, cotangent, cot_sib, w_down),
        [low(both, width), low(both, 3 * half), low(both, inner), low(width, both), full(1, width)],
        cuts={3: all_columns, 6: down_rows},
        scratch=[rows_of_vec, pltpu.VMEM((both, width), BF), pltpu.VMEM((both, width), BF), pltpu.VMEM((2, 3 * half), F32)],
    )

    far_a, qkv_near, dact = lax.optimization_barrier((far_a, qkv_near, dact))
    far_b = to_core(far_a)

    xhat_far, kv, attended, logsum = staged_call(
        functools.partial(attend_kernel, *names),
        where,
        (far_a, far_b, vec, w_qkv, qkv_near),
        [low(both, width), low(total_rows, width), low(both, half), full(half // (2 * HEAD_SIZE), rows // TILE, 4 * TILE)],
        cuts={3: kv_columns},
        scratch=[
            rows_of_vec,
            pltpu.VMEM((total_rows, 2 * half), BF),
            pltpu.VMEM((both, width), BF),
            pltpu.VMEM((rows // TILE, 2 * TILE, 2 * TILE), jnp.int32),
        ],
    )
    attended_sib = to_core(attended)

    unit_rows = share // 2
    lead = 32
    py, us, dz = low(2, 4 * lead + 2 * block, piece), low(2, 2, block, piece), low(2, 2, 2, 2 * share - lead, piece)
    (py_keep, py_send, ux_keep, ux_send, dz_keep, dz_send, xhat_two, inverse_two, mid, branch, swap, act,
     bias_up_sum) = staged_call(
        mlp_kernel,
        where,
        (attended, attended_sib, tokens, sib, vec, w_out, w_up, dact, dfeed_turned),
        [py, py, us, us, dz, dz, low(both, width), full(both, 1), full(rows, width), low(rows, width), low(both, width),
         low(both, inner), full(1, inner)],
        cuts={5: out_rows, 6: up_columns},
        late=(6, 7, 8),
        pairs=(0, 2, 4),
        scratch=[rows_of_vec, pltpu.VMEM((sets, piece), F32), pltpu.VMEM((both, width), F32),
                 pltpu.VMEM((both, width), BF), pltpu.VMEM((both, width), BF), pltpu.VMEM((width, 2 * piece), BF),
                 pltpu.VMEM((width, both), BF), pltpu.VMEM((both, inner), BF)],
    )
    swap_got = to_core(swap)
    ux_send, ux_keep = to_core(ux_send), to_core(ux_keep)
    py_got = to_y(py_send)
    ux_got = to_x(ux_send)
    dz_got = to_z(dz_send)

    dmid, a_keep, a_send, b_keep, b_send, o_keep, o_send, dquery, dkeys, dvalues, back_sums = staged_call(
        functools.partial(backward_kernel, *names),
        where,
        (swap, swap_got, xhat_two, inverse_two, cotangent, cot_sib, vec, attended, attended_sib, w_out, branch,
         qkv_near, kv, logsum, xhat_near, xhat_far),
        [full(rows, width)] + [low(2, 6 * unit_rows + 64, half)] * 2 + [low(2, 6, unit_rows, half)] * 2
        + [low(2, 4 * unit_rows - 64, half)] * 2
        + [low(both, half), low(total_rows, half), low(total_rows, half), full(8, width)],
        cuts={9: head_rows},
        late=tuple(range(7, 16)),
        pairs=(1, 3, 5),
        tables=True,
        scratch=[rows_of_vec, pltpu.VMEM((both, half), BF), pltpu.VMEM((both, width), BF),
                 pltpu.VMEM((both, half), BF), pltpu.VMEM((2, sets, unit_rows, half), BF),
                 pltpu.VMEM((total_rows, width), BF), pltpu.VMEM((4, 12, unit_rows, half), BF),
                 pltpu.VMEM((rows // TILE, 4 * TILE), jnp.int32), pltpu.VMEM((total_rows, 2 * TILE), jnp.int32),
                 pltpu.VMEM((half, total_rows), BF), pltpu.VMEM((total_rows, 2 * HEAD_SIZE), F32),
                 pltpu.VMEM((total_rows, 2 * HEAD_SIZE), F32),
                 pltpu.VMEM((rows // TILE, 2 * HEAD_SIZE, 4 * TILE), F32)],
    )
    six, top = 6 * unit_rows, 2 * share - lead
    step = functools.partial(staged_call, grant=STEP_GRANT)
    b_send, b_keep = to_core(b_send), to_core(b_keep)
    py_got, ux_got, dz_got, b_send, b_keep = after(back_sums, py_got, ux_got, dz_got, b_send, b_keep)
    count = py_keep.shape[1]
    dz_step, x_step, y_step = staged_call(
        second_step_kernel,
        where,
        (dz_keep, dz_got, py_keep, py_got, a_send, ux_keep, ux_got, b_send, o_send),
        [low(*dz_keep.shape[1:]), low(count + 2 * six + 128, half), low(2 * block + 2 * six + 8 * unit_rows - 128, half)],
        cuts={index: entry(array, 1)
              for index, array in ((0, dz_keep), (1, dz_got), (2, py_keep), (3, py_got), (5, ux_keep), (6, ux_got))},
    )
    dz_far, x_got, y_got = to_zz(dz_step), to_x(x_step), to_y(y_step)
    (back_sums,) = after(y_step, back_sums)
    dtok_own, dtok_far, late_send, feed_keep, sums = staged_call(
        functools.partial(tokens_grad_kernel, *names),
        where,
        (dquery, dkeys, dvalues, w_qkv, xhat_near, xhat_far, vec, act, w_down, cotangent, cot_sib, back_sums,
         bias_d_sum, bias_up_sum),
        [low(rows, width), low(rows, width), low(3 * rows, width), full(rows, width), full(16, width)],
        cuts={3: all_columns, 8: down_rows},
        scratch=[rows_of_vec],
        grant=LATE_GRANT,
    )
    sums_core, sums_y = to_core(sums), to_y(sums)
    sums_far = to_core(sums_y)
    dz_far, x_got, y_got, sums_core, sums_y, sums_far = lax.optimization_barrier(
        (dz_far, x_got, y_got, sums_core, sums_y, sums_far)
    )

    rest = 4 * unit_rows - 64
    first = 2 * block + 2 * six

    def mlp_cuts(side):
        pieces = [(side * 2 * lead, (side + 1) * 2 * lead), (4 * lead, 4 * lead + 2 * block)]
        return {0: entry(ux_keep, 0), 1: entry(ux_got, 0), 2: some_rows(y_got, 0, 2 * block),
                3: joined_rows(py_keep, 0, pieces), 4: joined_rows(py_got, 0, pieces), 5: joined_rows(x_got, None, pieces)}

    operands = (ux_keep, ux_got, y_got, py_keep, py_got, x_got)
    mlp_send, b_step, a_step = step(
        third_step_kernel,
        where,
        (*operands, b_keep, y_got, o_keep, y_got, sums, sums_core, sums_y, sums_far, a_keep, x_got),
        [low(2, lead + block, piece), low(six + rest + 32, half), low(six + 64, half)],
        cuts=mlp_cuts(1)
        | {6: entry(b_keep, 1), 7: some_rows(y_got, 2 * block + six, first), 8: entry(o_keep, 1),
           9: some_rows(y_got, first + rest, first + 2 * rest), 14: entry(a_keep, 1),
           15: some_rows(x_got, count + six + 64, count + 2 * (six + 64))},
    )
    mlp_got, b_far, a_far = to_z(mlp_send), to_x(b_step), to_y(a_step)
    (mlp_keep,) = step(
        mlp_kept_kernel, where, after(mlp_send, *operands), [low(2, lead + block, piece)], cuts=mlp_cuts(0)
    )
    (late_send,) = after(mlp_send, late_send)
    late_got = to_core(late_send)
    mlp_got, b_far, a_far, late_got, mlp_keep = lax.optimization_barrier((mlp_got, b_far, a_far, late_got, mlp_keep))

    first, part = 2 * block + 2 * six, rest // 2

    def side_cuts(side):
        start = 2 * block + side * six // 2
        return {
            0: entry(a_keep, 0), 1: some_rows(x_got, count, count + six + 64),
            3: rows_of_entry(b_keep, 0, 3 * side, 3 * side + 3),
            4: some_rows(y_got, start, start + six // 2),
            6: rows_of_entry(o_keep, 0, side * part, (side + 1) * part),
            7: some_rows(y_got, first + side * part, first + (side + 1) * part),
            8: some_rows(b_step, six + rest, six + rest + 32),
            9: rows_of_entry(dz_keep, 0, side, side + 1), 10: rows_of_entry(dz_got, 0, side, side + 1),
            11: some_rows(dz_far, side, side + 1),
        }

    operands = (a_keep, x_got, a_far, b_keep, y_got, b_far, o_keep, y_got, b_step, dz_keep, dz_got, dz_far)
    last = low(six + 2 * unit_rows + 32, half)
    last_send, dz_step, dtok_step = step(
        fourth_step_kernel,
        where,
        (*operands, dtok_far, late_got),
        [last, low(1, 2, top, piece), low(rows, width)],
        cuts=side_cuts(1) | {13: some_rows(late_got, rows, both)},
    )
    last_got, dz_x, dtok_x = to_z(last_send), to_x(dz_step), to_x(dtok_step)
    mlp_step, mlp_kept, last_keep, dz_kept = step(
        kept_kernel,
        where,
        after(last_send, *operands, mlp_keep, mlp_got),
        [low(lead + block, piece)] * 2 + [last, low(1, 2, top, piece)],
        cuts=side_cuts(0),
    )
    mlp_far = to_zz(mlp_step)
    last_send, dz_y, last_kept, dz_low = step(
        fifth_step_kernel,
        where,
        (last_keep, last_got, dz_kept, dz_x),
        [low(4 * unit_rows + 32, half), low(top, piece), low(4 * unit_rows + 32, half), low(top, piece)],
        scratch=[pltpu.VMEM((6, unit_rows, half), BF)],
        tables=True,
    )
    last_far, dz_y = to_zz(last_send), to_y(dz_y)

    (dtok_x,) = after(dz_low, dtok_x)
    grad_tokens, out = staged_call(
        functools.partial(rows_kernel, *names),
        where,
        (dtok_own, late_got, dtok_x, tokens, dmid, vec, feed_keep, mid),
        [low(rows, width), low(rows, width)],
        cuts={1: ((both, width), 2, first_and_last_rows(rows))},
        scratch=[rows_of_vec],
        grant=STEP_GRANT,
    )

    mlp_far, dz_y, last_far = after(grad_tokens, mlp_far, dz_y, last_far)
    g_w_down, g_w_up, g_w_out, g_vec, g_w_qkv = step(
        finish_kernel,
        where,
        (mlp_kept, mlp_far, dz_low, dz_y, last_kept, last_far),
        [full(share, 2 * piece), full(block, piece), full(block, share), full(1, vectors.shape[0] // (sets * parts)),
         full(block, 3 * share)],
        scratch=[pltpu.VMEM((384, 256), F32), pltpu.VMEM((128, 256), F32), pltpu.VMEM((1, 16 * width + 512), F32)],
    )
    return (out[None], grad_tokens[None], g_w_qkv, g_w_out, g_w_up, g_w_down.T, g_vec.reshape(-1))


def is_aligned(mesh, tokens, w_up):
    parts, sets = mesh.shape["blk"], mesh.shape["dp"]
    width, hidden = w_up.shape
    rows = tokens.shape[1] // parts
    return (
        parts == 4
        and sets == 2 * parts
        and rows == 4 * TILE
        and (hidden // sets) % 128 == 0
        and (width // 2) % 128 == 0
        and (width // sets) % 32 == 0
        and width == H * HEAD_SIZE
    )


def solution(mesh):
    def run(tokens, lengths, w_qkv, w_out, w_up, w_down, vectors, cotangent):
        body = on_device_aligned if is_aligned(mesh, tokens, w_up) else on_device
        return jax.shard_map(
            body,
            mesh=mesh,
            in_specs=(
                P("dp", "blk", None),
                P("dp", None),
                P(),
                P(),
                P(),
                P(),
                P(),
                P("dp", "blk", None),
            ),
            out_specs=(
                P("dp", "blk", None),
                P("dp", "blk", None),
                P("blk", "dp"),
                P("blk", "dp"),
                P("blk", "dp"),
                P("blk", "dp"),
                P(("dp", "blk")),
            ),
            check_vma=False,
        )(tokens, lengths, w_qkv, w_out, w_up, w_down, vectors, cotangent)

    return run
```
